32 devices in a mesh: section: 4 (over y, core), dp: 8 (over z, x).
Axes of the slice: x: 2, y: 2, z: 4, core: 2. Of those that a mesh axis runs over, the one named last changes fastest.
Arguments:
- inputs: bfloat16 [4, 8, 512, 512], P(None, 'dp'), may hold values from -6 to 6
- segment_ids: int32 [4, 8, 512], P(None, 'dp'), may hold values from 0 to 7, never falling along the last dimension, each value on 1 to 256 neighbouring positions
- cotangent: bfloat16 [4, 8, 512, 512], P(None, 'dp'), may hold values from -6 to 6
- conv_weight: bfloat16 [8, 7, 512], P('section'), may hold values from -2 to 2
- conv_bias: bfloat16 [8, 512], P('section'), may hold values from -3 to 3
- norm_gain: bfloat16 [8, 512], P('section'), may hold values from 0.5 to 1.5
- norm_bias: bfloat16 [8, 512], P('section'), may hold values from -2 to 2
- up_weight: bfloat16 [8, 512, 1536], P('section'), may hold values from -0.25 to 0.25
- up_bias: bfloat16 [8, 1536], P('section'), may hold values from -3 to 3
- down_weight: bfloat16 [8, 1536, 512], P('section'), may hold values from -0.21875 to 0.21875
- down_bias: bfloat16 [8, 512], P('section'), may hold values from -2 to 2
- layer_scale: bfloat16 [8, 512], P('section'), may hold values from 0.5 to 1.5
Outputs:
- section_outputs: float32 [4, 4, 8, 512, 512], P('section', None, 'dp')
- input_grads: float32 [4, 4, 8, 512, 512], P('section', None, 'dp')
- grad_conv_weight: float32 [8, 7, 512], P('section', None, 'dp')
- grad_conv_bias: float32 [8, 512], P('section', 'dp')
- grad_norm_gain: float32 [8, 512], P('section', 'dp')
- grad_norm_bias: float32 [8, 512], P('section', 'dp')
- grad_up_weight: float32 [8, 512, 1536], P('section', 'dp')
- grad_up_bias: float32 [8, 1536], P('section', 'dp')
- grad_down_weight: float32 [8, 1536, 512], P('section', 'dp')
- grad_down_bias: float32 [8, 512], P('section', 'dp')
- grad_layer_scale: float32 [8, 512], P('section', 'dp')
The draws below stay inside these ranges and needn't reach their ends.
Inputs may be any that keep to these rules, and one draw needn't show every extreme that they name: `segment_ids`: within each row of 512 frames the numbers never fall; a run of equal numbers is one utterance of at most half of 512 frames.
All inputs are finite; a program needn't handle non-finite values.
Results may differ from the reference program's by a relative error of at most 0.02.
Values may be sent and summed in bfloat16 or wider, within the bound.
No kernel may reach another device: no remote copies, remote signals or barrier semaphores. Data moves between devices by JAX's collectives and lax.ppermute only.
A program may use at most 320 MiB of HBM per device.

```python
import math
import jax
import jax.numpy as jnp
import numpy as np
from jax import lax

D = 512
H = 1536
K = 7
L = 512
M = 4
ROWS = 8
LAYERS = 8
N_SECTION = 4


def strengthened(drawn, stream_key, source, target, blocks, factor):
    owner, partner = [(jnp.arange(drawn.shape[position]) // (drawn.shape[position] // blocks)).reshape([-1 if axis == position else 1 for axis in range(drawn.ndim)]) for position in (source, target)]
    chosen = jax.random.permutation(stream_key, blocks)[partner]
    strong = (owner == chosen) | (owner == (partner + blocks // 2) % blocks)
    return jnp.where(strong, factor * drawn, drawn)


def block_scale(key, extent, split, low, top_value):
    gain = 1.0
    for dim, blocks in split:
        heights = jax.random.uniform(jax.random.fold_in(jax.random.fold_in(key, 6), dim), (blocks,), jnp.float32, low / len(split), top_value / len(split))
        gain = gain * jnp.repeat(jnp.exp(heights), extent[dim] // blocks).reshape((-1,) + (1,) * (len(extent) - 1 - dim))
    return gain


def split_up(count, total, reach, lean):
    loads = [(1 << 20) // math.isqrt(grade ** lean) + 1 for grade in range(2, count + 1)]
    spare, given = total - reach - (count - 1), [1] * (count - 1)
    while spare > 0:
        candidates = [i for i in range(count - 1) if given[i] < reach]
        mass, remaining = sum([loads[i] for i in candidates]), spare
        for i in candidates:
            extra = min(reach - given[i], max(1, remaining * loads[i] // mass), spare)
            given[i] = given[i] + extra
            spare = spare - extra
    return np.array([reach] + given)


def uneven(stream_key, number_of, total, limit, skew):
    if number_of == 2:
        one = jax.random.randint(stream_key, (), max(1, total - limit), min(limit, total - 1) + 1)
        return jnp.stack([one, total - one])
    sizes = jnp.asarray(split_up(number_of, total, limit, skew), jnp.int32)
    couples = (number_of - 1) // 2
    source_of, receiver = sizes[1:1 + 2 * couples:2], sizes[2:2 + 2 * couples:2]
    room = jnp.minimum(source_of - 1, limit - receiver)
    passed = jax.random.randint(jax.random.fold_in(stream_key, 1), (couples,), 0, 1 << 20) % (room + 1)
    sizes = sizes.at[1:1 + 2 * couples:2].set(source_of - passed).at[2:2 + 2 * couples:2].set(receiver + passed)
    return sizes[jax.random.permutation(jax.random.fold_in(stream_key, 2), number_of)]


def bell_draw(own_key, extent, spread, most, cuts=(), kind=jnp.bfloat16):
    drawn = jax.random.normal(own_key, extent, jnp.float32) * spread
    if len(cuts) > 0:
        drawn = block_scale(own_key, extent, cuts, -0.22, 0.18) * drawn
    return jnp.clip(drawn, min=-most, max=most).astype(kind)


def bell_draw_with(key, extent, width, reach, cuts, heavy, dtype=jnp.bfloat16):
    values = width * jax.random.normal(key, extent, jnp.float32)
    if cuts:
        values = values * block_scale(key, extent, cuts, -0.22, 0.18)
    return jnp.clip(strengthened(values, jax.random.fold_in(key, 3), *heavy), -reach, reach).astype(dtype)


def setup_inputs(seed: int = 0) -> dict:
    streams_of = jax.random.split(jax.random.key(seed), 13)
    return {
        "inputs": bell_draw_with(streams_of[0], (M, ROWS, L, D), 1.0, 6.0, ((1, 8),), (1, 3, 8, 2.0)),
        "segment_ids": jax.vmap(lambda own: jnp.searchsorted(jnp.cumsum(uneven(own, max(L // 64, 3), L, L // 2, 1)), jnp.arange(L), side="right"))(jax.random.split(streams_of[1], M * ROWS)).reshape((M, ROWS, L)).astype(jnp.int32),
        "cotangent": bell_draw_with(streams_of[2], (M, ROWS, L, D), 1.0, 6.0, ((1, 8),), (1, 3, 8, 2.0)),
        "conv_weight": bell_draw(streams_of[3], (LAYERS, K, D), K ** -0.5, 2.0, ((0, 4),)),
        "conv_bias": bell_draw(streams_of[4], (LAYERS, D), 0.5, 3.0, ((0, 4),)),
        "norm_gain": jnp.clip(1.0 + 0.1 * jax.random.normal(streams_of[5], (LAYERS, D), jnp.float32), 0.5, 1.5).astype(jnp.bfloat16),
        "norm_bias": bell_draw(streams_of[6], (LAYERS, D), 0.3, 2.0, ((0, 4),)),
        "up_weight": bell_draw(streams_of[7], (LAYERS, D, H), D ** -0.5, 0.25, ((0, 4),)),
        "up_bias": bell_draw(streams_of[8], (LAYERS, H), 0.5, 3.0, ((0, 4),)),
        "down_weight": bell_draw(streams_of[9], (LAYERS, H, D), (H // 2) ** -0.5, 0.21875, ((0, 4),)),
        "down_bias": bell_draw(streams_of[10], (LAYERS, D), 0.3, 2.0, ((0, 4),)),
        "layer_scale": jnp.clip(0.5 + 1.0 * jax.random.uniform(streams_of[11], (LAYERS, D), jnp.float32) ** block_scale(streams_of[11], (LAYERS, D), ((0, 4),), -0.2, 0.2), 0.5, 1.5).astype(jnp.bfloat16),
    }


@jax.custom_vjp
def low(v):
    return lax.optimization_barrier(v.astype(jnp.bfloat16)).astype(jnp.float32)

@jax.custom_vjp
def low_back(v):
    return v

def low_keep(v):
    return (low(v), None)

def low_pass(kept, grad):
    return (grad,)

def back_keep(v):
    return (v, None)

def back_low(kept, grad):
    return (low(grad),)
low.defvjp(low_keep, low_pass)
low_back.defvjp(back_keep, back_low)

def joint_mask(segments):
    side_cells = K // 2
    length = segments.shape[-1]
    padded = jnp.pad(segments, ((0, 0), (side_cells, side_cells)), constant_values=-1)
    return jnp.stack([(padded[:, offset:offset + length] == segments).astype(jnp.float32) for offset in range(K)])[..., None]

def depthwise(joined, stream, kernel, conv_bias):
    side_cells = kernel.shape[0] // 2
    length = stream.shape[1]
    padded = jnp.pad(stream, ((0, 0), (side_cells, side_cells), (0, 0)))
    running = conv_bias
    for offset in range(kernel.shape[0]):
        running = running + kernel[offset] * padded[:, offset:offset + length] * joined[offset]
    return running

def normalize(conv_out, norm_gain, norm_shift):
    row_mean = lax.optimization_barrier(jnp.mean(conv_out, axis=-1, keepdims=True))
    centred = conv_out - row_mean
    row_var = lax.optimization_barrier(jnp.mean(centred * centred, axis=-1, keepdims=True))
    return centred * lax.rsqrt(row_var + 1e-06) * norm_gain + norm_shift

def block(stream, joined, layer_params):
    kernel, conv_bias, norm_gain, norm_shift, up_weight, up_bias, down_weight, down_bias, scale_vec = layer_params
    conv_out = depthwise(joined, stream, kernel, conv_bias)
    normed = low(normalize(conv_out, norm_gain, norm_shift))
    hidden_in = low_back(jnp.einsum('rtd,dh->rth', normed, up_weight, precision=lax.Precision.HIGHEST) + up_bias)
    hidden = low(jax.nn.gelu(hidden_in, approximate=False))
    branch = low_back(jnp.einsum('rth,hd->rtd', hidden, down_weight, precision=lax.Precision.HIGHEST) + down_bias)
    return stream + scale_vec * branch

def stack_forward(params, offsets, start, joined):
    stream = start
    outputs = []
    for section_no in range(N_SECTION):
        if section_no > 0:
            stream = low(low_back(stream))
        stream = stream + offsets[section_no]
        for inner in range(2):
            layer_no = 2 * section_no + inner
            stream = block(stream, joined, tuple((member[layer_no] for member in params)))
        outputs.append(stream)
    return jnp.stack(outputs)

def reference(inputs, segment_ids, cotangent, conv_weight, conv_bias, norm_gain, norm_bias, up_weight, up_bias, down_weight, down_bias, layer_scale):
    params = tuple((member.astype(jnp.float32) for member in (conv_weight, conv_bias, norm_gain, norm_bias, up_weight, up_bias, down_weight, down_bias, layer_scale)))

    def one_batch(totals, item):
        start, segments, seed_grad = item
        joined = joint_mask(segments)
        start_value = start.astype(jnp.float32)
        offsets = jnp.zeros((N_SECTION,) + start.shape, jnp.float32)

        def run_stack(params_in, offsets_in):
            return stack_forward(params_in, offsets_in, start_value, joined)
        outputs, pull = jax.vjp(run_stack, params, offsets)
        seeds = jnp.zeros_like(outputs).at[N_SECTION - 1].set(seed_grad.astype(jnp.float32))
        param_grads, offset_grads = pull(seeds)
        totals = tuple((held + fresh_grad for held, fresh_grad in zip(totals, param_grads)))
        return (totals, (outputs, offset_grads))
    initial = tuple((jnp.zeros_like(member) for member in params))
    totals, (outputs, offset_grads) = lax.scan(one_batch, initial, (inputs, segment_ids, cotangent))
    section_outputs = jnp.swapaxes(outputs, 0, 1)
    input_grads = jnp.swapaxes(offset_grads, 0, 1)
    return (section_outputs, input_grads, totals[0], totals[1], totals[2], totals[3], totals[4], totals[5], totals[6], totals[7], totals[8])
```

```python
import functools

import jax
import jax.numpy as jnp
from jax import lax
from jax.experimental import pallas as pl
from jax.experimental.pallas import tpu as pltpu
from jax.sharding import PartitionSpec as P

EPSILON = 1e-06
INV_SQRT2 = 0.7071067811865476
INV_SQRT_2PI = 0.3989422804014327
F32 = jnp.float32
BF16 = jnp.bfloat16
TILE = 32
PAD = 8
COLS = 256
VMEM_LIMIT = 60 * 2**20

CONV_B, GAIN, SHIFT, DOWN_B, SCALE, UP_B, VEC_ROWS = 7, 8, 9, 10, 11, 12, 16
XHAT, STREAM, BRANCH, NORMED, KINDS = 0, 1, 2, 3, 4


def lanes(column, width):
    return jnp.broadcast_to(column, (column.shape[0], width))


def spread_masks(mask_in, mask_rep):
    frames = mask_in.shape[0]

    def body(i, carry):
        rows = pl.ds(pl.multiple_of(i * TILE, TILE), TILE)
        block = mask_in[rows, :]
        for k in range(6):
            mask_rep[k, rows, :] = lanes(block[:, k : k + 1], 128)
        return carry

    lax.fori_loop(0, frames // TILE, body, 0)


def shifted_rows(window, offset, count):
    size = window.shape[0]
    return pltpu.roll(window, (size - offset) % size, 0)[PAD : PAD + count]


def widen(mask, width):
    return jnp.concatenate([mask] * (width // 128), axis=1)


MASK_OF = {1: 0, 2: 1, 3: 2, -1: 3, -2: 4, -3: 5}


def forward_kernel(layers, aliased, flags, x_hbm, mask_hbm, vec, own_up, own_down, peer_up, peer_down, *rest):
    rest = rest[aliased:]
    hid, dge, saved, rst, own_out, peer_out, send = rest[:7]
    (up_v, down_v, hid_v, dge_v, saved_v, rst_v, stream, acc, out_v, x_v, mask_v, mask_rep, w_sem, in_sem, o_sem, s_sem) = rest[7:]
    frames, width = acc.shape
    hidden = hid_v.shape[2]

    @pl.when(flags[0] == 1)
    def _():
        core = flags[1]
        pltpu.make_async_copy(x_hbm.at[flags[2]], x_v, in_sem.at[0]).start()
        pltpu.make_async_copy(mask_hbm.at[flags[3]], mask_v, in_sem.at[1]).start()
        for j in range(layers):
            for mine, ups, downs in ((True, own_up, own_down), (False, peer_up, peer_down)):

                @pl.when((core == j // 2) == mine)
                def _():
                    pltpu.make_async_copy(ups.at[j % 2], up_v.at[j], w_sem.at[j, 0]).start()
                    pltpu.make_async_copy(downs.at[j % 2], down_v.at[j], w_sem.at[j, 1]).start()

        stream[0:PAD, :] = jnp.zeros((PAD, width), F32)
        stream[PAD + frames : PAD + frames + PAD, :] = jnp.zeros((PAD, width), F32)
        pltpu.make_async_copy(mask_hbm.at[0], mask_v, in_sem.at[1]).wait()
        spread_masks(mask_v, mask_rep)
        pltpu.make_async_copy(x_hbm.at[0], x_v, in_sem.at[0]).wait()
        stream[PAD : PAD + frames, :] = x_v[...].astype(F32)

        def layer(j, carry):
            def conv_norm(i, c):
                base = pl.multiple_of(i * TILE, TILE)
                rows = pl.ds(base, TILE)
                window = stream[pl.ds(base, TILE + 2 * PAD), :]
                centre = window[PAD : PAD + TILE]
                total = vec[j, CONV_B : CONV_B + 1, :] + vec[j, 3:4, :] * centre
                for offset in (1, 2, 3, -1, -2, -3):
                    mask = widen(mask_rep[MASK_OF[offset], rows, :], width)
                    total = total + vec[j, offset + 3 : offset + 4, :] * (shifted_rows(window, offset, TILE) * mask)
                mean = jnp.mean(total, axis=1, keepdims=True)
                centred = total - mean
                rstd = lax.rsqrt(jnp.mean(centred * centred, axis=1, keepdims=True) + EPSILON)
                xhat = centred * rstd
                normed = xhat * vec[j, GAIN : GAIN + 1, :] + vec[j, SHIFT : SHIFT + 1, :]
                saved_v[j, XHAT, rows, :] = xhat.astype(BF16)
                saved_v[j, STREAM, rows, :] = centre.astype(BF16)
                saved_v[j, NORMED, rows, :] = normed.astype(BF16)
                rst_v[j, rows, :] = lanes(rstd, 128)
                return c

            lax.fori_loop(0, frames // TILE, conv_norm, 0)
            pltpu.make_async_copy(own_up.at[0], up_v.at[j], w_sem.at[j, 0]).wait()
            for n in range(hidden // COLS):
                cols = slice(n * COLS, (n + 1) * COLS)
                bias = vec[j, UP_B + n * COLS // width : UP_B + n * COLS // width + 1, (n * COLS) % width : (n * COLS) % width + COLS]
                value = jnp.dot(saved_v[j, NORMED], up_v[j, :, cols], preferred_element_type=F32) + bias
                phi_sum = 0.5 + 0.5 * lax.erf(value * INV_SQRT2)
                density = jnp.exp(value * value * -0.5) * INV_SQRT_2PI
                hid_v[j, :, cols] = (value * phi_sum).astype(BF16)
                dge_v[j, :, cols] = (phi_sum + value * density).astype(BF16)
            pltpu.make_async_copy(hid_v.at[j], hid.at[j], o_sem.at[j, 0]).start()
            pltpu.make_async_copy(dge_v.at[j], dge.at[j], o_sem.at[j, 1]).start()
            pltpu.make_async_copy(rst_v.at[j], rst.at[j], o_sem.at[j, 2]).start()
            pltpu.make_async_copy(own_down.at[0], down_v.at[j], w_sem.at[j, 1]).wait()
            acc[...] = jnp.dot(hid_v[j], down_v[j], preferred_element_type=F32)
            odd = lax.rem(j, 2) == 1

            def finish(i, c):
                base = pl.multiple_of(i * TILE, TILE)
                rows = pl.ds(base, TILE)
                inner = pl.ds(pl.multiple_of(base + PAD, 8), TILE)
                branch = acc[rows, :] + vec[j, DOWN_B : DOWN_B + 1, :]
                fresh = stream[inner, :] + vec[j, SCALE : SCALE + 1, :] * branch
                rounded = fresh.astype(BF16)
                saved_v[j, BRANCH, rows, :] = branch.astype(BF16)
                out_v[lax.div(j, 2), rows, :] = fresh
                x_v[rows, :] = rounded
                stream[inner, :] = jnp.where(odd, rounded.astype(F32), fresh)
                return c

            lax.fori_loop(0, frames // TILE, finish, 0)
            pltpu.make_async_copy(saved_v.at[j], saved.at[j], o_sem.at[j, 3]).start()
            return carry

        lax.fori_loop(0, layers, layer, 0)
        pltpu.make_async_copy(out_v.at[core], own_out, s_sem.at[0]).start()
        pltpu.make_async_copy(out_v.at[1 - core], peer_out, s_sem.at[1]).start()
        pltpu.make_async_copy(x_v, send, s_sem.at[2]).start()
        for j in range(layers):
            pltpu.make_async_copy(hid_v.at[j], hid.at[j], o_sem.at[j, 0]).wait()
            pltpu.make_async_copy(dge_v.at[j], dge.at[j], o_sem.at[j, 1]).wait()
            pltpu.make_async_copy(rst_v.at[j], rst.at[j], o_sem.at[j, 2]).wait()
            pltpu.make_async_copy(saved_v.at[j], saved.at[j], o_sem.at[j, 3]).wait()
        pltpu.make_async_copy(out_v.at[core], own_out, s_sem.at[0]).wait()
        pltpu.make_async_copy(out_v.at[1 - core], peer_out, s_sem.at[1]).wait()
        pltpu.make_async_copy(x_v, send, s_sem.at[2]).wait()


def backward_kernel(layers, aliased, flags, g_hbm, mask_hbm, vec, own_up, own_down, peer_up, peer_down, dge, saved, rst, *rest):
    rest = rest[aliased:]
    gb, gp, vec_out, own_out, peer_out, send = rest[:6]
    (up_v, down_v, dge_v, saved_v, rst_v, gb_v, gp_v, vg_v, stream, padded, out_v, x_v, mask_v, mask_rep, w_sem, in_sem, o_sem, s_sem) = rest[6:]
    frames, width = stream.shape
    hidden = dge_v.shape[2]
    nt = (((1,), (1,)), ((), ()))

    @pl.when(flags[0] == 1)
    def _():
        core = flags[1]
        pltpu.make_async_copy(g_hbm.at[flags[2]], x_v, in_sem.at[0]).start()
        pltpu.make_async_copy(mask_hbm.at[flags[3]], mask_v, in_sem.at[1]).start()
        for j in range(layers - 1, -1, -1):
            pltpu.make_async_copy(saved.at[j, 0:3], saved_v.at[j], w_sem.at[j, 2]).start()
            for mine, downs in ((True, own_down), (False, peer_down)):

                @pl.when((core == j // 2) == mine)
                def _():
                    pltpu.make_async_copy(downs.at[j % 2], down_v.at[j], w_sem.at[j, 1]).start()

            pltpu.make_async_copy(dge.at[j], dge_v.at[j], w_sem.at[j, 3]).start()
            for mine, ups in ((True, own_up), (False, peer_up)):

                @pl.when((core == j // 2) == mine)
                def _():
                    pltpu.make_async_copy(ups.at[j % 2], up_v.at[j], w_sem.at[j, 0]).start()

            pltpu.make_async_copy(rst.at[j], rst_v.at[j], w_sem.at[j, 4]).start()

        padded[0:PAD, :] = jnp.zeros((PAD, width), F32)
        padded[PAD + frames : PAD + frames + PAD, :] = jnp.zeros((PAD, width), F32)
        pltpu.make_async_copy(mask_hbm.at[0], mask_v, in_sem.at[1]).wait()
        spread_masks(mask_v, mask_rep)
        pltpu.make_async_copy(g_hbm.at[0], x_v, in_sem.at[0]).wait()
        stream[...] = x_v[...].astype(F32)

        def fold(value):
            return functools.reduce(jnp.add, [value[8 * i : 8 * i + 8] for i in range(value.shape[0] // 8)])

        def layer(step, carry):
            j = layers - 1 - step
            pltpu.make_async_copy(saved.at[0, 0:3], saved_v.at[j], w_sem.at[j, 2]).wait()
            zero = jnp.zeros((8, width), F32)

            def enter(i, c):
                rows = pl.ds(pl.multiple_of(i * TILE, TILE), TILE)
                g = stream[rows, :]
                scaled = (vec[j, SCALE : SCALE + 1, :] * g).astype(BF16)
                gb_v[j, rows, :] = scaled
                return (c[0] + fold(scaled.astype(F32)), c[1] + fold(saved_v[j, BRANCH, rows, :].astype(F32) * g))

            sums = lax.fori_loop(0, frames // TILE, enter, (zero, zero))
            vg_v[j, DOWN_B : DOWN_B + 1, :] = jnp.sum(sums[0], axis=0, keepdims=True)
            vg_v[j, SCALE : SCALE + 1, :] = jnp.sum(sums[1], axis=0, keepdims=True)
            pltpu.make_async_copy(gb_v.at[j], gb.at[j], o_sem.at[j, 0]).start()
            pltpu.make_async_copy(own_down.at[0], down_v.at[j], w_sem.at[j, 1]).wait()
            pltpu.make_async_copy(dge.at[0], dge_v.at[j], w_sem.at[j, 3]).wait()
            for n in range(hidden // COLS):
                cols = slice(n * COLS, (n + 1) * COLS)
                value = lax.dot_general(gb_v[j], down_v[j, cols, :], nt, preferred_element_type=F32)
                rounded = (value * dge_v[j, :, cols].astype(F32)).astype(BF16)
                gp_v[j, :, cols] = rounded
                row, start = UP_B + n * COLS // width, (n * COLS) % width
                vg_v[j, row : row + 1, start : start + COLS] = jnp.sum(rounded.astype(F32), axis=0, keepdims=True)
            pltpu.make_async_copy(gp_v.at[j], gp.at[j], o_sem.at[j, 1]).start()
            pltpu.make_async_copy(own_up.at[0], up_v.at[j], w_sem.at[j, 0]).wait()
            pltpu.make_async_copy(rst.at[0], rst_v.at[j], w_sem.at[j, 4]).wait()
            padded[PAD : PAD + frames, :] = lax.dot_general(gp_v[j], up_v[j], nt, preferred_element_type=F32)

            def norm_back(i, c):
                base = pl.multiple_of(i * TILE, TILE)
                rows = pl.ds(base, TILE)
                inner = pl.ds(pl.multiple_of(base + PAD, 8), TILE)
                grad = padded[inner, :]
                xhat = saved_v[j, XHAT, rows, :].astype(F32)
                rstd = widen(rst_v[j, rows, :], width)
                q = grad * vec[j, GAIN : GAIN + 1, :]
                mean_q = jnp.mean(q, axis=1, keepdims=True)
                mean_qx = jnp.mean(q * xhat, axis=1, keepdims=True)
                grad_conv = rstd * (q - mean_q - xhat * mean_qx)
                padded[inner, :] = grad_conv
                return (c[0] + fold(grad * xhat), c[1] + fold(grad), c[2] + fold(grad_conv))

            sums = lax.fori_loop(0, frames // TILE, norm_back, (zero, zero, zero))
            vg_v[j, GAIN : GAIN + 1, :] = jnp.sum(sums[0], axis=0, keepdims=True)
            vg_v[j, SHIFT : SHIFT + 1, :] = jnp.sum(sums[1], axis=0, keepdims=True)
            vg_v[j, CONV_B : CONV_B + 1, :] = jnp.sum(sums[2], axis=0, keepdims=True)
            even = lax.rem(j, 2) == 0
            half = lax.div(j, 2)
            for col in range(width // 128):
                cols = slice(col * 128, (col + 1) * 128)

                def conv_back(i, c):
                    base = pl.multiple_of(i * 2 * TILE, 2 * TILE)
                    rows = pl.ds(base, 2 * TILE)
                    window = padded[pl.ds(base, 2 * TILE + 2 * PAD), cols]
                    source = saved_v[j, STREAM, rows, cols].astype(F32)
                    centre = window[PAD : PAD + 2 * TILE]
                    total = stream[rows, cols] + vec[j, 3:4, cols] * centre
                    taps = [None] * 7
                    taps[3] = c[3] + fold(centre * source)
                    for offset in (1, 2, 3, -1, -2, -3):
                        term = shifted_rows(window, -offset, 2 * TILE) * mask_rep[MASK_OF[-offset], rows, :]
                        total = total + vec[j, offset + 3 : offset + 4, cols] * term
                        taps[offset + 3] = c[offset + 3] + fold(term * source)
                    rounded = total.astype(BF16)
                    out_v[half, rows, cols] = total
                    x_v[rows, cols] = rounded
                    stream[rows, cols] = jnp.where(even, rounded.astype(F32), total)
                    return tuple(taps)

                sums = lax.fori_loop(0, frames // (2 * TILE), conv_back, (jnp.zeros((8, 128), F32),) * 7)
                for k in range(7):
                    vg_v[j, k : k + 1, cols] = jnp.sum(sums[k], axis=0, keepdims=True)
            vg_v[j, VEC_ROWS - 1 : VEC_ROWS, :] = jnp.zeros((1, width), F32)
            return carry

        lax.fori_loop(0, layers, layer, 0)
        pltpu.make_async_copy(out_v.at[core], own_out, s_sem.at[0]).start()
        pltpu.make_async_copy(out_v.at[1 - core], peer_out, s_sem.at[1]).start()
        pltpu.make_async_copy(x_v, send, s_sem.at[2]).start()
        pltpu.make_async_copy(vg_v, vec_out, s_sem.at[3]).start()
        for j in range(layers):
            pltpu.make_async_copy(gb_v.at[j], gb.at[j], o_sem.at[j, 0]).wait()
            pltpu.make_async_copy(gp_v.at[j], gp.at[j], o_sem.at[j, 1]).wait()
        pltpu.make_async_copy(out_v.at[core], own_out, s_sem.at[0]).wait()
        pltpu.make_async_copy(out_v.at[1 - core], peer_out, s_sem.at[1]).wait()
        pltpu.make_async_copy(x_v, send, s_sem.at[2]).wait()
        pltpu.make_async_copy(vg_v, vec_out, s_sem.at[3]).wait()


ANY = pl.BlockSpec(memory_space=pl.ANY)
SMEM = pl.BlockSpec(memory_space=pltpu.SMEM)
VMEM = pl.BlockSpec(memory_space=pltpu.VMEM)


def run_forward(flags, x, masks, vec, weights, earlier):
    layers = vec.shape[0]
    frames, width = x.shape[1:]
    hidden = weights[0].shape[2]
    shapes = (
        jax.ShapeDtypeStruct((layers, frames, hidden), BF16),
        jax.ShapeDtypeStruct((layers, frames, hidden), BF16),
        jax.ShapeDtypeStruct((layers, KINDS, frames, width), BF16),
        jax.ShapeDtypeStruct((layers, frames, 128), F32),
        jax.ShapeDtypeStruct((frames, width), F32),
        jax.ShapeDtypeStruct((frames, width), F32),
        jax.ShapeDtypeStruct((frames, width), BF16),
    )
    aliased = len(earlier)
    return pl.pallas_call(
        functools.partial(forward_kernel, layers, aliased),
        out_shape=shapes,
        in_specs=[SMEM, ANY, ANY, VMEM] + [ANY] * 4 + [ANY] * aliased,
        out_specs=(ANY,) * len(shapes),
        input_output_aliases={8 + i: i for i in range(aliased)},
        scratch_shapes=[
            pltpu.VMEM((layers, width, hidden), BF16),
            pltpu.VMEM((layers, hidden, width), BF16),
            pltpu.VMEM((layers, frames, hidden), BF16),
            pltpu.VMEM((layers, frames, hidden), BF16),
            pltpu.VMEM((layers, KINDS, frames, width), BF16),
            pltpu.VMEM((layers, frames, 128), F32),
            pltpu.VMEM((frames + 2 * PAD, width), F32),
            pltpu.VMEM((frames, width), F32),
            pltpu.VMEM((2, frames, width), F32),
            pltpu.VMEM((frames, width), BF16),
            pltpu.VMEM((frames, 8), F32),
            pltpu.VMEM((6, frames, 128), F32),
            pltpu.SemaphoreType.DMA((layers, 2)),
            pltpu.SemaphoreType.DMA((2,)),
            pltpu.SemaphoreType.DMA((layers, 4)),
            pltpu.SemaphoreType.DMA((3,)),
        ],
        compiler_params=pltpu.CompilerParams(vmem_limit_bytes=VMEM_LIMIT),
        cost_estimate=pl.CostEstimate(flops=layers * 4 * frames * width * hidden, bytes_accessed=40 * 2**20, transcendentals=0),
    )(flags, x, masks, vec, *weights, *earlier)


def run_backward(flags, g, masks, vec, weights, state, earlier):
    layers = vec.shape[0]
    frames, width = g.shape[1:]
    hidden = weights[0].shape[2]
    shapes = (
        jax.ShapeDtypeStruct((layers, frames, width), BF16),
        jax.ShapeDtypeStruct((layers, frames, hidden), BF16),
        jax.ShapeDtypeStruct((layers, VEC_ROWS, width), F32),
        jax.ShapeDtypeStruct((frames, width), F32),
        jax.ShapeDtypeStruct((frames, width), F32),
        jax.ShapeDtypeStruct((frames, width), BF16),
    )
    aliased = len(earlier)
    return pl.pallas_call(
        functools.partial(backward_kernel, layers, aliased),
        out_shape=shapes,
        in_specs=[SMEM, ANY, ANY, VMEM] + [ANY] * 7 + [ANY] * aliased,
        out_specs=(ANY,) * len(shapes),
        input_output_aliases={11 + i: i for i in range(aliased)},
        scratch_shapes=[
            pltpu.VMEM((layers, width, hidden), BF16),
            pltpu.VMEM((layers, hidden, width), BF16),
            pltpu.VMEM((layers, frames, hidden), BF16),
            pltpu.VMEM((layers, 3, frames, width), BF16),
            pltpu.VMEM((layers, frames, 128), F32),
            pltpu.VMEM((layers, frames, width), BF16),
            pltpu.VMEM((layers, frames, hidden), BF16),
            pltpu.VMEM((layers, VEC_ROWS, width), F32),
            pltpu.VMEM((frames, width), F32),
            pltpu.VMEM((frames + 2 * PAD, width), F32),
            pltpu.VMEM((2, frames, width), F32),
            pltpu.VMEM((frames, width), BF16),
            pltpu.VMEM((frames, 8), F32),
            pltpu.VMEM((6, frames, 128), F32),
            pltpu.SemaphoreType.DMA((layers, 5)),
            pltpu.SemaphoreType.DMA((2,)),
            pltpu.SemaphoreType.DMA((layers, 2)),
            pltpu.SemaphoreType.DMA((4,)),
        ],
        compiler_params=pltpu.CompilerParams(vmem_limit_bytes=VMEM_LIMIT),
        cost_estimate=pl.CostEstimate(flops=layers * 4 * frames * width * hidden, bytes_accessed=40 * 2**20, transcendentals=0),
    )(flags, g, masks, vec, *weights, *state, *earlier)


def weight_kernel(first, hid_a, hid_b, gb_a, gb_b, nrm_a, nrm_b, gp_a, gp_b, down_out, up_out):
    tn = (((0,), (0,)), ((), ()))
    down = lax.dot_general(hid_a[0], gb_a[0], tn, preferred_element_type=F32)
    down_out[0] = (down + lax.dot_general(hid_b[0], gb_b[0], tn, preferred_element_type=F32)).astype(BF16)
    up = lax.dot_general(nrm_a[0, 0], gp_a[0], tn, preferred_element_type=F32)
    up_out[0] = (up + lax.dot_general(nrm_b[0, 0], gp_b[0], tn, preferred_element_type=F32)).astype(BF16)


def run_weights(first, hid_a, hid_b, gb_a, gb_b, saved_a, saved_b, gp_a, gp_b):
    frames, hidden = hid_a.shape[1:]
    width = gb_a.shape[2]
    count = hid_a.shape[0] // 2
    wide = pl.BlockSpec((1, frames, hidden), lambda i, first: (first[0] + i, 0, 0))
    narrow = pl.BlockSpec((1, frames, width), lambda i, first: (first[0] + i, 0, 0))
    normed = pl.BlockSpec((1, 1, frames, width), lambda i, first: (first[0] + i, NORMED, 0, 0))
    return pl.pallas_call(
        weight_kernel,
        out_shape=(
            jax.ShapeDtypeStruct((count, hidden, width), BF16),
            jax.ShapeDtypeStruct((count, width, hidden), BF16),
        ),
        grid_spec=pltpu.PrefetchScalarGridSpec(
            num_scalar_prefetch=1,
            grid=(count,),
            in_specs=[wide, wide, narrow, narrow, normed, normed, wide, wide],
            out_specs=(
                pl.BlockSpec((1, hidden, width), lambda i, first: (i, 0, 0)),
                pl.BlockSpec((1, width, hidden), lambda i, first: (i, 0, 0)),
            ),
        ),
        compiler_params=pltpu.CompilerParams(vmem_limit_bytes=VMEM_LIMIT),
        cost_estimate=pl.CostEstimate(flops=count * 8 * frames * width * hidden, bytes_accessed=24 * 2**20, transcendentals=0),
    )(first, hid_a, hid_b, gb_a, gb_b, saved_a, saved_b, gp_a, gp_b)


def frame_masks(segments):
    length = segments.shape[-1]
    padded = jnp.pad(segments, ((0, 0), (3, 3)), constant_values=-1)
    columns = [padded[:, 3 + offset : 3 + offset + length] == segments for offset in (1, 2, 3, -1, -2, -3)]
    columns += [jnp.zeros_like(columns[0])] * 2
    return jnp.stack(columns, axis=-1).astype(F32)


def ring_order(count):
    return list(range(0, count, 2)) + list(range(count - 1, 0, -2))


def ring_scatter(parts, directions, slicers, axis):
    count = lax.axis_size(axis)
    order = ring_order(count)
    place_of = [order.index(d) for d in range(count)]
    place = jnp.array(place_of, jnp.int32)[lax.axis_index(axis)]
    order_table = jnp.array(order, jnp.int32)

    def local(i, owner_place):
        device = order_table[lax.rem(owner_place + 2 * count, count)]
        return functools.reduce(jnp.add, [slicers[i](addend, device).astype(F32) for addend in parts[i]])

    flowing = [local(i, place - way).astype(BF16) for i, way in enumerate(directions)]
    for step in range(count - 1):
        arrived = [
            lax.ppermute(value, axis, [(order[p], order[(p + way) % count]) for p in range(count)])
            for value, way in zip(flowing, directions)
        ]
        flowing = []
        for i, way in enumerate(directions):
            total = arrived[i].astype(F32) + local(i, place - way * (2 + step))
            flowing.append(total.astype(BF16) if step < count - 2 else total)
    return flowing


def per_device(
    inputs,
    segment_ids,
    cotangent,
    conv_weight,
    conv_bias,
    norm_gain,
    norm_bias,
    up_weight,
    up_bias,
    down_weight,
    down_bias,
    layer_scale,
):
    micro, _, frames, width = inputs.shape
    hidden = up_weight.shape[2]
    shares = lax.axis_size("dp")
    section = lax.axis_index("section")
    chip, core = section // 2, section % 2
    exchange = [(0, 1), (1, 0), (2, 3), (3, 2)]

    small = jnp.concatenate(
        [
            conv_weight,
            conv_bias[:, None],
            norm_gain[:, None],
            norm_bias[:, None],
            down_bias[:, None],
            layer_scale[:, None],
            up_bias.reshape(2, -1, width),
            jnp.zeros((2, 1, width), BF16),
        ],
        axis=1,
    )
    small_peer = lax.ppermute(small, "section", exchange)
    up_peer = lax.ppermute(up_weight, "section", exchange)
    down_peer = lax.ppermute(down_weight, "section", exchange)
    vec = jnp.where(core == 0, jnp.concatenate([small, small_peer]), jnp.concatenate([small_peer, small])).astype(F32)
    weights = (up_weight, down_weight, up_peer, down_peer)
    masks = frame_masks(segment_ids[:, 0])
    inputs, cotangent = inputs[:, 0], cotangent[:, 0]

    def flags(active, index, micro_slot):
        return jnp.stack([jnp.asarray(v, jnp.int32) for v in (active, core, index, 2 * core + micro_slot)])

    first, last = (chip == 0).astype(jnp.int32), (chip == 1).astype(jnp.int32)
    down_pairs, up_pairs = [(0, 2), (1, 3)], [(2, 0), (3, 1)]
    state_a = run_forward(flags(first, 2 * core, 0), inputs, masks, vec, weights, ())
    sent_a = lax.ppermute(state_a[6], "section", down_pairs)
    state_b = run_forward(flags(first, 2 * core + 1, 1), inputs, masks, vec, weights, ())
    sent_b = lax.ppermute(state_b[6], "section", down_pairs)
    state_a = run_forward(flags(last, 0, 0), sent_a[None], masks, vec, weights, state_a)
    state_b = run_forward(flags(last, 0, 1), sent_b[None], masks, vec, weights, state_b)

    back_b = run_backward(flags(last, 2 * core + 1, 1), cotangent, masks, vec, weights, state_b[1:4], ())
    sent_b = lax.ppermute(back_b[5], "section", up_pairs)
    back_a = run_backward(flags(last, 2 * core, 0), cotangent, masks, vec, weights, state_a[1:4], ())
    sent_a = lax.ppermute(back_a[5], "section", up_pairs)
    back_b = run_backward(flags(first, 0, 1), sent_b[None], masks, vec, weights, state_b[1:4], back_b)
    back_a = run_backward(flags(first, 0, 0), sent_a[None], masks, vec, weights, state_a[1:4], back_a)

    def grads(first_layer):
        return run_weights(
            first_layer.reshape(1).astype(jnp.int32), state_a[0], state_b[0], back_a[0], back_b[0], state_a[2], state_b[2], back_a[1], back_b[1]
        )

    down_other, up_other = grads(2 * (1 - core))
    down_recv = lax.ppermute(down_other, "section", exchange)
    up_recv = lax.ppermute(up_other, "section", exchange)
    down_own, up_own = grads(2 * core)

    vec_sum = back_a[2] + back_b[2]
    vec_own = lax.dynamic_slice_in_dim(vec_sum, 2 * core, 2, 0)
    vec_other = lax.dynamic_slice_in_dim(vec_sum, 2 * (1 - core), 2, 0)
    vec_own = vec_own + lax.ppermute(vec_other, "section", exchange)
    by_width = vec_own[:, :UP_B].reshape(2, UP_B, shares, -1)
    by_hidden = vec_own[:, UP_B : UP_B + hidden // width].reshape(2, shares, hidden // width, -1).swapaxes(1, 2)
    packed = jnp.concatenate([by_width, by_hidden], axis=1).transpose(2, 0, 1, 3).reshape(shares, -1)
    packed = lax.psum_scatter(packed.astype(BF16), "dp", scatter_dimension=0, tiled=True).astype(F32)
    vec_share = packed.reshape(2, UP_B + hidden // width, width // shares)

    def slice_up(value, device):
        size = width // shares
        return lax.dynamic_slice_in_dim(value, device * size, size, 1)

    def slice_down(value, device):
        size = hidden // shares
        return lax.dynamic_slice_in_dim(value, device * size, size, 1)

    up_share, down_share = ring_scatter([[up_own, up_recv], [down_own, down_recv]], [1, -1], [slice_up, slice_down], "dp")

    def assemble(own_a, own_b, peer_a, peer_b):
        own = jnp.stack([own_a, own_b])
        other = lax.ppermute(jnp.stack([peer_a, peer_b]), "section", exchange)
        return jnp.where(core == 0, jnp.concatenate([own, other]), jnp.concatenate([other, own]))[None, :, None]

    section_outputs = assemble(state_a[4], state_b[4], state_a[5], state_b[5])
    input_grads = assemble(back_a[3], back_b[3], back_a[4], back_b[4])
    return (
        section_outputs,
        input_grads,
        vec_share[:, :7],
        vec_share[:, CONV_B],
        vec_share[:, GAIN],
        vec_share[:, SHIFT],
        up_share,
        vec_share[:, UP_B:].reshape(2, -1),
        down_share,
        vec_share[:, DOWN_B],
        vec_share[:, SCALE],
    )


def solution(mesh):
    in_specs = (
        P(None, "dp", None, None),
        P(None, "dp", None),
        P(None, "dp", None, None),
        P("section", None, None),
        P("section", None),
        P("section", None),
        P("section", None),
        P("section", None, None),
        P("section", None),
        P("section", None, None),
        P("section", None),
        P("section", None),
    )
    out_specs = (
        P("section", None, "dp", None, None),
        P("section", None, "dp", None, None),
        P("section", None, "dp"),
        P("section", "dp"),
        P("section", "dp"),
        P("section", "dp"),
        P("section", "dp", None),
        P("section", "dp"),
        P("section", "dp", None),
        P("section", "dp"),
        P("section", "dp"),
    )
    return jax.shard_map(per_device, mesh=mesh, in_specs=in_specs, out_specs=out_specs, check_vma=False)
```

```python
import functools

import jax
import jax.numpy as jnp
from jax import lax
from jax.experimental import pallas as pl
from jax.experimental.pallas import tpu as pltpu
from jax.sharding import PartitionSpec as P

EPSILON = 1e-06
INV_SQRT2 = 0.7071067811865476
INV_SQRT_PI = 0.5641895835477563
LOG2_E = 1.4426950408889634
F32 = jnp.float32
BF16 = jnp.bfloat16
TILE = 32
PAD = 8
COLS = 256
VMEM_LIMIT = 60 * 2**20

CONV_B, GAIN, SHIFT, DOWN_B, SCALE, UP_B, VEC_ROWS = 7, 8, 9, 10, 11, 12, 16
XHAT, STREAM, NORMED, KINDS = 0, 1, 2, 3
LANES = 128
OFFSETS = (1, 2, 3, -1, -2, -3)
MASK_OF = {offset: k for k, offset in enumerate(OFFSETS)}


def slabs(width):
    return [slice(c, c + LANES) for c in range(0, width, LANES)]


def row_sum(parts):
    return jnp.sum(functools.reduce(jnp.add, parts), axis=1, keepdims=True)


def fold(value):
    return functools.reduce(jnp.add, [value[8 * i : 8 * i + 8] for i in range(value.shape[0] // 8)])


def clear_edges(padded, frames):
    for slab in range(padded.shape[0]):
        padded[slab, 0:PAD, :] = jnp.zeros((PAD, LANES), F32)
        padded[slab, PAD + frames : PAD + frames + PAD, :] = jnp.zeros((PAD, LANES), F32)


def build_masks(seg_v, masks):
    frames = masks.shape[1]
    seg_v[0:PAD, :] = jnp.full((PAD, LANES), -1.0, F32)
    seg_v[PAD + frames : PAD + frames + PAD, :] = jnp.full((PAD, LANES), -1.0, F32)

    def body(i, carry):
        base = pl.multiple_of(i * 64, 64)
        here = seg_v[pl.ds(base + PAD, 64), :]
        for k, offset in enumerate(OFFSETS):
            there = seg_v[pl.ds(base + PAD + offset, 64), :]
            masks[k, pl.ds(base, 64), :] = jnp.where(there == here, 1.0, 0.0)
        return carry

    lax.fori_loop(0, frames // 64, body, 0)


def forward_kernel(layers, aliased, flags, x_hbm, seg_hbm, vec, own_up, own_down, peer_up, peer_down, *rest):
    rest = rest[aliased:]
    hid, dge, saved, rst, own_out, peer_out, send = rest[:7]
    (up_v, down_v, hid_v, dge_v, saved_v, rst_v, stream, acc, out_v, x_v, seg_v, masks, w_sem, in_sem, o_sem, s_sem) = rest[7:]
    frames, width = acc.shape
    hidden = hid_v.shape[2]

    @pl.when(flags[0] == 1)
    def _():
        core = flags[1]
        pltpu.make_async_copy(x_hbm.at[flags[2]], x_v, in_sem.at[0]).start()
        pltpu.make_async_copy(seg_hbm.at[flags[3]], seg_v.at[pl.ds(PAD, frames)], in_sem.at[1]).start()
        for j in range(layers):
            for mine, ups, downs in ((True, own_up, own_down), (False, peer_up, peer_down)):

                @pl.when((core == j // 2) == mine)
                def _():
                    pltpu.make_async_copy(ups.at[j % 2], up_v.at[j], w_sem.at[j, 0]).start()
                    pltpu.make_async_copy(downs.at[j % 2], down_v.at[j], w_sem.at[j, 1]).start()

        clear_edges(stream, frames)
        pltpu.make_async_copy(seg_hbm.at[0], seg_v.at[pl.ds(PAD, frames)], in_sem.at[1]).wait()
        build_masks(seg_v, masks)
        pltpu.make_async_copy(x_hbm.at[0], x_v, in_sem.at[0]).wait()
        for c, cols in enumerate(slabs(width)):
            stream[c, PAD : PAD + frames, :] = x_v[:, cols].astype(F32)

        def layer(j, carry):
            def conv_norm(i, c):
                base = pl.multiple_of(i * TILE, TILE)
                rows = pl.ds(base, TILE)
                parts = []
                for s, cols in enumerate(slabs(width)):
                    centre = stream[s, pl.ds(base + PAD, TILE), :]
                    saved_v[j, STREAM, rows, cols] = centre.astype(BF16)
                    total = vec[j, CONV_B : CONV_B + 1, cols] + vec[j, 3:4, cols] * centre
                    for offset in OFFSETS:
                        neighbour = stream[s, pl.ds(base + PAD + offset, TILE), :] * masks[MASK_OF[offset], rows, :]
                        total = total + vec[j, offset + 3 : offset + 4, cols] * neighbour
                    parts.append(total)
                mean = row_sum(parts) * (1.0 / width)
                parts = [part - mean for part in parts]
                rstd = lax.rsqrt(row_sum([part * part for part in parts]) * (1.0 / width) + EPSILON)
                for part, cols in zip(parts, slabs(width)):
                    xhat = part * rstd
                    saved_v[j, XHAT, rows, cols] = xhat.astype(BF16)
                    saved_v[j, NORMED, rows, cols] = (xhat * vec[j, GAIN : GAIN + 1, cols] + vec[j, SHIFT : SHIFT + 1, cols]).astype(BF16)
                rst_v[j, rows, :] = jnp.broadcast_to(rstd, (TILE, LANES))
                return c

            lax.fori_loop(0, frames // TILE, conv_norm, 0, unroll=4)
            pltpu.make_async_copy(saved_v.at[j], saved.at[j], o_sem.at[j, 3]).start()
            pltpu.make_async_copy(rst_v.at[j], rst.at[j], o_sem.at[j, 2]).start()
            pltpu.make_async_copy(own_up.at[0], up_v.at[j], w_sem.at[j, 0]).wait()
            for n in range(hidden // COLS):
                cols = slice(n * COLS, (n + 1) * COLS)
                row, start = UP_B + n * COLS // width, (n * COLS) % width
                value = jnp.dot(saved_v[j, NORMED], up_v[j, :, cols], preferred_element_type=F32) + vec[j, row : row + 1, start : start + COLS]
                scaled = value * INV_SQRT2
                phi_sum = 0.5 + 0.5 * lax.erf(scaled)
                hid_v[j, :, cols] = (value * phi_sum).astype(BF16)
                dge_v[j, :, cols] = (phi_sum + scaled * INV_SQRT_PI * jnp.exp2(scaled * scaled * -LOG2_E)).astype(BF16)
            pltpu.make_async_copy(hid_v.at[j], hid.at[j], o_sem.at[j, 0]).start()
            pltpu.make_async_copy(dge_v.at[j], dge.at[j], o_sem.at[j, 1]).start()
            pltpu.make_async_copy(own_down.at[0], down_v.at[j], w_sem.at[j, 1]).wait()
            acc[...] = jnp.dot(hid_v[j], down_v[j], preferred_element_type=F32)

            def finish(ends_section, i, c):
                base = pl.multiple_of(i * TILE, TILE)
                rows = pl.ds(base, TILE)
                for s, cols in enumerate(slabs(width)):
                    inner = pl.ds(pl.multiple_of(base + PAD, 8), TILE)
                    branch = acc[rows, cols] + vec[j, DOWN_B : DOWN_B + 1, cols]
                    fresh = stream[s, inner, :] + vec[j, SCALE : SCALE + 1, cols] * branch
                    if ends_section:
                        rounded = fresh.astype(BF16)
                        out_v[lax.div(j, 2), rows, cols] = fresh
                        x_v[rows, cols] = rounded
                        fresh = rounded.astype(F32)
                    stream[s, inner, :] = fresh
                return c

            @pl.when(lax.rem(j, 2) == 1)
            def _():
                lax.fori_loop(0, frames // TILE, functools.partial(finish, True), 0)

            @pl.when(lax.rem(j, 2) == 0)
            def _():
                lax.fori_loop(0, frames // TILE, functools.partial(finish, False), 0)

            return carry

        lax.fori_loop(0, layers, layer, 0)
        pltpu.make_async_copy(out_v.at[core], own_out, s_sem.at[0]).start()
        pltpu.make_async_copy(out_v.at[1 - core], peer_out, s_sem.at[1]).start()
        pltpu.make_async_copy(x_v, send, s_sem.at[2]).start()
        for j in range(layers):
            pltpu.make_async_copy(hid_v.at[j], hid.at[j], o_sem.at[j, 0]).wait()
            pltpu.make_async_copy(dge_v.at[j], dge.at[j], o_sem.at[j, 1]).wait()
            pltpu.make_async_copy(rst_v.at[j], rst.at[j], o_sem.at[j, 2]).wait()
            pltpu.make_async_copy(saved_v.at[j], saved.at[j], o_sem.at[j, 3]).wait()
        pltpu.make_async_copy(out_v.at[core], own_out, s_sem.at[0]).wait()
        pltpu.make_async_copy(out_v.at[1 - core], peer_out, s_sem.at[1]).wait()
        pltpu.make_async_copy(x_v, send, s_sem.at[2]).wait()


def backward_kernel(layers, aliased, flags, g_hbm, seg_hbm, vec, own_up, own_down, peer_up, peer_down, dge, saved, rst, *rest):
    rest = rest[aliased:]
    gb, gp, vec_out, own_out, peer_out, send = rest[:6]
    (up_v, down_v, dge_v, saved_v, rst_v, gb_v, gp_v, vg_v, g_now, fresh_v, gn_v, padded, x_v, seg_v, masks, w_sem, in_sem, o_sem, s_sem) = rest[6:]
    frames, width = g_now.shape
    hidden = dge_v.shape[2]
    nt = (((1,), (1,)), ((), ()))
    tall = 2 * TILE

    @pl.when(flags[0] == 1)
    def _():
        core = flags[1]
        pltpu.make_async_copy(g_hbm.at[flags[2]], x_v, in_sem.at[0]).start()
        pltpu.make_async_copy(seg_hbm.at[flags[3]], seg_v.at[pl.ds(PAD, frames)], in_sem.at[1]).start()
        for j in range(layers - 1, -1, -1):
            for mine, downs in ((True, own_down), (False, peer_down)):

                @pl.when((core == j // 2) == mine)
                def _():
                    pltpu.make_async_copy(downs.at[j % 2], down_v.at[j], w_sem.at[j, 1]).start()

            pltpu.make_async_copy(dge.at[j], dge_v.at[j], w_sem.at[j, 3]).start()
            for mine, ups in ((True, own_up), (False, peer_up)):

                @pl.when((core == j // 2) == mine)
                def _():
                    pltpu.make_async_copy(ups.at[j % 2], up_v.at[j], w_sem.at[j, 0]).start()

            pltpu.make_async_copy(rst.at[j], rst_v.at[j], w_sem.at[j, 4]).start()
            pltpu.make_async_copy(saved.at[j, 0:2], saved_v.at[j], w_sem.at[j, 2]).start()

        clear_edges(padded, frames)
        pltpu.make_async_copy(seg_hbm.at[0], seg_v.at[pl.ds(PAD, frames)], in_sem.at[1]).wait()
        build_masks(seg_v, masks)
        pltpu.make_async_copy(g_hbm.at[0], x_v, in_sem.at[0]).wait()
        for cols in slabs(width):

            def enter(i, c):
                rows = pl.ds(pl.multiple_of(i * tall, tall), tall)
                scaled = (vec[layers - 1, SCALE : SCALE + 1, cols] * x_v[rows, cols].astype(F32)).astype(BF16)
                gb_v[layers, rows, cols] = scaled
                return c + fold(scaled.astype(F32))

            total = lax.fori_loop(0, frames // tall, enter, jnp.zeros((8, LANES), F32))
            vg_v[layers, DOWN_B : DOWN_B + 1, cols] = jnp.sum(total, axis=0, keepdims=True)

        def layer(step, carry):
            j = layers - 1 - step
            pltpu.make_async_copy(gb_v.at[j + 1], gb.at[j], o_sem.at[j, 0]).start()
            pltpu.make_async_copy(own_down.at[0], down_v.at[j], w_sem.at[j, 1]).wait()
            pltpu.make_async_copy(dge.at[0], dge_v.at[j], w_sem.at[j, 3]).wait()
            for n in range(hidden // COLS):
                cols = slice(n * COLS, (n + 1) * COLS)
                value = lax.dot_general(gb_v[j + 1], down_v[j, cols, :], nt, preferred_element_type=F32)
                rounded = (value * dge_v[j, :, cols].astype(F32)).astype(BF16)
                gp_v[j, :, cols] = rounded
                row, start = UP_B + n * COLS // width, (n * COLS) % width
                vg_v[j + 1, row : row + 1, start : start + COLS] = jnp.sum(rounded.astype(F32), axis=0, keepdims=True)
            pltpu.make_async_copy(gp_v.at[j], gp.at[j], o_sem.at[j, 1]).start()
            pltpu.make_async_copy(own_up.at[0], up_v.at[j], w_sem.at[j, 0]).wait()
            gn_v[...] = lax.dot_general(gp_v[j], up_v[j], nt, preferred_element_type=F32)
            pltpu.make_async_copy(rst.at[0], rst_v.at[j], w_sem.at[j, 4]).wait()
            pltpu.make_async_copy(saved.at[0, 0:2], saved_v.at[j], w_sem.at[j, 2]).wait()
            odd = lax.rem(j, 2) == 1

            def norm_back(i, c):
                base = pl.multiple_of(i * TILE, TILE)
                rows = pl.ds(base, TILE)
                grads = [gn_v[rows, cols] for cols in slabs(width)]
                xhats = [saved_v[j, XHAT, rows, cols].astype(F32) for cols in slabs(width)]
                qs = [grad * vec[j, GAIN : GAIN + 1, cols] for grad, cols in zip(grads, slabs(width))]
                mean_q = row_sum(qs) * (1.0 / width)
                mean_qx = row_sum([q * xhat for q, xhat in zip(qs, xhats)]) * (1.0 / width)
                rstd = rst_v[j, rows, :]
                out = []
                for s, cols in enumerate(slabs(width)):
                    grad_conv = rstd * (qs[s] - mean_q - xhats[s] * mean_qx)
                    padded[s, pl.ds(pl.multiple_of(base + PAD, 8), TILE), :] = grad_conv
                    g_now[rows, cols] = jnp.where(odd, x_v[rows, cols].astype(F32), fresh_v[rows, cols])
                    out += [c[3 * s] + fold(grads[s] * xhats[s]), c[3 * s + 1] + fold(grads[s]), c[3 * s + 2] + fold(grad_conv)]
                return tuple(out)

            count = 3 * (width // LANES)
            sums = lax.fori_loop(0, frames // TILE, norm_back, (jnp.zeros((8, LANES), F32),) * count, unroll=2)
            for s, cols in enumerate(slabs(width)):
                for k, row in enumerate((GAIN, SHIFT, CONV_B)):
                    vg_v[j + 1, row : row + 1, cols] = jnp.sum(sums[3 * s + k], axis=0, keepdims=True)

            @pl.when(j == layers // 2 - 1)
            def _():
                pltpu.make_async_copy(fresh_v, own_out, s_sem.at[0]).wait()

            below = lax.max(j - 1, 0)
            even = lax.rem(j, 2) == 0
            for s, cols in enumerate(slabs(width)):

                def conv_back(i, c):
                    base = pl.multiple_of(i * tall, tall)
                    rows = pl.ds(base, tall)
                    source = saved_v[j, STREAM, rows, cols].astype(F32)
                    centre = padded[s, pl.ds(pl.multiple_of(base + PAD, 8), tall), :]
                    total = g_now[rows, cols] + vec[j, 3:4, cols] * centre
                    taps = [None] * 7
                    taps[3] = c[3] + fold(centre * source)
                    for offset in OFFSETS:
                        term = padded[s, pl.ds(base + PAD - offset, tall), :] * masks[MASK_OF[-offset], rows, :]
                        total = total + vec[j, offset + 3 : offset + 4, cols] * term
                        taps[offset + 3] = c[offset + 3] + fold(term * source)
                    rounded = total.astype(BF16)
                    fresh_v[rows, cols] = total
                    x_v[rows, cols] = rounded
                    scaled = (vec[below, SCALE : SCALE + 1, cols] * jnp.where(even, rounded.astype(F32), total)).astype(BF16)
                    gb_v[j, rows, cols] = scaled
                    return tuple(taps) + (c[7] + fold(scaled.astype(F32)),)

                sums = lax.fori_loop(0, frames // tall, conv_back, (jnp.zeros((8, LANES), F32),) * 8, unroll=2)
                for k in range(7):
                    vg_v[j + 1, k : k + 1, cols] = jnp.sum(sums[k], axis=0, keepdims=True)
                vg_v[j, DOWN_B : DOWN_B + 1, cols] = jnp.sum(sums[7], axis=0, keepdims=True)

            @pl.when(even & (core == lax.div(j, 2)))
            def _():
                pltpu.make_async_copy(fresh_v, own_out, s_sem.at[0]).start()

            @pl.when(even & (core != lax.div(j, 2)))
            def _():
                pltpu.make_async_copy(fresh_v, peer_out, s_sem.at[0]).start()

            return carry

        for j in range(1, layers + 1):
            vg_v[j, SCALE : SCALE + 1, :] = jnp.zeros((1, width), F32)
            vg_v[j, VEC_ROWS - 1 : VEC_ROWS, :] = jnp.zeros((1, width), F32)
        lax.fori_loop(0, layers, layer, 0)
        pltpu.make_async_copy(x_v, send, s_sem.at[1]).start()
        pltpu.make_async_copy(vg_v.at[pl.ds(1, layers)], vec_out, s_sem.at[2]).start()
        for j in range(layers):
            pltpu.make_async_copy(gb_v.at[j + 1], gb.at[j], o_sem.at[j, 0]).wait()
            pltpu.make_async_copy(gp_v.at[j], gp.at[j], o_sem.at[j, 1]).wait()
        pltpu.make_async_copy(fresh_v, own_out, s_sem.at[0]).wait()
        pltpu.make_async_copy(x_v, send, s_sem.at[1]).wait()
        pltpu.make_async_copy(vg_v.at[pl.ds(1, layers)], vec_out, s_sem.at[2]).wait()


ANY = pl.BlockSpec(memory_space=pl.ANY)
SMEM = pl.BlockSpec(memory_space=pltpu.SMEM)
VMEM = pl.BlockSpec(memory_space=pltpu.VMEM)


def run_forward(flags, x, masks, vec, weights, earlier):
    layers = vec.shape[0]
    frames, width = x.shape[1:]
    hidden = weights[0].shape[2]
    shapes = (
        jax.ShapeDtypeStruct((layers, frames, hidden), BF16),
        jax.ShapeDtypeStruct((layers, frames, hidden), BF16),
        jax.ShapeDtypeStruct((layers, KINDS, frames, width), BF16),
        jax.ShapeDtypeStruct((layers, frames, LANES), F32),
        jax.ShapeDtypeStruct((frames, width), F32),
        jax.ShapeDtypeStruct((frames, width), F32),
        jax.ShapeDtypeStruct((frames, width), BF16),
    )
    earlier = earlier[:-1]
    aliased = len(earlier)
    return pl.pallas_call(
        functools.partial(forward_kernel, layers, aliased),
        out_shape=shapes,
        in_specs=[SMEM, ANY, ANY, VMEM] + [ANY] * 4 + [ANY] * aliased,
        out_specs=(ANY,) * len(shapes),
        input_output_aliases={8 + i: i for i in range(aliased)},
        scratch_shapes=[
            pltpu.VMEM((layers, width, hidden), BF16),
            pltpu.VMEM((layers, hidden, width), BF16),
            pltpu.VMEM((layers, frames, hidden), BF16),
            pltpu.VMEM((layers, frames, hidden), BF16),
            pltpu.VMEM((layers, KINDS, frames, width), BF16),
            pltpu.VMEM((layers, frames, LANES), F32),
            pltpu.VMEM((width // LANES, frames + 2 * PAD, LANES), F32),
            pltpu.VMEM((frames, width), F32),
            pltpu.VMEM((2, frames, width), F32),
            pltpu.VMEM((frames, width), BF16),
            pltpu.VMEM((frames + 2 * PAD, LANES), F32),
            pltpu.VMEM((6, frames, LANES), F32),
            pltpu.SemaphoreType.DMA((layers, 2)),
            pltpu.SemaphoreType.DMA((2,)),
            pltpu.SemaphoreType.DMA((layers, 4)),
            pltpu.SemaphoreType.DMA((3,)),
        ],
        compiler_params=pltpu.CompilerParams(vmem_limit_bytes=VMEM_LIMIT),
        cost_estimate=pl.CostEstimate(flops=layers * 4 * frames * width * hidden, bytes_accessed=40 * 2**20, transcendentals=0),
    )(flags, x, masks, vec, *weights, *earlier)


def run_backward(flags, g, masks, vec, weights, state, earlier):
    layers = vec.shape[0]
    frames, width = g.shape[1:]
    hidden = weights[0].shape[2]
    shapes = (
        jax.ShapeDtypeStruct((layers, frames, width), BF16),
        jax.ShapeDtypeStruct((layers, frames, hidden), BF16),
        jax.ShapeDtypeStruct((layers, VEC_ROWS, width), F32),
        jax.ShapeDtypeStruct((frames, width), F32),
        jax.ShapeDtypeStruct((frames, width), F32),
        jax.ShapeDtypeStruct((frames, width), BF16),
    )
    earlier = earlier[:-1]
    aliased = len(earlier)
    return pl.pallas_call(
        functools.partial(backward_kernel, layers, aliased),
        out_shape=shapes,
        in_specs=[SMEM, ANY, ANY, VMEM] + [ANY] * 7 + [ANY] * aliased,
        out_specs=(ANY,) * len(shapes),
        input_output_aliases={11 + i: i for i in range(aliased)},
        scratch_shapes=[
            pltpu.VMEM((layers, width, hidden), BF16),
            pltpu.VMEM((layers, hidden, width), BF16),
            pltpu.VMEM((layers, frames, hidden), BF16),
            pltpu.VMEM((layers, 2, frames, width), BF16),
            pltpu.VMEM((layers, frames, LANES), F32),
            pltpu.VMEM((layers + 1, frames, width), BF16),
            pltpu.VMEM((layers, frames, hidden), BF16),
            pltpu.VMEM((layers + 1, VEC_ROWS, width), F32),
            pltpu.VMEM((frames, width), F32),
            pltpu.VMEM((frames, width), F32),
            pltpu.VMEM((frames, width), F32),
            pltpu.VMEM((width // LANES, frames + 2 * PAD, LANES), F32),
            pltpu.VMEM((frames, width), BF16),
            pltpu.VMEM((frames + 2 * PAD, LANES), F32),
            pltpu.VMEM((6, frames, LANES), F32),
            pltpu.SemaphoreType.DMA((layers, 5)),
            pltpu.SemaphoreType.DMA((2,)),
            pltpu.SemaphoreType.DMA((layers, 2)),
            pltpu.SemaphoreType.DMA((3,)),
        ],
        compiler_params=pltpu.CompilerParams(vmem_limit_bytes=VMEM_LIMIT),
        cost_estimate=pl.CostEstimate(flops=layers * 4 * frames * width * hidden, bytes_accessed=40 * 2**20, transcendentals=0),
    )(flags, g, masks, vec, *weights, *state, *earlier)


def weight_kernel(first, hid_a, hid_b, gb_a, gb_b, nrm_a, nrm_b, gp_a, gp_b, weight, down_out, up_out, scale_out):
    tn = (((0,), (0,)), ((), ()))
    down = lax.dot_general(hid_a[0], gb_a[0], tn, preferred_element_type=F32)
    down = down + lax.dot_general(hid_b[0], gb_b[0], tn, preferred_element_type=F32)
    down_out[0] = down.astype(BF16)
    scale_out[0] = jnp.broadcast_to(jnp.sum(down * weight[0].astype(F32), axis=0, keepdims=True), scale_out.shape[1:])
    up = lax.dot_general(nrm_a[0, 0], gp_a[0], tn, preferred_element_type=F32)
    up_out[0] = (up + lax.dot_general(nrm_b[0, 0], gp_b[0], tn, preferred_element_type=F32)).astype(BF16)


def run_weights(first, hid_a, hid_b, gb_a, gb_b, saved_a, saved_b, gp_a, gp_b, down_weight):
    frames, hidden = hid_a.shape[1:]
    width = gb_a.shape[2]
    count = hid_a.shape[0] // 2
    wide = pl.BlockSpec((1, frames, hidden), lambda i, first: (first[0] + i, 0, 0))
    narrow = pl.BlockSpec((1, frames, width), lambda i, first: (first[0] + i, 0, 0))
    normed = pl.BlockSpec((1, 1, frames, width), lambda i, first: (first[0] + i, NORMED, 0, 0))
    return pl.pallas_call(
        weight_kernel,
        out_shape=(
            jax.ShapeDtypeStruct((count, hidden, width), BF16),
            jax.ShapeDtypeStruct((count, width, hidden), BF16),
            jax.ShapeDtypeStruct((count, 8, width), F32),
        ),
        grid_spec=pltpu.PrefetchScalarGridSpec(
            num_scalar_prefetch=1,
            grid=(count,),
            in_specs=[wide, wide, narrow, narrow, normed, normed, wide, wide, pl.BlockSpec((1, hidden, width), lambda i, first: (i, 0, 0))],
            out_specs=(
                pl.BlockSpec((1, hidden, width), lambda i, first: (i, 0, 0)),
                pl.BlockSpec((1, width, hidden), lambda i, first: (i, 0, 0)),
                pl.BlockSpec((1, 8, width), lambda i, first: (i, 0, 0)),
            ),
        ),
        compiler_params=pltpu.CompilerParams(vmem_limit_bytes=VMEM_LIMIT),
        cost_estimate=pl.CostEstimate(flops=count * 8 * frames * width * hidden, bytes_accessed=24 * 2**20, transcendentals=0),
    )(first, hid_a, hid_b, gb_a, gb_b, saved_a, saved_b, gp_a, gp_b, down_weight)


def sum_doubling(value, axis):
    count = lax.axis_size(axis)
    step = 1
    while step < count:
        value = value + lax.ppermute(value, axis, [(d, d ^ step) for d in range(count)])
        step *= 2
    return value


def ring_order(count):
    return list(range(0, count, 2)) + list(range(count - 1, 0, -2))


def ring_scatter(parts, directions, slicers, axis):
    count = lax.axis_size(axis)
    order = ring_order(count)
    place_of = [order.index(d) for d in range(count)]
    place = jnp.array(place_of, jnp.int32)[lax.axis_index(axis)]
    order_table = jnp.array(order, jnp.int32)

    def local(i, owner_place):
        device = order_table[lax.rem(owner_place + 2 * count, count)]
        return functools.reduce(jnp.add, [slicers[i](addend, device).astype(F32) for addend in parts[i]])

    flowing = [local(i, place - way).astype(BF16) for i, way in enumerate(directions)]
    for step in range(count - 1):
        arrived = [
            lax.ppermute(value, axis, [(order[p], order[(p + way) % count]) for p in range(count)])
            for value, way in zip(flowing, directions)
        ]
        flowing = []
        for i, way in enumerate(directions):
            total = arrived[i].astype(F32) + local(i, place - way * (2 + step))
            flowing.append(total.astype(BF16) if step < count - 2 else total)
    return flowing


def per_device(
    inputs,
    segment_ids,
    cotangent,
    conv_weight,
    conv_bias,
    norm_gain,
    norm_bias,
    up_weight,
    up_bias,
    down_weight,
    down_bias,
    layer_scale,
):
    micro, _, frames, width = inputs.shape
    hidden = up_weight.shape[2]
    shares = lax.axis_size("dp")
    section = lax.axis_index("section")
    chip, core = section // 2, section % 2
    exchange = [(0, 1), (1, 0), (2, 3), (3, 2)]

    small = jnp.concatenate(
        [
            conv_weight,
            conv_bias[:, None],
            norm_gain[:, None],
            norm_bias[:, None],
            down_bias[:, None],
            layer_scale[:, None],
            up_bias.reshape(2, -1, width),
            jnp.zeros((2, 1, width), BF16),
        ],
        axis=1,
    )
    small_peer = lax.ppermute(small, "section", exchange)
    up_peer = lax.ppermute(up_weight, "section", exchange)
    down_peer = lax.ppermute(down_weight, "section", exchange)
    vec = jnp.where(core == 0, jnp.concatenate([small, small_peer]), jnp.concatenate([small_peer, small])).astype(F32)
    weights = (up_weight, down_weight, up_peer, down_peer)
    masks = jnp.broadcast_to(segment_ids[:, 0, :, None].astype(F32), (micro, frames, LANES))
    inputs, cotangent = inputs[:, 0], cotangent[:, 0]

    def flags(active, index, micro_slot):
        return jnp.stack([jnp.asarray(v, jnp.int32) for v in (active, core, index, 2 * core + micro_slot)])

    first, last = (chip == 0).astype(jnp.int32), (chip == 1).astype(jnp.int32)
    down_pairs, up_pairs = [(0, 2), (1, 3)], [(2, 0), (3, 1)]
    state_a = run_forward(flags(first, 2 * core, 0), inputs, masks, vec, weights, ())
    sent_a = lax.ppermute(state_a[6], "section", down_pairs)
    state_b = run_forward(flags(first, 2 * core + 1, 1), inputs, masks, vec, weights, ())
    sent_b = lax.ppermute(state_b[6], "section", down_pairs)
    state_a = run_forward(flags(last, 0, 0), sent_a[None], masks, vec, weights, state_a)
    state_b = run_forward(flags(last, 0, 1), sent_b[None], masks, vec, weights, state_b)

    back_b = run_backward(flags(last, 2 * core + 1, 1), cotangent, masks, vec, weights, state_b[1:4], ())
    sent_b = lax.ppermute(back_b[5], "section", up_pairs)
    back_a = run_backward(flags(last, 2 * core, 0), cotangent, masks, vec, weights, state_a[1:4], ())
    sent_a = lax.ppermute(back_a[5], "section", up_pairs)
    back_b = run_backward(flags(first, 0, 1), sent_b[None], masks, vec, weights, state_b[1:4], back_b)
    back_a = run_backward(flags(first, 0, 0), sent_a[None], masks, vec, weights, state_a[1:4], back_a)

    def grads(first_layer, weight):
        return run_weights(
            first_layer.reshape(1).astype(jnp.int32), state_a[0], state_b[0], back_a[0], back_b[0], state_a[2], state_b[2], back_a[1], back_b[1], weight
        )

    down_other, up_other, scale_other = grads(2 * (1 - core), down_peer)
    down_recv = lax.ppermute(down_other, "section", exchange)
    up_recv = lax.ppermute(up_other, "section", exchange)
    down_own, up_own, scale_own = grads(2 * core, down_weight)

    def vectors(first_layer, scales):
        sums = lax.dynamic_slice_in_dim(back_a[2] + back_b[2], first_layer, 2, 0)
        return sums.at[:, SCALE].set(scales[:, 0])

    totals = vectors(2 * core, scale_own) + lax.ppermute(vectors(2 * (1 - core), scale_other), "section", exchange)
    totals = sum_doubling(totals, "dp")
    scale_grad = (totals[:, SCALE] + down_bias.astype(F32) * totals[:, DOWN_B]) / layer_scale.astype(F32)
    shard = lax.axis_index("dp")

    def share(value):
        size = value.shape[-1] // shares
        return lax.dynamic_slice_in_dim(value, shard * size, size, value.ndim - 1)

    def slice_up(value, device):
        size = width // shares
        return lax.dynamic_slice_in_dim(value, device * size, size, 1)

    def slice_down(value, device):
        size = hidden // shares
        return lax.dynamic_slice_in_dim(value, device * size, size, 1)

    up_share, down_share = ring_scatter([[up_own, up_recv], [down_own, down_recv]], [1, -1], [slice_up, slice_down], "dp")

    def assemble(own_a, own_b, peer_a, peer_b):
        own = jnp.stack([own_a, own_b])
        other = lax.ppermute(jnp.stack([peer_a, peer_b]), "section", exchange)
        return jnp.where(core == 0, jnp.concatenate([own, other]), jnp.concatenate([other, own]))[None, :, None]

    section_outputs = assemble(state_a[4], state_b[4], state_a[5], state_b[5])
    input_grads = assemble(back_a[3], back_b[3], back_a[4], back_b[4])
    return (
        section_outputs,
        input_grads,
        share(totals[:, :CONV_B]),
        share(totals[:, CONV_B]),
        share(totals[:, GAIN]),
        share(totals[:, SHIFT]),
        up_share,
        share(totals[:, UP_B : UP_B + hidden // width].reshape(2, -1)),
        down_share,
        share(totals[:, DOWN_B]),
        share(scale_grad),
    )


def solution(mesh):
    in_specs = (
        P(None, "dp", None, None),
        P(None, "dp", None),
        P(None, "dp", None, None),
        P("section", None, None),
        P("section", None),
        P("section", None),
        P("section", None),
        P("section", None, None),
        P("section", None),
        P("section", None, None),
        P("section", None),
        P("section", None),
    )
    out_specs = (
        P("section", None, "dp", None, None),
        P("section", None, "dp", None, None),
        P("section", None, "dp"),
        P("section", "dp"),
        P("section", "dp"),
        P("section", "dp"),
        P("section", "dp", None),
        P("section", "dp"),
        P("section", "dp", None),
        P("section", "dp"),
        P("section", "dp"),
    )
    return jax.shard_map(per_device, mesh=mesh, in_specs=in_specs, out_specs=out_specs, check_vma=False)
```

```python
import functools

import jax
import jax.numpy as jnp
from jax import lax
from jax.experimental import pallas as pl
from jax.experimental.pallas import tpu as pltpu
from jax.sharding import PartitionSpec as P

EPSILON = 1e-06
INV_SQRT2 = 0.7071067811865476
INV_SQRT_PI = 0.5641895835477563
LOG2_E = 1.4426950408889634
F32 = jnp.float32
BF16 = jnp.bfloat16
TILE = 32
PAD = 8
COLS = 256
VMEM_LIMIT = 60 * 2**20

CONV_B, GAIN, SHIFT, DOWN_B, SCALE, UP_B, VEC_ROWS = 7, 8, 9, 10, 11, 12, 16
XHAT, STREAM, NORMED, KINDS = 0, 1, 2, 3
LANES = 128
OFFSETS = (1, 2, 3, -1, -2, -3)
MASK_OF = {offset: k for k, offset in enumerate(OFFSETS)}


def slabs(width):
    return [slice(c, c + LANES) for c in range(0, width, LANES)]


def row_sum(parts):
    return jnp.sum(functools.reduce(jnp.add, parts), axis=1, keepdims=True)


def fold(value):
    return functools.reduce(jnp.add, [value[8 * i : 8 * i + 8] for i in range(value.shape[0] // 8)])


def clear_edges(padded, frames):
    for slab in range(padded.shape[0]):
        padded[slab, 0:PAD, :] = jnp.zeros((PAD, LANES), F32)
        padded[slab, PAD + frames : PAD + frames + PAD, :] = jnp.zeros((PAD, LANES), F32)


def build_masks(seg_v, masks):
    frames = masks.shape[1]
    seg_v[0:PAD, :] = jnp.full((PAD, LANES), -1.0, F32)
    seg_v[PAD + frames : PAD + frames + PAD, :] = jnp.full((PAD, LANES), -1.0, F32)

    def body(i, carry):
        base = pl.multiple_of(i * 64, 64)
        here = seg_v[pl.ds(base + PAD, 64), :]
        for k, offset in enumerate(OFFSETS):
            there = seg_v[pl.ds(base + PAD + offset, 64), :]
            masks[k, pl.ds(base, 64), :] = jnp.where(there == here, 1.0, 0.0)
        return carry

    lax.fori_loop(0, frames // 64, body, 0)


def start_weights(core, layer, own, peer, target, sem):
    @pl.when(core == lax.div(layer, 2))
    def _():
        pltpu.make_async_copy(own.at[lax.rem(layer, 2)], target, sem).start()

    @pl.when(core != lax.div(layer, 2))
    def _():
        pltpu.make_async_copy(peer.at[lax.rem(layer, 2)], target, sem).start()


def forward_kernel(layers, aliased, flags, x_hbm, seg_hbm, vec, own_up, own_down, peer_up, peer_down, *rest):
    rest = rest[aliased:]
    hid, dge, saved, rst, low_out, high_out, send = rest[:7]
    (up_v, down_v, hid_v, dge_v, saved_v, rst_v, stream, acc, out_v, x_v, seg_v, masks, w_sem, in_sem, o_sem, s_sem) = rest[7:]
    frames, width = acc.shape
    hidden = hid_v.shape[2]

    @pl.when(flags[0] == 1)
    def _():
        core = flags[1]
        pltpu.make_async_copy(x_hbm.at[flags[2]], x_v, in_sem.at[0]).start()
        pltpu.make_async_copy(seg_hbm.at[flags[3]], seg_v.at[pl.ds(PAD, frames)], in_sem.at[1]).start()
        def fetch(j):
            start_weights(core, j, own_up, peer_up, up_v.at[j], w_sem.at[j, 0])
            start_weights(core, j, own_down, peer_down, down_v.at[j], w_sem.at[j, 1])

        fetch(0)
        clear_edges(stream, frames)
        pltpu.make_async_copy(seg_hbm.at[0], seg_v.at[pl.ds(PAD, frames)], in_sem.at[1]).wait()
        build_masks(seg_v, masks)
        pltpu.make_async_copy(x_hbm.at[0], x_v, in_sem.at[0]).wait()
        for c, cols in enumerate(slabs(width)):
            stream[c, PAD : PAD + frames, :] = x_v[:, cols].astype(F32)

        def layer(j, carry):
            def conv_norm(i, c):
                base = pl.multiple_of(i * TILE, TILE)
                rows = pl.ds(base, TILE)
                parts = []
                for s, cols in enumerate(slabs(width)):
                    centre = stream[s, pl.ds(base + PAD, TILE), :]
                    saved_v[j, STREAM, rows, cols] = centre.astype(BF16)
                    total = vec[j, CONV_B : CONV_B + 1, cols] + vec[j, 3:4, cols] * centre
                    for offset in OFFSETS:
                        neighbour = stream[s, pl.ds(base + PAD + offset, TILE), :] * masks[MASK_OF[offset], rows, :]
                        total = total + vec[j, offset + 3 : offset + 4, cols] * neighbour
                    parts.append(total)
                mean = row_sum(parts) * (1.0 / width)
                parts = [part - mean for part in parts]
                rstd = lax.rsqrt(row_sum([part * part for part in parts]) * (1.0 / width) + EPSILON)
                for part, cols in zip(parts, slabs(width)):
                    xhat = part * rstd
                    saved_v[j, XHAT, rows, cols] = xhat.astype(BF16)
                    saved_v[j, NORMED, rows, cols] = (xhat * vec[j, GAIN : GAIN + 1, cols] + vec[j, SHIFT : SHIFT + 1, cols]).astype(BF16)
                rst_v[j, rows, :] = jnp.broadcast_to(rstd, (TILE, LANES))
                return c

            lax.fori_loop(0, frames // TILE, conv_norm, 0, unroll=16)
            pltpu.make_async_copy(saved_v.at[j], saved.at[j], o_sem.at[j, 3]).start()
            pltpu.make_async_copy(rst_v.at[j], rst.at[j], o_sem.at[j, 2]).start()
            pltpu.make_async_copy(own_up.at[0], up_v.at[j], w_sem.at[j, 0]).wait()

            @pl.when(j + 1 < layers)
            def _():
                fetch(j + 1)

            for n in range(hidden // COLS):
                cols = slice(n * COLS, (n + 1) * COLS)
                row, start = UP_B + n * COLS // width, (n * COLS) % width
                value = jnp.dot(saved_v[j, NORMED], up_v[j, :, cols], preferred_element_type=F32) + vec[j, row : row + 1, start : start + COLS]
                scaled = value * INV_SQRT2
                phi_sum = 0.5 + 0.5 * lax.erf(scaled)
                hid_v[j, :, cols] = (value * phi_sum).astype(BF16)
                dge_v[j, :, cols] = (phi_sum + scaled * INV_SQRT_PI * jnp.exp2(scaled * scaled * -LOG2_E)).astype(BF16)
            pltpu.make_async_copy(hid_v.at[j], hid.at[j], o_sem.at[j, 0]).start()
            pltpu.make_async_copy(dge_v.at[j], dge.at[j], o_sem.at[j, 1]).start()
            pltpu.make_async_copy(own_down.at[0], down_v.at[j], w_sem.at[j, 1]).wait()
            acc[...] = jnp.dot(hid_v[j], down_v[j], preferred_element_type=F32)

            def finish(ends_section, i, c):
                base = pl.multiple_of(i * TILE, TILE)
                rows = pl.ds(base, TILE)
                for s, cols in enumerate(slabs(width)):
                    inner = pl.ds(pl.multiple_of(base + PAD, 8), TILE)
                    branch = acc[rows, cols] + vec[j, DOWN_B : DOWN_B + 1, cols]
                    fresh = stream[s, inner, :] + vec[j, SCALE : SCALE + 1, cols] * branch
                    if ends_section:
                        rounded = fresh.astype(BF16)
                        out_v[lax.div(j, 2), rows, cols] = fresh
                        x_v[rows, cols] = rounded
                        fresh = rounded.astype(F32)
                    stream[s, inner, :] = fresh
                return c

            @pl.when(lax.rem(j, 2) == 1)
            def _():
                lax.fori_loop(0, frames // TILE, functools.partial(finish, True), 0)

            @pl.when(lax.rem(j, 2) == 0)
            def _():
                lax.fori_loop(0, frames // TILE, functools.partial(finish, False), 0)

            @pl.when(j == 1)
            def _():
                pltpu.make_async_copy(out_v.at[0], low_out, s_sem.at[0]).start()

            return carry

        lax.fori_loop(0, layers, layer, 0)
        pltpu.make_async_copy(out_v.at[1], high_out, s_sem.at[1]).start()
        pltpu.make_async_copy(x_v, send, s_sem.at[2]).start()
        for j in range(layers):
            pltpu.make_async_copy(hid_v.at[j], hid.at[j], o_sem.at[j, 0]).wait()
            pltpu.make_async_copy(dge_v.at[j], dge.at[j], o_sem.at[j, 1]).wait()
            pltpu.make_async_copy(rst_v.at[j], rst.at[j], o_sem.at[j, 2]).wait()
            pltpu.make_async_copy(saved_v.at[j], saved.at[j], o_sem.at[j, 3]).wait()
        pltpu.make_async_copy(out_v.at[0], low_out, s_sem.at[0]).wait()
        pltpu.make_async_copy(out_v.at[1], high_out, s_sem.at[1]).wait()
        pltpu.make_async_copy(x_v, send, s_sem.at[2]).wait()


def backward_kernel(low, count, final, aliased, flags, g_hbm, seg_hbm, vec, own_up, own_down, peer_up, peer_down, dge, saved, rst, *rest):
    if final:
        hid, hid_b, saved_b, gb_b, gp_b = rest[:5]
        rest = rest[5 + aliased :]
        dlow_out, up_out, vec_out, send = rest[:4]
        grads_out = rest[4:5]
        rest = rest[5:]
        (up_v, down_v, dge_v, saved_v, rst_v, gb_v, gp_v, vg_v, g_now, fresh_v, gn_v, padded, x_v, seg_v, masks, w_sem, in_sem, o_sem, s_sem) = rest[:19]
        (hid_v, nrm_v, dwd_v, dwu_v, b_sem) = rest[19:]
    else:
        rest = rest[aliased:]
        gb, gp, vec_out, send = rest[:4]
        grads_out = rest[4 : 4 + count // 2]
        rest = rest[4 + count // 2 :]
        (up_v, down_v, dge_v, saved_v, rst_v, gb_v, gp_v, vg_v, g_now, fresh_v, gn_v, padded, x_v, seg_v, masks, w_sem, in_sem, o_sem, s_sem) = rest
    frames, width = g_now.shape
    hidden = dge_v.shape[2]
    nt = (((1,), (1,)), ((), ()))
    tn = (((0,), (0,)), ((), ()))
    tall = 2 * TILE
    cols_of = slabs(width)

    @pl.when(flags[0] == 1)
    def _():
        core = flags[1]
        pltpu.make_async_copy(g_hbm.at[flags[2]], x_v, in_sem.at[0]).start()
        pltpu.make_async_copy(seg_hbm.at[flags[3]], seg_v.at[pl.ds(PAD, frames)], in_sem.at[1]).start()
        def fetch(i):
            j = low + i
            start_weights(core, j, own_down, peer_down, down_v.at[i], w_sem.at[i, 1])
            pltpu.make_async_copy(dge.at[j], dge_v.at[i], w_sem.at[i, 3]).start()
            start_weights(core, j, own_up, peer_up, up_v.at[i], w_sem.at[i, 0])
            pltpu.make_async_copy(rst.at[j], rst_v.at[i], w_sem.at[i, 4]).start()
            pltpu.make_async_copy(saved.at[j, 0:2], saved_v.at[i], w_sem.at[i, 2]).start()

        fetch(count - 1)
        clear_edges(padded, frames)
        pltpu.make_async_copy(seg_hbm.at[0], seg_v.at[pl.ds(PAD, frames)], in_sem.at[1]).wait()
        build_masks(seg_v, masks)
        pltpu.make_async_copy(g_hbm.at[0], x_v, in_sem.at[0]).wait()
        for cols in cols_of:

            def enter(t, c):
                rows = pl.ds(pl.multiple_of(t * tall, tall), tall)
                scaled = (vec[low + count - 1, SCALE : SCALE + 1, cols] * x_v[rows, cols].astype(F32)).astype(BF16)
                gb_v[count, 0, rows, cols] = scaled
                return c + fold(scaled.astype(F32))

            total = lax.fori_loop(0, frames // tall, enter, jnp.zeros((8, LANES), F32))
            vg_v[count, DOWN_B : DOWN_B + 1, cols] = jnp.sum(total, axis=0, keepdims=True)

        def layer(step, carry):
            i = count - 1 - step
            j = low + i
            if not final:
                pltpu.make_async_copy(gb_v.at[i + 1, 0], gb.at[j], o_sem.at[i, 0]).start()
            pltpu.make_async_copy(own_down.at[0], down_v.at[i], w_sem.at[i, 1]).wait()
            pltpu.make_async_copy(dge.at[0], dge_v.at[i], w_sem.at[i, 3]).wait()
            if final:
                pltpu.make_async_copy(hid.at[j], hid_v.at[i, 0], b_sem.at[i, 0]).start()
                pltpu.make_async_copy(hid_b.at[j], hid_v.at[i, 1], b_sem.at[i, 1]).start()
                pltpu.make_async_copy(gb_b.at[j], gb_v.at[i + 1, 1], b_sem.at[i, 4]).start()
                pltpu.make_async_copy(saved.at[j, NORMED], nrm_v.at[i, 0], b_sem.at[i, 2]).start()
                pltpu.make_async_copy(saved_b.at[j, NORMED], nrm_v.at[i, 1], b_sem.at[i, 3]).start()
                pltpu.make_async_copy(gp_b.at[j], gp_v.at[i, 1], b_sem.at[i, 5]).start()
            for n in range(hidden // COLS):
                cols = slice(n * COLS, (n + 1) * COLS)
                value = lax.dot_general(gb_v[i + 1, 0], down_v[i, cols, :], nt, preferred_element_type=F32)
                rounded = (value * dge_v[i, :, cols].astype(F32)).astype(BF16)
                gp_v[i, 0, :, cols] = rounded
                row, start = UP_B + n * COLS // width, (n * COLS) % width
                vg_v[i + 1, row : row + 1, start : start + COLS] = jnp.sum(rounded.astype(F32), axis=0, keepdims=True)
            if not final:
                pltpu.make_async_copy(gp_v.at[i, 0], gp.at[j], o_sem.at[i, 1]).start()
            pltpu.make_async_copy(own_up.at[0], up_v.at[i], w_sem.at[i, 0]).wait()
            gn_v[...] = lax.dot_general(gp_v[i, 0], up_v[i], nt, preferred_element_type=F32)
            pltpu.make_async_copy(rst.at[0], rst_v.at[i], w_sem.at[i, 4]).wait()
            pltpu.make_async_copy(saved.at[0, 0:2], saved_v.at[i], w_sem.at[i, 2]).wait()

            @pl.when(i > 0)
            def _():
                fetch(i - 1)

            if final:
                pltpu.make_async_copy(hid.at[0], hid_v.at[i, 0], b_sem.at[i, 0]).wait()
                pltpu.make_async_copy(hid.at[0], hid_v.at[i, 1], b_sem.at[i, 1]).wait()
                pltpu.make_async_copy(gb_b.at[0], gb_v.at[i + 1, 1], b_sem.at[i, 4]).wait()

            def down_chunk(n):
                rows = slice(n * COLS, (n + 1) * COLS)
                left = hid_v[i, :, :, rows].reshape(2 * frames, COLS)
                right = gb_v[i + 1].reshape(2 * frames, width)
                value = lax.dot_general(left, right, tn, preferred_element_type=F32)
                dwd_v[i, rows, :] = value.astype(BF16)
                return fold(value * down_v[i, rows, :].astype(F32))

            def up_chunk(m, n):
                rows = slice(m * COLS, (m + 1) * COLS)
                cols = slice(n * width, (n + 1) * width)
                left = nrm_v[i, :, :, rows].reshape(2 * frames, COLS)
                right = gp_v[i, :, :, cols].reshape(2 * frames, width)
                dwu_v[i, rows, cols] = lax.dot_general(left, right, tn, preferred_element_type=F32).astype(BF16)

            odd = lax.rem(i, 2) == 1

            def norm_back(t, c):
                base = t * TILE if isinstance(t, int) else pl.multiple_of(t * TILE, TILE)
                rows = pl.ds(base, TILE)
                inner = pl.ds(base + PAD if isinstance(t, int) else pl.multiple_of(base + PAD, 8), TILE)
                grads = [gn_v[rows, cols] for cols in cols_of]
                xhats = [saved_v[i, XHAT, rows, cols].astype(F32) for cols in cols_of]
                qs = [grad * vec[j, GAIN : GAIN + 1, cols] for grad, cols in zip(grads, cols_of)]
                mean_q = row_sum(qs) * (1.0 / width)
                mean_qx = row_sum([q * xhat for q, xhat in zip(qs, xhats)]) * (1.0 / width)
                rstd = rst_v[i, rows, :]
                out = []
                for s, cols in enumerate(cols_of):
                    grad_conv = rstd * (qs[s] - mean_q - xhats[s] * mean_qx)
                    padded[s, inner, :] = grad_conv
                    g_now[rows, cols] = jnp.where(odd, x_v[rows, cols].astype(F32), fresh_v[rows, cols])
                    out += [c[3 * s] + fold(grads[s] * xhats[s]), c[3 * s + 1] + fold(grads[s]), c[3 * s + 2] + fold(grad_conv)]
                return tuple(out)

            sums = (jnp.zeros((8, LANES), F32),) * (3 * len(cols_of))
            tiles = frames // TILE
            if final:
                parts = hidden // COLS
                scale = jnp.zeros((8, width), F32)
                done = 0
                for n in range(parts):
                    scale = scale + down_chunk(n)
                    while done < tiles * (n + 1) // parts:
                        sums = norm_back(done, sums)
                        done += 1
                vg_v[i + 1, SCALE : SCALE + 1, :] = jnp.sum(scale, axis=0, keepdims=True)
                pltpu.make_async_copy(dwd_v.at[i], dlow_out.at[i], o_sem.at[i, 0]).start()
                pltpu.make_async_copy(saved.at[0, 0], nrm_v.at[i, 0], b_sem.at[i, 2]).wait()
                pltpu.make_async_copy(saved.at[0, 0], nrm_v.at[i, 1], b_sem.at[i, 3]).wait()
                pltpu.make_async_copy(gp_b.at[0], gp_v.at[i, 1], b_sem.at[i, 5]).wait()
            else:
                sums = lax.fori_loop(0, tiles, norm_back, sums, unroll=8)
            for s, cols in enumerate(cols_of):
                for k, row in enumerate((GAIN, SHIFT, CONV_B)):
                    vg_v[i + 1, row : row + 1, cols] = jnp.sum(sums[3 * s + k], axis=0, keepdims=True)

            if count > 2:

                @pl.when(odd & (step > 0))
                def _():
                    pltpu.make_async_copy(fresh_v, grads_out[0], s_sem.at[0]).wait()

            below = lax.max(j - 1, 0)
            for s, cols in enumerate(cols_of):

                def conv_back(t, c):
                    base = t * tall if isinstance(t, int) else pl.multiple_of(t * tall, tall)
                    rows = pl.ds(base, tall)
                    source = saved_v[i, STREAM, rows, cols].astype(F32)
                    centre = padded[s, pl.ds(base + PAD if isinstance(t, int) else pl.multiple_of(base + PAD, 8), tall), :]
                    total = g_now[rows, cols] + vec[j, 3:4, cols] * centre
                    taps = [None] * 7
                    taps[3] = c[3] + fold(centre * source)
                    for offset in OFFSETS:
                        term = padded[s, pl.ds(base + PAD - offset, tall), :] * masks[MASK_OF[-offset], rows, :]
                        total = total + vec[j, offset + 3 : offset + 4, cols] * term
                        taps[offset + 3] = c[offset + 3] + fold(term * source)
                    rounded = total.astype(BF16)
                    fresh_v[rows, cols] = total
                    x_v[rows, cols] = rounded
                    scaled = (vec[below, SCALE : SCALE + 1, cols] * jnp.where(odd, total, rounded.astype(F32))).astype(BF16)
                    gb_v[i, 0, rows, cols] = scaled
                    return tuple(taps) + (c[7] + fold(scaled.astype(F32)),)

                sums = (jnp.zeros((8, LANES), F32),) * 8
                if final:
                    chunks = [(m, n) for m in range(width // COLS) for n in range(hidden // width)]
                    done = 0
                    each = -(-len(chunks) // len(cols_of))
                    for m, n in chunks[s * each : (s + 1) * each]:
                        up_chunk(m, n)
                        while done < frames // tall // each * (chunks[s * each : (s + 1) * each].index((m, n)) + 1):
                            sums = conv_back(done, sums)
                            done += 1
                    while done < frames // tall:
                        sums = conv_back(done, sums)
                        done += 1
                else:
                    sums = lax.fori_loop(0, frames // tall, conv_back, sums, unroll=8)
                for k in range(7):
                    vg_v[i + 1, k : k + 1, cols] = jnp.sum(sums[k], axis=0, keepdims=True)
                vg_v[i, DOWN_B : DOWN_B + 1, cols] = jnp.sum(sums[7], axis=0, keepdims=True)
            if final:
                pltpu.make_async_copy(dwu_v.at[i], up_out.at[i], o_sem.at[i, 1]).start()
            for p in range(count // 2):

                @pl.when(i == 2 * p)
                def _():
                    pltpu.make_async_copy(fresh_v, grads_out[p], s_sem.at[0]).start()

            return carry

        for i in range(1, count + 1):
            vg_v[i, SCALE : SCALE + 1, :] = jnp.zeros((1, width), F32)
            vg_v[i, VEC_ROWS - 1 : VEC_ROWS, :] = jnp.zeros((1, width), F32)
        lax.fori_loop(0, count, layer, 0)
        pltpu.make_async_copy(x_v, send, s_sem.at[1]).start()
        pltpu.make_async_copy(vg_v.at[pl.ds(1, count)], vec_out, s_sem.at[2]).start()
        for i in range(count):
            if final:
                pltpu.make_async_copy(dwd_v.at[i], dlow_out.at[i], o_sem.at[i, 0]).wait()
                pltpu.make_async_copy(dwu_v.at[i], up_out.at[i], o_sem.at[i, 1]).wait()
            else:
                pltpu.make_async_copy(gb_v.at[i + 1, 0], gb.at[low + i], o_sem.at[i, 0]).wait()
                pltpu.make_async_copy(gp_v.at[i, 0], gp.at[low + i], o_sem.at[i, 1]).wait()
        pltpu.make_async_copy(fresh_v, grads_out[0], s_sem.at[0]).wait()
        pltpu.make_async_copy(x_v, send, s_sem.at[1]).wait()
        pltpu.make_async_copy(vg_v.at[pl.ds(1, count)], vec_out, s_sem.at[2]).wait()


ANY = pl.BlockSpec(memory_space=pl.ANY)
SMEM = pl.BlockSpec(memory_space=pltpu.SMEM)
VMEM = pl.BlockSpec(memory_space=pltpu.VMEM)


def run_forward(flags, x, masks, vec, weights, earlier):
    layers = vec.shape[0]
    frames, width = x.shape[1:]
    hidden = weights[0].shape[2]
    shapes = (
        jax.ShapeDtypeStruct((layers, frames, hidden), BF16),
        jax.ShapeDtypeStruct((layers, frames, hidden), BF16),
        jax.ShapeDtypeStruct((layers, KINDS, frames, width), BF16),
        jax.ShapeDtypeStruct((layers, frames, LANES), F32),
        jax.ShapeDtypeStruct((frames, width), F32),
        jax.ShapeDtypeStruct((frames, width), F32),
        jax.ShapeDtypeStruct((frames, width), BF16),
    )
    earlier = earlier[:-1]
    aliased = len(earlier)
    return pl.pallas_call(
        functools.partial(forward_kernel, layers, aliased),
        out_shape=shapes,
        in_specs=[SMEM, ANY, ANY, VMEM] + [ANY] * 4 + [ANY] * aliased,
        out_specs=(ANY,) * len(shapes),
        input_output_aliases={8 + i: i for i in range(aliased)},
        scratch_shapes=[
            pltpu.VMEM((layers, width, hidden), BF16),
            pltpu.VMEM((layers, hidden, width), BF16),
            pltpu.VMEM((layers, frames, hidden), BF16),
            pltpu.VMEM((layers, frames, hidden), BF16),
            pltpu.VMEM((layers, KINDS, frames, width), BF16),
            pltpu.VMEM((layers, frames, LANES), F32),
            pltpu.VMEM((width // LANES, frames + 2 * PAD, LANES), F32),
            pltpu.VMEM((frames, width), F32),
            pltpu.VMEM((2, frames, width), F32),
            pltpu.VMEM((frames, width), BF16),
            pltpu.VMEM((frames + 2 * PAD, LANES), F32),
            pltpu.VMEM((6, frames, LANES), F32),
            pltpu.SemaphoreType.DMA((layers, 2)),
            pltpu.SemaphoreType.DMA((2,)),
            pltpu.SemaphoreType.DMA((layers, 4)),
            pltpu.SemaphoreType.DMA((3,)),
        ],
        compiler_params=pltpu.CompilerParams(vmem_limit_bytes=VMEM_LIMIT),
        cost_estimate=pl.CostEstimate(flops=layers * 4 * frames * width * hidden, bytes_accessed=40 * 2**20, transcendentals=0),
    )(flags, x, masks, vec, *weights, *earlier)


def run_backward(flags, g, masks, vec, weights, state, earlier, low=0, count=4, others=None):
    frames, width = g.shape[1:]
    hidden = weights[0].shape[2]
    final = others is not None
    rows = 2 if final else 1
    outs = (
        (
            jax.ShapeDtypeStruct((count, hidden, width), BF16),
            jax.ShapeDtypeStruct((count, width, hidden), BF16),
        )
        if final
        else (
            jax.ShapeDtypeStruct((count, frames, width), BF16),
            jax.ShapeDtypeStruct((count, frames, hidden), BF16),
        )
    )
    shapes = (
        *outs,
        jax.ShapeDtypeStruct((count, VEC_ROWS, width), F32),
        jax.ShapeDtypeStruct((frames, width), BF16),
        *(jax.ShapeDtypeStruct((frames, width), F32) for _ in range(count // 2)),
    )
    aliased = len(earlier)
    others = tuple(others or ())
    scratch = [
        pltpu.VMEM((count, width, hidden), BF16),
        pltpu.VMEM((count, hidden, width), BF16),
        pltpu.VMEM((count, frames, hidden), BF16),
        pltpu.VMEM((count, 2, frames, width), BF16),
        pltpu.VMEM((count, frames, LANES), F32),
        pltpu.VMEM((count + 1, rows, frames, width), BF16),
        pltpu.VMEM((count, rows, frames, hidden), BF16),
        pltpu.VMEM((count + 1, VEC_ROWS, width), F32),
        pltpu.VMEM((frames, width), F32),
        pltpu.VMEM((frames, width), F32),
        pltpu.VMEM((frames, width), F32),
        pltpu.VMEM((width // LANES, frames + 2 * PAD, LANES), F32),
        pltpu.VMEM((frames, width), BF16),
        pltpu.VMEM((frames + 2 * PAD, LANES), F32),
        pltpu.VMEM((6, frames, LANES), F32),
        pltpu.SemaphoreType.DMA((count, 5)),
        pltpu.SemaphoreType.DMA((2,)),
        pltpu.SemaphoreType.DMA((count, 2)),
        pltpu.SemaphoreType.DMA((3,)),
    ]
    if final:
        scratch += [
            pltpu.VMEM((count, 2, frames, hidden), BF16),
            pltpu.VMEM((count, 2, frames, width), BF16),
            pltpu.VMEM((count, hidden, width), BF16),
            pltpu.VMEM((count, width, hidden), BF16),
            pltpu.SemaphoreType.DMA((count, 6)),
        ]
    first_alias = 11 + len(others)
    return pl.pallas_call(
        functools.partial(backward_kernel, low, count, final, aliased),
        out_shape=shapes,
        in_specs=[SMEM, ANY, ANY, VMEM] + [ANY] * (7 + len(others) + aliased),
        out_specs=(ANY,) * len(shapes),
        input_output_aliases={first_alias + i: i for i in range(aliased)},
        scratch_shapes=scratch,
        compiler_params=pltpu.CompilerParams(vmem_limit_bytes=VMEM_LIMIT),
        cost_estimate=pl.CostEstimate(flops=count * (12 if final else 4) * frames * width * hidden, bytes_accessed=10 * count * 2**20, transcendentals=0),
    )(flags, g, masks, vec, *weights, *state, *others, *earlier)


def sum_doubling(value, axis):
    count = lax.axis_size(axis)
    step = 1
    while step < count:
        value = value + lax.ppermute(value, axis, [(d, d ^ step) for d in range(count)])
        step *= 2
    return value


def ring_order(count):
    return list(range(0, count, 2)) + list(range(count - 1, 0, -2))


def ring_scatter(parts, directions, slicers, axis):
    count = lax.axis_size(axis)
    order = ring_order(count)
    place_of = [order.index(d) for d in range(count)]
    place = jnp.array(place_of, jnp.int32)[lax.axis_index(axis)]
    order_table = jnp.array(order, jnp.int32)

    def local(i, owner_place):
        device = order_table[lax.rem(owner_place + 2 * count, count)]
        return functools.reduce(jnp.add, [slicers[i](addend, device).astype(F32) for addend in parts[i]])

    flowing = [local(i, place - way).astype(BF16) for i, way in enumerate(directions)]
    for step in range(count - 1):
        arrived = [
            lax.ppermute(value, axis, [(order[p], order[(p + way) % count]) for p in range(count)])
            for value, way in zip(flowing, directions)
        ]
        flowing = []
        for i, way in enumerate(directions):
            total = arrived[i].astype(F32) + local(i, place - way * (2 + step))
            flowing.append(total.astype(BF16) if step < count - 2 else total)
    return flowing


def per_device(
    inputs,
    segment_ids,
    cotangent,
    conv_weight,
    conv_bias,
    norm_gain,
    norm_bias,
    up_weight,
    up_bias,
    down_weight,
    down_bias,
    layer_scale,
):
    micro, _, frames, width = inputs.shape
    hidden = up_weight.shape[2]
    shares = lax.axis_size("dp")
    section = lax.axis_index("section")
    chip, core = section // 2, section % 2
    exchange = [(0, 1), (1, 0), (2, 3), (3, 2)]

    small = jnp.concatenate(
        [
            conv_weight,
            conv_bias[:, None],
            norm_gain[:, None],
            norm_bias[:, None],
            down_bias[:, None],
            layer_scale[:, None],
            up_bias.reshape(2, -1, width),
            jnp.zeros((2, 1, width), BF16),
        ],
        axis=1,
    )
    small_peer = lax.ppermute(small, "section", exchange)
    up_peer = lax.ppermute(up_weight, "section", exchange)
    down_peer = lax.ppermute(down_weight, "section", exchange)
    vec = jnp.where(core == 0, jnp.concatenate([small, small_peer]), jnp.concatenate([small_peer, small])).astype(F32)
    weights = (up_weight, down_weight, up_peer, down_peer)
    masks = jnp.broadcast_to(segment_ids[:, 0, :, None].astype(F32), (micro, frames, LANES))
    inputs, cotangent = inputs[:, 0], cotangent[:, 0]

    def flags(active, index, micro_slot):
        return jnp.stack([jnp.asarray(v, jnp.int32) for v in (active, core, index, 2 * core + micro_slot)])

    first, last = (chip == 0).astype(jnp.int32), (chip == 1).astype(jnp.int32)
    down_pairs, up_pairs = [(0, 2), (1, 3)], [(2, 0), (3, 1)]
    state_a = run_forward(flags(first, 2 * core, 0), inputs, masks, vec, weights, ())
    sent_a = lax.ppermute(state_a[6], "section", down_pairs)
    state_b = run_forward(flags(first, 2 * core + 1, 1), inputs, masks, vec, weights, ())
    sent_b = lax.ppermute(state_b[6], "section", down_pairs)
    state_a = run_forward(flags(last, 0, 0), sent_a[None], masks, vec, weights, state_a)
    state_b = run_forward(flags(last, 0, 1), sent_b[None], masks, vec, weights, state_b)

    def last_row(active, g, index, earlier):
        others = (state_a[0], state_b[0], state_b[2], back_b[0], back_b[1])
        high = run_backward(flags(active, index, 0), g, masks, vec, weights, state_a[1:4], earlier[:5], 2, 2, others)
        low = run_backward(flags(active, 0, 0), high[3][None], masks, vec, weights, state_a[1:4], earlier[5:], 0, 2, others)
        return high + low

    back_b = run_backward(flags(last, 2 * core + 1, 1), cotangent, masks, vec, weights, state_b[1:4], ())
    sent_b = lax.ppermute(back_b[3], "section", up_pairs)
    back_a = last_row(last, cotangent, 2 * core, ())
    sent_a = lax.ppermute(back_a[8], "section", up_pairs)
    back_b = run_backward(flags(first, 0, 1), sent_b[None], masks, vec, weights, state_b[1:4], back_b)
    back_a = last_row(first, sent_a[None], 0, back_a)
    down_high, up_high, vec_high, _, grad_high, down_low, up_low, vec_low, _, grad_low = back_a

    to_high, to_low = [(0, 1), (2, 3)], [(1, 0), (3, 2)]
    down_recv_high = lax.ppermute(down_high, "section", to_high)
    up_recv_high = lax.ppermute(up_high, "section", to_high)
    down_recv_low = lax.ppermute(down_low, "section", to_low)
    up_recv_low = lax.ppermute(up_low, "section", to_low)

    vec_high = vec_high + back_b[2][2:]
    vec_low = vec_low + back_b[2][:2]
    totals = jnp.where(core == 0, vec_low, vec_high) + lax.ppermute(jnp.where(core == 0, vec_high, vec_low), "section", exchange)
    totals = sum_doubling(totals, "dp")
    scale_grad = (totals[:, SCALE] + down_bias.astype(F32) * totals[:, DOWN_B]) / layer_scale.astype(F32)
    shard = lax.axis_index("dp")

    def share(value):
        size = value.shape[-1] // shares
        return lax.dynamic_slice_in_dim(value, shard * size, size, value.ndim - 1)

    def slice_of(pair, device, size):
        low, high = (lax.dynamic_slice_in_dim(value, device * size, size, 1) for value in pair)
        return jnp.where(core == 0, low, high)

    def slice_up(pair, device):
        return slice_of(pair, device, width // shares)

    def slice_down(pair, device):
        return slice_of(pair, device, hidden // shares)

    up_share, down_share = ring_scatter(
        [[(up_low, up_high), (up_recv_low, up_recv_high)], [(down_low, down_high), (down_recv_low, down_recv_high)]],
        [1, -1],
        [slice_up, slice_down],
        "dp",
    )

    def assemble(low_a, low_b, high_a, high_b):
        low, high = jnp.stack([low_a, low_b]), jnp.stack([high_a, high_b])
        other = lax.ppermute(jnp.where(core == 0, high, low), "section", exchange)
        return jnp.where(core == 0, jnp.concatenate([low, other]), jnp.concatenate([other, high]))[None, :, None]

    section_outputs = assemble(state_a[4], state_b[4], state_a[5], state_b[5])
    input_grads = assemble(grad_low, back_b[4], grad_high, back_b[5])
    return (
        section_outputs,
        input_grads,
        share(totals[:, :CONV_B]),
        share(totals[:, CONV_B]),
        share(totals[:, GAIN]),
        share(totals[:, SHIFT]),
        up_share,
        share(totals[:, UP_B : UP_B + hidden // width].reshape(2, -1)),
        down_share,
        share(totals[:, DOWN_B]),
        share(scale_grad),
    )


def solution(mesh):
    in_specs = (
        P(None, "dp", None, None),
        P(None, "dp", None),
        P(None, "dp", None, None),
        P("section", None, None),
        P("section", None),
        P("section", None),
        P("section", None),
        P("section", None, None),
        P("section", None),
        P("section", None, None),
        P("section", None),
        P("section", None),
    )
    out_specs = (
        P("section", None, "dp", None, None),
        P("section", None, "dp", None, None),
        P("section", None, "dp"),
        P("section", "dp"),
        P("section", "dp"),
        P("section", "dp"),
        P("section", "dp", None),
        P("section", "dp"),
        P("section", "dp", None),
        P("section", "dp"),
        P("section", "dp"),
    )
    return jax.shard_map(per_device, mesh=mesh, in_specs=in_specs, out_specs=out_specs, check_vma=False)
```

```python
import functools

import jax
import jax.numpy as jnp
from jax import lax
from jax.experimental import pallas as pl
from jax.experimental.pallas import tpu as pltpu
from jax.sharding import PartitionSpec as P

EPSILON = 1e-06
INV_SQRT2 = 0.7071067811865476
INV_SQRT_PI = 0.5641895835477563
LOG2_E = 1.4426950408889634
F32 = jnp.float32
BF16 = jnp.bfloat16
TILE = 32
PAD = 8
COLS = 256
VMEM_LIMIT = 60 * 2**20

CONV_B, GAIN, SHIFT, DOWN_B, SCALE, UP_B, VEC_ROWS = 7, 8, 9, 10, 11, 12, 16
XHAT, STREAM, NORMED, KINDS = 0, 1, 2, 3
LANES = 128
OFFSETS = (1, 2, 3, -1, -2, -3)
MASK_OF = {offset: k for k, offset in enumerate(OFFSETS)}


def slabs(width):
    return [slice(c, c + LANES) for c in range(0, width, LANES)]


def row_sum(parts):
    return jnp.sum(functools.reduce(jnp.add, parts), axis=1, keepdims=True)


def fold(value):
    return functools.reduce(jnp.add, [value[8 * i : 8 * i + 8] for i in range(value.shape[0] // 8)])


def clear_edges(padded, frames):
    for slab in range(padded.shape[0]):
        padded[slab, 0:PAD, :] = jnp.zeros((PAD, LANES), F32)
        padded[slab, PAD + frames : PAD + frames + PAD, :] = jnp.zeros((PAD, LANES), F32)


def build_masks(seg_v, masks):
    frames = masks.shape[1]
    seg_v[0:PAD, :] = jnp.full((PAD, LANES), -1.0, F32)
    seg_v[PAD + frames : PAD + frames + PAD, :] = jnp.full((PAD, LANES), -1.0, F32)

    def body(i, carry):
        base = pl.multiple_of(i * 64, 64)
        here = seg_v[pl.ds(base + PAD, 64), :]
        for k, offset in enumerate(OFFSETS):
            there = seg_v[pl.ds(base + PAD + offset, 64), :]
            masks[k, pl.ds(base, 64), :] = jnp.where(there == here, 1.0, 0.0)
        return carry

    lax.fori_loop(0, frames // 64, body, 0)


def start_weights(core, layer, own, peer, target, sem):
    @pl.when(core == lax.div(layer, 2))
    def _():
        pltpu.make_async_copy(own.at[lax.rem(layer, 2)], target, sem).start()

    @pl.when(core != lax.div(layer, 2))
    def _():
        pltpu.make_async_copy(peer.at[lax.rem(layer, 2)], target, sem).start()


def forward_kernel(call, layers, aliased, received, flags, x_hbm, seg_hbm, vec, own_up, own_down, peer_up, peer_down, *rest):
    rest = rest[aliased:]
    hid, dge, saved, rst, low_out, high_out, send = rest[:7]
    (up_v, down_v, hid_v, dge_v, saved_v, rst_v, stream, acc, out_v, x_v, seg_v, masks, w_sem, in_sem, o_sem, s_sem) = rest[7:]
    frames, width = acc.shape
    hidden = hid_v.shape[2]

    @pl.when(flags[call, 0] == 1)
    def _():
        core = flags[call, 1]
        if not received:
            pltpu.make_async_copy(x_hbm.at[flags[call, 2]], x_v, in_sem.at[0]).start()
        pltpu.make_async_copy(seg_hbm.at[flags[call, 2]], seg_v.at[pl.ds(PAD, frames)], in_sem.at[1]).start()
        def fetch(j):
            start_weights(core, j, own_up, peer_up, up_v.at[j], w_sem.at[j, 0])
            start_weights(core, j, own_down, peer_down, down_v.at[j], w_sem.at[j, 1])

        fetch(0)
        clear_edges(stream, frames)
        pltpu.make_async_copy(seg_hbm.at[0], seg_v.at[pl.ds(PAD, frames)], in_sem.at[1]).wait()
        build_masks(seg_v, masks)
        if not received:
            pltpu.make_async_copy(x_hbm.at[0], x_v, in_sem.at[0]).wait()
        start = x_hbm if received else x_v
        for c, cols in enumerate(slabs(width)):
            stream[c, PAD : PAD + frames, :] = start[:, cols].astype(F32)

        def layer(j, carry):
            def conv_norm(i, c):
                base = pl.multiple_of(i * TILE, TILE)
                rows = pl.ds(base, TILE)
                parts = []
                for s, cols in enumerate(slabs(width)):
                    centre = stream[s, pl.ds(base + PAD, TILE), :]
                    saved_v[j, STREAM, rows, cols] = centre.astype(BF16)
                    total = vec[j, CONV_B : CONV_B + 1, cols] + vec[j, 3:4, cols] * centre
                    for offset in OFFSETS:
                        neighbour = stream[s, pl.ds(base + PAD + offset, TILE), :] * masks[MASK_OF[offset], rows, :]
                        total = total + vec[j, offset + 3 : offset + 4, cols] * neighbour
                    parts.append(total)
                mean = row_sum(parts) * (1.0 / width)
                parts = [part - mean for part in parts]
                rstd = lax.rsqrt(row_sum([part * part for part in parts]) * (1.0 / width) + EPSILON)
                for part, cols in zip(parts, slabs(width)):
                    xhat = part * rstd
                    saved_v[j, XHAT, rows, cols] = xhat.astype(BF16)
                    saved_v[j, NORMED, rows, cols] = (xhat * vec[j, GAIN : GAIN + 1, cols] + vec[j, SHIFT : SHIFT + 1, cols]).astype(BF16)
                rst_v[j, rows, :] = jnp.broadcast_to(rstd, (TILE, LANES))
                return c

            lax.fori_loop(0, frames // TILE, conv_norm, 0, unroll=16)
            pltpu.make_async_copy(saved_v.at[j], saved.at[j], o_sem.at[j, 3]).start()
            pltpu.make_async_copy(rst_v.at[j], rst.at[j], o_sem.at[j, 2]).start()
            pltpu.make_async_copy(own_up.at[0], up_v.at[j], w_sem.at[j, 0]).wait()

            @pl.when(j + 1 < layers)
            def _():
                fetch(j + 1)

            for n in range(hidden // COLS):
                cols = slice(n * COLS, (n + 1) * COLS)
                row, start = UP_B + n * COLS // width, (n * COLS) % width
                value = jnp.dot(saved_v[j, NORMED], up_v[j, :, cols], preferred_element_type=F32) + vec[j, row : row + 1, start : start + COLS]
                scaled = value * INV_SQRT2
                phi_sum = 0.5 + 0.5 * lax.erf(scaled)
                hid_v[j, :, cols] = (value * phi_sum).astype(BF16)
                dge_v[j, :, cols] = (phi_sum + scaled * INV_SQRT_PI * jnp.exp2(scaled * scaled * -LOG2_E)).astype(BF16)
            pltpu.make_async_copy(hid_v.at[j], hid.at[j], o_sem.at[j, 0]).start()
            pltpu.make_async_copy(dge_v.at[j], dge.at[j], o_sem.at[j, 1]).start()
            pltpu.make_async_copy(own_down.at[0], down_v.at[j], w_sem.at[j, 1]).wait()
            acc[...] = jnp.dot(hid_v[j], down_v[j], preferred_element_type=F32)

            def finish(ends_section, i, c):
                base = pl.multiple_of(i * TILE, TILE)
                rows = pl.ds(base, TILE)
                for s, cols in enumerate(slabs(width)):
                    inner = pl.ds(pl.multiple_of(base + PAD, 8), TILE)
                    branch = acc[rows, cols] + vec[j, DOWN_B : DOWN_B + 1, cols]
                    fresh = stream[s, inner, :] + vec[j, SCALE : SCALE + 1, cols] * branch
                    if ends_section:
                        rounded = fresh.astype(BF16)
                        out_v[lax.div(j, 2), rows, cols] = fresh
                        x_v[rows, cols] = rounded
                        fresh = rounded.astype(F32)
                    stream[s, inner, :] = fresh
                return c

            @pl.when(lax.rem(j, 2) == 1)
            def _():
                lax.fori_loop(0, frames // TILE, functools.partial(finish, True), 0)

            @pl.when(lax.rem(j, 2) == 0)
            def _():
                lax.fori_loop(0, frames // TILE, functools.partial(finish, False), 0)

            @pl.when(j == 1)
            def _():
                pltpu.make_async_copy(out_v.at[0], low_out, s_sem.at[0]).start()

            return carry

        lax.fori_loop(0, layers, layer, 0)
        pltpu.make_async_copy(out_v.at[1], high_out, s_sem.at[1]).start()
        pltpu.make_async_copy(x_v, send, s_sem.at[2]).start()
        for j in range(layers):
            pltpu.make_async_copy(hid_v.at[j], hid.at[j], o_sem.at[j, 0]).wait()
            pltpu.make_async_copy(dge_v.at[j], dge.at[j], o_sem.at[j, 1]).wait()
            pltpu.make_async_copy(rst_v.at[j], rst.at[j], o_sem.at[j, 2]).wait()
            pltpu.make_async_copy(saved_v.at[j], saved.at[j], o_sem.at[j, 3]).wait()
        pltpu.make_async_copy(out_v.at[0], low_out, s_sem.at[0]).wait()
        pltpu.make_async_copy(out_v.at[1], high_out, s_sem.at[1]).wait()
        pltpu.make_async_copy(x_v, send, s_sem.at[2]).wait()


SUMS, HEAD = 6, 2


def send_sums(core, section, slots, kind, i, source, targets, sem):
    kept, head, tail = targets
    shares = kept.shape[0]
    size = source.shape[0] // shares
    for d in range(shares):
        piece = source.at[pl.ds(d * size, size)]
        place = slots[2 * kind + i, d]

        @pl.when(core == section)
        def _():
            pltpu.make_async_copy(piece, kept.at[place, i], sem).start()

        @pl.when((core != section) & (place < HEAD))
        def _():
            pltpu.make_async_copy(piece, head.at[place, i], sem).start()

        @pl.when((core != section) & (place >= HEAD))
        def _():
            pltpu.make_async_copy(piece, tail.at[place - HEAD, i], sem).start()


def backward_kernel(call, low, count, final, aliased, received, flags, g_hbm, seg_hbm, vec, own_up, own_down, peer_up, peer_down, dge, saved, rst, *rest):
    if final:
        slots, hid, hid_b, saved_b, gb_b, gp_b = rest[:6]
        rest = rest[6 + aliased :]
        sums_out, (vec_out, grad_out, send) = rest[:SUMS], rest[SUMS : SUMS + 3]
        grads_out = (grad_out,)
        rest = rest[SUMS + 3 :]
        (up_v, down_v, dge_v, saved_v, rst_v, gb_v, gp_v, vg_v, g_now, fresh_v, gn_v, padded, x_v, seg_v, masks, w_sem, in_sem, o_sem, s_sem) = rest[:19]
        (hid_v, nrm_v, dwd_v, dwu_v, b_sem) = rest[19:]
    else:
        rest = rest[aliased:]
        gb, gp, vec_out, send = rest[:4]
        grads_out = rest[4 : 4 + count // 2]
        rest = rest[4 + count // 2 :]
        (up_v, down_v, dge_v, saved_v, rst_v, gb_v, gp_v, vg_v, g_now, fresh_v, gn_v, padded, x_v, seg_v, masks, w_sem, in_sem, o_sem, s_sem) = rest
    frames, width = g_now.shape
    hidden = dge_v.shape[2]
    nt = (((1,), (1,)), ((), ()))
    tn = (((0,), (0,)), ((), ()))
    tall = 2 * TILE
    cols_of = slabs(width)

    @pl.when(flags[call, 0] == 1)
    def _():
        core = flags[call, 1]
        if not received:
            pltpu.make_async_copy(g_hbm.at[0 if final else flags[call, 2]], x_v, in_sem.at[0]).start()
        pltpu.make_async_copy(seg_hbm.at[flags[call, 2]], seg_v.at[pl.ds(PAD, frames)], in_sem.at[1]).start()
        def fetch(i):
            j = low + i
            start_weights(core, j, own_down, peer_down, down_v.at[i], w_sem.at[i, 1])
            pltpu.make_async_copy(dge.at[j], dge_v.at[i], w_sem.at[i, 3]).start()
            start_weights(core, j, own_up, peer_up, up_v.at[i], w_sem.at[i, 0])
            pltpu.make_async_copy(rst.at[j], rst_v.at[i], w_sem.at[i, 4]).start()
            pltpu.make_async_copy(saved.at[j, 0:2], saved_v.at[i], w_sem.at[i, 2]).start()

        fetch(count - 1)
        clear_edges(padded, frames)
        pltpu.make_async_copy(seg_hbm.at[0], seg_v.at[pl.ds(PAD, frames)], in_sem.at[1]).wait()
        build_masks(seg_v, masks)
        if received:
            x_v[...] = g_hbm[...]
        else:
            pltpu.make_async_copy(g_hbm.at[0], x_v, in_sem.at[0]).wait()
        for cols in cols_of:

            def enter(t, c):
                rows = pl.ds(pl.multiple_of(t * tall, tall), tall)
                scaled = (vec[low + count - 1, SCALE : SCALE + 1, cols] * x_v[rows, cols].astype(F32)).astype(BF16)
                gb_v[count, 0, rows, cols] = scaled
                return c + fold(scaled.astype(F32))

            total = lax.fori_loop(0, frames // tall, enter, jnp.zeros((8, LANES), F32))
            vg_v[count, DOWN_B : DOWN_B + 1, cols] = jnp.sum(total, axis=0, keepdims=True)

        def layer(step, carry):
            i = count - 1 - step
            j = low + i
            if not final:
                pltpu.make_async_copy(gb_v.at[i + 1, 0], gb.at[j], o_sem.at[i, 0]).start()
            pltpu.make_async_copy(own_down.at[0], down_v.at[i], w_sem.at[i, 1]).wait()
            pltpu.make_async_copy(dge.at[0], dge_v.at[i], w_sem.at[i, 3]).wait()
            if final:
                pltpu.make_async_copy(hid.at[j], hid_v.at[i, 0], b_sem.at[i, 0]).start()
                pltpu.make_async_copy(hid_b.at[j], hid_v.at[i, 1], b_sem.at[i, 1]).start()
                pltpu.make_async_copy(gb_b.at[j], gb_v.at[i + 1, 1], b_sem.at[i, 4]).start()
                pltpu.make_async_copy(saved.at[j, NORMED], nrm_v.at[i, 0], b_sem.at[i, 2]).start()
                pltpu.make_async_copy(saved_b.at[j, NORMED], nrm_v.at[i, 1], b_sem.at[i, 3]).start()
                pltpu.make_async_copy(gp_b.at[j], gp_v.at[i, 1], b_sem.at[i, 5]).start()
            for n in range(hidden // COLS):
                cols = slice(n * COLS, (n + 1) * COLS)
                value = lax.dot_general(gb_v[i + 1, 0], down_v[i, cols, :], nt, preferred_element_type=F32)
                rounded = (value * dge_v[i, :, cols].astype(F32)).astype(BF16)
                gp_v[i, 0, :, cols] = rounded
                row, start = UP_B + n * COLS // width, (n * COLS) % width
                vg_v[i + 1, row : row + 1, start : start + COLS] = jnp.sum(rounded.astype(F32), axis=0, keepdims=True)
            if not final:
                pltpu.make_async_copy(gp_v.at[i, 0], gp.at[j], o_sem.at[i, 1]).start()
            pltpu.make_async_copy(own_up.at[0], up_v.at[i], w_sem.at[i, 0]).wait()
            gn_v[...] = lax.dot_general(gp_v[i, 0], up_v[i], nt, preferred_element_type=F32)
            pltpu.make_async_copy(rst.at[0], rst_v.at[i], w_sem.at[i, 4]).wait()
            pltpu.make_async_copy(saved.at[0, 0:2], saved_v.at[i], w_sem.at[i, 2]).wait()

            @pl.when(i > 0)
            def _():
                fetch(i - 1)

            if final:
                pltpu.make_async_copy(hid.at[0], hid_v.at[i, 0], b_sem.at[i, 0]).wait()
                pltpu.make_async_copy(hid.at[0], hid_v.at[i, 1], b_sem.at[i, 1]).wait()
                pltpu.make_async_copy(gb_b.at[0], gb_v.at[i + 1, 1], b_sem.at[i, 4]).wait()

            def down_chunk(n):
                rows = slice(n * COLS, (n + 1) * COLS)
                left = hid_v[i, :, :, rows].reshape(2 * frames, COLS)
                right = gb_v[i + 1].reshape(2 * frames, width)
                value = lax.dot_general(left, right, tn, preferred_element_type=F32)
                dwd_v[i, rows, :] = value.astype(BF16)
                return fold(value * down_v[i, rows, :].astype(F32))

            def up_chunk(m, n):
                rows = slice(m * COLS, (m + 1) * COLS)
                cols = slice(n * width, (n + 1) * width)
                left = nrm_v[i, :, :, rows].reshape(2 * frames, COLS)
                right = gp_v[i, :, :, cols].reshape(2 * frames, width)
                dwu_v[i, rows, cols] = lax.dot_general(left, right, tn, preferred_element_type=F32).astype(BF16)

            odd = lax.rem(i, 2) == 1

            def norm_back(t, c):
                base = t * TILE if isinstance(t, int) else pl.multiple_of(t * TILE, TILE)
                rows = pl.ds(base, TILE)
                inner = pl.ds(base + PAD if isinstance(t, int) else pl.multiple_of(base + PAD, 8), TILE)
                grads = [gn_v[rows, cols] for cols in cols_of]
                xhats = [saved_v[i, XHAT, rows, cols].astype(F32) for cols in cols_of]
                qs = [grad * vec[j, GAIN : GAIN + 1, cols] for grad, cols in zip(grads, cols_of)]
                mean_q = row_sum(qs) * (1.0 / width)
                mean_qx = row_sum([q * xhat for q, xhat in zip(qs, xhats)]) * (1.0 / width)
                rstd = rst_v[i, rows, :]
                out = []
                for s, cols in enumerate(cols_of):
                    grad_conv = rstd * (qs[s] - mean_q - xhats[s] * mean_qx)
                    padded[s, inner, :] = grad_conv
                    g_now[rows, cols] = jnp.where(odd, x_v[rows, cols].astype(F32), fresh_v[rows, cols])
                    out += [c[3 * s] + fold(grads[s] * xhats[s]), c[3 * s + 1] + fold(grads[s]), c[3 * s + 2] + fold(grad_conv)]
                return tuple(out)

            sums = (jnp.zeros((8, LANES), F32),) * (3 * len(cols_of))
            tiles = frames // TILE
            if final:
                parts = hidden // COLS
                scale = jnp.zeros((8, width), F32)
                done = 0
                for n in range(parts):
                    scale = scale + down_chunk(n)
                    while done < tiles * (n + 1) // parts:
                        sums = norm_back(done, sums)
                        done += 1
                vg_v[i + 1, SCALE : SCALE + 1, :] = jnp.sum(scale, axis=0, keepdims=True)
                send_sums(core, low // 2, slots, 0, i, dwd_v.at[i], sums_out[:3], o_sem.at[i, 0])
                pltpu.make_async_copy(saved.at[0, 0], nrm_v.at[i, 0], b_sem.at[i, 2]).wait()
                pltpu.make_async_copy(saved.at[0, 0], nrm_v.at[i, 1], b_sem.at[i, 3]).wait()
                pltpu.make_async_copy(gp_b.at[0], gp_v.at[i, 1], b_sem.at[i, 5]).wait()
            else:
                sums = lax.fori_loop(0, tiles, norm_back, sums, unroll=8)
            for s, cols in enumerate(cols_of):
                for k, row in enumerate((GAIN, SHIFT, CONV_B)):
                    vg_v[i + 1, row : row + 1, cols] = jnp.sum(sums[3 * s + k], axis=0, keepdims=True)

            if count > 2:

                @pl.when(odd & (step > 0))
                def _():
                    pltpu.make_async_copy(fresh_v, grads_out[0], s_sem.at[0]).wait()

            below = lax.max(j - 1, 0)
            for s, cols in enumerate(cols_of):

                def conv_back(t, c):
                    base = t * tall if isinstance(t, int) else pl.multiple_of(t * tall, tall)
                    rows = pl.ds(base, tall)
                    source = saved_v[i, STREAM, rows, cols].astype(F32)
                    centre = padded[s, pl.ds(base + PAD if isinstance(t, int) else pl.multiple_of(base + PAD, 8), tall), :]
                    total = g_now[rows, cols] + vec[j, 3:4, cols] * centre
                    taps = [None] * 7
                    taps[3] = c[3] + fold(centre * source)
                    for offset in OFFSETS:
                        term = padded[s, pl.ds(base + PAD - offset, tall), :] * masks[MASK_OF[-offset], rows, :]
                        total = total + vec[j, offset + 3 : offset + 4, cols] * term
                        taps[offset + 3] = c[offset + 3] + fold(term * source)
                    rounded = total.astype(BF16)
                    fresh_v[rows, cols] = total
                    x_v[rows, cols] = rounded
                    scaled = (vec[below, SCALE : SCALE + 1, cols] * jnp.where(odd, total, rounded.astype(F32))).astype(BF16)
                    gb_v[i, 0, rows, cols] = scaled
                    return tuple(taps) + (c[7] + fold(scaled.astype(F32)),)

                sums = (jnp.zeros((8, LANES), F32),) * 8
                if final:
                    chunks = [(m, n) for m in range(width // COLS) for n in range(hidden // width)]
                    done = 0
                    each = -(-len(chunks) // len(cols_of))
                    for m, n in chunks[s * each : (s + 1) * each]:
                        up_chunk(m, n)
                        while done < frames // tall // each * (chunks[s * each : (s + 1) * each].index((m, n)) + 1):
                            sums = conv_back(done, sums)
                            done += 1
                    while done < frames // tall:
                        sums = conv_back(done, sums)
                        done += 1
                else:
                    sums = lax.fori_loop(0, frames // tall, conv_back, sums, unroll=8)
                for k in range(7):
                    vg_v[i + 1, k : k + 1, cols] = jnp.sum(sums[k], axis=0, keepdims=True)
                vg_v[i, DOWN_B : DOWN_B + 1, cols] = jnp.sum(sums[7], axis=0, keepdims=True)
            if final:
                send_sums(core, low // 2, slots, 1, i, dwu_v.at[i], sums_out[3:], o_sem.at[i, 1])
            for p in range(count // 2):

                @pl.when(i == 2 * p)
                def _():
                    pltpu.make_async_copy(fresh_v, grads_out[p], s_sem.at[0]).start()

            return carry

        for i in range(1, count + 1):
            vg_v[i, SCALE : SCALE + 1, :] = jnp.zeros((1, width), F32)
            vg_v[i, VEC_ROWS - 1 : VEC_ROWS, :] = jnp.zeros((1, width), F32)
        lax.fori_loop(0, count, layer, 0)
        pltpu.make_async_copy(x_v, send, s_sem.at[1]).start()
        pltpu.make_async_copy(vg_v.at[pl.ds(1, count)], vec_out.at[pl.ds(low, count)], s_sem.at[2]).start()
        for i in range(count):
            if final:
                pltpu.make_async_copy(dwd_v.at[i], dwd_v.at[i], o_sem.at[i, 0]).wait()
                pltpu.make_async_copy(dwu_v.at[i], dwu_v.at[i], o_sem.at[i, 1]).wait()
            else:
                pltpu.make_async_copy(gb_v.at[i + 1, 0], gb.at[low + i], o_sem.at[i, 0]).wait()
                pltpu.make_async_copy(gp_v.at[i, 0], gp.at[low + i], o_sem.at[i, 1]).wait()
        pltpu.make_async_copy(fresh_v, grads_out[0], s_sem.at[0]).wait()
        pltpu.make_async_copy(x_v, send, s_sem.at[1]).wait()
        pltpu.make_async_copy(vg_v.at[pl.ds(1, count)], vec_out.at[pl.ds(low, count)], s_sem.at[2]).wait()


def weight_kernel(call, aliased, flags, slots, down_a, down_b, *rest):
    hid_a, hid_b, gb_a, gb_b, saved_a, saved_b, gp_a, gp_b = rest[:8]
    rest = rest[8 + aliased :]
    sums_out, scale_out = rest[:SUMS], rest[SUMS]
    hid_v, gb_v, nrm_v, gp_v, down_v, dwd_v, dwu_v, scale_v, sem, o_sem, s_sem = rest[SUMS + 1 :]
    frames, width = gb_v.shape[2:]
    hidden = hid_v.shape[3]
    layers = hid_a.shape[0]
    tn = (((0,), (0,)), ((), ()))

    @pl.when(flags[call, 0] == 1)
    def _():
        core = flags[call, 1]

        def copies(j, slot):
            pairs = []
            for row, (hid, gb, saved, gp) in enumerate(((hid_a, gb_a, saved_a, gp_a), (hid_b, gb_b, saved_b, gp_b))):
                pairs += [
                    (hid.at[j], hid_v.at[slot, row]),
                    (gb.at[j], gb_v.at[slot, row]),
                    (saved.at[j, NORMED], nrm_v.at[slot, row]),
                    (gp.at[j], gp_v.at[slot, row]),
                ]
            return [pltpu.make_async_copy(a, b, sem.at[slot, k]) for k, (a, b) in enumerate(pairs)]

        def fetch(j):
            start_weights(core, j, down_a, down_b, down_v.at[j % 2], sem.at[j % 2, 8])
            for copy in copies(j, j % 2):
                copy.start()

        fetch(layers - 1)
        for j in range(layers - 1, -1, -1):
            slot = j % 2
            if j > 0:
                fetch(j - 1)
            pltpu.make_async_copy(down_a.at[0], down_v.at[slot], sem.at[slot, 8]).wait()
            for copy in copies(j, slot):
                copy.wait()
            if j + 2 < layers:
                pltpu.make_async_copy(dwd_v.at[slot], dwd_v.at[slot], o_sem.at[slot, 0]).wait()
                pltpu.make_async_copy(dwu_v.at[slot], dwu_v.at[slot], o_sem.at[slot, 1]).wait()
            value = lax.dot_general(hid_v[slot].reshape(2 * frames, hidden), gb_v[slot].reshape(2 * frames, width), tn, preferred_element_type=F32)
            dwd_v[slot] = value.astype(BF16)
            scale_v[j] = fold(value * down_v[slot].astype(F32))
            send_sums(core, j // 2, slots, 0, slot, dwd_v.at[slot], sums_out[:3], o_sem.at[slot, 0])
            value = lax.dot_general(nrm_v[slot].reshape(2 * frames, width), gp_v[slot].reshape(2 * frames, hidden), tn, preferred_element_type=F32)
            dwu_v[slot] = value.astype(BF16)
            send_sums(core, j // 2, slots, 1, slot, dwu_v.at[slot], sums_out[3:], o_sem.at[slot, 1])
        pltpu.make_async_copy(scale_v, scale_out, s_sem).start()
        for slot in range(2):
            pltpu.make_async_copy(dwd_v.at[slot], dwd_v.at[slot], o_sem.at[slot, 0]).wait()
            pltpu.make_async_copy(dwu_v.at[slot], dwu_v.at[slot], o_sem.at[slot, 1]).wait()
        pltpu.make_async_copy(scale_v, scale_out, s_sem).wait()


ANY = pl.BlockSpec(memory_space=pl.ANY)
SMEM = pl.BlockSpec(memory_space=pltpu.SMEM)
VMEM = pl.BlockSpec(memory_space=pltpu.VMEM)


def run_forward(flags, call, x, seg, vec, weights, earlier):
    layers = vec.shape[0]
    frames, width = x.shape[-2:]
    hidden = weights[0].shape[2]
    received = x.ndim == 2
    earlier = earlier[:-1]
    shapes = (
        jax.ShapeDtypeStruct((layers, frames, hidden), BF16),
        jax.ShapeDtypeStruct((layers, frames, hidden), BF16),
        jax.ShapeDtypeStruct((layers, KINDS, frames, width), BF16),
        jax.ShapeDtypeStruct((layers, frames, LANES), F32),
        jax.ShapeDtypeStruct((frames, width), F32),
        jax.ShapeDtypeStruct((frames, width), F32),
        jax.ShapeDtypeStruct((frames, width), BF16),
    )
    aliased = len(earlier)
    return pl.pallas_call(
        functools.partial(forward_kernel, call, layers, aliased, received),
        out_shape=shapes,
        in_specs=[SMEM, VMEM if received else ANY, ANY, VMEM] + [ANY] * (4 + aliased),
        out_specs=(ANY,) * len(shapes),
        input_output_aliases={8 + i: i for i in range(aliased)},
        scratch_shapes=[
            pltpu.VMEM((layers, width, hidden), BF16),
            pltpu.VMEM((layers, hidden, width), BF16),
            pltpu.VMEM((layers, frames, hidden), BF16),
            pltpu.VMEM((layers, frames, hidden), BF16),
            pltpu.VMEM((layers, KINDS, frames, width), BF16),
            pltpu.VMEM((layers, frames, LANES), F32),
            pltpu.VMEM((width // LANES, frames + 2 * PAD, LANES), F32),
            pltpu.VMEM((frames, width), F32),
            pltpu.VMEM((2, frames, width), F32),
            pltpu.VMEM((frames, width), BF16),
            pltpu.VMEM((frames + 2 * PAD, LANES), F32),
            pltpu.VMEM((6, frames, LANES), F32),
            pltpu.SemaphoreType.DMA((layers, 2)),
            pltpu.SemaphoreType.DMA((2,)),
            pltpu.SemaphoreType.DMA((layers, 4)),
            pltpu.SemaphoreType.DMA((3,)),
        ],
        compiler_params=pltpu.CompilerParams(vmem_limit_bytes=VMEM_LIMIT),
        cost_estimate=pl.CostEstimate(flops=layers * 4 * frames * width * hidden, bytes_accessed=40 * 2**20, transcendentals=0),
    )(flags, x, seg, vec, *weights, *earlier)


def sum_shapes(shares, hidden, width):
    down, up = (hidden // shares, width), (width // shares, hidden)
    return tuple(jax.ShapeDtypeStruct((count, 2, *part), BF16) for part in (down, up) for count in (shares, HEAD, shares - HEAD))


def run_backward(flags, call, g, seg, vec, weights, state, earlier, low=0, count=4, slots=None, others=()):
    frames, width = g.shape[-2:]
    hidden = weights[0].shape[2]
    final = slots is not None
    received = g.ndim == 2
    rows = 2 if final else 1
    layers = vec.shape[0]
    row_f32, row_bf16 = jax.ShapeDtypeStruct((frames, width), F32), jax.ShapeDtypeStruct((frames, width), BF16)
    vectors = jax.ShapeDtypeStruct((layers, VEC_ROWS, width), F32)
    if final:
        shapes = (*sum_shapes(slots.shape[1], hidden, width), vectors, row_f32, row_bf16)
    else:
        shapes = (
            jax.ShapeDtypeStruct((layers, frames, width), BF16),
            jax.ShapeDtypeStruct((layers, frames, hidden), BF16),
            vectors,
            row_bf16,
            row_f32,
            row_f32,
        )
    aliased = len(earlier)
    scratch = [
        pltpu.VMEM((count, width, hidden), BF16),
        pltpu.VMEM((count, hidden, width), BF16),
        pltpu.VMEM((count, frames, hidden), BF16),
        pltpu.VMEM((count, 2, frames, width), BF16),
        pltpu.VMEM((count, frames, LANES), F32),
        pltpu.VMEM((count + 1, rows, frames, width), BF16),
        pltpu.VMEM((count, rows, frames, hidden), BF16),
        pltpu.VMEM((count + 1, VEC_ROWS, width), F32),
        pltpu.VMEM((frames, width), F32),
        pltpu.VMEM((frames, width), F32),
        pltpu.VMEM((frames, width), F32),
        pltpu.VMEM((width // LANES, frames + 2 * PAD, LANES), F32),
        pltpu.VMEM((frames, width), BF16),
        pltpu.VMEM((frames + 2 * PAD, LANES), F32),
        pltpu.VMEM((6, frames, LANES), F32),
        pltpu.SemaphoreType.DMA((count, 5)),
        pltpu.SemaphoreType.DMA((2,)),
        pltpu.SemaphoreType.DMA((count, 2)),
        pltpu.SemaphoreType.DMA((3,)),
    ]
    if final:
        others = (slots, *others)
        scratch += [
            pltpu.VMEM((count, 2, frames, hidden), BF16),
            pltpu.VMEM((count, 2, frames, width), BF16),
            pltpu.VMEM((count, hidden, width), BF16),
            pltpu.VMEM((count, width, hidden), BF16),
            pltpu.SemaphoreType.DMA((count, 6)),
        ]
    first_alias = 11 + len(others)
    return pl.pallas_call(
        functools.partial(backward_kernel, call, low, count, final, aliased, received),
        out_shape=shapes,
        in_specs=[SMEM, VMEM if received else ANY, ANY, VMEM] + [ANY] * 7 + ([SMEM] if final else []) + [ANY] * (max(0, len(others) - 1) + aliased),
        out_specs=(ANY,) * len(shapes),
        input_output_aliases={first_alias + i: i for i in range(aliased)},
        scratch_shapes=scratch,
        compiler_params=pltpu.CompilerParams(vmem_limit_bytes=VMEM_LIMIT),
        cost_estimate=pl.CostEstimate(flops=count * (12 if final else 4) * frames * width * hidden, bytes_accessed=10 * count * 2**20, transcendentals=0),
    )(flags, g, seg, vec, *weights, *state, *others, *earlier)


def run_weights(flags, call, slots, weights, state_a, state_b, back_a, back_b):
    layers, frames, hidden = state_a[0].shape
    width = back_a[0].shape[2]
    scale = jax.ShapeDtypeStruct((layers, 8, width), F32)
    return pl.pallas_call(
        functools.partial(weight_kernel, call, 0),
        out_shape=(*sum_shapes(slots.shape[1], hidden, width), scale),
        in_specs=[SMEM, SMEM] + [ANY] * 10,
        out_specs=(ANY,) * (SUMS + 1),
        scratch_shapes=[
            pltpu.VMEM((2, 2, frames, hidden), BF16),
            pltpu.VMEM((2, 2, frames, width), BF16),
            pltpu.VMEM((2, 2, frames, width), BF16),
            pltpu.VMEM((2, 2, frames, hidden), BF16),
            pltpu.VMEM((2, hidden, width), BF16),
            pltpu.VMEM((2, hidden, width), BF16),
            pltpu.VMEM((2, width, hidden), BF16),
            pltpu.VMEM((layers, 8, width), F32),
            pltpu.SemaphoreType.DMA((2, 9)),
            pltpu.SemaphoreType.DMA((2, 2)),
            pltpu.SemaphoreType.DMA,
        ],
        compiler_params=pltpu.CompilerParams(vmem_limit_bytes=VMEM_LIMIT),
        cost_estimate=pl.CostEstimate(flops=layers * 8 * frames * width * hidden, bytes_accessed=48 * 2**20, transcendentals=0),
    )(flags, slots, weights[1], weights[3], state_a[0], state_b[0], back_a[0], back_b[0], state_a[2], state_b[2], back_a[1], back_b[1])


def sum_doubling(value, axis):
    count = lax.axis_size(axis)
    step = 1
    while step < count:
        value = value + lax.ppermute(value, axis, [(d, d ^ step) for d in range(count)])
        step *= 2
    return value


def ring_order(count):
    return list(range(0, count, 2)) + list(range(count - 1, 0, -2))


def ring_places(ways, axis):
    count = lax.axis_size(axis)
    order = ring_order(count)
    mine = jnp.array([order.index(d) for d in range(count)], jnp.int32)
    gap = mine[lax.axis_index(axis)] - mine
    return jnp.stack([lax.rem(way * gap - 1 + 2 * count, count) for way in ways])


def ring_scatter(parts, ways, axis):
    count = lax.axis_size(axis)
    order = ring_order(count)
    flowing = [part(0).astype(BF16) for part in parts]
    for step in range(1, count):
        arrived = [
            lax.ppermute(value, axis, [(order[p], order[(p + way) % count]) for p in range(count)])
            for value, way in zip(flowing, ways)
        ]
        flowing = [value.astype(F32) + part(step) for value, part in zip(arrived, parts)]
        if step < count - 1:
            flowing = [value.astype(BF16) for value in flowing]
    return flowing


def per_device(
    inputs,
    segment_ids,
    cotangent,
    conv_weight,
    conv_bias,
    norm_gain,
    norm_bias,
    up_weight,
    up_bias,
    down_weight,
    down_bias,
    layer_scale,
):
    micro, _, frames, width = inputs.shape
    hidden = up_weight.shape[2]
    shares = lax.axis_size("dp")
    section = lax.axis_index("section")
    chip, core = section // 2, section % 2
    exchange = [(0, 1), (1, 0), (2, 3), (3, 2)]

    small = jnp.concatenate(
        [
            conv_weight,
            conv_bias[:, None],
            norm_gain[:, None],
            norm_bias[:, None],
            down_bias[:, None],
            layer_scale[:, None],
            up_bias.reshape(2, -1, width),
            jnp.zeros((2, 1, width), BF16),
        ],
        axis=1,
    )
    small_peer = lax.ppermute(small, "section", exchange)
    up_peer = lax.ppermute(up_weight, "section", exchange)
    down_peer = lax.ppermute(down_weight, "section", exchange)
    vec = jnp.where(core == 0, jnp.concatenate([small, small_peer]), jnp.concatenate([small_peer, small])).astype(F32)
    weights = (up_weight, down_weight, up_peer, down_peer)
    masks = jnp.broadcast_to(segment_ids[:, 0, :, None].astype(F32), (micro, frames, LANES))
    inputs, cotangent = inputs[:, 0], cotangent[:, 0]

    first, last = (chip == 0).astype(jnp.int32), (chip == 1).astype(jnp.int32)
    calls = ((first, 0), (first, 1), (last, 0), (last, 1))
    flags = jnp.stack([jnp.stack([active, core.astype(jnp.int32), (2 * core + row).astype(jnp.int32)]) for active, row in calls])
    ways = (1, -1, -1, 1)
    slots = ring_places(ways, "dp")

    down_pairs, up_pairs = [(0, 2), (1, 3)], [(2, 0), (3, 1)]
    state_b = run_forward(flags, 1, inputs, masks, vec, weights, ())
    sent_b = lax.ppermute(state_b[6], "section", down_pairs)
    state_a = run_forward(flags, 0, inputs, masks, vec, weights, ())
    sent_a = lax.ppermute(state_a[6], "section", down_pairs)
    state_b = run_forward(flags, 3, sent_b, masks, vec, weights, state_b)
    back_b = run_backward(flags, 3, cotangent, masks, vec, weights, state_b[1:4], ())
    sent_b = lax.ppermute(back_b[3], "section", up_pairs)
    state_a = run_forward(flags, 2, sent_a, masks, vec, weights, state_a)
    back_a = run_backward(flags, 2, cotangent, masks, vec, weights, state_a[1:4], ())
    sent_a = lax.ppermute(back_a[3], "section", up_pairs)
    *sums, scales = run_weights(flags, 2, slots, weights, state_a, state_b, back_a, back_b)
    back_b = run_backward(flags, 1, sent_b, masks, vec, weights, state_b[1:4], back_b)
    others = (state_a[0], state_b[0], state_b[2], back_b[0], back_b[1])
    *sums, vectors, grad_high, middle = run_backward(
        flags, 0, sent_a, masks, vec, weights, state_a[1:4], (*sums, back_a[2], back_a[5]), 2, 2, slots, others
    )
    *sums, vectors, grad_low, _ = run_backward(
        flags, 0, middle[None], masks, vec, weights, state_a[1:4], (*sums, vectors, back_a[4]), 0, 2, slots, others
    )
    down_kept, down_head, down_tail, up_kept, up_head, up_tail = sums
    down_head, up_head, down_tail, up_tail = (lax.ppermute(v, "section", exchange) for v in (down_head, up_head, down_tail, up_tail))

    def addend(kept, head, tail, layer):
        def at(k):
            other = head[k, layer] if k < HEAD else tail[k - HEAD, layer]
            return kept[k, layer].astype(F32) + other.astype(F32)

        return at

    shares_of = ring_scatter(
        [addend(down_kept, down_head, down_tail, 0), addend(down_kept, down_head, down_tail, 1)]
        + [addend(up_kept, up_head, up_tail, 0), addend(up_kept, up_head, up_tail, 1)],
        ways,
        "dp",
    )
    down_share, up_share = jnp.stack(shares_of[:2]), jnp.stack(shares_of[2:])

    vectors = (vectors + back_b[2]).at[:, SCALE].add(jnp.where(chip == 1, jnp.sum(scales, axis=1), 0.0))
    low_high = vectors.reshape(2, 2, *vectors.shape[1:])
    totals = lax.dynamic_index_in_dim(low_high, core, 0, keepdims=False)
    totals = totals + lax.ppermute(lax.dynamic_index_in_dim(low_high, 1 - core, 0, keepdims=False), "section", exchange)
    totals = sum_doubling(totals, "dp")
    scale_grad = (totals[:, SCALE] + down_bias.astype(F32) * totals[:, DOWN_B]) / layer_scale.astype(F32)
    shard = lax.axis_index("dp")

    def share(value):
        size = value.shape[-1] // shares
        return lax.dynamic_slice_in_dim(value, shard * size, size, value.ndim - 1)

    def assemble(low_a, low_b, high_a, high_b):
        low, high = jnp.stack([low_a, low_b]), jnp.stack([high_a, high_b])
        other = lax.ppermute(jnp.where(core == 0, high, low), "section", exchange)
        return jnp.where(core == 0, jnp.concatenate([low, other]), jnp.concatenate([other, high]))[None, :, None]

    section_outputs = assemble(state_a[4], state_b[4], state_a[5], state_b[5])
    input_grads = assemble(grad_low, back_b[4], grad_high, back_b[5])
    return (
        section_outputs,
        input_grads,
        share(totals[:, :CONV_B]),
        share(totals[:, CONV_B]),
        share(totals[:, GAIN]),
        share(totals[:, SHIFT]),
        up_share,
        share(totals[:, UP_B : UP_B + hidden // width].reshape(2, -1)),
        down_share,
        share(totals[:, DOWN_B]),
        share(scale_grad),
    )


def solution(mesh):
    in_specs = (
        P(None, "dp", None, None),
        P(None, "dp", None),
        P(None, "dp", None, None),
        P("section", None, None),
        P("section", None),
        P("section", None),
        P("section", None),
        P("section", None, None),
        P("section", None),
        P("section", None, None),
        P("section", None),
        P("section", None),
    )
    out_specs = (
        P("section", None, "dp", None, None),
        P("section", None, "dp", None, None),
        P("section", None, "dp"),
        P("section", "dp"),
        P("section", "dp"),
        P("section", "dp"),
        P("section", "dp", None),
        P("section", "dp"),
        P("section", "dp", None),
        P("section", "dp"),
        P("section", "dp"),
    )
    return jax.shard_map(per_device, mesh=mesh, in_specs=in_specs, out_specs=out_specs, check_vma=False)
```

```python
import functools

import jax
import jax.numpy as jnp
from jax import lax
from jax.experimental import pallas as pl
from jax.experimental.pallas import tpu as pltpu
from jax.sharding import PartitionSpec as P

EPSILON = 1e-06
INV_SQRT2 = 0.7071067811865476
INV_SQRT_PI = 0.5641895835477563
LOG2_E = 1.4426950408889634
F32 = jnp.float32
BF16 = jnp.bfloat16
TILE = 32
PAD = 8
COLS = 256
VMEM_LIMIT = 60 * 2**20

CONV_B, GAIN, SHIFT, DOWN_B, SCALE, UP_B, VEC_ROWS = 7, 8, 9, 10, 11, 12, 16
XHAT, STREAM, NORMED, KINDS = 0, 1, 2, 3
LANES = 128
OFFSETS = (1, 2, 3, -1, -2, -3)
MASK_OF = {offset: k for k, offset in enumerate(OFFSETS)}


def slabs(width):
    return [slice(c, c + LANES) for c in range(0, width, LANES)]


def row_sum(parts):
    return jnp.sum(functools.reduce(jnp.add, parts), axis=1, keepdims=True)


def fold(value):
    return functools.reduce(jnp.add, [value[8 * i : 8 * i + 8] for i in range(value.shape[0] // 8)])


def clear_edges(padded, frames):
    for slab in range(padded.shape[0]):
        padded[slab, 0:PAD, :] = jnp.zeros((PAD, LANES), F32)
        padded[slab, PAD + frames : PAD + frames + PAD, :] = jnp.zeros((PAD, LANES), F32)


def build_masks(seg_v, masks):
    frames = masks.shape[1]
    seg_v[0:PAD, :] = jnp.full((PAD, LANES), -1.0, F32)
    seg_v[PAD + frames : PAD + frames + PAD, :] = jnp.full((PAD, LANES), -1.0, F32)

    def body(i, carry):
        base = pl.multiple_of(i * 64, 64)
        here = seg_v[pl.ds(base + PAD, 64), :]
        for k, offset in enumerate(OFFSETS):
            there = seg_v[pl.ds(base + PAD + offset, 64), :]
            masks[k, pl.ds(base, 64), :] = jnp.where(there == here, 1.0, 0.0)
        return carry

    lax.fori_loop(0, frames // 64, body, 0)


def start_weights(core, layer, own, peer, target, sem):
    @pl.when(core == lax.div(layer, 2))
    def _():
        pltpu.make_async_copy(own.at[lax.rem(layer, 2)], target, sem).start()

    @pl.when(core != lax.div(layer, 2))
    def _():
        pltpu.make_async_copy(peer.at[lax.rem(layer, 2)], target, sem).start()


def send_row(core, section, source, kept, other, sem):
    @pl.when(core == section)
    def _():
        pltpu.make_async_copy(source, kept, sem).start()

    @pl.when(core != section)
    def _():
        pltpu.make_async_copy(source, other, sem).start()


def forward_kernel(layers, aliased, flags, x_in, seg_hbm, vec, own_up, own_down, peer_up, peer_down, *rest):
    rest = rest[aliased:]
    hid, dge, saved, rst, kept, other, send = rest[:7]
    (up_v, down_v, hid_v, dge_v, saved_v, rst_v, stream, acc, out_v, x_v, seg_v, masks, w_sem, in_sem, o_sem, s_sem) = rest[7:]
    frames, width = acc.shape
    hidden = hid_v.shape[2]

    @pl.when(flags[0] == 1)
    def _():
        core, micro, row = flags[1], flags[2], flags[3]
        pltpu.make_async_copy(seg_hbm.at[micro], seg_v.at[pl.ds(PAD, frames)], in_sem).start()
        def fetch(j):
            start_weights(core, j, own_up, peer_up, up_v.at[j], w_sem.at[j, 0])
            start_weights(core, j, own_down, peer_down, down_v.at[j], w_sem.at[j, 1])

        fetch(0)
        clear_edges(stream, frames)
        pltpu.make_async_copy(seg_hbm.at[0], seg_v.at[pl.ds(PAD, frames)], in_sem).wait()
        build_masks(seg_v, masks)
        for c, cols in enumerate(slabs(width)):
            stream[c, PAD : PAD + frames, :] = x_in[:, cols].astype(F32)

        def layer(j, carry):
            def conv_norm(i, c):
                base = pl.multiple_of(i * TILE, TILE)
                rows = pl.ds(base, TILE)
                parts = []
                for s, cols in enumerate(slabs(width)):
                    centre = stream[s, pl.ds(base + PAD, TILE), :]
                    saved_v[j, STREAM, rows, cols] = centre.astype(BF16)
                    total = vec[j, CONV_B : CONV_B + 1, cols] + vec[j, 3:4, cols] * centre
                    for offset in OFFSETS:
                        neighbour = stream[s, pl.ds(base + PAD + offset, TILE), :] * masks[MASK_OF[offset], rows, :]
                        total = total + vec[j, offset + 3 : offset + 4, cols] * neighbour
                    parts.append(total)
                mean = row_sum(parts) * (1.0 / width)
                parts = [part - mean for part in parts]
                rstd = lax.rsqrt(row_sum([part * part for part in parts]) * (1.0 / width) + EPSILON)
                for part, cols in zip(parts, slabs(width)):
                    xhat = part * rstd
                    saved_v[j, XHAT, rows, cols] = xhat.astype(BF16)
                    saved_v[j, NORMED, rows, cols] = (xhat * vec[j, GAIN : GAIN + 1, cols] + vec[j, SHIFT : SHIFT + 1, cols]).astype(BF16)
                rst_v[j, rows, :] = jnp.broadcast_to(rstd, (TILE, LANES))
                return c

            lax.fori_loop(0, frames // TILE, conv_norm, 0, unroll=16)
            pltpu.make_async_copy(saved_v.at[j], saved.at[row, j], o_sem.at[j, 3]).start()
            pltpu.make_async_copy(rst_v.at[j], rst.at[row, j], o_sem.at[j, 2]).start()
            pltpu.make_async_copy(own_up.at[0], up_v.at[j], w_sem.at[j, 0]).wait()

            @pl.when(j + 1 < layers)
            def _():
                fetch(j + 1)

            for n in range(hidden // COLS):
                cols = slice(n * COLS, (n + 1) * COLS)
                at, start = UP_B + n * COLS // width, (n * COLS) % width
                value = jnp.dot(saved_v[j, NORMED], up_v[j, :, cols], preferred_element_type=F32) + vec[j, at : at + 1, start : start + COLS]
                scaled = value * INV_SQRT2
                phi_sum = 0.5 + 0.5 * lax.erf(scaled)
                hid_v[j, :, cols] = (value * phi_sum).astype(BF16)
                dge_v[j, :, cols] = (phi_sum + scaled * INV_SQRT_PI * jnp.exp2(scaled * scaled * -LOG2_E)).astype(BF16)
            pltpu.make_async_copy(hid_v.at[j], hid.at[row, j], o_sem.at[j, 0]).start()
            pltpu.make_async_copy(dge_v.at[j], dge.at[row, j], o_sem.at[j, 1]).start()
            pltpu.make_async_copy(own_down.at[0], down_v.at[j], w_sem.at[j, 1]).wait()
            acc[...] = jnp.dot(hid_v[j], down_v[j], preferred_element_type=F32)

            def finish(ends_section, i, c):
                base = pl.multiple_of(i * TILE, TILE)
                rows = pl.ds(base, TILE)
                for s, cols in enumerate(slabs(width)):
                    inner = pl.ds(pl.multiple_of(base + PAD, 8), TILE)
                    branch = acc[rows, cols] + vec[j, DOWN_B : DOWN_B + 1, cols]
                    fresh = stream[s, inner, :] + vec[j, SCALE : SCALE + 1, cols] * branch
                    if ends_section:
                        rounded = fresh.astype(BF16)
                        out_v[lax.div(j, 2), rows, cols] = fresh
                        x_v[rows, cols] = rounded
                        fresh = rounded.astype(F32)
                    stream[s, inner, :] = fresh
                return c

            @pl.when(lax.rem(j, 2) == 1)
            def _():
                lax.fori_loop(0, frames // TILE, functools.partial(finish, True), 0)

            @pl.when(lax.rem(j, 2) == 0)
            def _():
                lax.fori_loop(0, frames // TILE, functools.partial(finish, False), 0)

            @pl.when(j == 1)
            def _():
                send_row(core, 0, out_v.at[0], kept.at[micro], other.at[row], s_sem.at[0])

            return carry

        lax.fori_loop(0, layers, layer, 0)
        send_row(core, 1, out_v.at[1], kept.at[micro], other.at[row], s_sem.at[1])
        pltpu.make_async_copy(x_v, send, s_sem.at[2]).start()
        for j in range(layers):
            pltpu.make_async_copy(hid_v.at[j], hid.at[row, j], o_sem.at[j, 0]).wait()
            pltpu.make_async_copy(dge_v.at[j], dge.at[row, j], o_sem.at[j, 1]).wait()
            pltpu.make_async_copy(rst_v.at[j], rst.at[row, j], o_sem.at[j, 2]).wait()
            pltpu.make_async_copy(saved_v.at[j], saved.at[row, j], o_sem.at[j, 3]).wait()
        pltpu.make_async_copy(out_v.at[0], other.at[row], s_sem.at[0]).wait()
        pltpu.make_async_copy(out_v.at[1], other.at[row], s_sem.at[1]).wait()
        pltpu.make_async_copy(x_v, send, s_sem.at[2]).wait()


SUMS, HEAD = 3, 2
DOWN, UP = 0, 1


def send_sums(core, section, slots, kind, layer, source, targets, sem):
    kept, head, tail = targets
    shares, _, _, size, width = kept.shape
    blocks = source.shape[1] // width
    for d in range(shares):
        place = slots[2 * kind + layer, d]
        for b in range(blocks):
            rows = size // blocks
            piece = source.at[pl.ds(d * rows, rows), pl.ds(b * width, width)]
            inner = pl.ds(b * rows, rows)

            @pl.when(core == section)
            def _():
                pltpu.make_async_copy(piece, kept.at[place, layer, kind, inner], sem).start()

            @pl.when((core != section) & (place < HEAD))
            def _():
                pltpu.make_async_copy(piece, head.at[place, layer, kind, inner], sem).start()

            @pl.when((core != section) & (place >= HEAD))
            def _():
                pltpu.make_async_copy(piece, tail.at[place - HEAD, layer, kind, inner], sem).start()


def backward_kernel(final, aliased, flags, g_in, seg_hbm, vec, own_up, own_down, peer_up, peer_down, dge, saved, rst, *rest):
    if final:
        slots, hid, gb, gp = rest[:4]
        rest = rest[4 + aliased :]
        sums_out, (scale_out, vec_out, kept, other) = rest[:SUMS], rest[SUMS : SUMS + 4]
        rest = rest[SUMS + 4 :]
    else:
        rest = rest[aliased:]
        gb, gp, vec_out, kept, other, send = rest[:6]
        rest = rest[6:]
    (up_v, down_v, dge_v, saved_v, rst_v, gb_v, gp_v, vg_v, g_now, fresh_v, gn_v, padded, x_v, seg_v, masks, w_sem, in_sem, o_sem, s_sem) = rest[:19]
    if final:
        (hid_v, nrm_v, dwd_v, dwu_v, scale_v, b_sem) = rest[19:]
    frames, width = g_now.shape
    held, _, hidden = dge_v.shape
    layers = vec.shape[0]
    nt = (((1,), (1,)), ((), ()))
    tn = (((0,), (0,)), ((), ()))
    tall = 2 * TILE
    cols_of = slabs(width)

    @pl.when(flags[0] == 1)
    def _():
        core, micro, row = flags[1], flags[2], flags[3]
        pltpu.make_async_copy(seg_hbm.at[micro], seg_v.at[pl.ds(PAD, frames)], in_sem).start()

        def fetch(j):
            h = lax.rem(j, held)
            start_weights(core, j, own_down, peer_down, down_v.at[h], w_sem.at[h, 1])
            pltpu.make_async_copy(dge.at[row, j], dge_v.at[h], w_sem.at[h, 3]).start()
            start_weights(core, j, own_up, peer_up, up_v.at[h], w_sem.at[h, 0])
            pltpu.make_async_copy(rst.at[row, j], rst_v.at[h], w_sem.at[h, 4]).start()
            pltpu.make_async_copy(saved.at[row, j, 0:2], saved_v.at[h], w_sem.at[h, 2]).start()

        fetch(layers - 1)
        clear_edges(padded, frames)
        x_v[...] = g_in[...]
        for cols in cols_of:

            def enter(t, c):
                rows = pl.ds(pl.multiple_of(t * tall, tall), tall)
                scaled = (vec[layers - 1, SCALE : SCALE + 1, cols] * x_v[rows, cols].astype(F32)).astype(BF16)
                gb_v[layers, 0, rows, cols] = scaled
                return c + fold(scaled.astype(F32))

            total = lax.fori_loop(0, frames // tall, enter, jnp.zeros((8, LANES), F32))
            vg_v[layers, DOWN_B : DOWN_B + 1, cols] = jnp.sum(total, axis=0, keepdims=True)
        pltpu.make_async_copy(seg_hbm.at[0], seg_v.at[pl.ds(PAD, frames)], in_sem).wait()
        build_masks(seg_v, masks)

        def layer(step, carry):
            j = layers - 1 - step
            h = lax.rem(j, held)
            if not final:
                pltpu.make_async_copy(gb_v.at[j + 1, 0], gb.at[row, j], o_sem.at[j, 0]).start()
            pltpu.make_async_copy(own_down.at[0], down_v.at[h], w_sem.at[h, 1]).wait()
            pltpu.make_async_copy(dge.at[0, 0], dge_v.at[h], w_sem.at[h, 3]).wait()
            if final:
                pltpu.make_async_copy(hid.at[row, j], hid_v.at[h, 0], b_sem.at[h, 0]).start()
                pltpu.make_async_copy(hid.at[1 - row, j], hid_v.at[h, 1], b_sem.at[h, 1]).start()
                pltpu.make_async_copy(gb.at[1 - row, j], gb_v.at[j + 1, 1], b_sem.at[h, 4]).start()
                pltpu.make_async_copy(saved.at[row, j, NORMED], nrm_v.at[h, 0], b_sem.at[h, 2]).start()
                pltpu.make_async_copy(saved.at[1 - row, j, NORMED], nrm_v.at[h, 1], b_sem.at[h, 3]).start()
                pltpu.make_async_copy(gp.at[1 - row, j], gp_v.at[h, 1], b_sem.at[h, 5]).start()
            for n in range(hidden // COLS):
                cols = slice(n * COLS, (n + 1) * COLS)
                value = lax.dot_general(gb_v[j + 1, 0], down_v[h, cols, :], nt, preferred_element_type=F32)
                rounded = (value * dge_v[h, :, cols].astype(F32)).astype(BF16)
                gp_v[h, 0, :, cols] = rounded
                at, start = UP_B + n * COLS // width, (n * COLS) % width
                vg_v[j + 1, at : at + 1, start : start + COLS] = jnp.sum(rounded.astype(F32), axis=0, keepdims=True)
            if not final:
                pltpu.make_async_copy(gp_v.at[h, 0], gp.at[row, j], o_sem.at[j, 1]).start()
            pltpu.make_async_copy(own_up.at[0], up_v.at[h], w_sem.at[h, 0]).wait()
            gn_v[...] = lax.dot_general(gp_v[h, 0], up_v[h], nt, preferred_element_type=F32)
            pltpu.make_async_copy(rst.at[0, 0], rst_v.at[h], w_sem.at[h, 4]).wait()
            pltpu.make_async_copy(saved.at[0, 0, 0:2], saved_v.at[h], w_sem.at[h, 2]).wait()

            @pl.when(j > 0)
            def _():
                fetch(j - 1)

            if final:
                pltpu.make_async_copy(hid.at[0, 0], hid_v.at[h, 0], b_sem.at[h, 0]).wait()
                pltpu.make_async_copy(hid.at[0, 0], hid_v.at[h, 1], b_sem.at[h, 1]).wait()
                pltpu.make_async_copy(gb.at[0, 0], gb_v.at[j + 1, 1], b_sem.at[h, 4]).wait()

                @pl.when(j + held < layers)
                def _():
                    pltpu.make_async_copy(dwd_v.at[h], dwd_v.at[h], o_sem.at[h, 0]).wait()
                    pltpu.make_async_copy(dwu_v.at[h], dwu_v.at[h], o_sem.at[h, 1]).wait()

            def down_chunk(n):
                rows = slice(n * COLS, (n + 1) * COLS)
                left = hid_v[h, :, :, rows].reshape(2 * frames, COLS)
                right = gb_v[j + 1].reshape(2 * frames, width)
                value = lax.dot_general(left, right, tn, preferred_element_type=F32)
                dwd_v[h, rows, :] = value.astype(BF16)
                return fold(value * down_v[h, rows, :].astype(F32))

            def up_chunk(m, n):
                rows = slice(m * COLS, (m + 1) * COLS)
                cols = slice(n * width, (n + 1) * width)
                left = nrm_v[h, :, :, rows].reshape(2 * frames, COLS)
                right = gp_v[h, :, :, cols].reshape(2 * frames, width)
                dwu_v[h, rows, cols] = lax.dot_general(left, right, tn, preferred_element_type=F32).astype(BF16)

            odd = lax.rem(j, 2) == 1

            def norm_back(t, c):
                base = t * TILE if isinstance(t, int) else pl.multiple_of(t * TILE, TILE)
                rows = pl.ds(base, TILE)
                inner = pl.ds(base + PAD if isinstance(t, int) else pl.multiple_of(base + PAD, 8), TILE)
                grads = [gn_v[rows, cols] for cols in cols_of]
                xhats = [saved_v[h, XHAT, rows, cols].astype(F32) for cols in cols_of]
                qs = [grad * vec[j, GAIN : GAIN + 1, cols] for grad, cols in zip(grads, cols_of)]
                mean_q = row_sum(qs) * (1.0 / width)
                mean_qx = row_sum([q * xhat for q, xhat in zip(qs, xhats)]) * (1.0 / width)
                rstd = rst_v[h, rows, :]
                out = []
                for s, cols in enumerate(cols_of):
                    grad_conv = rstd * (qs[s] - mean_q - xhats[s] * mean_qx)
                    padded[s, inner, :] = grad_conv
                    g_now[rows, cols] = jnp.where(odd, x_v[rows, cols].astype(F32), fresh_v[rows, cols])
                    out += [c[3 * s] + fold(grads[s] * xhats[s]), c[3 * s + 1] + fold(grads[s]), c[3 * s + 2] + fold(grad_conv)]
                return tuple(out)

            sums = (jnp.zeros((8, LANES), F32),) * (3 * len(cols_of))
            tiles = frames // TILE
            if final:
                parts = hidden // COLS
                scale = jnp.zeros((8, width), F32)
                done = 0
                for n in range(parts):
                    scale = scale + down_chunk(n)
                    while done < tiles * (n + 1) // parts:
                        sums = norm_back(done, sums)
                        done += 1
                scale_v[j] = scale
                send_sums(core, lax.div(j, 2), slots, DOWN, lax.rem(j, 2), dwd_v.at[h], sums_out, o_sem.at[h, 0])
                pltpu.make_async_copy(saved.at[0, 0, 0], nrm_v.at[h, 0], b_sem.at[h, 2]).wait()
                pltpu.make_async_copy(saved.at[0, 0, 0], nrm_v.at[h, 1], b_sem.at[h, 3]).wait()
                pltpu.make_async_copy(gp.at[0, 0], gp_v.at[h, 1], b_sem.at[h, 5]).wait()
            else:
                sums = lax.fori_loop(0, tiles, norm_back, sums, unroll=8)
            for s, cols in enumerate(cols_of):
                for k, at in enumerate((GAIN, SHIFT, CONV_B)):
                    vg_v[j + 1, at : at + 1, cols] = jnp.sum(sums[3 * s + k], axis=0, keepdims=True)

            @pl.when(odd & (step > 0))
            def _():
                pltpu.make_async_copy(fresh_v, other.at[row], s_sem.at[0]).wait()

            below = lax.max(j - 1, 0)
            for s, cols in enumerate(cols_of):

                def conv_back(t, c):
                    base = t * tall if isinstance(t, int) else pl.multiple_of(t * tall, tall)
                    rows = pl.ds(base, tall)
                    source = saved_v[h, STREAM, rows, cols].astype(F32)
                    centre = padded[s, pl.ds(base + PAD if isinstance(t, int) else pl.multiple_of(base + PAD, 8), tall), :]
                    total = g_now[rows, cols] + vec[j, 3:4, cols] * centre
                    taps = [None] * 7
                    taps[3] = c[3] + fold(centre * source)
                    for offset in OFFSETS:
                        term = padded[s, pl.ds(base + PAD - offset, tall), :] * masks[MASK_OF[-offset], rows, :]
                        total = total + vec[j, offset + 3 : offset + 4, cols] * term
                        taps[offset + 3] = c[offset + 3] + fold(term * source)
                    rounded = total.astype(BF16)
                    fresh_v[rows, cols] = total
                    x_v[rows, cols] = rounded
                    scaled = (vec[below, SCALE : SCALE + 1, cols] * jnp.where(odd, total, rounded.astype(F32))).astype(BF16)
                    gb_v[j, 0, rows, cols] = scaled
                    return tuple(taps) + (c[7] + fold(scaled.astype(F32)),)

                sums = (jnp.zeros((8, LANES), F32),) * 8
                if final:
                    chunks = [(m, n) for m in range(width // COLS) for n in range(hidden // width)]
                    each = -(-len(chunks) // len(cols_of))
                    mine = chunks[s * each : (s + 1) * each]
                    done = 0
                    for k, (m, n) in enumerate(mine):
                        up_chunk(m, n)
                        while done < frames // tall * (k + 1) // len(mine):
                            sums = conv_back(done, sums)
                            done += 1
                    while done < frames // tall:
                        sums = conv_back(done, sums)
                        done += 1
                else:
                    sums = lax.fori_loop(0, frames // tall, conv_back, sums, unroll=8)
                for k in range(7):
                    vg_v[j + 1, k : k + 1, cols] = jnp.sum(sums[k], axis=0, keepdims=True)
                vg_v[j, DOWN_B : DOWN_B + 1, cols] = jnp.sum(sums[7], axis=0, keepdims=True)
            if final:
                send_sums(core, lax.div(j, 2), slots, UP, lax.rem(j, 2), dwu_v.at[h], sums_out, o_sem.at[h, 1])

            @pl.when(jnp.logical_not(odd))
            def _():
                send_row(core, lax.div(j, 2), fresh_v, kept.at[micro], other.at[row], s_sem.at[0])

            return carry

        for i in range(1, layers + 1):
            vg_v[i, SCALE : SCALE + 1, :] = jnp.zeros((1, width), F32)
            vg_v[i, VEC_ROWS - 1 : VEC_ROWS, :] = jnp.zeros((1, width), F32)
        lax.fori_loop(0, layers, layer, 0)
        pltpu.make_async_copy(vg_v.at[pl.ds(1, layers)], vec_out.at[row], s_sem.at[2]).start()
        if final:
            pltpu.make_async_copy(scale_v, scale_out, s_sem.at[1]).start()
            for h in range(held):
                pltpu.make_async_copy(dwd_v.at[h], dwd_v.at[h], o_sem.at[h, 0]).wait()
                pltpu.make_async_copy(dwu_v.at[h], dwu_v.at[h], o_sem.at[h, 1]).wait()
            pltpu.make_async_copy(scale_v, scale_out, s_sem.at[1]).wait()
        else:
            pltpu.make_async_copy(x_v, send, s_sem.at[1]).start()
            for j in range(layers):
                pltpu.make_async_copy(gb_v.at[j + 1, 0], gb.at[row, j], o_sem.at[j, 0]).wait()
                pltpu.make_async_copy(gp_v.at[j, 0], gp.at[row, j], o_sem.at[j, 1]).wait()
            pltpu.make_async_copy(x_v, send, s_sem.at[1]).wait()
        pltpu.make_async_copy(fresh_v, other.at[row], s_sem.at[0]).wait()
        pltpu.make_async_copy(vg_v.at[pl.ds(1, layers)], vec_out.at[row], s_sem.at[2]).wait()


def weight_kernel(flags, slots, own_down, peer_down, all_hid, all_gb, all_saved, all_gp, *rest):
    sums_out, scale_out = rest[:SUMS], rest[SUMS]
    hid_v, gb_v, nrm_v, gp_v, down_v, dwd_v, dwu_v, scale_v, sem, o_sem, s_sem = rest[SUMS + 1 :]
    frames, width = gb_v.shape[2:]
    hidden = hid_v.shape[3]
    layers = all_hid.shape[1]
    tn = (((0,), (0,)), ((), ()))

    @pl.when(flags[0] == 1)
    def _():
        core = flags[1]

        def copies(j, h):
            pairs = []
            for row in range(2):
                pairs += [
                    (all_hid.at[row, j], hid_v.at[h, row]),
                    (all_gb.at[row, j], gb_v.at[h, row]),
                    (all_saved.at[row, j, NORMED], nrm_v.at[h, row]),
                    (all_gp.at[row, j], gp_v.at[h, row]),
                ]
            return [pltpu.make_async_copy(a, b, sem.at[h, k]) for k, (a, b) in enumerate(pairs)]

        def fetch(j):
            h = lax.rem(j, 2)
            start_weights(core, j, own_down, peer_down, down_v.at[h], sem.at[h, 8])
            for copy in copies(j, h):
                copy.start()

        fetch(layers - 1)

        def layer(step, carry):
            j = layers - 1 - step
            h = lax.rem(j, 2)

            @pl.when(j > 0)
            def _():
                fetch(j - 1)

            pltpu.make_async_copy(own_down.at[0], down_v.at[h], sem.at[h, 8]).wait()
            for copy in copies(j, h):
                copy.wait()

            @pl.when(j + 2 < layers)
            def _():
                pltpu.make_async_copy(dwd_v.at[h], dwd_v.at[h], o_sem.at[h, 0]).wait()
                pltpu.make_async_copy(dwu_v.at[h], dwu_v.at[h], o_sem.at[h, 1]).wait()

            value = lax.dot_general(hid_v[h].reshape(2 * frames, hidden), gb_v[h].reshape(2 * frames, width), tn, preferred_element_type=F32)
            dwd_v[h] = value.astype(BF16)
            scale_v[j] = fold(value * down_v[h].astype(F32))
            send_sums(core, lax.div(j, 2), slots, DOWN, lax.rem(j, 2), dwd_v.at[h], sums_out, o_sem.at[h, 0])
            value = lax.dot_general(nrm_v[h].reshape(2 * frames, width), gp_v[h].reshape(2 * frames, hidden), tn, preferred_element_type=F32)
            dwu_v[h] = value.astype(BF16)
            send_sums(core, lax.div(j, 2), slots, UP, lax.rem(j, 2), dwu_v.at[h], sums_out, o_sem.at[h, 1])
            return carry

        lax.fori_loop(0, layers, layer, 0)
        pltpu.make_async_copy(scale_v, scale_out, s_sem).start()
        for h in range(2):
            pltpu.make_async_copy(dwd_v.at[h], dwd_v.at[h], o_sem.at[h, 0]).wait()
            pltpu.make_async_copy(dwu_v.at[h], dwu_v.at[h], o_sem.at[h, 1]).wait()
        pltpu.make_async_copy(scale_v, scale_out, s_sem).wait()


ANY = pl.BlockSpec(memory_space=pl.ANY)
SMEM = pl.BlockSpec(memory_space=pltpu.SMEM)
VMEM = pl.BlockSpec(memory_space=pltpu.VMEM)


def run_forward(flags, x, seg, vec, weights, earlier):
    layers = vec.shape[0]
    micro = seg.shape[0]
    frames, width = x.shape
    hidden = weights[0].shape[2]
    shapes = (
        jax.ShapeDtypeStruct((2, layers, frames, hidden), BF16),
        jax.ShapeDtypeStruct((2, layers, frames, hidden), BF16),
        jax.ShapeDtypeStruct((2, layers, KINDS, frames, width), BF16),
        jax.ShapeDtypeStruct((2, layers, frames, LANES), F32),
        jax.ShapeDtypeStruct((micro, frames, width), F32),
        jax.ShapeDtypeStruct((2, frames, width), F32),
        jax.ShapeDtypeStruct((frames, width), BF16),
    )
    aliased = len(earlier)
    return pl.pallas_call(
        functools.partial(forward_kernel, layers, aliased),
        out_shape=shapes,
        in_specs=[SMEM, VMEM, ANY, VMEM] + [ANY] * (4 + aliased),
        out_specs=(ANY,) * len(shapes),
        input_output_aliases={8 + i: i for i in range(aliased)},
        scratch_shapes=[
            pltpu.VMEM((layers, width, hidden), BF16),
            pltpu.VMEM((layers, hidden, width), BF16),
            pltpu.VMEM((layers, frames, hidden), BF16),
            pltpu.VMEM((layers, frames, hidden), BF16),
            pltpu.VMEM((layers, KINDS, frames, width), BF16),
            pltpu.VMEM((layers, frames, LANES), F32),
            pltpu.VMEM((width // LANES, frames + 2 * PAD, LANES), F32),
            pltpu.VMEM((frames, width), F32),
            pltpu.VMEM((2, frames, width), F32),
            pltpu.VMEM((frames, width), BF16),
            pltpu.VMEM((frames + 2 * PAD, LANES), F32),
            pltpu.VMEM((6, frames, LANES), F32),
            pltpu.SemaphoreType.DMA((layers, 2)),
            pltpu.SemaphoreType.DMA,
            pltpu.SemaphoreType.DMA((layers, 4)),
            pltpu.SemaphoreType.DMA((3,)),
        ],
        compiler_params=pltpu.CompilerParams(vmem_limit_bytes=VMEM_LIMIT),
        cost_estimate=pl.CostEstimate(flops=layers * 4 * frames * width * hidden, bytes_accessed=40 * 2**20, transcendentals=0),
    )(flags, x, seg, vec, *weights, *earlier)


def sum_shapes(shares, hidden, width):
    return tuple(jax.ShapeDtypeStruct((count, 2, 2, hidden // shares, width), BF16) for count in (shares, HEAD, shares - HEAD))


def run_backward(flags, g, seg, vec, weights, state, earlier, final=()):
    frames, width = g.shape
    hidden = weights[0].shape[2]
    layers, micro = vec.shape[0], seg.shape[0]
    rows, held = (2, 2) if final else (1, layers)
    vectors = (
        jax.ShapeDtypeStruct((2, layers, VEC_ROWS, width), F32),
        jax.ShapeDtypeStruct((micro, frames, width), F32),
        jax.ShapeDtypeStruct((2, frames, width), F32),
    )
    if final:
        shapes = (*sum_shapes(final[0].shape[1], hidden, width), jax.ShapeDtypeStruct((layers, 8, width), F32), *vectors)
    else:
        shapes = (
            jax.ShapeDtypeStruct((2, layers, frames, width), BF16),
            jax.ShapeDtypeStruct((2, layers, frames, hidden), BF16),
            *vectors,
            jax.ShapeDtypeStruct((frames, width), BF16),
        )
    aliased = len(earlier)
    scratch = [
        pltpu.VMEM((held, width, hidden), BF16),
        pltpu.VMEM((held, hidden, width), BF16),
        pltpu.VMEM((held, frames, hidden), BF16),
        pltpu.VMEM((held, 2, frames, width), BF16),
        pltpu.VMEM((held, frames, LANES), F32),
        pltpu.VMEM((layers + 1, rows, frames, width), BF16),
        pltpu.VMEM((held, rows, frames, hidden), BF16),
        pltpu.VMEM((layers + 1, VEC_ROWS, width), F32),
        pltpu.VMEM((frames, width), F32),
        pltpu.VMEM((frames, width), F32),
        pltpu.VMEM((frames, width), F32),
        pltpu.VMEM((width // LANES, frames + 2 * PAD, LANES), F32),
        pltpu.VMEM((frames, width), BF16),
        pltpu.VMEM((frames + 2 * PAD, LANES), F32),
        pltpu.VMEM((6, frames, LANES), F32),
        pltpu.SemaphoreType.DMA((held, 5)),
        pltpu.SemaphoreType.DMA,
        pltpu.SemaphoreType.DMA((held, 2)),
        pltpu.SemaphoreType.DMA((3,)),
    ]
    if final:
        scratch += [
            pltpu.VMEM((held, 2, frames, hidden), BF16),
            pltpu.VMEM((held, 2, frames, width), BF16),
            pltpu.VMEM((held, hidden, width), BF16),
            pltpu.VMEM((held, width, hidden), BF16),
            pltpu.VMEM((layers, 8, width), F32),
            pltpu.SemaphoreType.DMA((held, 6)),
        ]
    first_alias = 11 + len(final)
    return pl.pallas_call(
        functools.partial(backward_kernel, bool(final), aliased),
        out_shape=shapes,
        in_specs=[SMEM, VMEM, ANY, VMEM] + [ANY] * 7 + ([SMEM] + [ANY] * 3 if final else []) + [ANY] * aliased,
        out_specs=(ANY,) * len(shapes),
        input_output_aliases={first_alias + i: i for i in range(aliased)},
        scratch_shapes=scratch,
        compiler_params=pltpu.CompilerParams(vmem_limit_bytes=VMEM_LIMIT),
        cost_estimate=pl.CostEstimate(flops=layers * (12 if final else 4) * frames * width * hidden, bytes_accessed=40 * 2**20, transcendentals=0),
    )(flags, g, seg, vec, *weights, *state, *final, *earlier)


def run_weights(flags, slots, weights, hid, gb, saved, gp):
    _, layers, frames, hidden = hid.shape
    width = gb.shape[3]
    return pl.pallas_call(
        weight_kernel,
        out_shape=(*sum_shapes(slots.shape[1], hidden, width), jax.ShapeDtypeStruct((layers, 8, width), F32)),
        in_specs=[SMEM, SMEM] + [ANY] * 6,
        out_specs=(ANY,) * (SUMS + 1),
        scratch_shapes=[
            pltpu.VMEM((2, 2, frames, hidden), BF16),
            pltpu.VMEM((2, 2, frames, width), BF16),
            pltpu.VMEM((2, 2, frames, width), BF16),
            pltpu.VMEM((2, 2, frames, hidden), BF16),
            pltpu.VMEM((2, hidden, width), BF16),
            pltpu.VMEM((2, hidden, width), BF16),
            pltpu.VMEM((2, width, hidden), BF16),
            pltpu.VMEM((layers, 8, width), F32),
            pltpu.SemaphoreType.DMA((2, 9)),
            pltpu.SemaphoreType.DMA((2, 2)),
            pltpu.SemaphoreType.DMA,
        ],
        compiler_params=pltpu.CompilerParams(vmem_limit_bytes=VMEM_LIMIT),
        cost_estimate=pl.CostEstimate(flops=layers * 8 * frames * width * hidden, bytes_accessed=48 * 2**20, transcendentals=0),
    )(flags, slots, weights[1], weights[3], hid, gb, saved, gp)


def sum_doubling(value, axis):
    count = lax.axis_size(axis)
    step = 1
    while step < count:
        value = value + lax.ppermute(value, axis, [(d, d ^ step) for d in range(count)])
        step *= 2
    return value


def ring_order(count):
    return list(range(0, count, 2)) + list(range(count - 1, 0, -2))


def ring_places(ways, axis):
    count = lax.axis_size(axis)
    order = ring_order(count)
    mine = jnp.array([order.index(d) for d in range(count)], jnp.int32)
    gap = mine[lax.axis_index(axis)] - mine
    return jnp.stack([lax.rem(way * gap - 1 + 2 * count, count) for way in ways])


def after(value, earlier):
    return lax.optimization_barrier((value, earlier))[0]


def ring_step(flows, ways, axis):
    count = lax.axis_size(axis)
    order = ring_order(count)
    return [
        lax.ppermute(value, axis, [(order[p], order[(p + way) % count]) for p in range(count)]) for value, way in zip(flows, ways)
    ]


def per_device(
    inputs,
    segment_ids,
    cotangent,
    conv_weight,
    conv_bias,
    norm_gain,
    norm_bias,
    up_weight,
    up_bias,
    down_weight,
    down_bias,
    layer_scale,
):
    micro, _, frames, width = inputs.shape
    hidden = up_weight.shape[2]
    shares = lax.axis_size("dp")
    section = lax.axis_index("section")
    chip, core = section // 2, section % 2
    exchange = [(0, 1), (1, 0), (2, 3), (3, 2)]

    small = jnp.concatenate(
        [
            conv_weight,
            conv_bias[:, None],
            norm_gain[:, None],
            norm_bias[:, None],
            down_bias[:, None],
            layer_scale[:, None],
            up_bias.reshape(2, -1, width),
            jnp.zeros((2, 1, width), BF16),
        ],
        axis=1,
    )
    small_peer = lax.ppermute(small, "section", exchange)
    up_peer = lax.ppermute(up_weight, "section", exchange)
    down_peer = lax.ppermute(down_weight, "section", exchange)
    vec = jnp.where(core == 0, jnp.concatenate([small, small_peer]), jnp.concatenate([small_peer, small])).astype(F32)
    weights = (up_weight, down_weight, up_peer, down_peer)
    masks = jnp.broadcast_to(segment_ids[:, 0, :, None].astype(F32), (micro, frames, LANES))
    inputs, cotangent = inputs[:, 0], cotangent[:, 0]

    def flags(active, row):
        return jnp.stack([jnp.asarray(v, jnp.int32) for v in (active, core, 2 * core + row, row)])

    first, last = chip == 0, chip == 1
    ways = ((1, -1), (-1, 1))
    slots = ring_places([way for kind in ways for way in kind], "dp")

    def row_of(array, row):
        return lax.dynamic_index_in_dim(array, 2 * core + row, 0, keepdims=False)

    down_pairs, up_pairs = [(0, 2), (1, 3)], [(2, 0), (3, 1)]
    state = run_forward(flags(first, 0), row_of(inputs, 0), masks, vec, weights, ())
    arrived = lax.ppermute(state[6], "section", down_pairs)
    state = run_forward(flags(True, jnp.where(first, 1, 0)), jnp.where(first, row_of(inputs, 1), arrived), masks, vec, weights, state[:6])
    arrived = lax.ppermute(state[6], "section", down_pairs)
    back = run_backward(flags(last, 0), row_of(cotangent, 0), masks, vec, weights, state[1:4], ())
    returned = lax.ppermute(back[5], "section", up_pairs)
    state = run_forward(flags(last, 1), arrived, masks, vec, weights, state[:6])
    gradient = jnp.where(last, row_of(cotangent, 1), returned)
    back = run_backward(flags(True, jnp.where(last, 1, 0)), gradient, masks, vec, weights, state[1:4], back[:5])
    returned = lax.ppermute(back[5], "section", up_pairs)
    gb, gp, vectors, grads_kept, grads_other, _ = back
    *sums, scales = run_weights(flags(last, 0), slots, weights, state[0], gb, state[2], gp)
    *sums, scales, vectors, grads_kept, grads_other = run_backward(
        flags(first, 1),
        returned,
        masks,
        vec,
        weights,
        state[1:4],
        (*sums, scales, vectors, grads_kept, grads_other),
        (slots, state[0], gb, gp),
    )

    kept, head, tail = sums
    head = lax.ppermute(head, "section", exchange)
    tail = lax.ppermute(after(tail, head), "section", exchange)

    def addend(k, kind, layer):
        other = head[k, layer, kind] if k < HEAD else tail[k - HEAD, layer, kind]
        return kept[k, layer, kind].astype(F32) + other.astype(F32)

    flows = [[addend(0, kind, layer).astype(BF16) for layer in range(2)] for kind in (DOWN, UP)]
    for step in range(1, shares):
        for kind in (DOWN, UP):
            moved = ring_step(flows[kind], ways[kind], "dp")
            if kind == DOWN or step > 1:
                moved = after(moved, flows[1 - kind])
            total = [value.astype(F32) + addend(step, kind, layer) for layer, value in enumerate(moved)]
            flows[kind] = [value.astype(BF16) for value in total] if step < shares - 1 else total
        if step == 1:
            vectors, scales, grads_other = after((vectors, scales, grads_other), flows)
            outputs_other = after(state[5], flows)
    down_share = jnp.stack(flows[DOWN])
    up_share = jnp.stack([value.reshape(-1, width // shares, width).swapaxes(0, 1).reshape(width // shares, hidden) for value in flows[UP]])

    vectors = (vectors[0] + vectors[1]).at[:, SCALE].set(jnp.sum(scales, axis=1))
    low_high = vectors.reshape(2, 2, *vectors.shape[1:])
    totals = jnp.where(core == 0, low_high[0], low_high[1])
    totals = totals + lax.ppermute(jnp.where(core == 0, low_high[1], low_high[0]), "section", exchange)
    totals = sum_doubling(totals, "dp")
    scale_grad = (totals[:, SCALE] + down_bias.astype(F32) * totals[:, DOWN_B]) / layer_scale.astype(F32)
    shard = lax.axis_index("dp")

    def share(value):
        size = value.shape[-1] // shares
        return lax.dynamic_slice_in_dim(value, shard * size, size, value.ndim - 1)

    def assemble(mine, other):
        other = lax.ppermute(other, "section", exchange)
        return lax.dynamic_update_slice_in_dim(mine, other, 2 * (1 - core), 0)[None, :, None]

    section_outputs = assemble(state[4], outputs_other)
    input_grads = assemble(grads_kept, grads_other)
    return (
        section_outputs,
        input_grads,
        share(totals[:, :CONV_B]),
        share(totals[:, CONV_B]),
        share(totals[:, GAIN]),
        share(totals[:, SHIFT]),
        up_share,
        share(totals[:, UP_B : UP_B + hidden // width].reshape(2, -1)),
        down_share,
        share(totals[:, DOWN_B]),
        share(scale_grad),
    )


def solution(mesh):
    in_specs = (
        P(None, "dp", None, None),
        P(None, "dp", None),
        P(None, "dp", None, None),
        P("section", None, None),
        P("section", None),
        P("section", None),
        P("section", None),
        P("section", None, None),
        P("section", None),
        P("section", None, None),
        P("section", None),
        P("section", None),
    )
    out_specs = (
        P("section", None, "dp", None, None),
        P("section", None, "dp", None, None),
        P("section", None, "dp"),
        P("section", "dp"),
        P("section", "dp"),
        P("section", "dp"),
        P("section", "dp", None),
        P("section", "dp"),
        P("section", "dp", None),
        P("section", "dp"),
        P("section", "dp"),
    )
    return jax.shard_map(per_device, mesh=mesh, in_specs=in_specs, out_specs=out_specs, check_vma=False)
```

```python
import functools

import jax
import jax.numpy as jnp
from jax import lax
from jax.experimental import pallas as pl
from jax.experimental.pallas import tpu as pltpu
from jax.sharding import PartitionSpec as P

EPSILON = 1e-06
INV_SQRT2 = 0.7071067811865476
INV_SQRT_PI = 0.5641895835477563
LOG2_E = 1.4426950408889634
F32 = jnp.float32
BF16 = jnp.bfloat16
TILE = 32
PAD = 8
COLS = 256
VMEM_LIMIT = 60 * 2**20
COST = pl.CostEstimate(flops=1, bytes_accessed=1, transcendentals=0)

CONV_B, GAIN, SHIFT, DOWN_B, SCALE, UP_B, VEC_ROWS = 7, 8, 9, 10, 11, 12, 16
XHAT, STREAM, NORMED, KINDS = 0, 1, 2, 3
LANES = 128
OFFSETS = (1, 2, 3, -1, -2, -3)
MASK_OF = {offset: k for k, offset in enumerate(OFFSETS)}


def slabs(width):
    return [slice(c, c + LANES) for c in range(0, width, LANES)]


def row_sum(parts):
    return jnp.sum(functools.reduce(jnp.add, parts), axis=1, keepdims=True)


def fold(value):
    return functools.reduce(jnp.add, [value[8 * i : 8 * i + 8] for i in range(value.shape[0] // 8)])


def clear_edges(padded, frames):
    for slab in range(padded.shape[0]):
        padded[slab, 0:PAD, :] = jnp.zeros((PAD, LANES), F32)
        padded[slab, PAD + frames : PAD + frames + PAD, :] = jnp.zeros((PAD, LANES), F32)


def build_masks(seg_v, masks):
    frames = masks.shape[1]
    seg_v[0:PAD, :] = jnp.full((PAD, LANES), -1.0, F32)
    seg_v[PAD + frames : PAD + frames + PAD, :] = jnp.full((PAD, LANES), -1.0, F32)

    def body(i, carry):
        base = pl.multiple_of(i * 64, 64)
        here = seg_v[pl.ds(base + PAD, 64), :]
        for k, offset in enumerate(OFFSETS):
            there = seg_v[pl.ds(base + PAD + offset, 64), :]
            masks[k, pl.ds(base, 64), :] = jnp.where(there == here, 1.0, 0.0)
        return carry

    lax.fori_loop(0, frames // 64, body, 0)


def start_weights(core, layer, own, peer, target, sem):
    @pl.when(core == lax.div(layer, 2))
    def _():
        pltpu.make_async_copy(own.at[lax.rem(layer, 2)], target, sem).start()

    @pl.when(core != lax.div(layer, 2))
    def _():
        pltpu.make_async_copy(peer.at[lax.rem(layer, 2)], target, sem).start()


def send_row(core, section, source, kept, other, sem):
    @pl.when(core == section)
    def _():
        pltpu.make_async_copy(source, kept, sem).start()

    @pl.when(core != section)
    def _():
        pltpu.make_async_copy(source, other, sem).start()


def forward_kernel(layers, aliased, flags, x_in, seg_hbm, vec, own_up, own_down, peer_up, peer_down, *rest):
    rest = rest[aliased:]
    hid, dge, saved, rst, kept, other, send = rest[:7]
    (up_v, down_v, hid_v, dge_v, saved_v, rst_v, stream, acc, out_v, x_v, seg_v, masks, w_sem, in_sem, o_sem, s_sem) = rest[7:]
    frames, width = acc.shape
    hidden = hid_v.shape[2]

    @pl.when(flags[0] == 1)
    def _():
        core, micro, row = flags[1], flags[2], flags[3]
        pltpu.make_async_copy(x_in, x_v, s_sem.at[2]).start()
        pltpu.make_async_copy(seg_hbm.at[micro], seg_v.at[pl.ds(PAD, frames)], in_sem).start()
        def fetch(j):
            start_weights(core, j, own_up, peer_up, up_v.at[j], w_sem.at[j, 0])
            start_weights(core, j, own_down, peer_down, down_v.at[j], w_sem.at[j, 1])

        fetch(0)
        clear_edges(stream, frames)
        pltpu.make_async_copy(seg_hbm.at[0], seg_v.at[pl.ds(PAD, frames)], in_sem).wait()
        build_masks(seg_v, masks)
        pltpu.make_async_copy(x_in, x_v, s_sem.at[2]).wait()
        for c, cols in enumerate(slabs(width)):
            stream[c, PAD : PAD + frames, :] = x_v[:, cols].astype(F32)

        def layer(j, carry):
            def conv_norm(i, c):
                base = pl.multiple_of(i * TILE, TILE)
                rows = pl.ds(base, TILE)
                parts = []
                for s, cols in enumerate(slabs(width)):
                    centre = stream[s, pl.ds(base + PAD, TILE), :]
                    saved_v[j, STREAM, rows, cols] = centre.astype(BF16)
                    total = vec[j, CONV_B : CONV_B + 1, cols] + vec[j, 3:4, cols] * centre
                    for offset in OFFSETS:
                        neighbour = stream[s, pl.ds(base + PAD + offset, TILE), :] * masks[MASK_OF[offset], rows, :]
                        total = total + vec[j, offset + 3 : offset + 4, cols] * neighbour
                    parts.append(total)
                mean = row_sum(parts) * (1.0 / width)
                parts = [part - mean for part in parts]
                rstd = lax.rsqrt(row_sum([part * part for part in parts]) * (1.0 / width) + EPSILON)
                for part, cols in zip(parts, slabs(width)):
                    xhat = part * rstd
                    saved_v[j, XHAT, rows, cols] = xhat.astype(BF16)
                    saved_v[j, NORMED, rows, cols] = (xhat * vec[j, GAIN : GAIN + 1, cols] + vec[j, SHIFT : SHIFT + 1, cols]).astype(BF16)
                rst_v[j, rows, :] = jnp.broadcast_to(rstd, (TILE, LANES))
                return c

            lax.fori_loop(0, frames // TILE, conv_norm, 0, unroll=8)
            pltpu.make_async_copy(saved_v.at[j], saved.at[row, j], o_sem.at[j, 3]).start()
            pltpu.make_async_copy(rst_v.at[j], rst.at[row, j], o_sem.at[j, 2]).start()
            pltpu.make_async_copy(own_up.at[0], up_v.at[j], w_sem.at[j, 0]).wait()

            @pl.when(j + 1 < layers)
            def _():
                fetch(j + 1)

            for n in range(hidden // COLS):
                cols = slice(n * COLS, (n + 1) * COLS)
                at, start = UP_B + n * COLS // width, (n * COLS) % width
                value = jnp.dot(saved_v[j, NORMED], up_v[j, :, cols], preferred_element_type=F32) + vec[j, at : at + 1, start : start + COLS]
                scaled = value * INV_SQRT2
                phi_sum = 0.5 + 0.5 * lax.erf(scaled)
                hid_v[j, :, cols] = (value * phi_sum).astype(BF16)
                dge_v[j, :, cols] = (phi_sum + scaled * INV_SQRT_PI * jnp.exp2(scaled * scaled * -LOG2_E)).astype(BF16)
            pltpu.make_async_copy(hid_v.at[j], hid.at[row, j], o_sem.at[j, 0]).start()
            pltpu.make_async_copy(dge_v.at[j], dge.at[row, j], o_sem.at[j, 1]).start()
            pltpu.make_async_copy(own_down.at[0], down_v.at[j], w_sem.at[j, 1]).wait()
            acc[...] = jnp.dot(hid_v[j], down_v[j], preferred_element_type=F32)

            def finish(ends_section, i, c):
                base = pl.multiple_of(i * TILE, TILE)
                rows = pl.ds(base, TILE)
                for s, cols in enumerate(slabs(width)):
                    inner = pl.ds(pl.multiple_of(base + PAD, 8), TILE)
                    branch = acc[rows, cols] + vec[j, DOWN_B : DOWN_B + 1, cols]
                    fresh = stream[s, inner, :] + vec[j, SCALE : SCALE + 1, cols] * branch
                    if ends_section:
                        rounded = fresh.astype(BF16)
                        out_v[lax.div(j, 2), rows, cols] = fresh
                        x_v[rows, cols] = rounded
                        fresh = rounded.astype(F32)
                    stream[s, inner, :] = fresh
                return c

            @pl.when(lax.rem(j, 2) == 1)
            def _():
                lax.fori_loop(0, frames // TILE, functools.partial(finish, True), 0)

            @pl.when(lax.rem(j, 2) == 0)
            def _():
                lax.fori_loop(0, frames // TILE, functools.partial(finish, False), 0)

            @pl.when(j == 1)
            def _():
                send_row(core, 0, out_v.at[0], kept.at[micro], other.at[row], s_sem.at[0])

            return carry

        lax.fori_loop(0, layers, layer, 0)
        send_row(core, 1, out_v.at[1], kept.at[micro], other.at[row], s_sem.at[1])
        pltpu.make_async_copy(x_v, send, s_sem.at[2]).start()
        for j in range(layers):
            pltpu.make_async_copy(hid_v.at[j], hid.at[row, j], o_sem.at[j, 0]).wait()
            pltpu.make_async_copy(dge_v.at[j], dge.at[row, j], o_sem.at[j, 1]).wait()
            pltpu.make_async_copy(rst_v.at[j], rst.at[row, j], o_sem.at[j, 2]).wait()
            pltpu.make_async_copy(saved_v.at[j], saved.at[row, j], o_sem.at[j, 3]).wait()
        pltpu.make_async_copy(out_v.at[0], other.at[row], s_sem.at[0]).wait()
        pltpu.make_async_copy(out_v.at[1], other.at[row], s_sem.at[1]).wait()
        pltpu.make_async_copy(x_v, send, s_sem.at[2]).wait()


DOWN, UP = 0, 1
VECTORS = 16


def send_sums(core, section, owners, kind, layer, source, vectors, targets, sem):
    kept, others = targets[0], targets[1:]
    shares, _, block, width = kept.shape
    size = (block - VECTORS) // 2
    first = 0 if kind == DOWN else size + VECTORS
    columns = source.shape[1] // width
    rows = size // columns
    for stop in range(shares):
        owner = owners[2 * kind + layer, stop]
        pieces = [
            (source.at[pl.ds(pl.multiple_of(owner * rows, 16), rows), pl.ds(b * width, width)], pl.ds(first + b * rows, rows))
            for b in range(columns)
        ]
        if vectors is not None:
            pieces.append((vectors.at[owners[2 * DOWN + layer, stop]], pl.ds(size, VECTORS)))
        for piece, place in pieces:

            @pl.when(core == section)
            def _():
                pltpu.make_async_copy(piece, kept.at[stop, layer, place], sem).start()

            @pl.when(core != section)
            def _():
                pltpu.make_async_copy(piece, others[stop].at[layer, place], sem).start()


def pack_vectors(sums, packed):
    shares, _, width = packed.shape
    parts = [sums[r : r + 1, :] for r in range(UP_B, VEC_ROWS - 1)]
    wide = jnp.broadcast_to(jnp.concatenate(parts, axis=1), (8, width * len(parts)))
    size, wide_size = width // shares, width * len(parts) // shares
    is_bias = lax.broadcasted_iota(jnp.int32, (VECTORS, width), 0) == UP_B
    for d in range(shares):
        part = sums if d == 0 else pltpu.roll(sums, width - d * size, 1)
        bias = wide if d == 0 else pltpu.roll(wide, wide.shape[1] - d * wide_size, 1)
        packed[d] = jnp.where(is_bias, jnp.broadcast_to(bias[0:1, :width], (VECTORS, width)), part).astype(BF16)


def backward_kernel(final, aliased, ties, riders, flags, g_one, g_two, seg_hbm, vec, own_up, own_down, peer_up, peer_down, dge, saved, rst, *rest):
    if final:
        owners, hid, gb, gp, vec_in = rest[:5]
        rest = rest[5 + ties + aliased :]
        sums = owners.shape[1] + 1
        sums_out, (kept, other) = rest[:sums], rest[sums : sums + 2]
        rest = rest[sums + 2 :]
    else:
        rest = rest[aliased:]
        gb, gp, vec_out, kept, other, send = rest[:6]
        rest = rest[6 + riders :]
    (up_v, down_v, dge_v, saved_v, rst_v, gb_v, gp_v, vg_v, g_now, fresh_v, gn_v, padded, x_v, seg_v, masks, w_sem, in_sem, g_sem, o_sem, s_sem) = rest[:20]
    if final:
        (hid_v, nrm_v, dwd_v, dwu_v, early_v, packed, b_sem) = rest[20:]
    frames, width = g_now.shape
    held, _, hidden = dge_v.shape
    layers = vec.shape[0]
    nt = (((1,), (1,)), ((), ()))
    tn = (((0,), (0,)), ((), ()))
    tall = 2 * TILE
    cols_of = slabs(width)

    @pl.when(flags[0] == 1)
    def _():
        core, micro, row = flags[1], flags[2], flags[3]
        pltpu.make_async_copy(seg_hbm.at[micro], seg_v.at[pl.ds(PAD, frames)], in_sem).start()

        def fetch(j):
            h = lax.rem(j, held)
            start_weights(core, j, own_down, peer_down, down_v.at[h], w_sem.at[h, 1])
            pltpu.make_async_copy(dge.at[row, j], dge_v.at[h], w_sem.at[h, 3]).start()
            start_weights(core, j, own_up, peer_up, up_v.at[h], w_sem.at[h, 0])
            pltpu.make_async_copy(rst.at[row, j], rst_v.at[h], w_sem.at[h, 4]).start()
            pltpu.make_async_copy(saved.at[row, j, 0:2], saved_v.at[h], w_sem.at[h, 2]).start()

        if final:
            pltpu.make_async_copy(vec_in.at[1 - row], early_v, s_sem.at[2]).start()
        source = [pltpu.make_async_copy(g, x_v, g_sem) for g in (g_one, g_two)]
        for k in range(2):

            @pl.when(flags[4] == k)
            def _():
                source[k].start()

        fetch(layers - 1)
        clear_edges(padded, frames)
        source[0].wait()
        for cols in cols_of:

            def enter(t, c):
                rows = pl.ds(pl.multiple_of(t * tall, tall), tall)
                scaled = (vec[layers - 1, SCALE : SCALE + 1, cols] * x_v[rows, cols].astype(F32)).astype(BF16)
                gb_v[layers, 0, rows, cols] = scaled
                return c + fold(scaled.astype(F32))

            total = lax.fori_loop(0, frames // tall, enter, jnp.zeros((8, LANES), F32))
            vg_v[layers, DOWN_B : DOWN_B + 1, cols] = jnp.sum(total, axis=0, keepdims=True)
        pltpu.make_async_copy(seg_hbm.at[0], seg_v.at[pl.ds(PAD, frames)], in_sem).wait()
        build_masks(seg_v, masks)

        def layer(step, carry):
            j = layers - 1 - step
            h = lax.rem(j, held)
            if not final:
                pltpu.make_async_copy(gb_v.at[j + 1, 0], gb.at[row, j], o_sem.at[j, 0]).start()
            pltpu.make_async_copy(own_down.at[0], down_v.at[h], w_sem.at[h, 1]).wait()
            pltpu.make_async_copy(dge.at[0, 0], dge_v.at[h], w_sem.at[h, 3]).wait()
            if final:
                pltpu.make_async_copy(hid.at[row, j], hid_v.at[h, 0], b_sem.at[h, 0]).start()
                pltpu.make_async_copy(hid.at[1 - row, j], hid_v.at[h, 1], b_sem.at[h, 1]).start()
                pltpu.make_async_copy(gb.at[1 - row, j], gb_v.at[j + 1, 1], b_sem.at[h, 4]).start()
                pltpu.make_async_copy(saved.at[row, j, NORMED], nrm_v.at[h, 0], b_sem.at[h, 2]).start()
                pltpu.make_async_copy(saved.at[1 - row, j, NORMED], nrm_v.at[h, 1], b_sem.at[h, 3]).start()
                pltpu.make_async_copy(gp.at[1 - row, j], gp_v.at[h, 1], b_sem.at[h, 5]).start()
            for n in range(hidden // COLS):
                cols = slice(n * COLS, (n + 1) * COLS)
                value = lax.dot_general(gb_v[j + 1, 0], down_v[h, cols, :], nt, preferred_element_type=F32)
                rounded = (value * dge_v[h, :, cols].astype(F32)).astype(BF16)
                gp_v[h, 0, :, cols] = rounded
                at, start = UP_B + n * COLS // width, (n * COLS) % width
                vg_v[j + 1, at : at + 1, start : start + COLS] = jnp.sum(rounded.astype(F32), axis=0, keepdims=True)
            if not final:
                pltpu.make_async_copy(gp_v.at[h, 0], gp.at[row, j], o_sem.at[j, 1]).start()
            pltpu.make_async_copy(own_up.at[0], up_v.at[h], w_sem.at[h, 0]).wait()
            gn_v[...] = lax.dot_general(gp_v[h, 0], up_v[h], nt, preferred_element_type=F32)
            pltpu.make_async_copy(rst.at[0, 0], rst_v.at[h], w_sem.at[h, 4]).wait()
            pltpu.make_async_copy(saved.at[0, 0, 0:2], saved_v.at[h], w_sem.at[h, 2]).wait()

            @pl.when(j > 0)
            def _():
                fetch(j - 1)

            if final:
                pltpu.make_async_copy(hid.at[0, 0], hid_v.at[h, 0], b_sem.at[h, 0]).wait()
                pltpu.make_async_copy(hid.at[0, 0], hid_v.at[h, 1], b_sem.at[h, 1]).wait()
                pltpu.make_async_copy(gb.at[0, 0], gb_v.at[j + 1, 1], b_sem.at[h, 4]).wait()

                @pl.when(j + held < layers)
                def _():
                    pltpu.make_async_copy(dwd_v.at[h], dwd_v.at[h], o_sem.at[h, 0]).wait()
                    pltpu.make_async_copy(dwu_v.at[h], dwu_v.at[h], o_sem.at[h, 1]).wait()
                    pltpu.make_async_copy(packed.at[h], packed.at[h], o_sem.at[h, 1]).wait()

            def down_chunk(n):
                rows = slice(n * COLS, (n + 1) * COLS)
                left = hid_v[h, :, :, rows].reshape(2 * frames, COLS)
                right = gb_v[j + 1].reshape(2 * frames, width)
                value = lax.dot_general(left, right, tn, preferred_element_type=F32)
                dwd_v[h, rows, :] = value.astype(BF16)
                return fold(value * down_v[h, rows, :].astype(F32))

            def up_chunk(m, n):
                rows = slice(m * COLS, (m + 1) * COLS)
                cols = slice(n * width, (n + 1) * width)
                left = nrm_v[h, :, :, rows].reshape(2 * frames, COLS)
                right = gp_v[h, :, :, cols].reshape(2 * frames, width)
                dwu_v[h, rows, cols] = lax.dot_general(left, right, tn, preferred_element_type=F32).astype(BF16)

            odd = lax.rem(j, 2) == 1

            def norm_back(t, c):
                base = t * TILE if isinstance(t, int) else pl.multiple_of(t * TILE, TILE)
                rows = pl.ds(base, TILE)
                inner = pl.ds(base + PAD if isinstance(t, int) else pl.multiple_of(base + PAD, 8), TILE)
                grads = [gn_v[rows, cols] for cols in cols_of]
                xhats = [saved_v[h, XHAT, rows, cols].astype(F32) for cols in cols_of]
                qs = [grad * vec[j, GAIN : GAIN + 1, cols] for grad, cols in zip(grads, cols_of)]
                mean_q = row_sum(qs) * (1.0 / width)
                mean_qx = row_sum([q * xhat for q, xhat in zip(qs, xhats)]) * (1.0 / width)
                rstd = rst_v[h, rows, :]
                out = []
                for s, cols in enumerate(cols_of):
                    grad_conv = rstd * (qs[s] - mean_q - xhats[s] * mean_qx)
                    padded[s, inner, :] = grad_conv
                    g_now[rows, cols] = jnp.where(odd, x_v[rows, cols].astype(F32), fresh_v[rows, cols])
                    out += [c[3 * s] + fold(grads[s] * xhats[s]), c[3 * s + 1] + fold(grads[s]), c[3 * s + 2] + fold(grad_conv)]
                return tuple(out)

            sums = (jnp.zeros((8, LANES), F32),) * (3 * len(cols_of))
            tiles = frames // TILE
            if final:
                parts = hidden // COLS
                scale = jnp.zeros((8, width), F32)
                done = 0
                for n in range(parts):
                    scale = scale + down_chunk(n)
                    while done < tiles * (n + 1) // parts:
                        sums = norm_back(done, sums)
                        done += 1
                vg_v[j + 1, SCALE : SCALE + 1, :] = jnp.sum(scale, axis=0, keepdims=True)
                send_sums(core, lax.div(j, 2), owners, DOWN, lax.rem(j, 2), dwd_v.at[h], None, sums_out, o_sem.at[h, 0])
                pltpu.make_async_copy(saved.at[0, 0, 0], nrm_v.at[h, 0], b_sem.at[h, 2]).wait()
                pltpu.make_async_copy(saved.at[0, 0, 0], nrm_v.at[h, 1], b_sem.at[h, 3]).wait()
                pltpu.make_async_copy(gp.at[0, 0], gp_v.at[h, 1], b_sem.at[h, 5]).wait()
            else:
                sums = lax.fori_loop(0, tiles, norm_back, sums, unroll=8)
            for s, cols in enumerate(cols_of):
                for k, at in enumerate((GAIN, SHIFT, CONV_B)):
                    vg_v[j + 1, at : at + 1, cols] = jnp.sum(sums[3 * s + k], axis=0, keepdims=True)

            @pl.when(odd & (step > 0))
            def _():
                pltpu.make_async_copy(fresh_v, other.at[row], s_sem.at[0]).wait()

            below = lax.max(j - 1, 0)
            for s, cols in enumerate(cols_of):

                def conv_back(t, c):
                    base = t * tall if isinstance(t, int) else pl.multiple_of(t * tall, tall)
                    rows = pl.ds(base, tall)
                    source = saved_v[h, STREAM, rows, cols].astype(F32)
                    centre = padded[s, pl.ds(base + PAD if isinstance(t, int) else pl.multiple_of(base + PAD, 8), tall), :]
                    total = g_now[rows, cols] + vec[j, 3:4, cols] * centre
                    taps = [None] * 7
                    taps[3] = c[3] + fold(centre * source)
                    for offset in OFFSETS:
                        term = padded[s, pl.ds(base + PAD - offset, tall), :] * masks[MASK_OF[-offset], rows, :]
                        total = total + vec[j, offset + 3 : offset + 4, cols] * term
                        taps[offset + 3] = c[offset + 3] + fold(term * source)
                    rounded = total.astype(BF16)
                    fresh_v[rows, cols] = total
                    x_v[rows, cols] = rounded
                    scaled = (vec[below, SCALE : SCALE + 1, cols] * jnp.where(odd, total, rounded.astype(F32))).astype(BF16)
                    gb_v[j, 0, rows, cols] = scaled
                    return tuple(taps) + (c[7] + fold(scaled.astype(F32)),)

                sums = (jnp.zeros((8, LANES), F32),) * 8
                if final:
                    chunks = [(m, n) for m in range(width // COLS) for n in range(hidden // width)]
                    each = -(-len(chunks) // len(cols_of))
                    mine = chunks[s * each : (s + 1) * each]
                    done = 0
                    for k, (m, n) in enumerate(mine):
                        up_chunk(m, n)
                        while done < frames // tall * (k + 1) // len(mine):
                            sums = conv_back(done, sums)
                            done += 1
                    while done < frames // tall:
                        sums = conv_back(done, sums)
                        done += 1
                else:
                    sums = lax.fori_loop(0, frames // tall, conv_back, sums, unroll=8)
                for k in range(7):
                    vg_v[j + 1, k : k + 1, cols] = jnp.sum(sums[k], axis=0, keepdims=True)
                vg_v[j, DOWN_B : DOWN_B + 1, cols] = jnp.sum(sums[7], axis=0, keepdims=True)
            if final:

                @pl.when(step == 0)
                def _():
                    pltpu.make_async_copy(vec_in.at[0], early_v, s_sem.at[2]).wait()

                pack_vectors(vg_v[j + 1] + early_v[j], packed.at[h])
                send_vectors = packed.at[h]
                send_sums(core, lax.div(j, 2), owners, UP, lax.rem(j, 2), dwu_v.at[h], send_vectors, sums_out, o_sem.at[h, 1])

            @pl.when(jnp.logical_not(odd))
            def _():
                send_row(core, lax.div(j, 2), fresh_v, kept.at[micro], other.at[row], s_sem.at[0])

            return carry

        for i in range(1, layers + 1):
            vg_v[i, SCALE : SCALE + 1, :] = jnp.zeros((1, width), F32)
            vg_v[i, VEC_ROWS - 1 : VEC_ROWS, :] = jnp.zeros((1, width), F32)
        lax.fori_loop(0, layers, layer, 0)
        if final:
            for h in range(held):
                pltpu.make_async_copy(dwd_v.at[h], dwd_v.at[h], o_sem.at[h, 0]).wait()
                pltpu.make_async_copy(dwu_v.at[h], dwu_v.at[h], o_sem.at[h, 1]).wait()
                pltpu.make_async_copy(packed.at[h], packed.at[h], o_sem.at[h, 1]).wait()
        else:
            pltpu.make_async_copy(vg_v.at[pl.ds(1, layers)], vec_out.at[row], s_sem.at[2]).start()
            pltpu.make_async_copy(x_v, send, s_sem.at[1]).start()
            for j in range(layers):
                pltpu.make_async_copy(gb_v.at[j + 1, 0], gb.at[row, j], o_sem.at[j, 0]).wait()
                pltpu.make_async_copy(gp_v.at[j, 0], gp.at[row, j], o_sem.at[j, 1]).wait()
            pltpu.make_async_copy(x_v, send, s_sem.at[1]).wait()
            pltpu.make_async_copy(vg_v.at[pl.ds(1, layers)], vec_out.at[row], s_sem.at[2]).wait()
        pltpu.make_async_copy(fresh_v, other.at[row], s_sem.at[0]).wait()


def weight_kernel(ties, flags, owners, own_down, peer_down, all_hid, all_gb, all_saved, all_gp, vec_in, *rest):
    rest = rest[ties:]
    sums_out, rest = rest[: owners.shape[1] + 1], rest[owners.shape[1] + 1 :]
    hid_v, gb_v, nrm_v, gp_v, down_v, dwd_v, dwu_v, vec_v, packed, sem, o_sem, s_sem = rest
    frames, width = gb_v.shape[2:]
    hidden = hid_v.shape[3]
    layers = all_hid.shape[1]
    tn = (((0,), (0,)), ((), ()))

    @pl.when(flags[0] == 1)
    def _():
        core = flags[1]

        def copies(j, h):
            pairs = []
            for row in range(2):
                pairs += [
                    (all_hid.at[row, j], hid_v.at[h, row]),
                    (all_gb.at[row, j], gb_v.at[h, row]),
                    (all_saved.at[row, j, NORMED], nrm_v.at[h, row]),
                    (all_gp.at[row, j], gp_v.at[h, row]),
                ]
            return [pltpu.make_async_copy(a, b, sem.at[h, k]) for k, (a, b) in enumerate(pairs)]

        def fetch(j):
            h = lax.rem(j, 2)
            start_weights(core, j, own_down, peer_down, down_v.at[h], sem.at[h, 8])
            for copy in copies(j, h):
                copy.start()

        fetch(layers - 1)
        pltpu.make_async_copy(vec_in, vec_v, s_sem).start()
        pltpu.make_async_copy(vec_in, vec_v, s_sem).wait()

        def layer(step, carry):
            j = layers - 1 - step
            h = lax.rem(j, 2)

            @pl.when(j > 0)
            def _():
                fetch(j - 1)

            pltpu.make_async_copy(own_down.at[0], down_v.at[h], sem.at[h, 8]).wait()
            for copy in copies(j, h):
                copy.wait()

            @pl.when(j + 2 < layers)
            def _():
                pltpu.make_async_copy(dwd_v.at[h], dwd_v.at[h], o_sem.at[h, 0]).wait()
                pltpu.make_async_copy(dwu_v.at[h], dwu_v.at[h], o_sem.at[h, 1]).wait()
                pltpu.make_async_copy(packed.at[h], packed.at[h], o_sem.at[h, 1]).wait()

            def down_chunk(n, scale):
                rows = pl.ds(pl.multiple_of(n * COLS, COLS), COLS)
                left = hid_v[h, :, :, rows].reshape(2 * frames, COLS)
                value = lax.dot_general(left, gb_v[h].reshape(2 * frames, width), tn, preferred_element_type=F32)
                dwd_v[h, rows, :] = value.astype(BF16)
                return scale + fold(value * down_v[h, rows, :].astype(F32))

            scale = lax.fori_loop(0, hidden // COLS, down_chunk, jnp.zeros((8, width), F32))
            scale = jnp.sum(scale, axis=0, keepdims=True)
            vectors = vec_v[0, j] + vec_v[1, j]
            is_scale = lax.broadcasted_iota(jnp.int32, vectors.shape, 0) == SCALE
            pack_vectors(jnp.where(is_scale, jnp.broadcast_to(scale, vectors.shape), vectors), packed.at[h])
            send_sums(core, lax.div(j, 2), owners, DOWN, lax.rem(j, 2), dwd_v.at[h], None, sums_out, o_sem.at[h, 0])

            def up_chunk(n, c):
                cols = pl.ds(pl.multiple_of(n * width, width), width)
                right = gp_v[h, :, :, cols].reshape(2 * frames, width)
                value = lax.dot_general(nrm_v[h].reshape(2 * frames, width), right, tn, preferred_element_type=F32)
                dwu_v[h, :, cols] = value.astype(BF16)
                return c

            lax.fori_loop(0, hidden // width, up_chunk, 0)
            send_sums(core, lax.div(j, 2), owners, UP, lax.rem(j, 2), dwu_v.at[h], packed.at[h], sums_out, o_sem.at[h, 1])
            return carry

        lax.fori_loop(0, layers, layer, 0)
        for h in range(2):
            pltpu.make_async_copy(dwd_v.at[h], dwd_v.at[h], o_sem.at[h, 0]).wait()
            pltpu.make_async_copy(dwu_v.at[h], dwu_v.at[h], o_sem.at[h, 1]).wait()
            pltpu.make_async_copy(packed.at[h], packed.at[h], o_sem.at[h, 1]).wait()


def place_kernel(at, kept_in, rows, tie, kept, sem):
    copy = pltpu.make_async_copy(rows, kept.at[pl.ds(at[0], rows.shape[0])], sem)
    copy.start()
    copy.wait()


def final_kernel(down_0, down_1, up_0, up_1, kept, other, scales, *rest):
    conv_out, conv_b_out, gain_out, shift_out, up_out, up_b_out, down_out, down_b_out, scale_out, kept_v, sem = rest
    copy = pltpu.make_async_copy(kept.at[kept.shape[0] - 1], kept_v, sem)
    copy.start()
    copy.wait()
    size, wide = conv_b_out.shape[1], up_b_out.shape[1]
    rows, width = down_out.shape[1:]
    for layer, (down, up) in enumerate(((down_0, up_0), (down_1, up_1))):
        total = down[...].astype(F32) + kept_v[layer, : rows + VECTORS].astype(F32) + other[layer, : rows + VECTORS].astype(F32)
        down_out[layer] = total[:rows]
        vectors = total[rows:]
        at = slice(layer, layer + 1)
        conv_out[layer] = vectors[:CONV_B, :size]
        conv_b_out[at, :] = vectors[CONV_B : CONV_B + 1, :size]
        gain_out[at, :] = vectors[GAIN : GAIN + 1, :size]
        shift_out[at, :] = vectors[SHIFT : SHIFT + 1, :size]
        down_b = vectors[DOWN_B : DOWN_B + 1, :size]
        down_b_out[at, :] = down_b
        scale_out[at, :] = (vectors[SCALE : SCALE + 1, :size] + scales[0, at, :] * down_b) / scales[1, at, :]
        up_b_out[at, :] = vectors[UP_B : UP_B + 1, :wide]
        total = up[...].astype(F32) + kept_v[layer, rows + VECTORS :].astype(F32) + other[layer, rows + VECTORS :].astype(F32)
        for b in range(up_out.shape[2] // width):
            up_out[layer, :, b * width : (b + 1) * width] = total[b * size : (b + 1) * size]


ANY = pl.BlockSpec(memory_space=pl.ANY)
SMEM = pl.BlockSpec(memory_space=pltpu.SMEM)
VMEM = pl.BlockSpec(memory_space=pltpu.VMEM)


def run_forward(flags, x, seg, vec, weights, earlier):
    layers = vec.shape[0]
    micro = seg.shape[0]
    frames, width = x.shape
    hidden = weights[0].shape[2]
    shapes = (
        jax.ShapeDtypeStruct((2, layers, frames, hidden), BF16),
        jax.ShapeDtypeStruct((2, layers, frames, hidden), BF16),
        jax.ShapeDtypeStruct((2, layers, KINDS, frames, width), BF16),
        jax.ShapeDtypeStruct((2, layers, frames, LANES), F32),
        jax.ShapeDtypeStruct((micro, frames, width), F32),
        jax.ShapeDtypeStruct((2, frames, width), F32),
        jax.ShapeDtypeStruct((frames, width), BF16),
    )
    aliased = len(earlier)
    return pl.pallas_call(
        functools.partial(forward_kernel, layers, aliased),
        out_shape=shapes,
        in_specs=[SMEM, ANY, ANY, VMEM] + [ANY] * (4 + aliased),
        out_specs=(ANY,) * len(shapes),
        input_output_aliases={8 + i: i for i in range(aliased)},
        scratch_shapes=[
            pltpu.VMEM((layers, width, hidden), BF16),
            pltpu.VMEM((layers, hidden, width), BF16),
            pltpu.VMEM((layers, frames, hidden), BF16),
            pltpu.VMEM((layers, frames, hidden), BF16),
            pltpu.VMEM((layers, KINDS, frames, width), BF16),
            pltpu.VMEM((layers, frames, LANES), F32),
            pltpu.VMEM((width // LANES, frames + 2 * PAD, LANES), F32),
            pltpu.VMEM((frames, width), F32),
            pltpu.VMEM((2, frames, width), F32),
            pltpu.VMEM((frames, width), BF16),
            pltpu.VMEM((frames + 2 * PAD, LANES), F32),
            pltpu.VMEM((6, frames, LANES), F32),
            pltpu.SemaphoreType.DMA((layers, 2)),
            pltpu.SemaphoreType.DMA,
            pltpu.SemaphoreType.DMA((layers, 4)),
            pltpu.SemaphoreType.DMA((3,)),
        ],
        compiler_params=pltpu.CompilerParams(vmem_limit_bytes=VMEM_LIMIT),
        cost_estimate=COST,
    )(flags, x, seg, vec, *weights, *earlier)


def sum_shapes(shares, hidden, width):
    block = (2, 2 * (hidden // shares) + VECTORS, width)
    return tuple(jax.ShapeDtypeStruct(shape, BF16) for shape in [(shares, *block)] + [block] * shares)


def run_backward(flags, g, seg, vec, weights, state, earlier, final=(), ties=(), riders=()):
    frames, width = g[0].shape
    hidden = weights[0].shape[2]
    layers, micro = vec.shape[0], seg.shape[0]
    rows, held = (2, 2) if final else (1, layers)
    grads = (
        jax.ShapeDtypeStruct((micro, frames, width), F32),
        jax.ShapeDtypeStruct((2, frames, width), F32),
    )
    if final:
        shapes = (*sum_shapes(final[0].shape[1], hidden, width), *grads)
    else:
        shapes = (
            jax.ShapeDtypeStruct((2, layers, frames, width), BF16),
            jax.ShapeDtypeStruct((2, layers, frames, hidden), BF16),
            jax.ShapeDtypeStruct((2, layers, VEC_ROWS, width), F32),
            *grads,
            jax.ShapeDtypeStruct((frames, width), BF16),
        )
    earlier = (*earlier, *riders)
    shapes = (*shapes, *(jax.ShapeDtypeStruct(rider.shape, rider.dtype) for rider in riders))
    aliased = len(earlier)
    targets = [*range(len(earlier) - len(riders)), *range(len(shapes) - len(riders), len(shapes))]
    scratch = [
        pltpu.VMEM((held, width, hidden), BF16),
        pltpu.VMEM((held, hidden, width), BF16),
        pltpu.VMEM((held, frames, hidden), BF16),
        pltpu.VMEM((held, 2, frames, width), BF16),
        pltpu.VMEM((held, frames, LANES), F32),
        pltpu.VMEM((layers + 1, rows, frames, width), BF16),
        pltpu.VMEM((held, rows, frames, hidden), BF16),
        pltpu.VMEM((layers + 1, VEC_ROWS, width), F32),
        pltpu.VMEM((frames, width), F32),
        pltpu.VMEM((frames, width), F32),
        pltpu.VMEM((frames, width), F32),
        pltpu.VMEM((width // LANES, frames + 2 * PAD, LANES), F32),
        pltpu.VMEM((frames, width), BF16),
        pltpu.VMEM((frames + 2 * PAD, LANES), F32),
        pltpu.VMEM((6, frames, LANES), F32),
        pltpu.SemaphoreType.DMA((held, 5)),
        pltpu.SemaphoreType.DMA,
        pltpu.SemaphoreType.DMA,
        pltpu.SemaphoreType.DMA((held, 2)),
        pltpu.SemaphoreType.DMA((3,)),
    ]
    if final:
        scratch += [
            pltpu.VMEM((held, 2, frames, hidden), BF16),
            pltpu.VMEM((held, 2, frames, width), BF16),
            pltpu.VMEM((held, hidden, width), BF16),
            pltpu.VMEM((held, width, hidden), BF16),
            pltpu.VMEM((layers, VEC_ROWS, width), F32),
            pltpu.VMEM((held, final[0].shape[1], VECTORS, width), BF16),
            pltpu.SemaphoreType.DMA((held, 6)),
        ]
    first_alias = 12 + len(final) + len(ties)
    return pl.pallas_call(
        functools.partial(backward_kernel, bool(final), aliased, len(ties), len(riders)),
        out_shape=shapes,
        in_specs=[SMEM, ANY, ANY, ANY, VMEM] + [ANY] * 7 + ([SMEM] + [ANY] * 4 if final else []) + [ANY] * (len(ties) + aliased),
        out_specs=(ANY,) * len(shapes),
        input_output_aliases={first_alias + i: target for i, target in enumerate(targets)},
        scratch_shapes=scratch,
        compiler_params=pltpu.CompilerParams(vmem_limit_bytes=VMEM_LIMIT),
        cost_estimate=COST,
    )(flags, *g, seg, vec, *weights, *state, *final, *ties, *earlier)


def run_weights(flags, owners, weights, hid, gb, saved, gp, vectors, ties):
    _, layers, frames, hidden = hid.shape
    width = gb.shape[3]
    shares = owners.shape[1]
    return pl.pallas_call(
        functools.partial(weight_kernel, len(ties)),
        out_shape=sum_shapes(shares, hidden, width),
        in_specs=[SMEM, SMEM] + [ANY] * (7 + len(ties)),
        out_specs=(ANY,) * (shares + 1),
        scratch_shapes=[
            pltpu.VMEM((2, 2, frames, hidden), BF16),
            pltpu.VMEM((2, 2, frames, width), BF16),
            pltpu.VMEM((2, 2, frames, width), BF16),
            pltpu.VMEM((2, 2, frames, hidden), BF16),
            pltpu.VMEM((2, hidden, width), BF16),
            pltpu.VMEM((2, hidden, width), BF16),
            pltpu.VMEM((2, width, hidden), BF16),
            pltpu.VMEM(vectors.shape, F32),
            pltpu.VMEM((2, shares, VECTORS, width), BF16),
            pltpu.SemaphoreType.DMA((2, 9)),
            pltpu.SemaphoreType.DMA((2, 2)),
            pltpu.SemaphoreType.DMA,
        ],
        compiler_params=pltpu.CompilerParams(vmem_limit_bytes=VMEM_LIMIT),
        cost_estimate=COST,
    )(flags, owners, weights[1], weights[3], hid, gb, saved, gp, vectors, *ties)


def run_place(kept, rows, at, tie):
    return pl.pallas_call(
        place_kernel,
        out_shape=jax.ShapeDtypeStruct(kept.shape, kept.dtype),
        in_specs=[SMEM, ANY, ANY, ANY],
        out_specs=ANY,
        input_output_aliases={1: 0},
        scratch_shapes=[pltpu.SemaphoreType.DMA],
        cost_estimate=COST,
    )(at.reshape(1).astype(jnp.int32), kept, rows, tie)


def run_final(down, up, kept, other, scales, hidden):
    shares, _, _, width = kept.shape
    size, wide = width // shares, hidden // shares
    shapes = ((2, CONV_B, size), (2, size), (2, size), (2, size), (2, size, hidden), (2, wide), (2, wide, width), (2, size), (2, size))
    return pl.pallas_call(
        final_kernel,
        out_shape=tuple(jax.ShapeDtypeStruct(shape, F32) for shape in shapes),
        in_specs=[VMEM] * 4 + [ANY] + [VMEM] * 2,
        out_specs=(VMEM,) * len(shapes),
        scratch_shapes=[pltpu.VMEM(kept.shape[1:], BF16), pltpu.SemaphoreType.DMA],
        compiler_params=pltpu.CompilerParams(vmem_limit_bytes=VMEM_LIMIT // 2),
        cost_estimate=COST,
    )(*down, *up, kept, other, scales)


def ring_order(count):
    return list(range(0, count, 2)) + list(range(count - 1, 0, -2))


def ring_owners(ways, axis):
    count = lax.axis_size(axis)
    device = lax.axis_index(axis)
    mine = jnp.where(device % 2 == 0, device // 2, count - 1 - device // 2)
    places = jnp.stack([lax.rem(mine - way * (1 + jnp.arange(count, dtype=jnp.int32)) + 2 * count, count) for way in ways])
    return jnp.where(places < count - count // 2, 2 * places, 2 * (count - places) - 1)


def after(value, earlier):
    return lax.optimization_barrier((value, earlier))[0]


def ring_step(flows, ways, axis):
    count = lax.axis_size(axis)
    order = ring_order(count)
    return [
        lax.ppermute(value, axis, [(order[p], order[(p + way) % count]) for p in range(count)]) for value, way in zip(flows, ways)
    ]


def per_device(
    inputs,
    segment_ids,
    cotangent,
    conv_weight,
    conv_bias,
    norm_gain,
    norm_bias,
    up_weight,
    up_bias,
    down_weight,
    down_bias,
    layer_scale,
):
    micro, _, frames, width = inputs.shape
    hidden = up_weight.shape[2]
    shares = lax.axis_size("dp")
    section = lax.axis_index("section")
    chip, core = section // 2, section % 2
    exchange = [(0, 1), (1, 0), (2, 3), (3, 2)]

    small = jnp.concatenate(
        [
            conv_weight,
            conv_bias[:, None],
            norm_gain[:, None],
            norm_bias[:, None],
            down_bias[:, None],
            layer_scale[:, None],
            up_bias.reshape(2, -1, width),
            jnp.zeros((2, 1, width), BF16),
        ],
        axis=1,
    )
    small_peer = lax.ppermute(small, "section", exchange)
    up_peer = lax.ppermute(up_weight, "section", exchange)
    down_peer = lax.ppermute(down_weight, "section", exchange)
    vec = jnp.where(core == 0, jnp.concatenate([small, small_peer]), jnp.concatenate([small_peer, small])).astype(F32)
    weights = (up_weight, down_weight, up_peer, down_peer)
    masks = jnp.broadcast_to(segment_ids[:, 0, :, None].astype(F32), (micro, frames, LANES))
    inputs, cotangent = inputs[:, 0], cotangent[:, 0]

    def flags(active, row, choice=0):
        return jnp.stack([jnp.asarray(v, jnp.int32) for v in (active, core, 2 * core + row, row, choice)])

    first, last = chip == 0, chip == 1
    ways = ((1, -1), (-1, 1))
    owners = ring_owners([way for kind in ways for way in kind], "dp")

    def row_of(array, row):
        return lax.dynamic_index_in_dim(array, 2 * core + row, 0, keepdims=False)

    down_pairs, up_pairs = [(0, 2), (1, 3)], [(2, 0), (3, 1)]
    state = run_forward(flags(first, 0), row_of(inputs, 0), masks, vec, weights, ())
    arrived = lax.ppermute(state[6], "section", down_pairs)
    state = run_forward(flags(first, 1), row_of(inputs, 1), masks, vec, weights, state[:6])
    arrived_next = lax.ppermute(state[6], "section", down_pairs)
    state = run_forward(flags(last, 0), arrived, masks, vec, weights, state[:6])
    gradient = row_of(cotangent, 0)
    back = run_backward(flags(last, 0), (gradient, gradient), masks, vec, weights, state[1:4], ())
    returned = lax.ppermute(back[5], "section", up_pairs)
    state = run_forward(flags(last, 1), arrived_next, masks, vec, weights, state[:6])
    gradients = (row_of(cotangent, 1), returned)
    back = run_backward(flags(True, jnp.where(last, 1, 0), first), gradients, masks, vec, weights, state[1:4], back[:5], riders=state[4:6])
    returned = lax.ppermute(back[5], "section", up_pairs)
    gb, gp, vectors, grads_kept, grads_other, _, outputs_kept, outputs_other = back

    def assemble(mine, other, tie):
        return run_place(mine, lax.ppermute(other, "section", exchange), 2 * (1 - core), tie)[None, :, None]

    section_outputs = assemble(outputs_kept, outputs_other, vectors)
    sums = run_weights(flags(last, 0), owners, weights, state[0], gb, state[2], gp, vectors, (returned, section_outputs))
    shard = lax.axis_index("dp")
    scales = jnp.stack([down_bias, layer_scale]).astype(F32)
    scales = lax.dynamic_slice_in_dim(scales, shard * (width // shares), width // shares, 2)
    *sums, grads_kept, grads_other = run_backward(
        flags(first, 1),
        (returned, returned),
        masks,
        vec,
        weights,
        state[1:4],
        (*sums, grads_kept, grads_other),
        (owners, state[0], gb, gp, vectors),
        (scales,),
    )

    kept, others = sums[0], sums[1:]
    size = hidden // shares
    spans = (slice(0, size + VECTORS), slice(size + VECTORS, None))

    def addend(stop, kind, layer):
        return kept[stop, layer, spans[kind]].astype(F32) + arrived[stop][layer, spans[kind]].astype(F32)

    ahead = 2
    arrived = [lax.ppermute(others[stop], "section", exchange) for stop in range(ahead)]
    flows = [[addend(0, kind, layer).astype(BF16) for layer in range(2)] for kind in (DOWN, UP)]
    for stop in range(1, shares):
        if stop + ahead - 1 < shares:
            arrived.append(lax.ppermute(after(others[stop + ahead - 1], flows[DOWN]), "section", exchange))
        for kind in (DOWN, UP):
            moved = ring_step(flows[kind], ways[kind], "dp")
            if kind == DOWN or stop > 1:
                moved = after(moved, flows[1 - kind])
            if stop < shares - 1:
                moved = [(value.astype(F32) + addend(stop, kind, layer)).astype(BF16) for layer, value in enumerate(moved)]
            flows[kind] = moved
        if stop == 2:
            input_grads = assemble(grads_kept, grads_other, flows[UP][0])
    grads = run_final(flows[DOWN], flows[UP], kept, arrived[-1], scales, hidden)
    return (section_outputs, input_grads, *grads)


def solution(mesh):
    in_specs = (
        P(None, "dp", None, None),
        P(None, "dp", None),
        P(None, "dp", None, None),
        P("section", None, None),
        P("section", None),
        P("section", None),
        P("section", None),
        P("section", None, None),
        P("section", None),
        P("section", None, None),
        P("section", None),
        P("section", None),
    )
    out_specs = (
        P("section", None, "dp", None, None),
        P("section", None, "dp", None, None),
        P("section", None, "dp"),
        P("section", "dp"),
        P("section", "dp"),
        P("section", "dp"),
        P("section", "dp", None),
        P("section", "dp"),
        P("section", "dp", None),
        P("section", "dp"),
        P("section", "dp"),
    )
    return jax.shard_map(per_device, mesh=mesh, in_specs=in_specs, out_specs=out_specs, check_vma=False)
```

```python
import functools

import jax
import jax.numpy as jnp
from jax import lax
from jax.experimental import pallas as pl
from jax.experimental.pallas import tpu as pltpu
from jax.sharding import PartitionSpec as P

EPSILON = 1e-06
INV_SQRT2 = 0.7071067811865476
INV_SQRT_PI = 0.5641895835477563
LOG2_E = 1.4426950408889634
F32 = jnp.float32
BF16 = jnp.bfloat16
TILE = 32
PAD = 8
COLS = 256
VMEM_LIMIT = 60 * 2**20
COST = pl.CostEstimate(flops=1, bytes_accessed=1, transcendentals=0)

CONV_B, GAIN, SHIFT, DOWN_B, SCALE, UP_B, VEC_ROWS = 7, 8, 9, 10, 11, 12, 16
XHAT, STREAM, NORMED, KINDS = 0, 1, 2, 3
LANES = 128
OFFSETS = (1, 2, 3, -1, -2, -3)
MASK_OF = {offset: k for k, offset in enumerate(OFFSETS)}


def slabs(width):
    return [slice(c, c + LANES) for c in range(0, width, LANES)]


def row_sum(parts):
    return jnp.sum(functools.reduce(jnp.add, parts), axis=1, keepdims=True)


def fold(value):
    return functools.reduce(jnp.add, [value[8 * i : 8 * i + 8] for i in range(value.shape[0] // 8)])


def clear_edges(padded, frames):
    for slab in range(padded.shape[0]):
        padded[slab, 0:PAD, :] = jnp.zeros((PAD, LANES), F32)
        padded[slab, PAD + frames : PAD + frames + PAD, :] = jnp.zeros((PAD, LANES), F32)


def build_masks(seg_v, masks):
    frames = masks.shape[1]
    seg_v[0:PAD, :] = jnp.full((PAD, LANES), -1.0, F32)
    seg_v[PAD + frames : PAD + frames + PAD, :] = jnp.full((PAD, LANES), -1.0, F32)

    def body(i, carry):
        base = pl.multiple_of(i * 64, 64)
        here = seg_v[pl.ds(base + PAD, 64), :]
        for k, offset in enumerate(OFFSETS):
            there = seg_v[pl.ds(base + PAD + offset, 64), :]
            masks[k, pl.ds(base, 64), :] = jnp.where(there == here, 1.0, 0.0)
        return carry

    lax.fori_loop(0, frames // 64, body, 0)


def start_weights(core, layer, own, peer, target, sem):
    @pl.when(core == lax.div(layer, 2))
    def _():
        pltpu.make_async_copy(own.at[lax.rem(layer, 2)], target, sem).start()

    @pl.when(core != lax.div(layer, 2))
    def _():
        pltpu.make_async_copy(peer.at[lax.rem(layer, 2)], target, sem).start()


def send_row(core, section, source, kept, other, sem):
    @pl.when(core == section)
    def _():
        pltpu.make_async_copy(source, kept, sem).start()

    @pl.when(core != section)
    def _():
        pltpu.make_async_copy(source, other, sem).start()


def forward_kernel(layers, aliased, flags, x_in, seg_hbm, vec, own_up, own_down, peer_up, peer_down, *rest):
    rest = rest[aliased:]
    hid, dge, saved, rst, kept, other, send = rest[:7]
    (up_v, down_v, hid_v, dge_v, saved_v, rst_v, stream, acc, out_v, x_v, seg_v, masks, w_sem, in_sem, o_sem, s_sem) = rest[7:]
    frames, width = acc.shape
    hidden = hid_v.shape[2]

    @pl.when(flags[0] == 1)
    def _():
        core, micro, row = flags[1], flags[2], flags[3]
        pltpu.make_async_copy(x_in, x_v, s_sem.at[2]).start()
        pltpu.make_async_copy(seg_hbm.at[micro], seg_v.at[pl.ds(PAD, frames)], in_sem).start()
        def fetch(j):
            start_weights(core, j, own_up, peer_up, up_v.at[j], w_sem.at[j, 0])
            start_weights(core, j, own_down, peer_down, down_v.at[j], w_sem.at[j, 1])

        fetch(0)
        clear_edges(stream, frames)
        pltpu.make_async_copy(seg_hbm.at[0], seg_v.at[pl.ds(PAD, frames)], in_sem).wait()
        build_masks(seg_v, masks)
        pltpu.make_async_copy(x_in, x_v, s_sem.at[2]).wait()
        for c, cols in enumerate(slabs(width)):
            stream[c, PAD : PAD + frames, :] = x_v[:, cols].astype(F32)

        def layer(j, carry):
            def conv_norm(i, c):
                base = pl.multiple_of(i * TILE, TILE)
                rows = pl.ds(base, TILE)
                parts = []
                for s, cols in enumerate(slabs(width)):
                    centre = stream[s, pl.ds(base + PAD, TILE), :]
                    saved_v[j, STREAM, rows, cols] = centre.astype(BF16)
                    total = vec[j, CONV_B : CONV_B + 1, cols] + vec[j, 3:4, cols] * centre
                    for offset in OFFSETS:
                        neighbour = stream[s, pl.ds(base + PAD + offset, TILE), :] * masks[MASK_OF[offset], rows, :]
                        total = total + vec[j, offset + 3 : offset + 4, cols] * neighbour
                    parts.append(total)
                mean = row_sum(parts) * (1.0 / width)
                parts = [part - mean for part in parts]
                rstd = lax.rsqrt(row_sum([part * part for part in parts]) * (1.0 / width) + EPSILON)
                for part, cols in zip(parts, slabs(width)):
                    xhat = part * rstd
                    saved_v[j, XHAT, rows, cols] = xhat.astype(BF16)
                    saved_v[j, NORMED, rows, cols] = (xhat * vec[j, GAIN : GAIN + 1, cols] + vec[j, SHIFT : SHIFT + 1, cols]).astype(BF16)
                rst_v[j, rows, :] = jnp.broadcast_to(rstd, (TILE, LANES))
                return c

            lax.fori_loop(0, frames // TILE, conv_norm, 0, unroll=8)
            pltpu.make_async_copy(saved_v.at[j], saved.at[row, j], o_sem.at[j, 3]).start()
            pltpu.make_async_copy(rst_v.at[j], rst.at[row, j], o_sem.at[j, 2]).start()
            pltpu.make_async_copy(own_up.at[0], up_v.at[j], w_sem.at[j, 0]).wait()

            @pl.when(j + 1 < layers)
            def _():
                fetch(j + 1)

            for n in range(hidden // COLS):
                cols = slice(n * COLS, (n + 1) * COLS)
                at, start = UP_B + n * COLS // width, (n * COLS) % width
                value = jnp.dot(saved_v[j, NORMED], up_v[j, :, cols], preferred_element_type=F32) + vec[j, at : at + 1, start : start + COLS]
                scaled = value * INV_SQRT2
                phi_sum = 0.5 + 0.5 * lax.erf(scaled)
                hid_v[j, :, cols] = (value * phi_sum).astype(BF16)
                dge_v[j, :, cols] = (phi_sum + scaled * INV_SQRT_PI * jnp.exp2(scaled * scaled * -LOG2_E)).astype(BF16)
            pltpu.make_async_copy(hid_v.at[j], hid.at[row, j], o_sem.at[j, 0]).start()
            pltpu.make_async_copy(dge_v.at[j], dge.at[row, j], o_sem.at[j, 1]).start()
            pltpu.make_async_copy(own_down.at[0], down_v.at[j], w_sem.at[j, 1]).wait()
            acc[...] = jnp.dot(hid_v[j], down_v[j], preferred_element_type=F32)

            def finish(ends_section, i, c):
                base = pl.multiple_of(i * TILE, TILE)
                rows = pl.ds(base, TILE)
                for s, cols in enumerate(slabs(width)):
                    inner = pl.ds(pl.multiple_of(base + PAD, 8), TILE)
                    branch = acc[rows, cols] + vec[j, DOWN_B : DOWN_B + 1, cols]
                    fresh = stream[s, inner, :] + vec[j, SCALE : SCALE + 1, cols] * branch
                    if ends_section:
                        rounded = fresh.astype(BF16)
                        out_v[lax.div(j, 2), rows, cols] = fresh
                        x_v[rows, cols] = rounded
                        fresh = rounded.astype(F32)
                    stream[s, inner, :] = fresh
                return c

            @pl.when(lax.rem(j, 2) == 1)
            def _():
                lax.fori_loop(0, frames // TILE, functools.partial(finish, True), 0)

            @pl.when(lax.rem(j, 2) == 0)
            def _():
                lax.fori_loop(0, frames // TILE, functools.partial(finish, False), 0)

            @pl.when(j == 1)
            def _():
                send_row(core, 0, out_v.at[0], kept.at[micro], other.at[row], s_sem.at[0])

            return carry

        lax.fori_loop(0, layers, layer, 0)
        send_row(core, 1, out_v.at[1], kept.at[micro], other.at[row], s_sem.at[1])
        pltpu.make_async_copy(x_v, send, s_sem.at[2]).start()
        for j in range(layers):
            pltpu.make_async_copy(hid_v.at[j], hid.at[row, j], o_sem.at[j, 0]).wait()
            pltpu.make_async_copy(dge_v.at[j], dge.at[row, j], o_sem.at[j, 1]).wait()
            pltpu.make_async_copy(rst_v.at[j], rst.at[row, j], o_sem.at[j, 2]).wait()
            pltpu.make_async_copy(saved_v.at[j], saved.at[row, j], o_sem.at[j, 3]).wait()
        pltpu.make_async_copy(out_v.at[0], other.at[row], s_sem.at[0]).wait()
        pltpu.make_async_copy(out_v.at[1], other.at[row], s_sem.at[1]).wait()
        pltpu.make_async_copy(x_v, send, s_sem.at[2]).wait()


SUMS, HEAD = 3, 2
DOWN, UP = 0, 1
VECTORS = 16


def send_sums(core, section, owners, kind, layer, source, vectors, targets, sem):
    kept, head, tail = targets
    shares, _, block, width = kept.shape
    size = (block - VECTORS) // 2
    first = 0 if kind == DOWN else size + VECTORS
    columns = source.shape[1] // width
    rows = size // columns
    for stop in range(shares):
        owner = owners[2 * kind + layer, stop]
        pieces = [
            (source.at[pl.ds(pl.multiple_of(owner * rows, 16), rows), pl.ds(b * width, width)], pl.ds(first + b * rows, rows))
            for b in range(columns)
        ]
        if vectors is not None:
            pieces.append((vectors.at[owners[2 * DOWN + layer, stop]], pl.ds(size, VECTORS)))
        for piece, place in pieces:

            @pl.when(core == section)
            def _():
                pltpu.make_async_copy(piece, kept.at[stop, layer, place], sem).start()

            @pl.when(core != section)
            def _():
                target = head.at[stop, layer] if stop < HEAD else tail.at[stop - HEAD, layer]
                pltpu.make_async_copy(piece, target.at[place], sem).start()


def pack_vectors(sums, packed):
    shares, _, width = packed.shape
    parts = [sums[r : r + 1, :] for r in range(UP_B, VEC_ROWS - 1)]
    wide = jnp.broadcast_to(jnp.concatenate(parts, axis=1), (8, width * len(parts)))
    size, wide_size = width // shares, width * len(parts) // shares
    is_bias = lax.broadcasted_iota(jnp.int32, (VECTORS, width), 0) == UP_B
    for d in range(shares):
        part = sums if d == 0 else pltpu.roll(sums, width - d * size, 1)
        bias = wide if d == 0 else pltpu.roll(wide, wide.shape[1] - d * wide_size, 1)
        packed[d] = jnp.where(is_bias, jnp.broadcast_to(bias[0:1, :width], (VECTORS, width)), part).astype(BF16)


def backward_kernel(final, aliased, ties, riders, flags, g_one, g_two, seg_hbm, vec, own_up, own_down, peer_up, peer_down, dge, saved, rst, *rest):
    if final:
        owners, hid, gb, gp, vec_in = rest[:5]
        rest = rest[5 + ties + aliased :]
        sums_out, (kept, other) = rest[:SUMS], rest[SUMS : SUMS + 2]
        rest = rest[SUMS + 2 :]
    else:
        rest = rest[aliased:]
        gb, gp, vec_out, kept, other, send = rest[:6]
        rest = rest[6 + riders :]
    (up_v, down_v, dge_v, saved_v, rst_v, gb_v, gp_v, vg_v, g_now, fresh_v, gn_v, padded, x_v, seg_v, masks, w_sem, in_sem, g_sem, o_sem, s_sem) = rest[:20]
    if final:
        (hid_v, nrm_v, dwd_v, dwu_v, early_v, packed, b_sem) = rest[20:]
    frames, width = g_now.shape
    held, _, hidden = dge_v.shape
    layers = vec.shape[0]
    nt = (((1,), (1,)), ((), ()))
    tn = (((0,), (0,)), ((), ()))
    tall = 2 * TILE
    cols_of = slabs(width)

    @pl.when(flags[0] == 1)
    def _():
        core, micro, row = flags[1], flags[2], flags[3]
        pltpu.make_async_copy(seg_hbm.at[micro], seg_v.at[pl.ds(PAD, frames)], in_sem).start()

        def fetch(j):
            h = lax.rem(j, held)
            start_weights(core, j, own_down, peer_down, down_v.at[h], w_sem.at[h, 1])
            pltpu.make_async_copy(dge.at[row, j], dge_v.at[h], w_sem.at[h, 3]).start()
            start_weights(core, j, own_up, peer_up, up_v.at[h], w_sem.at[h, 0])
            pltpu.make_async_copy(rst.at[row, j], rst_v.at[h], w_sem.at[h, 4]).start()
            pltpu.make_async_copy(saved.at[row, j, 0:2], saved_v.at[h], w_sem.at[h, 2]).start()

        if final:
            pltpu.make_async_copy(vec_in.at[1 - row], early_v, s_sem.at[2]).start()
        source = [pltpu.make_async_copy(g, x_v, g_sem) for g in (g_one, g_two)]
        for k in range(2):

            @pl.when(flags[4] == k)
            def _():
                source[k].start()

        fetch(layers - 1)
        clear_edges(padded, frames)
        source[0].wait()
        for cols in cols_of:

            def enter(t, c):
                rows = pl.ds(pl.multiple_of(t * tall, tall), tall)
                scaled = (vec[layers - 1, SCALE : SCALE + 1, cols] * x_v[rows, cols].astype(F32)).astype(BF16)
                gb_v[layers, 0, rows, cols] = scaled
                return c + fold(scaled.astype(F32))

            total = lax.fori_loop(0, frames // tall, enter, jnp.zeros((8, LANES), F32))
            vg_v[layers, DOWN_B : DOWN_B + 1, cols] = jnp.sum(total, axis=0, keepdims=True)
        pltpu.make_async_copy(seg_hbm.at[0], seg_v.at[pl.ds(PAD, frames)], in_sem).wait()
        build_masks(seg_v, masks)

        def layer(step, carry):
            j = layers - 1 - step
            h = lax.rem(j, held)
            if not final:
                pltpu.make_async_copy(gb_v.at[j + 1, 0], gb.at[row, j], o_sem.at[j, 0]).start()
            pltpu.make_async_copy(own_down.at[0], down_v.at[h], w_sem.at[h, 1]).wait()
            pltpu.make_async_copy(dge.at[0, 0], dge_v.at[h], w_sem.at[h, 3]).wait()
            if final:
                pltpu.make_async_copy(hid.at[row, j], hid_v.at[h, 0], b_sem.at[h, 0]).start()
                pltpu.make_async_copy(hid.at[1 - row, j], hid_v.at[h, 1], b_sem.at[h, 1]).start()
                pltpu.make_async_copy(gb.at[1 - row, j], gb_v.at[j + 1, 1], b_sem.at[h, 4]).start()
                pltpu.make_async_copy(saved.at[row, j, NORMED], nrm_v.at[h, 0], b_sem.at[h, 2]).start()
                pltpu.make_async_copy(saved.at[1 - row, j, NORMED], nrm_v.at[h, 1], b_sem.at[h, 3]).start()
                pltpu.make_async_copy(gp.at[1 - row, j], gp_v.at[h, 1], b_sem.at[h, 5]).start()
            for n in range(hidden // COLS):
                cols = slice(n * COLS, (n + 1) * COLS)
                value = lax.dot_general(gb_v[j + 1, 0], down_v[h, cols, :], nt, preferred_element_type=F32)
                rounded = (value * dge_v[h, :, cols].astype(F32)).astype(BF16)
                gp_v[h, 0, :, cols] = rounded
                at, start = UP_B + n * COLS // width, (n * COLS) % width
                vg_v[j + 1, at : at + 1, start : start + COLS] = jnp.sum(rounded.astype(F32), axis=0, keepdims=True)
            if not final:
                pltpu.make_async_copy(gp_v.at[h, 0], gp.at[row, j], o_sem.at[j, 1]).start()
            pltpu.make_async_copy(own_up.at[0], up_v.at[h], w_sem.at[h, 0]).wait()
            gn_v[...] = lax.dot_general(gp_v[h, 0], up_v[h], nt, preferred_element_type=F32)
            pltpu.make_async_copy(rst.at[0, 0], rst_v.at[h], w_sem.at[h, 4]).wait()
            pltpu.make_async_copy(saved.at[0, 0, 0:2], saved_v.at[h], w_sem.at[h, 2]).wait()

            @pl.when(j > 0)
            def _():
                fetch(j - 1)

            if final:
                pltpu.make_async_copy(hid.at[0, 0], hid_v.at[h, 0], b_sem.at[h, 0]).wait()
                pltpu.make_async_copy(hid.at[0, 0], hid_v.at[h, 1], b_sem.at[h, 1]).wait()
                pltpu.make_async_copy(gb.at[0, 0], gb_v.at[j + 1, 1], b_sem.at[h, 4]).wait()

                @pl.when(j + held < layers)
                def _():
                    pltpu.make_async_copy(dwd_v.at[h], dwd_v.at[h], o_sem.at[h, 0]).wait()
                    pltpu.make_async_copy(dwu_v.at[h], dwu_v.at[h], o_sem.at[h, 1]).wait()
                    pltpu.make_async_copy(packed.at[h], packed.at[h], o_sem.at[h, 1]).wait()

            def down_chunk(n):
                rows = slice(n * COLS, (n + 1) * COLS)
                left = hid_v[h, :, :, rows].reshape(2 * frames, COLS)
                right = gb_v[j + 1].reshape(2 * frames, width)
                value = lax.dot_general(left, right, tn, preferred_element_type=F32)
                dwd_v[h, rows, :] = value.astype(BF16)
                return fold(value * down_v[h, rows, :].astype(F32))

            def up_chunk(m, n):
                rows = slice(m * COLS, (m + 1) * COLS)
                cols = slice(n * width, (n + 1) * width)
                left = nrm_v[h, :, :, rows].reshape(2 * frames, COLS)
                right = gp_v[h, :, :, cols].reshape(2 * frames, width)
                dwu_v[h, rows, cols] = lax.dot_general(left, right, tn, preferred_element_type=F32).astype(BF16)

            odd = lax.rem(j, 2) == 1

            def norm_back(t, c):
                base = t * TILE if isinstance(t, int) else pl.multiple_of(t * TILE, TILE)
                rows = pl.ds(base, TILE)
                inner = pl.ds(base + PAD if isinstance(t, int) else pl.multiple_of(base + PAD, 8), TILE)
                grads = [gn_v[rows, cols] for cols in cols_of]
                xhats = [saved_v[h, XHAT, rows, cols].astype(F32) for cols in cols_of]
                qs = [grad * vec[j, GAIN : GAIN + 1, cols] for grad, cols in zip(grads, cols_of)]
                mean_q = row_sum(qs) * (1.0 / width)
                mean_qx = row_sum([q * xhat for q, xhat in zip(qs, xhats)]) * (1.0 / width)
                rstd = rst_v[h, rows, :]
                out = []
                for s, cols in enumerate(cols_of):
                    grad_conv = rstd * (qs[s] - mean_q - xhats[s] * mean_qx)
                    padded[s, inner, :] = grad_conv
                    g_now[rows, cols] = jnp.where(odd, x_v[rows, cols].astype(F32), fresh_v[rows, cols])
                    out += [c[3 * s] + fold(grads[s] * xhats[s]), c[3 * s + 1] + fold(grads[s]), c[3 * s + 2] + fold(grad_conv)]
                return tuple(out)

            sums = (jnp.zeros((8, LANES), F32),) * (3 * len(cols_of))
            tiles = frames // TILE
            if final:
                parts = hidden // COLS
                scale = jnp.zeros((8, width), F32)
                done = 0
                for n in range(parts):
                    scale = scale + down_chunk(n)
                    while done < tiles * (n + 1) // parts:
                        sums = norm_back(done, sums)
                        done += 1
                vg_v[j + 1, SCALE : SCALE + 1, :] = jnp.sum(scale, axis=0, keepdims=True)
                send_sums(core, lax.div(j, 2), owners, DOWN, lax.rem(j, 2), dwd_v.at[h], None, sums_out, o_sem.at[h, 0])
                pltpu.make_async_copy(saved.at[0, 0, 0], nrm_v.at[h, 0], b_sem.at[h, 2]).wait()
                pltpu.make_async_copy(saved.at[0, 0, 0], nrm_v.at[h, 1], b_sem.at[h, 3]).wait()
                pltpu.make_async_copy(gp.at[0, 0], gp_v.at[h, 1], b_sem.at[h, 5]).wait()
            else:
                sums = lax.fori_loop(0, tiles, norm_back, sums, unroll=8)
            for s, cols in enumerate(cols_of):
                for k, at in enumerate((GAIN, SHIFT, CONV_B)):
                    vg_v[j + 1, at : at + 1, cols] = jnp.sum(sums[3 * s + k], axis=0, keepdims=True)

            @pl.when(odd & (step > 0))
            def _():
                pltpu.make_async_copy(fresh_v, other.at[row], s_sem.at[0]).wait()

            below = lax.max(j - 1, 0)
            for s, cols in enumerate(cols_of):

                def conv_back(t, c):
                    base = t * tall if isinstance(t, int) else pl.multiple_of(t * tall, tall)
                    rows = pl.ds(base, tall)
                    source = saved_v[h, STREAM, rows, cols].astype(F32)
                    centre = padded[s, pl.ds(base + PAD if isinstance(t, int) else pl.multiple_of(base + PAD, 8), tall), :]
                    total = g_now[rows, cols] + vec[j, 3:4, cols] * centre
                    taps = [None] * 7
                    taps[3] = c[3] + fold(centre * source)
                    for offset in OFFSETS:
                        term = padded[s, pl.ds(base + PAD - offset, tall), :] * masks[MASK_OF[-offset], rows, :]
                        total = total + vec[j, offset + 3 : offset + 4, cols] * term
                        taps[offset + 3] = c[offset + 3] + fold(term * source)
                    rounded = total.astype(BF16)
                    fresh_v[rows, cols] = total
                    x_v[rows, cols] = rounded
                    scaled = (vec[below, SCALE : SCALE + 1, cols] * jnp.where(odd, total, rounded.astype(F32))).astype(BF16)
                    gb_v[j, 0, rows, cols] = scaled
                    return tuple(taps) + (c[7] + fold(scaled.astype(F32)),)

                sums = (jnp.zeros((8, LANES), F32),) * 8
                if final:
                    chunks = [(m, n) for m in range(width // COLS) for n in range(hidden // width)]
                    each = -(-len(chunks) // len(cols_of))
                    mine = chunks[s * each : (s + 1) * each]
                    done = 0
                    for k, (m, n) in enumerate(mine):
                        up_chunk(m, n)
                        while done < frames // tall * (k + 1) // len(mine):
                            sums = conv_back(done, sums)
                            done += 1
                    while done < frames // tall:
                        sums = conv_back(done, sums)
                        done += 1
                else:
                    sums = lax.fori_loop(0, frames // tall, conv_back, sums, unroll=8)
                for k in range(7):
                    vg_v[j + 1, k : k + 1, cols] = jnp.sum(sums[k], axis=0, keepdims=True)
                vg_v[j, DOWN_B : DOWN_B + 1, cols] = jnp.sum(sums[7], axis=0, keepdims=True)
            if final:

                @pl.when(step == 0)
                def _():
                    pltpu.make_async_copy(vec_in.at[0], early_v, s_sem.at[2]).wait()

                pack_vectors(vg_v[j + 1] + early_v[j], packed.at[h])
                send_vectors = packed.at[h]
                send_sums(core, lax.div(j, 2), owners, UP, lax.rem(j, 2), dwu_v.at[h], send_vectors, sums_out, o_sem.at[h, 1])

            @pl.when(jnp.logical_not(odd))
            def _():
                send_row(core, lax.div(j, 2), fresh_v, kept.at[micro], other.at[row], s_sem.at[0])

            return carry

        for i in range(1, layers + 1):
            vg_v[i, SCALE : SCALE + 1, :] = jnp.zeros((1, width), F32)
            vg_v[i, VEC_ROWS - 1 : VEC_ROWS, :] = jnp.zeros((1, width), F32)
        lax.fori_loop(0, layers, layer, 0)
        if final:
            for h in range(held):
                pltpu.make_async_copy(dwd_v.at[h], dwd_v.at[h], o_sem.at[h, 0]).wait()
                pltpu.make_async_copy(dwu_v.at[h], dwu_v.at[h], o_sem.at[h, 1]).wait()
                pltpu.make_async_copy(packed.at[h], packed.at[h], o_sem.at[h, 1]).wait()
        else:
            pltpu.make_async_copy(vg_v.at[pl.ds(1, layers)], vec_out.at[row], s_sem.at[2]).start()
            pltpu.make_async_copy(x_v, send, s_sem.at[1]).start()
            for j in range(layers):
                pltpu.make_async_copy(gb_v.at[j + 1, 0], gb.at[row, j], o_sem.at[j, 0]).wait()
                pltpu.make_async_copy(gp_v.at[j, 0], gp.at[row, j], o_sem.at[j, 1]).wait()
            pltpu.make_async_copy(x_v, send, s_sem.at[1]).wait()
            pltpu.make_async_copy(vg_v.at[pl.ds(1, layers)], vec_out.at[row], s_sem.at[2]).wait()
        pltpu.make_async_copy(fresh_v, other.at[row], s_sem.at[0]).wait()


def weight_kernel(ties, flags, owners, own_down, peer_down, all_hid, all_gb, all_saved, all_gp, vec_in, *rest):
    rest = rest[ties:]
    sums_out, rest = rest[:SUMS], rest[SUMS:]
    hid_v, gb_v, nrm_v, gp_v, down_v, dwd_v, dwu_v, vec_v, packed, sem, o_sem, s_sem = rest
    frames, width = gb_v.shape[2:]
    hidden = hid_v.shape[3]
    layers = all_hid.shape[1]
    tn = (((0,), (0,)), ((), ()))

    @pl.when(flags[0] == 1)
    def _():
        core = flags[1]

        def copies(j, h):
            pairs = []
            for row in range(2):
                pairs += [
                    (all_hid.at[row, j], hid_v.at[h, row]),
                    (all_gb.at[row, j], gb_v.at[h, row]),
                    (all_saved.at[row, j, NORMED], nrm_v.at[h, row]),
                    (all_gp.at[row, j], gp_v.at[h, row]),
                ]
            return [pltpu.make_async_copy(a, b, sem.at[h, k]) for k, (a, b) in enumerate(pairs)]

        def fetch(j):
            h = lax.rem(j, 2)
            start_weights(core, j, own_down, peer_down, down_v.at[h], sem.at[h, 8])
            for copy in copies(j, h):
                copy.start()

        fetch(layers - 1)
        pltpu.make_async_copy(vec_in, vec_v, s_sem).start()
        pltpu.make_async_copy(vec_in, vec_v, s_sem).wait()

        def layer(step, carry):
            j = layers - 1 - step
            h = lax.rem(j, 2)

            @pl.when(j > 0)
            def _():
                fetch(j - 1)

            pltpu.make_async_copy(own_down.at[0], down_v.at[h], sem.at[h, 8]).wait()
            for copy in copies(j, h):
                copy.wait()

            @pl.when(j + 2 < layers)
            def _():
                pltpu.make_async_copy(dwd_v.at[h], dwd_v.at[h], o_sem.at[h, 0]).wait()
                pltpu.make_async_copy(dwu_v.at[h], dwu_v.at[h], o_sem.at[h, 1]).wait()
                pltpu.make_async_copy(packed.at[h], packed.at[h], o_sem.at[h, 1]).wait()

            def down_chunk(n, scale):
                rows = pl.ds(pl.multiple_of(n * COLS, COLS), COLS)
                left = hid_v[h, :, :, rows].reshape(2 * frames, COLS)
                value = lax.dot_general(left, gb_v[h].reshape(2 * frames, width), tn, preferred_element_type=F32)
                dwd_v[h, rows, :] = value.astype(BF16)
                return scale + fold(value * down_v[h, rows, :].astype(F32))

            scale = lax.fori_loop(0, hidden // COLS, down_chunk, jnp.zeros((8, width), F32))
            scale = jnp.sum(scale, axis=0, keepdims=True)
            vectors = vec_v[0, j] + vec_v[1, j]
            is_scale = lax.broadcasted_iota(jnp.int32, vectors.shape, 0) == SCALE
            pack_vectors(jnp.where(is_scale, jnp.broadcast_to(scale, vectors.shape), vectors), packed.at[h])
            send_sums(core, lax.div(j, 2), owners, DOWN, lax.rem(j, 2), dwd_v.at[h], None, sums_out, o_sem.at[h, 0])

            def up_chunk(n, c):
                cols = pl.ds(pl.multiple_of(n * width, width), width)
                right = gp_v[h, :, :, cols].reshape(2 * frames, width)
                value = lax.dot_general(nrm_v[h].reshape(2 * frames, width), right, tn, preferred_element_type=F32)
                dwu_v[h, :, cols] = value.astype(BF16)
                return c

            lax.fori_loop(0, hidden // width, up_chunk, 0)
            send_sums(core, lax.div(j, 2), owners, UP, lax.rem(j, 2), dwu_v.at[h], packed.at[h], sums_out, o_sem.at[h, 1])
            return carry

        lax.fori_loop(0, layers, layer, 0)
        for h in range(2):
            pltpu.make_async_copy(dwd_v.at[h], dwd_v.at[h], o_sem.at[h, 0]).wait()
            pltpu.make_async_copy(dwu_v.at[h], dwu_v.at[h], o_sem.at[h, 1]).wait()
            pltpu.make_async_copy(packed.at[h], packed.at[h], o_sem.at[h, 1]).wait()


def place_kernel(at, kept_in, rows, tie, kept, held, sem):
    count = rows.shape[0]
    for i in range(count):
        pltpu.make_async_copy(rows.at[i], held.at[i], sem.at[i]).start()
    for i in range(count):
        pltpu.make_async_copy(rows.at[i], held.at[i], sem.at[i]).wait()
        pltpu.make_async_copy(held.at[i], kept.at[at[0] + i], sem.at[i]).start()
    for i in range(count):
        pltpu.make_async_copy(held.at[i], kept.at[at[0] + i], sem.at[i]).wait()


def hold_kernel(value_in, tie, value):
    pass


def final_kernel(down_0, down_1, up_0, up_1, kept, other, scales, *rest):
    conv_out, conv_b_out, gain_out, shift_out, up_out, up_b_out, down_out, down_b_out, scale_out = rest
    size, wide = conv_b_out.shape[1], up_b_out.shape[1]
    rows, width = down_out.shape[1:]
    for layer, (down, up) in enumerate(((down_0, up_0), (down_1, up_1))):
        total = down[...].astype(F32) + kept[layer, : rows + VECTORS].astype(F32) + other[layer, : rows + VECTORS].astype(F32)
        down_out[layer] = total[:rows]
        vectors = total[rows:]
        at = slice(layer, layer + 1)
        conv_out[layer] = vectors[:CONV_B, :size]
        conv_b_out[at, :] = vectors[CONV_B : CONV_B + 1, :size]
        gain_out[at, :] = vectors[GAIN : GAIN + 1, :size]
        shift_out[at, :] = vectors[SHIFT : SHIFT + 1, :size]
        down_b = vectors[DOWN_B : DOWN_B + 1, :size]
        down_b_out[at, :] = down_b
        scale_out[at, :] = (vectors[SCALE : SCALE + 1, :size] + scales[0, at, :] * down_b) / scales[1, at, :]
        up_b_out[at, :] = vectors[UP_B : UP_B + 1, :wide]
        total = up[...].astype(F32) + kept[layer, rows + VECTORS :].astype(F32) + other[layer, rows + VECTORS :].astype(F32)
        for b in range(up_out.shape[2] // width):
            up_out[layer, :, b * width : (b + 1) * width] = total[b * size : (b + 1) * size]


ANY = pl.BlockSpec(memory_space=pl.ANY)
SMEM = pl.BlockSpec(memory_space=pltpu.SMEM)
VMEM = pl.BlockSpec(memory_space=pltpu.VMEM)


def run_forward(flags, x, seg, vec, weights, earlier):
    layers = vec.shape[0]
    micro = seg.shape[0]
    frames, width = x.shape
    hidden = weights[0].shape[2]
    shapes = (
        jax.ShapeDtypeStruct((2, layers, frames, hidden), BF16),
        jax.ShapeDtypeStruct((2, layers, frames, hidden), BF16),
        jax.ShapeDtypeStruct((2, layers, KINDS, frames, width), BF16),
        jax.ShapeDtypeStruct((2, layers, frames, LANES), F32),
        jax.ShapeDtypeStruct((micro, frames, width), F32),
        jax.ShapeDtypeStruct((2, frames, width), F32),
        jax.ShapeDtypeStruct((frames, width), BF16),
    )
    aliased = len(earlier)
    return pl.pallas_call(
        functools.partial(forward_kernel, layers, aliased),
        out_shape=shapes,
        in_specs=[SMEM, ANY, ANY, VMEM] + [ANY] * (4 + aliased),
        out_specs=(ANY,) * len(shapes),
        input_output_aliases={8 + i: i for i in range(aliased)},
        scratch_shapes=[
            pltpu.VMEM((layers, width, hidden), BF16),
            pltpu.VMEM((layers, hidden, width), BF16),
            pltpu.VMEM((layers, frames, hidden), BF16),
            pltpu.VMEM((layers, frames, hidden), BF16),
            pltpu.VMEM((layers, KINDS, frames, width), BF16),
            pltpu.VMEM((layers, frames, LANES), F32),
            pltpu.VMEM((width // LANES, frames + 2 * PAD, LANES), F32),
            pltpu.VMEM((frames, width), F32),
            pltpu.VMEM((2, frames, width), F32),
            pltpu.VMEM((frames, width), BF16),
            pltpu.VMEM((frames + 2 * PAD, LANES), F32),
            pltpu.VMEM((6, frames, LANES), F32),
            pltpu.SemaphoreType.DMA((layers, 2)),
            pltpu.SemaphoreType.DMA,
            pltpu.SemaphoreType.DMA((layers, 4)),
            pltpu.SemaphoreType.DMA((3,)),
        ],
        compiler_params=pltpu.CompilerParams(vmem_limit_bytes=VMEM_LIMIT),
        cost_estimate=COST,
    )(flags, x, seg, vec, *weights, *earlier)


def sum_shapes(shares, hidden, width):
    block = (2, 2 * (hidden // shares) + VECTORS, width)
    return tuple(jax.ShapeDtypeStruct((count, *block), BF16) for count in (shares, HEAD, shares - HEAD))


def run_backward(flags, g, seg, vec, weights, state, earlier, final=(), ties=(), riders=()):
    frames, width = g[0].shape
    hidden = weights[0].shape[2]
    layers, micro = vec.shape[0], seg.shape[0]
    rows, held = (2, 2) if final else (1, layers)
    grads = (
        jax.ShapeDtypeStruct((micro, frames, width), F32),
        jax.ShapeDtypeStruct((2, frames, width), F32),
    )
    if final:
        shapes = (*sum_shapes(final[0].shape[1], hidden, width), *grads)
    else:
        shapes = (
            jax.ShapeDtypeStruct((2, layers, frames, width), BF16),
            jax.ShapeDtypeStruct((2, layers, frames, hidden), BF16),
            jax.ShapeDtypeStruct((2, layers, VEC_ROWS, width), F32),
            *grads,
            jax.ShapeDtypeStruct((frames, width), BF16),
        )
    earlier = (*earlier, *riders)
    shapes = (*shapes, *(jax.ShapeDtypeStruct(rider.shape, rider.dtype) for rider in riders))
    aliased = len(earlier)
    targets = [*range(len(earlier) - len(riders)), *range(len(shapes) - len(riders), len(shapes))]
    scratch = [
        pltpu.VMEM((held, width, hidden), BF16),
        pltpu.VMEM((held, hidden, width), BF16),
        pltpu.VMEM((held, frames, hidden), BF16),
        pltpu.VMEM((held, 2, frames, width), BF16),
        pltpu.VMEM((held, frames, LANES), F32),
        pltpu.VMEM((layers + 1, rows, frames, width), BF16),
        pltpu.VMEM((held, rows, frames, hidden), BF16),
        pltpu.VMEM((layers + 1, VEC_ROWS, width), F32),
        pltpu.VMEM((frames, width), F32),
        pltpu.VMEM((frames, width), F32),
        pltpu.VMEM((frames, width), F32),
        pltpu.VMEM((width // LANES, frames + 2 * PAD, LANES), F32),
        pltpu.VMEM((frames, width), BF16),
        pltpu.VMEM((frames + 2 * PAD, LANES), F32),
        pltpu.VMEM((6, frames, LANES), F32),
        pltpu.SemaphoreType.DMA((held, 5)),
        pltpu.SemaphoreType.DMA,
        pltpu.SemaphoreType.DMA,
        pltpu.SemaphoreType.DMA((held, 2)),
        pltpu.SemaphoreType.DMA((3,)),
    ]
    if final:
        scratch += [
            pltpu.VMEM((held, 2, frames, hidden), BF16),
            pltpu.VMEM((held, 2, frames, width), BF16),
            pltpu.VMEM((held, hidden, width), BF16),
            pltpu.VMEM((held, width, hidden), BF16),
            pltpu.VMEM((layers, VEC_ROWS, width), F32),
            pltpu.VMEM((held, final[0].shape[1], VECTORS, width), BF16),
            pltpu.SemaphoreType.DMA((held, 6)),
        ]
    first_alias = 12 + len(final) + len(ties)
    return pl.pallas_call(
        functools.partial(backward_kernel, bool(final), aliased, len(ties), len(riders)),
        out_shape=shapes,
        in_specs=[SMEM, ANY, ANY, ANY, VMEM] + [ANY] * 7 + ([SMEM] + [ANY] * 4 if final else []) + [ANY] * (len(ties) + aliased),
        out_specs=(ANY,) * len(shapes),
        input_output_aliases={first_alias + i: target for i, target in enumerate(targets)},
        scratch_shapes=scratch,
        compiler_params=pltpu.CompilerParams(vmem_limit_bytes=VMEM_LIMIT),
        cost_estimate=COST,
    )(flags, *g, seg, vec, *weights, *state, *final, *ties, *earlier)


def run_weights(flags, owners, weights, hid, gb, saved, gp, vectors, ties):
    _, layers, frames, hidden = hid.shape
    width = gb.shape[3]
    shares = owners.shape[1]
    return pl.pallas_call(
        functools.partial(weight_kernel, len(ties)),
        out_shape=sum_shapes(shares, hidden, width),
        in_specs=[SMEM, SMEM] + [ANY] * (7 + len(ties)),
        out_specs=(ANY,) * SUMS,
        scratch_shapes=[
            pltpu.VMEM((2, 2, frames, hidden), BF16),
            pltpu.VMEM((2, 2, frames, width), BF16),
            pltpu.VMEM((2, 2, frames, width), BF16),
            pltpu.VMEM((2, 2, frames, hidden), BF16),
            pltpu.VMEM((2, hidden, width), BF16),
            pltpu.VMEM((2, hidden, width), BF16),
            pltpu.VMEM((2, width, hidden), BF16),
            pltpu.VMEM(vectors.shape, F32),
            pltpu.VMEM((2, shares, VECTORS, width), BF16),
            pltpu.SemaphoreType.DMA((2, 9)),
            pltpu.SemaphoreType.DMA((2, 2)),
            pltpu.SemaphoreType.DMA,
        ],
        compiler_params=pltpu.CompilerParams(vmem_limit_bytes=VMEM_LIMIT),
        cost_estimate=COST,
    )(flags, owners, weights[1], weights[3], hid, gb, saved, gp, vectors, *ties)


def run_place(kept, rows, at, tie):
    return pl.pallas_call(
        place_kernel,
        out_shape=jax.ShapeDtypeStruct(kept.shape, kept.dtype),
        in_specs=[SMEM, ANY, ANY, ANY],
        out_specs=ANY,
        input_output_aliases={1: 0},
        scratch_shapes=[pltpu.VMEM(rows.shape, rows.dtype), pltpu.SemaphoreType.DMA(rows.shape[:1])],
        cost_estimate=COST,
    )(at.reshape(1).astype(jnp.int32), kept, rows, tie)


def hold(value, tie):
    return pl.pallas_call(
        hold_kernel,
        out_shape=jax.ShapeDtypeStruct(value.shape, value.dtype),
        in_specs=[ANY, ANY],
        out_specs=ANY,
        input_output_aliases={0: 0},
        cost_estimate=COST,
    )(value, tie)


def run_final(down, up, kept, other, scales, shares, hidden):
    width = kept.shape[2]
    size, wide = width // shares, hidden // shares
    shapes = ((2, CONV_B, size), (2, size), (2, size), (2, size), (2, size, hidden), (2, wide), (2, wide, width), (2, size), (2, size))
    return pl.pallas_call(
        final_kernel,
        out_shape=tuple(jax.ShapeDtypeStruct(shape, F32) for shape in shapes),
        in_specs=[VMEM] * 7,
        out_specs=(VMEM,) * len(shapes),
        compiler_params=pltpu.CompilerParams(vmem_limit_bytes=VMEM_LIMIT // 2),
        cost_estimate=COST,
    )(*down, *up, kept, other, scales)


def ring_order(count):
    return list(range(0, count, 2)) + list(range(count - 1, 0, -2))


def ring_owners(ways, axis):
    count = lax.axis_size(axis)
    device = lax.axis_index(axis)
    mine = jnp.where(device % 2 == 0, device // 2, count - 1 - device // 2)
    places = jnp.stack([lax.rem(mine - way * (1 + jnp.arange(count, dtype=jnp.int32)) + 2 * count, count) for way in ways])
    return jnp.where(places < count - count // 2, 2 * places, 2 * (count - places) - 1)


def after(value, earlier):
    return lax.optimization_barrier((value, earlier))[0]


def ring_step(flows, ways, axis):
    count = lax.axis_size(axis)
    order = ring_order(count)
    return [
        lax.ppermute(value, axis, [(order[p], order[(p + way) % count]) for p in range(count)]) for value, way in zip(flows, ways)
    ]


def per_device(
    inputs,
    segment_ids,
    cotangent,
    conv_weight,
    conv_bias,
    norm_gain,
    norm_bias,
    up_weight,
    up_bias,
    down_weight,
    down_bias,
    layer_scale,
):
    micro, _, frames, width = inputs.shape
    hidden = up_weight.shape[2]
    shares = lax.axis_size("dp")
    section = lax.axis_index("section")
    chip, core = section // 2, section % 2
    exchange = [(0, 1), (1, 0), (2, 3), (3, 2)]

    small = jnp.concatenate(
        [
            conv_weight,
            conv_bias[:, None],
            norm_gain[:, None],
            norm_bias[:, None],
            down_bias[:, None],
            layer_scale[:, None],
            up_bias.reshape(2, -1, width),
            jnp.zeros((2, 1, width), BF16),
        ],
        axis=1,
    )
    small_peer = lax.ppermute(small, "section", exchange)
    up_peer = lax.ppermute(up_weight, "section", exchange)
    down_peer = lax.ppermute(down_weight, "section", exchange)
    vec = jnp.where(core == 0, jnp.concatenate([small, small_peer]), jnp.concatenate([small_peer, small])).astype(F32)
    weights = (up_weight, down_weight, up_peer, down_peer)
    masks = jnp.broadcast_to(segment_ids[:, 0, :, None].astype(F32), (micro, frames, LANES))
    inputs, cotangent = inputs[:, 0], cotangent[:, 0]

    def flags(active, row, choice=0):
        return jnp.stack([jnp.asarray(v, jnp.int32) for v in (active, core, 2 * core + row, row, choice)])

    first, last = chip == 0, chip == 1
    ways = ((1, -1), (-1, 1))
    owners = ring_owners([way for kind in ways for way in kind], "dp")

    def row_of(array, row):
        return lax.dynamic_index_in_dim(array, 2 * core + row, 0, keepdims=False)

    down_pairs, up_pairs = [(0, 2), (1, 3)], [(2, 0), (3, 1)]
    state = run_forward(flags(first, 0), row_of(inputs, 0), masks, vec, weights, ())
    arrived = lax.ppermute(state[6], "section", down_pairs)
    state = run_forward(flags(first, 1), row_of(inputs, 1), masks, vec, weights, state[:6])
    arrived_next = lax.ppermute(state[6], "section", down_pairs)
    state = run_forward(flags(last, 0), arrived, masks, vec, weights, state[:6])
    gradient = row_of(cotangent, 0)
    back = run_backward(flags(last, 0), (gradient, gradient), masks, vec, weights, state[1:4], ())
    returned = lax.ppermute(back[5], "section", up_pairs)
    state = run_forward(flags(last, 1), arrived_next, masks, vec, weights, state[:6])
    gradients = (row_of(cotangent, 1), returned)
    back = run_backward(flags(True, jnp.where(last, 1, 0), first), gradients, masks, vec, weights, state[1:4], back[:5], riders=state[4:6])
    returned = lax.ppermute(back[5], "section", up_pairs)
    gb, gp, vectors, grads_kept, grads_other, _, outputs_kept, outputs_other = back

    def assemble(mine, other, tie):
        return run_place(mine, lax.ppermute(other, "section", exchange), 2 * (1 - core), tie)[None, :, None]

    section_outputs = assemble(outputs_kept, outputs_other, vectors)
    sums = run_weights(flags(last, 0), owners, weights, state[0], gb, state[2], gp, vectors, (returned, section_outputs))
    shard = lax.axis_index("dp")
    scales = jnp.stack([down_bias, layer_scale]).astype(F32)
    scales = lax.dynamic_slice_in_dim(scales, shard * (width // shares), width // shares, 2)
    *sums, grads_kept, grads_other = run_backward(
        flags(first, 1),
        (returned, returned),
        masks,
        vec,
        weights,
        state[1:4],
        (*sums, grads_kept, grads_other),
        (owners, state[0], gb, gp, vectors),
        (scales,),
    )

    kept, head, tail = sums
    head = lax.ppermute(head, "section", exchange)
    tail = lax.ppermute(hold(tail, head), "section", exchange)
    size = hidden // shares
    spans = (slice(0, size + VECTORS), slice(size + VECTORS, None))

    def addend(stop, kind, layer):
        other = head[stop, layer, spans[kind]] if stop < HEAD else tail[stop - HEAD, layer, spans[kind]]
        return kept[stop, layer, spans[kind]].astype(F32) + other.astype(F32)

    flows = [[addend(0, kind, layer).astype(BF16) for layer in range(2)] for kind in (DOWN, UP)]
    for stop in range(1, shares):
        for kind in (DOWN, UP):
            moved = ring_step(flows[kind], ways[kind], "dp")
            if kind == DOWN or stop > 1:
                moved = after(moved, flows[1 - kind])
            if stop < shares - 1:
                moved = [(value.astype(F32) + addend(stop, kind, layer)).astype(BF16) for layer, value in enumerate(moved)]
            flows[kind] = moved
        if stop == 3:
            input_grads = assemble(grads_kept, grads_other, flows[UP][0])
    grads = run_final(flows[DOWN], flows[UP], kept[-1], tail[-1], scales, shares, hidden)
    return (section_outputs, input_grads, *grads)


def solution(mesh):
    in_specs = (
        P(None, "dp", None, None),
        P(None, "dp", None),
        P(None, "dp", None, None),
        P("section", None, None),
        P("section", None),
        P("section", None),
        P("section", None),
        P("section", None, None),
        P("section", None),
        P("section", None, None),
        P("section", None),
        P("section", None),
    )
    out_specs = (
        P("section", None, "dp", None, None),
        P("section", None, "dp", None, None),
        P("section", None, "dp"),
        P("section", "dp"),
        P("section", "dp"),
        P("section", "dp"),
        P("section", "dp", None),
        P("section", "dp"),
        P("section", "dp", None),
        P("section", "dp"),
        P("section", "dp"),
    )
    return jax.shard_map(per_device, mesh=mesh, in_specs=in_specs, out_specs=out_specs, check_vma=False)
```

```python
import functools

import jax
import jax.numpy as jnp
from jax import lax
from jax.experimental import pallas as pl
from jax.experimental.pallas import tpu as pltpu
from jax.sharding import PartitionSpec as P

EPSILON = 1e-06
INV_SQRT2 = 0.7071067811865476
INV_SQRT_PI = 0.5641895835477563
LOG2_E = 1.4426950408889634
F32 = jnp.float32
BF16 = jnp.bfloat16
TILE = 32
PAD = 8
COLS = 256
VMEM_LIMIT = 60 * 2**20
COST = pl.CostEstimate(flops=1, bytes_accessed=1, transcendentals=0)

CONV_B, GAIN, SHIFT, DOWN_B, SCALE, UP_B, VEC_ROWS = 7, 8, 9, 10, 11, 12, 16
XHAT, STREAM, NORMED, KINDS = 0, 1, 2, 3
LANES = 128
OFFSETS = (1, 2, 3, -1, -2, -3)
MASK_OF = {offset: k for k, offset in enumerate(OFFSETS)}


def slabs(width):
    return [slice(c, c + LANES) for c in range(0, width, LANES)]


def row_sum(parts):
    return jnp.sum(functools.reduce(jnp.add, parts), axis=1, keepdims=True)


def fold(value):
    return functools.reduce(jnp.add, [value[8 * i : 8 * i + 8] for i in range(value.shape[0] // 8)])


def clear_edges(padded, frames):
    for slab in range(padded.shape[0]):
        padded[slab, 0:PAD, :] = jnp.zeros((PAD, LANES), F32)
        padded[slab, PAD + frames : PAD + frames + PAD, :] = jnp.zeros((PAD, LANES), F32)


def build_masks(seg_v, masks):
    frames = masks.shape[1]
    seg_v[0:PAD, :] = jnp.full((PAD, LANES), -1.0, F32)
    seg_v[PAD + frames : PAD + frames + PAD, :] = jnp.full((PAD, LANES), -1.0, F32)

    def body(i, carry):
        base = pl.multiple_of(i * 64, 64)
        here = seg_v[pl.ds(base + PAD, 64), :]
        for k, offset in enumerate(OFFSETS):
            there = seg_v[pl.ds(base + PAD + offset, 64), :]
            masks[k, pl.ds(base, 64), :] = jnp.where(there == here, 1.0, 0.0)
        return carry

    lax.fori_loop(0, frames // 64, body, 0)


def start_weights(core, layer, own, peer, target, sem):
    @pl.when(core == lax.div(layer, 2))
    def _():
        pltpu.make_async_copy(own.at[lax.rem(layer, 2)], target, sem).start()

    @pl.when(core != lax.div(layer, 2))
    def _():
        pltpu.make_async_copy(peer.at[lax.rem(layer, 2)], target, sem).start()


def send_row(core, section, source, kept, other, sem):
    @pl.when(core == section)
    def _():
        pltpu.make_async_copy(source, kept, sem).start()

    @pl.when(core != section)
    def _():
        pltpu.make_async_copy(source, other, sem).start()


def forward_kernel(layers, aliased, flags, x_in, seg_hbm, vec, own_up, own_down, peer_up, peer_down, *rest):
    rest = rest[aliased:]
    hid, dge, saved, rst, kept, other, send = rest[:7]
    (up_v, down_v, hid_v, dge_v, saved_v, rst_v, stream, acc, out_v, x_v, seg_v, masks, w_sem, in_sem, o_sem, s_sem) = rest[7:]
    frames, width = acc.shape
    hidden = hid_v.shape[2]

    @pl.when(flags[0] == 1)
    def _():
        core, micro, row = flags[1], flags[2], flags[3]
        pltpu.make_async_copy(x_in, x_v, s_sem.at[2]).start()
        pltpu.make_async_copy(seg_hbm.at[micro], seg_v.at[pl.ds(PAD, frames)], in_sem).start()
        def fetch(j):
            start_weights(core, j, own_up, peer_up, up_v.at[j], w_sem.at[j, 0])
            start_weights(core, j, own_down, peer_down, down_v.at[j], w_sem.at[j, 1])

        fetch(0)
        clear_edges(stream, frames)
        pltpu.make_async_copy(seg_hbm.at[0], seg_v.at[pl.ds(PAD, frames)], in_sem).wait()
        build_masks(seg_v, masks)
        pltpu.make_async_copy(x_in, x_v, s_sem.at[2]).wait()
        for c, cols in enumerate(slabs(width)):
            stream[c, PAD : PAD + frames, :] = x_v[:, cols].astype(F32)

        def layer(j, carry):
            def conv_norm(i, c):
                base = pl.multiple_of(i * TILE, TILE)
                rows = pl.ds(base, TILE)
                parts = []
                for s, cols in enumerate(slabs(width)):
                    centre = stream[s, pl.ds(base + PAD, TILE), :]
                    saved_v[j, STREAM, rows, cols] = centre.astype(BF16)
                    total = vec[j, CONV_B : CONV_B + 1, cols] + vec[j, 3:4, cols] * centre
                    for offset in OFFSETS:
                        neighbour = stream[s, pl.ds(base + PAD + offset, TILE), :] * masks[MASK_OF[offset], rows, :]
                        total = total + vec[j, offset + 3 : offset + 4, cols] * neighbour
                    parts.append(total)
                mean = row_sum(parts) * (1.0 / width)
                parts = [part - mean for part in parts]
                rstd = lax.rsqrt(row_sum([part * part for part in parts]) * (1.0 / width) + EPSILON)
                for part, cols in zip(parts, slabs(width)):
                    xhat = part * rstd
                    saved_v[j, XHAT, rows, cols] = xhat.astype(BF16)
                    saved_v[j, NORMED, rows, cols] = (xhat * vec[j, GAIN : GAIN + 1, cols] + vec[j, SHIFT : SHIFT + 1, cols]).astype(BF16)
                rst_v[j, rows, :] = jnp.broadcast_to(rstd, (TILE, LANES))
                return c

            lax.fori_loop(0, frames // TILE, conv_norm, 0, unroll=8)
            pltpu.make_async_copy(saved_v.at[j], saved.at[row, j], o_sem.at[j, 3]).start()
            pltpu.make_async_copy(rst_v.at[j], rst.at[row, j], o_sem.at[j, 2]).start()
            pltpu.make_async_copy(own_up.at[0], up_v.at[j], w_sem.at[j, 0]).wait()

            @pl.when(j + 1 < layers)
            def _():
                fetch(j + 1)

            pltpu.make_async_copy(own_down.at[0], down_v.at[j], w_sem.at[j, 1]).wait()
            half = frames // 2
            for part in range(2):
                here = slice(part * half, (part + 1) * half)
                for n in range(hidden // COLS):
                    cols = slice(n * COLS, (n + 1) * COLS)
                    if part == 1 and n % 2 == 1 and n // 2 < width // COLS:
                        out = slice(n // 2 * COLS, (n // 2 + 1) * COLS)
                        acc[0:half, out] = jnp.dot(hid_v[j, 0:half, :], down_v[j, :, out], preferred_element_type=F32)
                    at, start = UP_B + n * COLS // width, (n * COLS) % width
                    value = jnp.dot(saved_v[j, NORMED, here], up_v[j, :, cols], preferred_element_type=F32) + vec[j, at : at + 1, start : start + COLS]
                    scaled = value * INV_SQRT2
                    phi_sum = 0.5 + 0.5 * lax.erf(scaled)
                    hid_v[j, here, cols] = (value * phi_sum).astype(BF16)
                    dge_v[j, here, cols] = (phi_sum + scaled * INV_SQRT_PI * jnp.exp2(scaled * scaled * -LOG2_E)).astype(BF16)
            pltpu.make_async_copy(hid_v.at[j], hid.at[row, j], o_sem.at[j, 0]).start()
            pltpu.make_async_copy(dge_v.at[j], dge.at[row, j], o_sem.at[j, 1]).start()
            acc[half:, :] = jnp.dot(hid_v[j, half:, :], down_v[j], preferred_element_type=F32)

            def finish(ends_section, i, c):
                base = pl.multiple_of(i * TILE, TILE)
                rows = pl.ds(base, TILE)
                for s, cols in enumerate(slabs(width)):
                    inner = pl.ds(pl.multiple_of(base + PAD, 8), TILE)
                    branch = acc[rows, cols] + vec[j, DOWN_B : DOWN_B + 1, cols]
                    fresh = stream[s, inner, :] + vec[j, SCALE : SCALE + 1, cols] * branch
                    if ends_section:
                        rounded = fresh.astype(BF16)
                        out_v[lax.div(j, 2), rows, cols] = fresh
                        x_v[rows, cols] = rounded
                        fresh = rounded.astype(F32)
                    stream[s, inner, :] = fresh
                return c

            @pl.when(lax.rem(j, 2) == 1)
            def _():
                lax.fori_loop(0, frames // TILE, functools.partial(finish, True), 0)

            @pl.when(lax.rem(j, 2) == 0)
            def _():
                lax.fori_loop(0, frames // TILE, functools.partial(finish, False), 0)

            @pl.when(j == 1)
            def _():
                send_row(core, 0, out_v.at[0], kept.at[micro], other.at[row], s_sem.at[0])

            return carry

        lax.fori_loop(0, layers, layer, 0)
        send_row(core, 1, out_v.at[1], kept.at[micro], other.at[row], s_sem.at[1])
        pltpu.make_async_copy(x_v, send, s_sem.at[2]).start()
        for j in range(layers):
            pltpu.make_async_copy(hid_v.at[j], hid.at[row, j], o_sem.at[j, 0]).wait()
            pltpu.make_async_copy(dge_v.at[j], dge.at[row, j], o_sem.at[j, 1]).wait()
            pltpu.make_async_copy(rst_v.at[j], rst.at[row, j], o_sem.at[j, 2]).wait()
            pltpu.make_async_copy(saved_v.at[j], saved.at[row, j], o_sem.at[j, 3]).wait()
        pltpu.make_async_copy(out_v.at[0], other.at[row], s_sem.at[0]).wait()
        pltpu.make_async_copy(out_v.at[1], other.at[row], s_sem.at[1]).wait()
        pltpu.make_async_copy(x_v, send, s_sem.at[2]).wait()


SUMS, HEAD = 4, 2
DOWN, UP = 0, 1
VECTORS = 16


def send_sums(core, section, owners, kind, layer, source, vectors, targets, sem):
    kept, kept_last, head, tail = targets
    _, _, block, width = kept.shape
    shares = kept.shape[0] + 1
    size = (block - VECTORS) // 2
    first = 0 if kind == DOWN else size + VECTORS
    columns = source.shape[1] // width
    rows = size // columns
    for stop in range(shares):
        owner = owners[2 * kind + layer, stop]
        pieces = [
            (source.at[pl.ds(pl.multiple_of(owner * rows, 16), rows), pl.ds(b * width, width)], pl.ds(first + b * rows, rows))
            for b in range(columns)
        ]
        if vectors is not None:
            pieces.append((vectors.at[owners[2 * DOWN + layer, stop]], pl.ds(size, VECTORS)))
        for piece, place in pieces:

            @pl.when(core == section)
            def _():
                target = kept.at[stop, layer] if stop < shares - 1 else kept_last.at[layer]
                pltpu.make_async_copy(piece, target.at[place], sem).start()

            @pl.when(core != section)
            def _():
                target = head.at[stop, layer] if stop < HEAD else tail.at[stop - HEAD, layer]
                pltpu.make_async_copy(piece, target.at[place], sem).start()


def pack_vectors(sums, packed):
    shares, _, width = packed.shape
    parts = [sums[r : r + 1, :] for r in range(UP_B, VEC_ROWS - 1)]
    wide = jnp.broadcast_to(jnp.concatenate(parts, axis=1), (8, width * len(parts)))
    size, wide_size = width // shares, width * len(parts) // shares
    is_bias = lax.broadcasted_iota(jnp.int32, (VECTORS, width), 0) == UP_B
    for d in range(shares):
        part = sums if d == 0 else pltpu.roll(sums, width - d * size, 1)
        bias = wide if d == 0 else pltpu.roll(wide, wide.shape[1] - d * wide_size, 1)
        packed[d] = jnp.where(is_bias, jnp.broadcast_to(bias[0:1, :width], (VECTORS, width)), part).astype(BF16)


def backward_kernel(final, aliased, ties, riders, flags, g_one, g_two, seg_hbm, vec, own_up, own_down, peer_up, peer_down, dge, saved, rst, *rest):
    if final:
        owners, hid, gb, gp, vec_in = rest[:5]
        rest = rest[5 + ties + aliased :]
        sums_out, (kept, other) = rest[:SUMS], rest[SUMS : SUMS + 2]
        rest = rest[SUMS + 2 :]
    else:
        rest = rest[aliased:]
        gb, gp, vec_out, kept, other, send = rest[:6]
        rest = rest[6 + riders :]
    (up_v, down_v, dge_v, saved_v, rst_v, gb_v, gp_v, vg_v, g_now, fresh_v, gn_v, padded, x_v, seg_v, masks, w_sem, in_sem, g_sem, o_sem, s_sem) = rest[:20]
    if final:
        (hid_v, nrm_v, dwd_v, dwu_v, early_v, packed, b_sem) = rest[20:]
    frames, width = g_now.shape
    held, _, hidden = dge_v.shape
    layers = vec.shape[0]
    nt = (((1,), (1,)), ((), ()))
    tn = (((0,), (0,)), ((), ()))
    tall = 2 * TILE
    cols_of = slabs(width)

    @pl.when(flags[0] == 1)
    def _():
        core, micro, row = flags[1], flags[2], flags[3]
        pltpu.make_async_copy(seg_hbm.at[micro], seg_v.at[pl.ds(PAD, frames)], in_sem).start()

        def fetch(j):
            h = lax.rem(j, held)
            start_weights(core, j, own_down, peer_down, down_v.at[h], w_sem.at[h, 1])
            pltpu.make_async_copy(dge.at[row, j], dge_v.at[h], w_sem.at[h, 3]).start()
            start_weights(core, j, own_up, peer_up, up_v.at[h], w_sem.at[h, 0])
            pltpu.make_async_copy(rst.at[row, j], rst_v.at[h], w_sem.at[h, 4]).start()
            pltpu.make_async_copy(saved.at[row, j, 0:2], saved_v.at[h], w_sem.at[h, 2]).start()

        if final:
            pltpu.make_async_copy(vec_in.at[1 - row], early_v, s_sem.at[2]).start()
        source = [pltpu.make_async_copy(g, x_v, g_sem) for g in (g_one, g_two)]
        for k in range(2):

            @pl.when(flags[4] == k)
            def _():
                source[k].start()

        fetch(layers - 1)
        clear_edges(padded, frames)
        source[0].wait()
        for cols in cols_of:

            def enter(t, c):
                rows = pl.ds(pl.multiple_of(t * tall, tall), tall)
                scaled = (vec[layers - 1, SCALE : SCALE + 1, cols] * x_v[rows, cols].astype(F32)).astype(BF16)
                gb_v[layers, 0, rows, cols] = scaled
                return c + fold(scaled.astype(F32))

            total = lax.fori_loop(0, frames // tall, enter, jnp.zeros((8, LANES), F32))
            vg_v[layers, DOWN_B : DOWN_B + 1, cols] = jnp.sum(total, axis=0, keepdims=True)
        pltpu.make_async_copy(seg_hbm.at[0], seg_v.at[pl.ds(PAD, frames)], in_sem).wait()
        build_masks(seg_v, masks)

        def layer(step, carry):
            j = layers - 1 - step
            h = lax.rem(j, held)
            if not final:
                pltpu.make_async_copy(gb_v.at[j + 1, 0], gb.at[row, j], o_sem.at[j, 0]).start()
            pltpu.make_async_copy(own_down.at[0], down_v.at[h], w_sem.at[h, 1]).wait()
            pltpu.make_async_copy(dge.at[0, 0], dge_v.at[h], w_sem.at[h, 3]).wait()
            if final:
                pltpu.make_async_copy(hid.at[row, j], hid_v.at[h, 0], b_sem.at[h, 0]).start()
                pltpu.make_async_copy(hid.at[1 - row, j], hid_v.at[h, 1], b_sem.at[h, 1]).start()
                pltpu.make_async_copy(gb.at[1 - row, j], gb_v.at[j + 1, 1], b_sem.at[h, 4]).start()
                pltpu.make_async_copy(saved.at[row, j, NORMED], nrm_v.at[h, 0], b_sem.at[h, 2]).start()
                pltpu.make_async_copy(saved.at[1 - row, j, NORMED], nrm_v.at[h, 1], b_sem.at[h, 3]).start()
                pltpu.make_async_copy(gp.at[1 - row, j], gp_v.at[h, 1], b_sem.at[h, 5]).start()
            for n in range(hidden // COLS):
                cols = slice(n * COLS, (n + 1) * COLS)
                value = lax.dot_general(gb_v[j + 1, 0], down_v[h, cols, :], nt, preferred_element_type=F32)
                rounded = (value * dge_v[h, :, cols].astype(F32)).astype(BF16)
                gp_v[h, 0, :, cols] = rounded
                at, start = UP_B + n * COLS // width, (n * COLS) % width
                vg_v[j + 1, at : at + 1, start : start + COLS] = jnp.sum(rounded.astype(F32), axis=0, keepdims=True)
            if not final:
                pltpu.make_async_copy(gp_v.at[h, 0], gp.at[row, j], o_sem.at[j, 1]).start()
            pltpu.make_async_copy(own_up.at[0], up_v.at[h], w_sem.at[h, 0]).wait()
            gn_v[...] = lax.dot_general(gp_v[h, 0], up_v[h], nt, preferred_element_type=F32)
            pltpu.make_async_copy(rst.at[0, 0], rst_v.at[h], w_sem.at[h, 4]).wait()
            pltpu.make_async_copy(saved.at[0, 0, 0:2], saved_v.at[h], w_sem.at[h, 2]).wait()

            @pl.when(j > 0)
            def _():
                fetch(j - 1)

            if final:
                pltpu.make_async_copy(hid.at[0, 0], hid_v.at[h, 0], b_sem.at[h, 0]).wait()
                pltpu.make_async_copy(hid.at[0, 0], hid_v.at[h, 1], b_sem.at[h, 1]).wait()
                pltpu.make_async_copy(gb.at[0, 0], gb_v.at[j + 1, 1], b_sem.at[h, 4]).wait()

                @pl.when(j + held < layers)
                def _():
                    pltpu.make_async_copy(dwd_v.at[h], dwd_v.at[h], o_sem.at[h, 0]).wait()
                    pltpu.make_async_copy(dwu_v.at[h], dwu_v.at[h], o_sem.at[h, 1]).wait()
                    pltpu.make_async_copy(packed.at[h], packed.at[h], o_sem.at[h, 1]).wait()

            def down_chunk(n):
                rows = slice(n * COLS, (n + 1) * COLS)
                left = hid_v[h, :, :, rows].reshape(2 * frames, COLS)
                right = gb_v[j + 1].reshape(2 * frames, width)
                value = lax.dot_general(left, right, tn, preferred_element_type=F32)
                dwd_v[h, rows, :] = value.astype(BF16)
                return fold(value * down_v[h, rows, :].astype(F32))

            def up_chunk(m, n):
                rows = slice(m * COLS, (m + 1) * COLS)
                cols = slice(n * width, (n + 1) * width)
                left = nrm_v[h, :, :, rows].reshape(2 * frames, COLS)
                right = gp_v[h, :, :, cols].reshape(2 * frames, width)
                dwu_v[h, rows, cols] = lax.dot_general(left, right, tn, preferred_element_type=F32).astype(BF16)

            odd = lax.rem(j, 2) == 1

            def norm_back(t, c):
                base = t * TILE if isinstance(t, int) else pl.multiple_of(t * TILE, TILE)
                rows = pl.ds(base, TILE)
                inner = pl.ds(base + PAD if isinstance(t, int) else pl.multiple_of(base + PAD, 8), TILE)
                grads = [gn_v[rows, cols] for cols in cols_of]
                xhats = [saved_v[h, XHAT, rows, cols].astype(F32) for cols in cols_of]
                qs = [grad * vec[j, GAIN : GAIN + 1, cols] for grad, cols in zip(grads, cols_of)]
                mean_q = row_sum(qs) * (1.0 / width)
                mean_qx = row_sum([q * xhat for q, xhat in zip(qs, xhats)]) * (1.0 / width)
                rstd = rst_v[h, rows, :]
                out = []
                for s, cols in enumerate(cols_of):
                    grad_conv = rstd * (qs[s] - mean_q - xhats[s] * mean_qx)
                    padded[s, inner, :] = grad_conv
                    g_now[rows, cols] = jnp.where(odd, x_v[rows, cols].astype(F32), fresh_v[rows, cols])
                    out += [c[3 * s] + fold(grads[s] * xhats[s]), c[3 * s + 1] + fold(grads[s]), c[3 * s + 2] + fold(grad_conv)]
                return tuple(out)

            sums = (jnp.zeros((8, LANES), F32),) * (3 * len(cols_of))
            tiles = frames // TILE
            if final:
                parts = hidden // COLS
                scale = jnp.zeros((8, width), F32)
                done = 0
                for n in range(parts):
                    scale = scale + down_chunk(n)
                    while done < tiles * (n + 1) // parts:
                        sums = norm_back(done, sums)
                        done += 1
                vg_v[j + 1, SCALE : SCALE + 1, :] = jnp.sum(scale, axis=0, keepdims=True)
                send_sums(core, lax.div(j, 2), owners, DOWN, lax.rem(j, 2), dwd_v.at[h], None, sums_out, o_sem.at[h, 0])
                pltpu.make_async_copy(saved.at[0, 0, 0], nrm_v.at[h, 0], b_sem.at[h, 2]).wait()
                pltpu.make_async_copy(saved.at[0, 0, 0], nrm_v.at[h, 1], b_sem.at[h, 3]).wait()
                pltpu.make_async_copy(gp.at[0, 0], gp_v.at[h, 1], b_sem.at[h, 5]).wait()
            else:
                sums = lax.fori_loop(0, tiles, norm_back, sums, unroll=8)
            for s, cols in enumerate(cols_of):
                for k, at in enumerate((GAIN, SHIFT, CONV_B)):
                    vg_v[j + 1, at : at + 1, cols] = jnp.sum(sums[3 * s + k], axis=0, keepdims=True)

            @pl.when(odd & (step > 0))
            def _():
                pltpu.make_async_copy(fresh_v, other.at[row], s_sem.at[0]).wait()

            below = lax.max(j - 1, 0)
            for s, cols in enumerate(cols_of):

                def conv_back(t, c):
                    base = t * tall if isinstance(t, int) else pl.multiple_of(t * tall, tall)
                    rows = pl.ds(base, tall)
                    source = saved_v[h, STREAM, rows, cols].astype(F32)
                    centre = padded[s, pl.ds(base + PAD if isinstance(t, int) else pl.multiple_of(base + PAD, 8), tall), :]
                    total = g_now[rows, cols] + vec[j, 3:4, cols] * centre
                    taps = [None] * 7
                    taps[3] = c[3] + fold(centre * source)
                    for offset in OFFSETS:
                        term = padded[s, pl.ds(base + PAD - offset, tall), :] * masks[MASK_OF[-offset], rows, :]
                        total = total + vec[j, offset + 3 : offset + 4, cols] * term
                        taps[offset + 3] = c[offset + 3] + fold(term * source)
                    rounded = total.astype(BF16)
                    fresh_v[rows, cols] = total
                    x_v[rows, cols] = rounded
                    scaled = (vec[below, SCALE : SCALE + 1, cols] * jnp.where(odd, total, rounded.astype(F32))).astype(BF16)
                    gb_v[j, 0, rows, cols] = scaled
                    return tuple(taps) + (c[7] + fold(scaled.astype(F32)),)

                sums = (jnp.zeros((8, LANES), F32),) * 8
                if final:
                    chunks = [(m, n) for m in range(width // COLS) for n in range(hidden // width)]
                    each = -(-len(chunks) // len(cols_of))
                    mine = chunks[s * each : (s + 1) * each]
                    done = 0
                    for k, (m, n) in enumerate(mine):
                        up_chunk(m, n)
                        while done < frames // tall * (k + 1) // len(mine):
                            sums = conv_back(done, sums)
                            done += 1
                    while done < frames // tall:
                        sums = conv_back(done, sums)
                        done += 1
                else:
                    sums = lax.fori_loop(0, frames // tall, conv_back, sums, unroll=8)
                for k in range(7):
                    vg_v[j + 1, k : k + 1, cols] = jnp.sum(sums[k], axis=0, keepdims=True)
                vg_v[j, DOWN_B : DOWN_B + 1, cols] = jnp.sum(sums[7], axis=0, keepdims=True)
            if final:

                @pl.when(step == 0)
                def _():
                    pltpu.make_async_copy(vec_in.at[0], early_v, s_sem.at[2]).wait()

                pack_vectors(vg_v[j + 1] + early_v[j], packed.at[h])
                send_vectors = packed.at[h]
                send_sums(core, lax.div(j, 2), owners, UP, lax.rem(j, 2), dwu_v.at[h], send_vectors, sums_out, o_sem.at[h, 1])

            @pl.when(jnp.logical_not(odd))
            def _():
                send_row(core, lax.div(j, 2), fresh_v, kept.at[micro], other.at[row], s_sem.at[0])

            return carry

        for i in range(1, layers + 1):
            vg_v[i, SCALE : SCALE + 1, :] = jnp.zeros((1, width), F32)
            vg_v[i, VEC_ROWS - 1 : VEC_ROWS, :] = jnp.zeros((1, width), F32)
        lax.fori_loop(0, layers, layer, 0)
        if final:
            for h in range(held):
                pltpu.make_async_copy(dwd_v.at[h], dwd_v.at[h], o_sem.at[h, 0]).wait()
                pltpu.make_async_copy(dwu_v.at[h], dwu_v.at[h], o_sem.at[h, 1]).wait()
                pltpu.make_async_copy(packed.at[h], packed.at[h], o_sem.at[h, 1]).wait()
        else:
            pltpu.make_async_copy(vg_v.at[pl.ds(1, layers)], vec_out.at[row], s_sem.at[2]).start()
            pltpu.make_async_copy(x_v, send, s_sem.at[1]).start()
            for j in range(layers):
                pltpu.make_async_copy(gb_v.at[j + 1, 0], gb.at[row, j], o_sem.at[j, 0]).wait()
                pltpu.make_async_copy(gp_v.at[j, 0], gp.at[row, j], o_sem.at[j, 1]).wait()
            pltpu.make_async_copy(x_v, send, s_sem.at[1]).wait()
            pltpu.make_async_copy(vg_v.at[pl.ds(1, layers)], vec_out.at[row], s_sem.at[2]).wait()
        pltpu.make_async_copy(fresh_v, other.at[row], s_sem.at[0]).wait()


def weight_kernel(ties, flags, owners, own_down, peer_down, all_hid, all_gb, all_saved, all_gp, vec_in, *rest):
    rest = rest[ties:]
    sums_out, rest = rest[:SUMS], rest[SUMS:]
    hid_v, gb_v, nrm_v, gp_v, down_v, dwd_v, dwu_v, vec_v, packed, sem, o_sem, s_sem = rest
    frames, width = gb_v.shape[2:]
    hidden = hid_v.shape[3]
    layers = all_hid.shape[1]
    tn = (((0,), (0,)), ((), ()))

    @pl.when(flags[0] == 1)
    def _():
        core = flags[1]

        def copies(j, h):
            pairs = []
            for row in range(2):
                pairs += [
                    (all_hid.at[row, j], hid_v.at[h, row]),
                    (all_gb.at[row, j], gb_v.at[h, row]),
                    (all_saved.at[row, j, NORMED], nrm_v.at[h, row]),
                    (all_gp.at[row, j], gp_v.at[h, row]),
                ]
            return [pltpu.make_async_copy(a, b, sem.at[h, k]) for k, (a, b) in enumerate(pairs)]

        def fetch(j):
            h = lax.rem(j, 2)
            start_weights(core, j, own_down, peer_down, down_v.at[h], sem.at[h, 8])
            for copy in copies(j, h):
                copy.start()

        fetch(layers - 1)
        pltpu.make_async_copy(vec_in, vec_v, s_sem).start()
        pltpu.make_async_copy(vec_in, vec_v, s_sem).wait()

        def layer(step, carry):
            j = layers - 1 - step
            h = lax.rem(j, 2)

            @pl.when(j > 0)
            def _():
                fetch(j - 1)

            pltpu.make_async_copy(own_down.at[0], down_v.at[h], sem.at[h, 8]).wait()
            for copy in copies(j, h):
                copy.wait()

            @pl.when(j + 2 < layers)
            def _():
                pltpu.make_async_copy(dwd_v.at[h], dwd_v.at[h], o_sem.at[h, 0]).wait()
                pltpu.make_async_copy(dwu_v.at[h], dwu_v.at[h], o_sem.at[h, 1]).wait()
                pltpu.make_async_copy(packed.at[h], packed.at[h], o_sem.at[h, 1]).wait()

            def down_chunk(n, scale):
                rows = pl.ds(pl.multiple_of(n * COLS, COLS), COLS)
                left = hid_v[h, :, :, rows].reshape(2 * frames, COLS)
                value = lax.dot_general(left, gb_v[h].reshape(2 * frames, width), tn, preferred_element_type=F32)
                dwd_v[h, rows, :] = value.astype(BF16)
                return scale + fold(value * down_v[h, rows, :].astype(F32))

            scale = lax.fori_loop(0, hidden // COLS, down_chunk, jnp.zeros((8, width), F32))
            scale = jnp.sum(scale, axis=0, keepdims=True)
            vectors = vec_v[0, j] + vec_v[1, j]
            is_scale = lax.broadcasted_iota(jnp.int32, vectors.shape, 0) == SCALE
            pack_vectors(jnp.where(is_scale, jnp.broadcast_to(scale, vectors.shape), vectors), packed.at[h])
            send_sums(core, lax.div(j, 2), owners, DOWN, lax.rem(j, 2), dwd_v.at[h], None, sums_out, o_sem.at[h, 0])

            def up_chunk(n, c):
                cols = pl.ds(pl.multiple_of(n * width, width), width)
                right = gp_v[h, :, :, cols].reshape(2 * frames, width)
                value = lax.dot_general(nrm_v[h].reshape(2 * frames, width), right, tn, preferred_element_type=F32)
                dwu_v[h, :, cols] = value.astype(BF16)
                return c

            lax.fori_loop(0, hidden // width, up_chunk, 0)
            send_sums(core, lax.div(j, 2), owners, UP, lax.rem(j, 2), dwu_v.at[h], packed.at[h], sums_out, o_sem.at[h, 1])
            return carry

        lax.fori_loop(0, layers, layer, 0)
        for h in range(2):
            pltpu.make_async_copy(dwd_v.at[h], dwd_v.at[h], o_sem.at[h, 0]).wait()
            pltpu.make_async_copy(dwu_v.at[h], dwu_v.at[h], o_sem.at[h, 1]).wait()
            pltpu.make_async_copy(packed.at[h], packed.at[h], o_sem.at[h, 1]).wait()


def place_kernel(at, kept_in, rows, tie, kept, held, sem):
    count = rows.shape[0]
    for i in range(count):
        pltpu.make_async_copy(rows.at[i], held.at[i], sem.at[i]).start()
    for i in range(count):
        pltpu.make_async_copy(rows.at[i], held.at[i], sem.at[i]).wait()
        pltpu.make_async_copy(held.at[i], kept.at[at[0] + i], sem.at[i]).start()
    for i in range(count):
        pltpu.make_async_copy(held.at[i], kept.at[at[0] + i], sem.at[i]).wait()


def hold_kernel(value_in, tie, value):
    pass


def final_kernel(down_0, down_1, up_0, up_1, kept, other, scales, *rest):
    conv_out, conv_b_out, gain_out, shift_out, up_out, up_b_out, down_out, down_b_out, scale_out = rest
    size, wide = conv_b_out.shape[1], up_b_out.shape[1]
    rows, width = down_out.shape[1:]
    for layer, (down, up) in enumerate(((down_0, up_0), (down_1, up_1))):
        total = down[...].astype(F32) + kept[layer, : rows + VECTORS].astype(F32) + other[layer, : rows + VECTORS].astype(F32)
        down_out[layer] = total[:rows]
        vectors = total[rows:]
        at = slice(layer, layer + 1)
        conv_out[layer] = vectors[:CONV_B, :size]
        conv_b_out[at, :] = vectors[CONV_B : CONV_B + 1, :size]
        gain_out[at, :] = vectors[GAIN : GAIN + 1, :size]
        shift_out[at, :] = vectors[SHIFT : SHIFT + 1, :size]
        down_b = vectors[DOWN_B : DOWN_B + 1, :size]
        down_b_out[at, :] = down_b
        scale_out[at, :] = (vectors[SCALE : SCALE + 1, :size] + scales[0, at, :] * down_b) / scales[1, at, :]
        up_b_out[at, :] = vectors[UP_B : UP_B + 1, :wide]
        total = up[...].astype(F32) + kept[layer, rows + VECTORS :].astype(F32) + other[layer, rows + VECTORS :].astype(F32)
        for b in range(up_out.shape[2] // width):
            up_out[layer, :, b * width : (b + 1) * width] = total[b * size : (b + 1) * size]


ANY = pl.BlockSpec(memory_space=pl.ANY)
HBM = pl.BlockSpec(memory_space=pltpu.HBM)
SMEM = pl.BlockSpec(memory_space=pltpu.SMEM)
VMEM = pl.BlockSpec(memory_space=pltpu.VMEM)


def near(value):
    return pltpu.with_memory_space_constraint(value, pltpu.VMEM)


def run_forward(flags, x, seg, vec, weights, earlier):
    layers = vec.shape[0]
    micro = seg.shape[0]
    frames, width = x.shape
    hidden = weights[0].shape[2]
    shapes = (
        jax.ShapeDtypeStruct((2, layers, frames, hidden), BF16),
        jax.ShapeDtypeStruct((2, layers, frames, hidden), BF16),
        jax.ShapeDtypeStruct((2, layers, KINDS, frames, width), BF16),
        jax.ShapeDtypeStruct((2, layers, frames, LANES), F32),
        jax.ShapeDtypeStruct((micro, frames, width), F32),
        jax.ShapeDtypeStruct((2, frames, width), F32),
        jax.ShapeDtypeStruct((frames, width), BF16),
    )
    aliased = len(earlier)
    return pl.pallas_call(
        functools.partial(forward_kernel, layers, aliased),
        out_shape=shapes,
        in_specs=[SMEM, ANY, ANY, VMEM] + [ANY] * (4 + aliased),
        out_specs=(ANY,) * len(shapes),
        input_output_aliases={8 + i: i for i in range(aliased)},
        scratch_shapes=[
            pltpu.VMEM((layers, width, hidden), BF16),
            pltpu.VMEM((layers, hidden, width), BF16),
            pltpu.VMEM((layers, frames, hidden), BF16),
            pltpu.VMEM((layers, frames, hidden), BF16),
            pltpu.VMEM((layers, KINDS, frames, width), BF16),
            pltpu.VMEM((layers, frames, LANES), F32),
            pltpu.VMEM((width // LANES, frames + 2 * PAD, LANES), F32),
            pltpu.VMEM((frames, width), F32),
            pltpu.VMEM((2, frames, width), F32),
            pltpu.VMEM((frames, width), BF16),
            pltpu.VMEM((frames + 2 * PAD, LANES), F32),
            pltpu.VMEM((6, frames, LANES), F32),
            pltpu.SemaphoreType.DMA((layers, 2)),
            pltpu.SemaphoreType.DMA,
            pltpu.SemaphoreType.DMA((layers, 4)),
            pltpu.SemaphoreType.DMA((3,)),
        ],
        compiler_params=pltpu.CompilerParams(vmem_limit_bytes=VMEM_LIMIT),
        cost_estimate=COST,
    )(flags, x, seg, vec, *weights, *earlier)


def sum_shapes(shares, hidden, width):
    block = (2, 2 * (hidden // shares) + VECTORS, width)
    return tuple(jax.ShapeDtypeStruct(shape, BF16) for shape in ((shares - 1, *block), block, (HEAD, *block), (shares - HEAD, *block)))


def run_backward(flags, g, seg, vec, weights, state, earlier, final=(), ties=(), riders=()):
    frames, width = g[0].shape
    hidden = weights[0].shape[2]
    layers, micro = vec.shape[0], seg.shape[0]
    rows, held = (2, 2) if final else (1, layers)
    grads = (
        jax.ShapeDtypeStruct((micro, frames, width), F32),
        jax.ShapeDtypeStruct((2, frames, width), F32),
    )
    if final:
        shapes = (*sum_shapes(final[0].shape[1], hidden, width), *grads)
    else:
        shapes = (
            jax.ShapeDtypeStruct((2, layers, frames, width), BF16),
            jax.ShapeDtypeStruct((2, layers, frames, hidden), BF16),
            jax.ShapeDtypeStruct((2, layers, VEC_ROWS, width), F32),
            *grads,
            jax.ShapeDtypeStruct((frames, width), BF16),
        )
    earlier = (*earlier, *riders)
    shapes = (*shapes, *(jax.ShapeDtypeStruct(rider.shape, rider.dtype) for rider in riders))
    aliased = len(earlier)
    targets = [*range(len(earlier) - len(riders)), *range(len(shapes) - len(riders), len(shapes))]
    scratch = [
        pltpu.VMEM((held, width, hidden), BF16),
        pltpu.VMEM((held, hidden, width), BF16),
        pltpu.VMEM((held, frames, hidden), BF16),
        pltpu.VMEM((held, 2, frames, width), BF16),
        pltpu.VMEM((held, frames, LANES), F32),
        pltpu.VMEM((layers + 1, rows, frames, width), BF16),
        pltpu.VMEM((held, rows, frames, hidden), BF16),
        pltpu.VMEM((layers + 1, VEC_ROWS, width), F32),
        pltpu.VMEM((frames, width), F32),
        pltpu.VMEM((frames, width), F32),
        pltpu.VMEM((frames, width), F32),
        pltpu.VMEM((width // LANES, frames + 2 * PAD, LANES), F32),
        pltpu.VMEM((frames, width), BF16),
        pltpu.VMEM((frames + 2 * PAD, LANES), F32),
        pltpu.VMEM((6, frames, LANES), F32),
        pltpu.SemaphoreType.DMA((held, 5)),
        pltpu.SemaphoreType.DMA,
        pltpu.SemaphoreType.DMA,
        pltpu.SemaphoreType.DMA((held, 2)),
        pltpu.SemaphoreType.DMA((3,)),
    ]
    if final:
        scratch += [
            pltpu.VMEM((held, 2, frames, hidden), BF16),
            pltpu.VMEM((held, 2, frames, width), BF16),
            pltpu.VMEM((held, hidden, width), BF16),
            pltpu.VMEM((held, width, hidden), BF16),
            pltpu.VMEM((layers, VEC_ROWS, width), F32),
            pltpu.VMEM((held, final[0].shape[1], VECTORS, width), BF16),
            pltpu.SemaphoreType.DMA((held, 6)),
        ]
    first_alias = 12 + len(final) + len(ties)
    return pl.pallas_call(
        functools.partial(backward_kernel, bool(final), aliased, len(ties), len(riders)),
        out_shape=shapes,
        in_specs=[SMEM, ANY, ANY, ANY, VMEM] + [ANY] * 7 + ([SMEM] + [ANY] * 4 if final else []) + [ANY] * (len(ties) + aliased),
        out_specs=tuple(HBM if final and k < SUMS else ANY for k in range(len(shapes))),
        input_output_aliases={first_alias + i: target for i, target in enumerate(targets)},
        scratch_shapes=scratch,
        compiler_params=pltpu.CompilerParams(vmem_limit_bytes=VMEM_LIMIT),
        cost_estimate=COST,
    )(flags, *g, seg, vec, *weights, *state, *final, *ties, *earlier)


def run_weights(flags, owners, weights, hid, gb, saved, gp, vectors, ties):
    _, layers, frames, hidden = hid.shape
    width = gb.shape[3]
    shares = owners.shape[1]
    return pl.pallas_call(
        functools.partial(weight_kernel, len(ties)),
        out_shape=sum_shapes(shares, hidden, width),
        in_specs=[SMEM, SMEM] + [ANY] * (7 + len(ties)),
        out_specs=(HBM,) * SUMS,
        scratch_shapes=[
            pltpu.VMEM((2, 2, frames, hidden), BF16),
            pltpu.VMEM((2, 2, frames, width), BF16),
            pltpu.VMEM((2, 2, frames, width), BF16),
            pltpu.VMEM((2, 2, frames, hidden), BF16),
            pltpu.VMEM((2, hidden, width), BF16),
            pltpu.VMEM((2, hidden, width), BF16),
            pltpu.VMEM((2, width, hidden), BF16),
            pltpu.VMEM(vectors.shape, F32),
            pltpu.VMEM((2, shares, VECTORS, width), BF16),
            pltpu.SemaphoreType.DMA((2, 9)),
            pltpu.SemaphoreType.DMA((2, 2)),
            pltpu.SemaphoreType.DMA,
        ],
        compiler_params=pltpu.CompilerParams(vmem_limit_bytes=VMEM_LIMIT),
        cost_estimate=COST,
    )(flags, owners, weights[1], weights[3], hid, gb, saved, gp, vectors, *ties)


def run_place(kept, rows, at, tie):
    return pl.pallas_call(
        place_kernel,
        out_shape=jax.ShapeDtypeStruct(kept.shape, kept.dtype),
        in_specs=[SMEM, ANY, ANY, ANY],
        out_specs=ANY,
        input_output_aliases={1: 0},
        scratch_shapes=[pltpu.VMEM(rows.shape, rows.dtype), pltpu.SemaphoreType.DMA(rows.shape[:1])],
        cost_estimate=COST,
    )(at.reshape(1).astype(jnp.int32), kept, rows, tie)


def hold(value, tie):
    return pl.pallas_call(
        hold_kernel,
        out_shape=jax.ShapeDtypeStruct(value.shape, value.dtype),
        in_specs=[HBM, ANY],
        out_specs=HBM,
        input_output_aliases={0: 0},
        cost_estimate=COST,
    )(value, tie)


def run_final(down, up, kept, other, scales, shares, hidden):
    width = kept.shape[2]
    size, wide = width // shares, hidden // shares
    shapes = ((2, CONV_B, size), (2, size), (2, size), (2, size), (2, size, hidden), (2, wide), (2, wide, width), (2, size), (2, size))
    return pl.pallas_call(
        final_kernel,
        out_shape=tuple(jax.ShapeDtypeStruct(shape, F32) for shape in shapes),
        in_specs=[VMEM] * 7,
        out_specs=(VMEM,) * len(shapes),
        compiler_params=pltpu.CompilerParams(vmem_limit_bytes=VMEM_LIMIT // 2),
        cost_estimate=COST,
    )(*down, *up, kept, other, scales)


def ring_order(count):
    return list(range(0, count, 2)) + list(range(count - 1, 0, -2))


def ring_owners(ways, axis):
    count = lax.axis_size(axis)
    device = lax.axis_index(axis)
    mine = jnp.where(device % 2 == 0, device // 2, count - 1 - device // 2)
    places = jnp.stack([lax.rem(mine - way * (1 + jnp.arange(count, dtype=jnp.int32)) + 2 * count, count) for way in ways])
    return jnp.where(places < count - count // 2, 2 * places, 2 * (count - places) - 1)


def after(value, earlier):
    return lax.optimization_barrier((value, earlier))[0]


def ring_step(flows, ways, axis):
    count = lax.axis_size(axis)
    order = ring_order(count)
    return [
        lax.ppermute(value, axis, [(order[p], order[(p + way) % count]) for p in range(count)]) for value, way in zip(flows, ways)
    ]


def per_device(
    inputs,
    segment_ids,
    cotangent,
    conv_weight,
    conv_bias,
    norm_gain,
    norm_bias,
    up_weight,
    up_bias,
    down_weight,
    down_bias,
    layer_scale,
):
    micro, _, frames, width = inputs.shape
    hidden = up_weight.shape[2]
    shares = lax.axis_size("dp")
    section = lax.axis_index("section")
    chip, core = section // 2, section % 2
    exchange = [(0, 1), (1, 0), (2, 3), (3, 2)]

    small = jnp.concatenate(
        [
            conv_weight,
            conv_bias[:, None],
            norm_gain[:, None],
            norm_bias[:, None],
            down_bias[:, None],
            layer_scale[:, None],
            up_bias.reshape(2, -1, width),
            jnp.zeros((2, 1, width), BF16),
        ],
        axis=1,
    )
    small_peer = lax.ppermute(small, "section", exchange)
    up_peer = lax.ppermute(up_weight, "section", exchange)
    down_peer = lax.ppermute(down_weight, "section", exchange)
    vec = jnp.where(core == 0, jnp.concatenate([small, small_peer]), jnp.concatenate([small_peer, small])).astype(F32)
    weights = (up_weight, down_weight, up_peer, down_peer)
    masks = jnp.broadcast_to(segment_ids[:, 0, :, None].astype(F32), (micro, frames, LANES))
    inputs, cotangent = inputs[:, 0], cotangent[:, 0]

    def flags(active, row, choice=0):
        return jnp.stack([jnp.asarray(v, jnp.int32) for v in (active, core, 2 * core + row, row, choice)])

    first, last = chip == 0, chip == 1
    ways = ((1, -1), (-1, 1))
    owners = ring_owners([way for kind in ways for way in kind], "dp")

    def row_of(array, row):
        return lax.dynamic_index_in_dim(array, 2 * core + row, 0, keepdims=False)

    down_pairs, up_pairs = [(0, 2), (1, 3)], [(2, 0), (3, 1)]
    state = run_forward(flags(first, 0), row_of(inputs, 0), masks, vec, weights, ())
    arrived = lax.ppermute(state[6], "section", down_pairs)
    state = run_forward(flags(first, 1), row_of(inputs, 1), masks, vec, weights, state[:6])
    arrived_next = lax.ppermute(state[6], "section", down_pairs)
    state = run_forward(flags(last, 0), near(arrived), masks, vec, weights, state[:6])
    gradient = row_of(cotangent, 0)
    back = run_backward(flags(last, 0), (gradient, gradient), masks, vec, weights, state[1:4], ())
    returned = lax.ppermute(back[5], "section", up_pairs)
    state = run_forward(flags(last, 1), near(arrived_next), masks, vec, weights, state[:6])
    gradients = (row_of(cotangent, 1), near(returned))
    back = run_backward(flags(True, jnp.where(last, 1, 0), first), gradients, masks, vec, weights, state[1:4], back[:5], riders=state[4:6])
    returned = near(lax.ppermute(back[5], "section", up_pairs))
    gb, gp, vectors, grads_kept, grads_other, _, outputs_kept, outputs_other = back

    def assemble(mine, other, tie):
        return run_place(mine, lax.ppermute(other, "section", exchange), 2 * (1 - core), tie)[None, :, None]

    section_outputs = assemble(outputs_kept, outputs_other, vectors)
    sums = run_weights(flags(last, 0), owners, weights, state[0], gb, state[2], gp, vectors, (returned, section_outputs))
    shard = lax.axis_index("dp")
    scales = jnp.stack([down_bias, layer_scale]).astype(F32)
    scales = lax.dynamic_slice_in_dim(scales, shard * (width // shares), width // shares, 2)
    *sums, grads_kept, grads_other = run_backward(
        flags(first, 1),
        (returned, returned),
        masks,
        vec,
        weights,
        state[1:4],
        (*sums, grads_kept, grads_other),
        (owners, state[0], gb, gp, vectors),
        (scales,),
    )

    kept, kept_last, head, tail = sums
    head = lax.ppermute(head, "section", exchange)
    tail = lax.ppermute(hold(tail, head), "section", exchange)
    size = hidden // shares
    spans = (slice(0, size + VECTORS), slice(size + VECTORS, None))

    def addend(stop, kind, layer):
        other = head[stop, layer, spans[kind]] if stop < HEAD else tail[stop - HEAD, layer, spans[kind]]
        return kept[stop, layer, spans[kind]].astype(F32) + other.astype(F32)

    flows = [[addend(0, kind, layer).astype(BF16) for layer in range(2)] for kind in (DOWN, UP)]
    for stop in range(1, shares):
        for kind in (DOWN, UP):
            moved = ring_step(flows[kind], ways[kind], "dp")
            if kind == DOWN or stop > 1:
                moved = after(moved, flows[1 - kind])
            if stop < shares - 1:
                moved = [(value.astype(F32) + addend(stop, kind, layer)).astype(BF16) for layer, value in enumerate(moved)]
            flows[kind] = moved
        if stop == 3:
            input_grads = assemble(grads_kept, hold(grads_other, flows[UP][0]), flows[UP][0])
    grads = run_final(flows[DOWN], flows[UP], kept_last, tail[-1], scales, shares, hidden)
    return (section_outputs, input_grads, *grads)


def solution(mesh):
    in_specs = (
        P(None, "dp", None, None),
        P(None, "dp", None),
        P(None, "dp", None, None),
        P("section", None, None),
        P("section", None),
        P("section", None),
        P("section", None),
        P("section", None, None),
        P("section", None),
        P("section", None, None),
        P("section", None),
        P("section", None),
    )
    out_specs = (
        P("section", None, "dp", None, None),
        P("section", None, "dp", None, None),
        P("section", None, "dp"),
        P("section", "dp"),
        P("section", "dp"),
        P("section", "dp"),
        P("section", "dp", None),
        P("section", "dp"),
        P("section", "dp", None),
        P("section", "dp"),
        P("section", "dp"),
    )
    return jax.shard_map(per_device, mesh=mesh, in_specs=in_specs, out_specs=out_specs, check_vma=False)
```

```python
import functools

import jax
import jax.numpy as jnp
from jax import lax
from jax.experimental import pallas as pl
from jax.experimental.pallas import tpu as pltpu
from jax.sharding import PartitionSpec as P

EPSILON = 1e-06
INV_SQRT2 = 0.7071067811865476
INV_SQRT_PI = 0.5641895835477563
LOG2_E = 1.4426950408889634
F32 = jnp.float32
BF16 = jnp.bfloat16
TILE = 32
PAD = 8
COLS = 256
VMEM_LIMIT = 60 * 2**20
COST = pl.CostEstimate(flops=1, bytes_accessed=1, transcendentals=0)

CONV_B, GAIN, SHIFT, DOWN_B, SCALE, UP_B, VEC_ROWS = 7, 8, 9, 10, 11, 12, 16
XHAT, STREAM, NORMED, KINDS = 0, 1, 2, 3
LANES = 128
OFFSETS = (1, 2, 3, -1, -2, -3)
MASK_OF = {offset: k for k, offset in enumerate(OFFSETS)}


def slabs(width):
    return [slice(c, c + LANES) for c in range(0, width, LANES)]


def row_sum(parts):
    return jnp.sum(functools.reduce(jnp.add, parts), axis=1, keepdims=True)


def fold(value):
    return functools.reduce(jnp.add, [value[8 * i : 8 * i + 8] for i in range(value.shape[0] // 8)])


def clear_edges(padded, frames):
    for slab in range(padded.shape[0]):
        padded[slab, 0:PAD, :] = jnp.zeros((PAD, LANES), F32)
        padded[slab, PAD + frames : PAD + frames + PAD, :] = jnp.zeros((PAD, LANES), F32)


def build_masks(seg_v, masks):
    frames = masks.shape[1]
    seg_v[0:PAD, :] = jnp.full((PAD, LANES), -1.0, F32)
    seg_v[PAD + frames : PAD + frames + PAD, :] = jnp.full((PAD, LANES), -1.0, F32)

    def body(i, carry):
        base = pl.multiple_of(i * 64, 64)
        here = seg_v[pl.ds(base + PAD, 64), :]
        for k, offset in enumerate(OFFSETS):
            there = seg_v[pl.ds(base + PAD + offset, 64), :]
            masks[k, pl.ds(base, 64), :] = jnp.where(there == here, 1.0, 0.0)
        return carry

    lax.fori_loop(0, frames // 64, body, 0)


def start_weights(core, layer, own, peer, target, sem):
    @pl.when(core == lax.div(layer, 2))
    def _():
        pltpu.make_async_copy(own.at[lax.rem(layer, 2)], target, sem).start()

    @pl.when(core != lax.div(layer, 2))
    def _():
        pltpu.make_async_copy(peer.at[lax.rem(layer, 2)], target, sem).start()


def send_row(core, section, source, kept, other, sem):
    @pl.when(core == section)
    def _():
        pltpu.make_async_copy(source, kept, sem).start()

    @pl.when(core != section)
    def _():
        pltpu.make_async_copy(source, other, sem).start()


def forward_kernel(layers, aliased, flags, x_in, seg_hbm, vec, own_up, own_down, peer_up, peer_down, *rest):
    rest = rest[aliased:]
    hid, dge, saved, rst, kept, other, send = rest[:7]
    (up_v, down_v, hid_v, dge_v, saved_v, rst_v, stream, acc, out_v, x_v, seg_v, masks, w_sem, in_sem, o_sem, s_sem) = rest[7:]
    frames, width = acc.shape
    hidden = hid_v.shape[2]

    @pl.when(flags[0] == 1)
    def _():
        core, micro, row = flags[1], flags[2], flags[3]
        pltpu.make_async_copy(x_in, x_v, s_sem.at[2]).start()
        pltpu.make_async_copy(seg_hbm.at[micro], seg_v.at[pl.ds(PAD, frames)], in_sem).start()
        def fetch(j):
            start_weights(core, j, own_up, peer_up, up_v.at[j], w_sem.at[j, 0])
            start_weights(core, j, own_down, peer_down, down_v.at[j], w_sem.at[j, 1])

        fetch(0)
        clear_edges(stream, frames)
        pltpu.make_async_copy(seg_hbm.at[0], seg_v.at[pl.ds(PAD, frames)], in_sem).wait()
        build_masks(seg_v, masks)
        pltpu.make_async_copy(x_in, x_v, s_sem.at[2]).wait()
        for c, cols in enumerate(slabs(width)):
            stream[c, PAD : PAD + frames, :] = x_v[:, cols].astype(F32)

        def layer(j, carry):
            def conv_norm(i, c):
                base = pl.multiple_of(i * TILE, TILE)
                rows = pl.ds(base, TILE)
                parts = []
                for s, cols in enumerate(slabs(width)):
                    centre = stream[s, pl.ds(base + PAD, TILE), :]
                    saved_v[j, STREAM, rows, cols] = centre.astype(BF16)
                    total = vec[j, CONV_B : CONV_B + 1, cols] + vec[j, 3:4, cols] * centre
                    for offset in OFFSETS:
                        neighbour = stream[s, pl.ds(base + PAD + offset, TILE), :] * masks[MASK_OF[offset], rows, :]
                        total = total + vec[j, offset + 3 : offset + 4, cols] * neighbour
                    parts.append(total)
                mean = row_sum(parts) * (1.0 / width)
                parts = [part - mean for part in parts]
                rstd = lax.rsqrt(row_sum([part * part for part in parts]) * (1.0 / width) + EPSILON)
                for part, cols in zip(parts, slabs(width)):
                    xhat = part * rstd
                    saved_v[j, XHAT, rows, cols] = xhat.astype(BF16)
                    saved_v[j, NORMED, rows, cols] = (xhat * vec[j, GAIN : GAIN + 1, cols] + vec[j, SHIFT : SHIFT + 1, cols]).astype(BF16)
                rst_v[j, rows, :] = jnp.broadcast_to(rstd, (TILE, LANES))
                return c

            lax.fori_loop(0, frames // TILE, conv_norm, 0, unroll=8)
            pltpu.make_async_copy(saved_v.at[j], saved.at[row, j], o_sem.at[j, 3]).start()
            pltpu.make_async_copy(rst_v.at[j], rst.at[row, j], o_sem.at[j, 2]).start()
            pltpu.make_async_copy(own_up.at[0], up_v.at[j], w_sem.at[j, 0]).wait()

            @pl.when(j + 1 < layers)
            def _():
                fetch(j + 1)

            pltpu.make_async_copy(own_down.at[0], down_v.at[j], w_sem.at[j, 1]).wait()
            half = frames // 2
            for part in range(2):
                here = slice(part * half, (part + 1) * half)
                for n in range(hidden // COLS):
                    cols = slice(n * COLS, (n + 1) * COLS)
                    if part == 1 and n % 2 == 1 and n // 2 < width // COLS:
                        out = slice(n // 2 * COLS, (n // 2 + 1) * COLS)
                        acc[0:half, out] = jnp.dot(hid_v[j, 0:half, :], down_v[j, :, out], preferred_element_type=F32)
                    at, start = UP_B + n * COLS // width, (n * COLS) % width
                    value = jnp.dot(saved_v[j, NORMED, here], up_v[j, :, cols], preferred_element_type=F32) + vec[j, at : at + 1, start : start + COLS]
                    scaled = value * INV_SQRT2
                    phi_sum = 0.5 + 0.5 * lax.erf(scaled)
                    hid_v[j, here, cols] = (value * phi_sum).astype(BF16)
                    dge_v[j, here, cols] = (phi_sum + scaled * INV_SQRT_PI * jnp.exp2(scaled * scaled * -LOG2_E)).astype(BF16)
            pltpu.make_async_copy(hid_v.at[j], hid.at[row, j], o_sem.at[j, 0]).start()
            pltpu.make_async_copy(dge_v.at[j], dge.at[row, j], o_sem.at[j, 1]).start()
            acc[half:, :] = jnp.dot(hid_v[j, half:, :], down_v[j], preferred_element_type=F32)

            def finish(ends_section, i, c):
                base = pl.multiple_of(i * TILE, TILE)
                rows = pl.ds(base, TILE)
                for s, cols in enumerate(slabs(width)):
                    inner = pl.ds(pl.multiple_of(base + PAD, 8), TILE)
                    branch = acc[rows, cols] + vec[j, DOWN_B : DOWN_B + 1, cols]
                    fresh = stream[s, inner, :] + vec[j, SCALE : SCALE + 1, cols] * branch
                    if ends_section:
                        rounded = fresh.astype(BF16)
                        out_v[lax.div(j, 2), rows, cols] = fresh
                        x_v[rows, cols] = rounded
                        fresh = rounded.astype(F32)
                    stream[s, inner, :] = fresh
                return c

            @pl.when(lax.rem(j, 2) == 1)
            def _():
                lax.fori_loop(0, frames // TILE, functools.partial(finish, True), 0)

            @pl.when(lax.rem(j, 2) == 0)
            def _():
                lax.fori_loop(0, frames // TILE, functools.partial(finish, False), 0)

            @pl.when(j == 1)
            def _():
                send_row(core, 0, out_v.at[0], kept.at[micro], other.at[row], s_sem.at[0])

            return carry

        lax.fori_loop(0, layers, layer, 0)
        send_row(core, 1, out_v.at[1], kept.at[micro], other.at[row], s_sem.at[1])
        pltpu.make_async_copy(x_v, send, s_sem.at[2]).start()
        for j in range(layers):
            pltpu.make_async_copy(hid_v.at[j], hid.at[row, j], o_sem.at[j, 0]).wait()
            pltpu.make_async_copy(dge_v.at[j], dge.at[row, j], o_sem.at[j, 1]).wait()
            pltpu.make_async_copy(rst_v.at[j], rst.at[row, j], o_sem.at[j, 2]).wait()
            pltpu.make_async_copy(saved_v.at[j], saved.at[row, j], o_sem.at[j, 3]).wait()
        pltpu.make_async_copy(out_v.at[0], other.at[row], s_sem.at[0]).wait()
        pltpu.make_async_copy(out_v.at[1], other.at[row], s_sem.at[1]).wait()
        pltpu.make_async_copy(x_v, send, s_sem.at[2]).wait()


SUMS, HEAD = 4, 2
DOWN, UP = 0, 1
VECTORS = 16


def send_sums(core, section, owners, kind, layer, source, vectors, targets, sem):
    kept, kept_last, head, tail = targets
    _, _, block, width = kept.shape
    shares = kept.shape[0] + 1
    size = (block - VECTORS) // 2
    first = 0 if kind == DOWN else size + VECTORS
    columns = source.shape[1] // width
    rows = size // columns
    for stop in range(shares):
        owner = owners[2 * kind + layer, stop]
        pieces = [
            (source.at[pl.ds(pl.multiple_of(owner * rows, 16), rows), pl.ds(b * width, width)], pl.ds(first + b * rows, rows))
            for b in range(columns)
        ]
        if vectors is not None:
            pieces.append((vectors.at[owners[2 * DOWN + layer, stop]], pl.ds(size, VECTORS)))
        for piece, place in pieces:

            @pl.when(core == section)
            def _():
                target = kept.at[stop, layer] if stop < shares - 1 else kept_last.at[layer]
                pltpu.make_async_copy(piece, target.at[place], sem).start()

            @pl.when(core != section)
            def _():
                target = head.at[stop, layer] if stop < HEAD else tail.at[stop - HEAD, layer]
                pltpu.make_async_copy(piece, target.at[place], sem).start()


def pack_vectors(sums, packed):
    shares, _, width = packed.shape
    parts = [sums[r : r + 1, :] for r in range(UP_B, VEC_ROWS - 1)]
    wide = jnp.broadcast_to(jnp.concatenate(parts, axis=1), (8, width * len(parts)))
    size, wide_size = width // shares, width * len(parts) // shares
    is_bias = lax.broadcasted_iota(jnp.int32, (VECTORS, width), 0) == UP_B
    for d in range(shares):
        part = sums if d == 0 else pltpu.roll(sums, width - d * size, 1)
        bias = wide if d == 0 else pltpu.roll(wide, wide.shape[1] - d * wide_size, 1)
        packed[d] = jnp.where(is_bias, jnp.broadcast_to(bias[0:1, :width], (VECTORS, width)), part).astype(BF16)


def backward_kernel(final, aliased, ties, riders, flags, g_one, g_two, seg_hbm, vec, own_up, own_down, peer_up, peer_down, dge, saved, rst, *rest):
    if final:
        owners, hid, gb, gp, vec_in = rest[:5]
        rest = rest[5 + ties + aliased :]
        sums_out, (kept, other) = rest[:SUMS], rest[SUMS : SUMS + 2]
        rest = rest[SUMS + 2 :]
    else:
        rest = rest[aliased:]
        gb, gp, vec_out, kept, other, send = rest[:6]
        rest = rest[6 + riders :]
    (up_v, down_v, dge_v, saved_v, rst_v, gb_v, gp_v, vg_v, g_now, fresh_v, gn_v, padded, x_v, seg_v, masks, w_sem, in_sem, g_sem, o_sem, s_sem) = rest[:20]
    if final:
        (hid_v, nrm_v, dwd_v, dwu_v, early_v, packed, b_sem) = rest[20:]
    frames, width = g_now.shape
    held, _, hidden = dge_v.shape
    layers = vec.shape[0]
    nt = (((1,), (1,)), ((), ()))
    tn = (((0,), (0,)), ((), ()))
    tall = 2 * TILE
    cols_of = slabs(width)

    @pl.when(flags[0] == 1)
    def _():
        core, micro, row = flags[1], flags[2], flags[3]
        pltpu.make_async_copy(seg_hbm.at[micro], seg_v.at[pl.ds(PAD, frames)], in_sem).start()

        def fetch(j):
            h = lax.rem(j, held)
            start_weights(core, j, own_down, peer_down, down_v.at[h], w_sem.at[h, 1])
            pltpu.make_async_copy(dge.at[row, j], dge_v.at[h], w_sem.at[h, 3]).start()
            start_weights(core, j, own_up, peer_up, up_v.at[h], w_sem.at[h, 0])
            pltpu.make_async_copy(rst.at[row, j], rst_v.at[h], w_sem.at[h, 4]).start()
            pltpu.make_async_copy(saved.at[row, j, 0:2], saved_v.at[h], w_sem.at[h, 2]).start()

        if final:
            pltpu.make_async_copy(vec_in.at[1 - row], early_v, s_sem.at[2]).start()
        source = [pltpu.make_async_copy(g, x_v, g_sem) for g in (g_one, g_two)]
        for k in range(2):

            @pl.when(flags[4] == k)
            def _():
                source[k].start()

        fetch(layers - 1)
        clear_edges(padded, frames)
        source[0].wait()
        for cols in cols_of:

            def enter(t, c):
                rows = pl.ds(pl.multiple_of(t * tall, tall), tall)
                scaled = (vec[layers - 1, SCALE : SCALE + 1, cols] * x_v[rows, cols].astype(F32)).astype(BF16)
                gb_v[layers, 0, rows, cols] = scaled
                return c + fold(scaled.astype(F32))

            total = lax.fori_loop(0, frames // tall, enter, jnp.zeros((8, LANES), F32))
            vg_v[layers, DOWN_B : DOWN_B + 1, cols] = jnp.sum(total, axis=0, keepdims=True)
        pltpu.make_async_copy(seg_hbm.at[0], seg_v.at[pl.ds(PAD, frames)], in_sem).wait()
        build_masks(seg_v, masks)

        def layer(step, carry):
            j = layers - 1 - step
            h = lax.rem(j, held)
            if not final:
                pltpu.make_async_copy(gb_v.at[j + 1, 0], gb.at[row, j], o_sem.at[j, 0]).start()
            pltpu.make_async_copy(own_down.at[0], down_v.at[h], w_sem.at[h, 1]).wait()
            pltpu.make_async_copy(dge.at[0, 0], dge_v.at[h], w_sem.at[h, 3]).wait()
            if final:
                pltpu.make_async_copy(hid.at[row, j], hid_v.at[h, 0], b_sem.at[h, 0]).start()
                pltpu.make_async_copy(hid.at[1 - row, j], hid_v.at[h, 1], b_sem.at[h, 1]).start()
                pltpu.make_async_copy(gb.at[1 - row, j], gb_v.at[j + 1, 1], b_sem.at[h, 4]).start()
                pltpu.make_async_copy(saved.at[row, j, NORMED], nrm_v.at[h, 0], b_sem.at[h, 2]).start()
                pltpu.make_async_copy(saved.at[1 - row, j, NORMED], nrm_v.at[h, 1], b_sem.at[h, 3]).start()
                pltpu.make_async_copy(gp.at[1 - row, j], gp_v.at[h, 1], b_sem.at[h, 5]).start()
            for n in range(hidden // COLS):
                cols = slice(n * COLS, (n + 1) * COLS)
                value = lax.dot_general(gb_v[j + 1, 0], down_v[h, cols, :], nt, preferred_element_type=F32)
                rounded = (value * dge_v[h, :, cols].astype(F32)).astype(BF16)
                gp_v[h, 0, :, cols] = rounded
                at, start = UP_B + n * COLS // width, (n * COLS) % width
                vg_v[j + 1, at : at + 1, start : start + COLS] = jnp.sum(rounded.astype(F32), axis=0, keepdims=True)
            if not final:
                pltpu.make_async_copy(gp_v.at[h, 0], gp.at[row, j], o_sem.at[j, 1]).start()
            pltpu.make_async_copy(own_up.at[0], up_v.at[h], w_sem.at[h, 0]).wait()
            gn_v[...] = lax.dot_general(gp_v[h, 0], up_v[h], nt, preferred_element_type=F32)
            pltpu.make_async_copy(rst.at[0, 0], rst_v.at[h], w_sem.at[h, 4]).wait()
            pltpu.make_async_copy(saved.at[0, 0, 0:2], saved_v.at[h], w_sem.at[h, 2]).wait()

            @pl.when(j > 0)
            def _():
                fetch(j - 1)

            if final:
                pltpu.make_async_copy(hid.at[0, 0], hid_v.at[h, 0], b_sem.at[h, 0]).wait()
                pltpu.make_async_copy(hid.at[0, 0], hid_v.at[h, 1], b_sem.at[h, 1]).wait()
                pltpu.make_async_copy(gb.at[0, 0], gb_v.at[j + 1, 1], b_sem.at[h, 4]).wait()

                @pl.when(j + held < layers)
                def _():
                    pltpu.make_async_copy(dwd_v.at[h], dwd_v.at[h], o_sem.at[h, 0]).wait()
                    pltpu.make_async_copy(dwu_v.at[h], dwu_v.at[h], o_sem.at[h, 1]).wait()
                    pltpu.make_async_copy(packed.at[h], packed.at[h], o_sem.at[h, 1]).wait()

            def down_chunk(n):
                rows = slice(n * COLS, (n + 1) * COLS)
                left = hid_v[h, :, :, rows].reshape(2 * frames, COLS)
                right = gb_v[j + 1].reshape(2 * frames, width)
                value = lax.dot_general(left, right, tn, preferred_element_type=F32)
                dwd_v[h, rows, :] = value.astype(BF16)
                return fold(value * down_v[h, rows, :].astype(F32))

            def up_chunk(m, n):
                rows = slice(m * COLS, (m + 1) * COLS)
                cols = slice(n * width, (n + 1) * width)
                left = nrm_v[h, :, :, rows].reshape(2 * frames, COLS)
                right = gp_v[h, :, :, cols].reshape(2 * frames, width)
                dwu_v[h, rows, cols] = lax.dot_general(left, right, tn, preferred_element_type=F32).astype(BF16)

            odd = lax.rem(j, 2) == 1

            def norm_back(t, c):
                base = t * TILE if isinstance(t, int) else pl.multiple_of(t * TILE, TILE)
                rows = pl.ds(base, TILE)
                inner = pl.ds(base + PAD if isinstance(t, int) else pl.multiple_of(base + PAD, 8), TILE)
                grads = [gn_v[rows, cols] for cols in cols_of]
                xhats = [saved_v[h, XHAT, rows, cols].astype(F32) for cols in cols_of]
                qs = [grad * vec[j, GAIN : GAIN + 1, cols] for grad, cols in zip(grads, cols_of)]
                mean_q = row_sum(qs) * (1.0 / width)
                mean_qx = row_sum([q * xhat for q, xhat in zip(qs, xhats)]) * (1.0 / width)
                rstd = rst_v[h, rows, :]
                out = []
                for s, cols in enumerate(cols_of):
                    grad_conv = rstd * (qs[s] - mean_q - xhats[s] * mean_qx)
                    padded[s, inner, :] = grad_conv
                    g_now[rows, cols] = jnp.where(odd, x_v[rows, cols].astype(F32), fresh_v[rows, cols])
                    out += [c[3 * s] + fold(grads[s] * xhats[s]), c[3 * s + 1] + fold(grads[s]), c[3 * s + 2] + fold(grad_conv)]
                return tuple(out)

            sums = (jnp.zeros((8, LANES), F32),) * (3 * len(cols_of))
            tiles = frames // TILE
            if final:
                parts = hidden // COLS
                scale = jnp.zeros((8, width), F32)
                done = 0
                for n in range(parts):
                    scale = scale + down_chunk(n)
                    while done < tiles * (n + 1) // parts:
                        sums = norm_back(done, sums)
                        done += 1
                vg_v[j + 1, SCALE : SCALE + 1, :] = jnp.sum(scale, axis=0, keepdims=True)
                send_sums(core, lax.div(j, 2), owners, DOWN, lax.rem(j, 2), dwd_v.at[h], None, sums_out, o_sem.at[h, 0])
                pltpu.make_async_copy(saved.at[0, 0, 0], nrm_v.at[h, 0], b_sem.at[h, 2]).wait()
                pltpu.make_async_copy(saved.at[0, 0, 0], nrm_v.at[h, 1], b_sem.at[h, 3]).wait()
                pltpu.make_async_copy(gp.at[0, 0], gp_v.at[h, 1], b_sem.at[h, 5]).wait()
            else:
                sums = lax.fori_loop(0, tiles, norm_back, sums, unroll=8)
            for s, cols in enumerate(cols_of):
                for k, at in enumerate((GAIN, SHIFT, CONV_B)):
                    vg_v[j + 1, at : at + 1, cols] = jnp.sum(sums[3 * s + k], axis=0, keepdims=True)

            @pl.when(odd & (step > 0))
            def _():
                pltpu.make_async_copy(fresh_v, other.at[row], s_sem.at[0]).wait()

            below = lax.max(j - 1, 0)
            for s, cols in enumerate(cols_of):

                def conv_back(t, c):
                    base = t * tall if isinstance(t, int) else pl.multiple_of(t * tall, tall)
                    rows = pl.ds(base, tall)
                    source = saved_v[h, STREAM, rows, cols].astype(F32)
                    centre = padded[s, pl.ds(base + PAD if isinstance(t, int) else pl.multiple_of(base + PAD, 8), tall), :]
                    total = g_now[rows, cols] + vec[j, 3:4, cols] * centre
                    taps = [None] * 7
                    taps[3] = c[3] + fold(centre * source)
                    for offset in OFFSETS:
                        term = padded[s, pl.ds(base + PAD - offset, tall), :] * masks[MASK_OF[-offset], rows, :]
                        total = total + vec[j, offset + 3 : offset + 4, cols] * term
                        taps[offset + 3] = c[offset + 3] + fold(term * source)
                    rounded = total.astype(BF16)
                    fresh_v[rows, cols] = total
                    x_v[rows, cols] = rounded
                    scaled = (vec[below, SCALE : SCALE + 1, cols] * jnp.where(odd, total, rounded.astype(F32))).astype(BF16)
                    gb_v[j, 0, rows, cols] = scaled
                    return tuple(taps) + (c[7] + fold(scaled.astype(F32)),)

                sums = (jnp.zeros((8, LANES), F32),) * 8
                if final:
                    chunks = [(m, n) for m in range(width // COLS) for n in range(hidden // width)]
                    each = -(-len(chunks) // len(cols_of))
                    mine = chunks[s * each : (s + 1) * each]
                    done = 0
                    for k, (m, n) in enumerate(mine):
                        up_chunk(m, n)
                        while done < frames // tall * (k + 1) // len(mine):
                            sums = conv_back(done, sums)
                            done += 1
                    while done < frames // tall:
                        sums = conv_back(done, sums)
                        done += 1
                else:
                    sums = lax.fori_loop(0, frames // tall, conv_back, sums, unroll=8)
                for k in range(7):
                    vg_v[j + 1, k : k + 1, cols] = jnp.sum(sums[k], axis=0, keepdims=True)
                vg_v[j, DOWN_B : DOWN_B + 1, cols] = jnp.sum(sums[7], axis=0, keepdims=True)
            if final:

                @pl.when(step == 0)
                def _():
                    pltpu.make_async_copy(vec_in.at[0], early_v, s_sem.at[2]).wait()

                pack_vectors(vg_v[j + 1] + early_v[j], packed.at[h])
                send_vectors = packed.at[h]
                send_sums(core, lax.div(j, 2), owners, UP, lax.rem(j, 2), dwu_v.at[h], send_vectors, sums_out, o_sem.at[h, 1])

            @pl.when(jnp.logical_not(odd))
            def _():
                send_row(core, lax.div(j, 2), fresh_v, kept.at[micro], other.at[row], s_sem.at[0])

            return carry

        for i in range(1, layers + 1):
            vg_v[i, SCALE : SCALE + 1, :] = jnp.zeros((1, width), F32)
            vg_v[i, VEC_ROWS - 1 : VEC_ROWS, :] = jnp.zeros((1, width), F32)
        lax.fori_loop(0, layers, layer, 0)
        if final:
            for h in range(held):
                pltpu.make_async_copy(dwd_v.at[h], dwd_v.at[h], o_sem.at[h, 0]).wait()
                pltpu.make_async_copy(dwu_v.at[h], dwu_v.at[h], o_sem.at[h, 1]).wait()
                pltpu.make_async_copy(packed.at[h], packed.at[h], o_sem.at[h, 1]).wait()
        else:
            pltpu.make_async_copy(vg_v.at[pl.ds(1, layers)], vec_out.at[row], s_sem.at[2]).start()
            pltpu.make_async_copy(x_v, send, s_sem.at[1]).start()
            for j in range(layers):
                pltpu.make_async_copy(gb_v.at[j + 1, 0], gb.at[row, j], o_sem.at[j, 0]).wait()
                pltpu.make_async_copy(gp_v.at[j, 0], gp.at[row, j], o_sem.at[j, 1]).wait()
            pltpu.make_async_copy(x_v, send, s_sem.at[1]).wait()
            pltpu.make_async_copy(vg_v.at[pl.ds(1, layers)], vec_out.at[row], s_sem.at[2]).wait()
        pltpu.make_async_copy(fresh_v, other.at[row], s_sem.at[0]).wait()


def weight_kernel(ties, flags, owners, own_down, peer_down, all_hid, all_gb, all_saved, all_gp, vec_in, *rest):
    rest = rest[ties:]
    sums_out, rest = rest[:SUMS], rest[SUMS:]
    hid_v, gb_v, nrm_v, gp_v, down_v, dwd_v, dwu_v, vec_v, packed, sem, o_sem, s_sem = rest
    frames, width = gb_v.shape[2:]
    hidden = hid_v.shape[3]
    layers = all_hid.shape[1]
    tn = (((0,), (0,)), ((), ()))

    @pl.when(flags[0] == 1)
    def _():
        core = flags[1]

        def copies(j, h):
            pairs = []
            for row in range(2):
                pairs += [
                    (all_hid.at[row, j], hid_v.at[h, row]),
                    (all_gb.at[row, j], gb_v.at[h, row]),
                    (all_saved.at[row, j, NORMED], nrm_v.at[h, row]),
                    (all_gp.at[row, j], gp_v.at[h, row]),
                ]
            return [pltpu.make_async_copy(a, b, sem.at[h, k]) for k, (a, b) in enumerate(pairs)]

        def fetch(j):
            h = lax.rem(j, 2)
            start_weights(core, j, own_down, peer_down, down_v.at[h], sem.at[h, 8])
            for copy in copies(j, h):
                copy.start()

        fetch(layers - 1)
        pltpu.make_async_copy(vec_in, vec_v, s_sem).start()
        pltpu.make_async_copy(vec_in, vec_v, s_sem).wait()

        def layer(step, carry):
            j = layers - 1 - step
            h = lax.rem(j, 2)

            @pl.when(j > 0)
            def _():
                fetch(j - 1)

            pltpu.make_async_copy(own_down.at[0], down_v.at[h], sem.at[h, 8]).wait()
            for copy in copies(j, h):
                copy.wait()

            @pl.when(j + 2 < layers)
            def _():
                pltpu.make_async_copy(dwd_v.at[h], dwd_v.at[h], o_sem.at[h, 0]).wait()
                pltpu.make_async_copy(dwu_v.at[h], dwu_v.at[h], o_sem.at[h, 1]).wait()
                pltpu.make_async_copy(packed.at[h], packed.at[h], o_sem.at[h, 1]).wait()

            def down_chunk(n, scale):
                rows = pl.ds(pl.multiple_of(n * COLS, COLS), COLS)
                left = hid_v[h, :, :, rows].reshape(2 * frames, COLS)
                value = lax.dot_general(left, gb_v[h].reshape(2 * frames, width), tn, preferred_element_type=F32)
                dwd_v[h, rows, :] = value.astype(BF16)
                return scale + fold(value * down_v[h, rows, :].astype(F32))

            scale = lax.fori_loop(0, hidden // COLS, down_chunk, jnp.zeros((8, width), F32))
            scale = jnp.sum(scale, axis=0, keepdims=True)
            vectors = vec_v[0, j] + vec_v[1, j]
            is_scale = lax.broadcasted_iota(jnp.int32, vectors.shape, 0) == SCALE
            pack_vectors(jnp.where(is_scale, jnp.broadcast_to(scale, vectors.shape), vectors), packed.at[h])
            send_sums(core, lax.div(j, 2), owners, DOWN, lax.rem(j, 2), dwd_v.at[h], None, sums_out, o_sem.at[h, 0])

            def up_chunk(n, c):
                cols = pl.ds(pl.multiple_of(n * width, width), width)
                right = gp_v[h, :, :, cols].reshape(2 * frames, width)
                value = lax.dot_general(nrm_v[h].reshape(2 * frames, width), right, tn, preferred_element_type=F32)
                dwu_v[h, :, cols] = value.astype(BF16)
                return c

            lax.fori_loop(0, hidden // width, up_chunk, 0)
            send_sums(core, lax.div(j, 2), owners, UP, lax.rem(j, 2), dwu_v.at[h], packed.at[h], sums_out, o_sem.at[h, 1])
            return carry

        lax.fori_loop(0, layers, layer, 0)
        for h in range(2):
            pltpu.make_async_copy(dwd_v.at[h], dwd_v.at[h], o_sem.at[h, 0]).wait()
            pltpu.make_async_copy(dwu_v.at[h], dwu_v.at[h], o_sem.at[h, 1]).wait()
            pltpu.make_async_copy(packed.at[h], packed.at[h], o_sem.at[h, 1]).wait()


def place_kernel(at, kept_in, rows, tie, kept, held, sem):
    count = rows.shape[0]
    for i in range(count):
        pltpu.make_async_copy(rows.at[i], held.at[i], sem.at[i]).start()
    for i in range(count):
        pltpu.make_async_copy(rows.at[i], held.at[i], sem.at[i]).wait()
        pltpu.make_async_copy(held.at[i], kept.at[at[0] + i], sem.at[i]).start()
    for i in range(count):
        pltpu.make_async_copy(held.at[i], kept.at[at[0] + i], sem.at[i]).wait()


def hold_kernel(value_in, tie, value):
    pass


def final_kernel(down_0, down_1, up_0, up_1, kept, other, scales, *rest):
    conv_out, conv_b_out, gain_out, shift_out, up_out, up_b_out, down_out, down_b_out, scale_out = rest
    size, wide = conv_b_out.shape[1], up_b_out.shape[1]
    rows, width = down_out.shape[1:]
    for layer, (down, up) in enumerate(((down_0, up_0), (down_1, up_1))):
        total = down[...].astype(F32) + kept[layer, : rows + VECTORS].astype(F32) + other[layer, : rows + VECTORS].astype(F32)
        down_out[layer] = total[:rows]
        vectors = total[rows:]
        at = slice(layer, layer + 1)
        conv_out[layer] = vectors[:CONV_B, :size]
        conv_b_out[at, :] = vectors[CONV_B : CONV_B + 1, :size]
        gain_out[at, :] = vectors[GAIN : GAIN + 1, :size]
        shift_out[at, :] = vectors[SHIFT : SHIFT + 1, :size]
        down_b = vectors[DOWN_B : DOWN_B + 1, :size]
        down_b_out[at, :] = down_b
        scale_out[at, :] = (vectors[SCALE : SCALE + 1, :size] + scales[0, at, :] * down_b) / scales[1, at, :]
        up_b_out[at, :] = vectors[UP_B : UP_B + 1, :wide]
        total = up[...].astype(F32) + kept[layer, rows + VECTORS :].astype(F32) + other[layer, rows + VECTORS :].astype(F32)
        for b in range(up_out.shape[2] // width):
            up_out[layer, :, b * width : (b + 1) * width] = total[b * size : (b + 1) * size]


ANY = pl.BlockSpec(memory_space=pl.ANY)
HBM = pl.BlockSpec(memory_space=pltpu.HBM)
SMEM = pl.BlockSpec(memory_space=pltpu.SMEM)
VMEM = pl.BlockSpec(memory_space=pltpu.VMEM)


def near(value):
    return pltpu.with_memory_space_constraint(value, pltpu.VMEM)


def run_forward(flags, x, seg, vec, weights, earlier):
    layers = vec.shape[0]
    micro = seg.shape[0]
    frames, width = x.shape
    hidden = weights[0].shape[2]
    shapes = (
        jax.ShapeDtypeStruct((2, layers, frames, hidden), BF16),
        jax.ShapeDtypeStruct((2, layers, frames, hidden), BF16),
        jax.ShapeDtypeStruct((2, layers, KINDS, frames, width), BF16),
        jax.ShapeDtypeStruct((2, layers, frames, LANES), F32),
        jax.ShapeDtypeStruct((micro, frames, width), F32),
        jax.ShapeDtypeStruct((2, frames, width), F32),
        jax.ShapeDtypeStruct((frames, width), BF16),
    )
    aliased = len(earlier)
    return pl.pallas_call(
        functools.partial(forward_kernel, layers, aliased),
        out_shape=shapes,
        in_specs=[SMEM, ANY, ANY, VMEM] + [ANY] * (4 + aliased),
        out_specs=(ANY,) * len(shapes),
        input_output_aliases={8 + i: i for i in range(aliased)},
        scratch_shapes=[
            pltpu.VMEM((layers, width, hidden), BF16),
            pltpu.VMEM((layers, hidden, width), BF16),
            pltpu.VMEM((layers, frames, hidden), BF16),
            pltpu.VMEM((layers, frames, hidden), BF16),
            pltpu.VMEM((layers, KINDS, frames, width), BF16),
            pltpu.VMEM((layers, frames, LANES), F32),
            pltpu.VMEM((width // LANES, frames + 2 * PAD, LANES), F32),
            pltpu.VMEM((frames, width), F32),
            pltpu.VMEM((2, frames, width), F32),
            pltpu.VMEM((frames, width), BF16),
            pltpu.VMEM((frames + 2 * PAD, LANES), F32),
            pltpu.VMEM((6, frames, LANES), F32),
            pltpu.SemaphoreType.DMA((layers, 2)),
            pltpu.SemaphoreType.DMA,
            pltpu.SemaphoreType.DMA((layers, 4)),
            pltpu.SemaphoreType.DMA((3,)),
        ],
        compiler_params=pltpu.CompilerParams(vmem_limit_bytes=VMEM_LIMIT),
        cost_estimate=COST,
    )(flags, x, seg, vec, *weights, *earlier)


def sum_shapes(shares, hidden, width):
    block = (2, 2 * (hidden // shares) + VECTORS, width)
    return tuple(jax.ShapeDtypeStruct(shape, BF16) for shape in ((shares - 1, *block), block, (HEAD, *block), (shares - HEAD, *block)))


def run_backward(flags, g, seg, vec, weights, state, earlier, final=(), ties=(), riders=()):
    frames, width = g[0].shape
    hidden = weights[0].shape[2]
    layers, micro = vec.shape[0], seg.shape[0]
    rows, held = (2, 2) if final else (1, layers)
    grads = (
        jax.ShapeDtypeStruct((micro, frames, width), F32),
        jax.ShapeDtypeStruct((2, frames, width), F32),
    )
    if final:
        shapes = (*sum_shapes(final[0].shape[1], hidden, width), *grads)
    else:
        shapes = (
            jax.ShapeDtypeStruct((2, layers, frames, width), BF16),
            jax.ShapeDtypeStruct((2, layers, frames, hidden), BF16),
            jax.ShapeDtypeStruct((2, layers, VEC_ROWS, width), F32),
            *grads,
            jax.ShapeDtypeStruct((frames, width), BF16),
        )
    earlier = (*earlier, *riders)
    shapes = (*shapes, *(jax.ShapeDtypeStruct(rider.shape, rider.dtype) for rider in riders))
    aliased = len(earlier)
    targets = [*range(len(earlier) - len(riders)), *range(len(shapes) - len(riders), len(shapes))]
    scratch = [
        pltpu.VMEM((held, width, hidden), BF16),
        pltpu.VMEM((held, hidden, width), BF16),
        pltpu.VMEM((held, frames, hidden), BF16),
        pltpu.VMEM((held, 2, frames, width), BF16),
        pltpu.VMEM((held, frames, LANES), F32),
        pltpu.VMEM((layers + 1, rows, frames, width), BF16),
        pltpu.VMEM((held, rows, frames, hidden), BF16),
        pltpu.VMEM((layers + 1, VEC_ROWS, width), F32),
        pltpu.VMEM((frames, width), F32),
        pltpu.VMEM((frames, width), F32),
        pltpu.VMEM((frames, width), F32),
        pltpu.VMEM((width // LANES, frames + 2 * PAD, LANES), F32),
        pltpu.VMEM((frames, width), BF16),
        pltpu.VMEM((frames + 2 * PAD, LANES), F32),
        pltpu.VMEM((6, frames, LANES), F32),
        pltpu.SemaphoreType.DMA((held, 5)),
        pltpu.SemaphoreType.DMA,
        pltpu.SemaphoreType.DMA,
        pltpu.SemaphoreType.DMA((held, 2)),
        pltpu.SemaphoreType.DMA((3,)),
    ]
    if final:
        scratch += [
            pltpu.VMEM((held, 2, frames, hidden), BF16),
            pltpu.VMEM((held, 2, frames, width), BF16),
            pltpu.VMEM((held, hidden, width), BF16),
            pltpu.VMEM((held, width, hidden), BF16),
            pltpu.VMEM((layers, VEC_ROWS, width), F32),
            pltpu.VMEM((held, final[0].shape[1], VECTORS, width), BF16),
            pltpu.SemaphoreType.DMA((held, 6)),
        ]
    first_alias = 12 + len(final) + len(ties)
    return pl.pallas_call(
        functools.partial(backward_kernel, bool(final), aliased, len(ties), len(riders)),
        out_shape=shapes,
        in_specs=[SMEM, ANY, ANY, ANY, VMEM] + [ANY] * 7 + ([SMEM] + [ANY] * 4 if final else []) + [ANY] * (len(ties) + aliased),
        out_specs=tuple(HBM if final and k < SUMS else ANY for k in range(len(shapes))),
        input_output_aliases={first_alias + i: target for i, target in enumerate(targets)},
        scratch_shapes=scratch,
        compiler_params=pltpu.CompilerParams(vmem_limit_bytes=VMEM_LIMIT),
        cost_estimate=COST,
    )(flags, *g, seg, vec, *weights, *state, *final, *ties, *earlier)


def run_weights(flags, owners, weights, hid, gb, saved, gp, vectors, ties):
    _, layers, frames, hidden = hid.shape
    width = gb.shape[3]
    shares = owners.shape[1]
    return pl.pallas_call(
        functools.partial(weight_kernel, len(ties)),
        out_shape=sum_shapes(shares, hidden, width),
        in_specs=[SMEM, SMEM] + [ANY] * (7 + len(ties)),
        out_specs=(HBM,) * SUMS,
        scratch_shapes=[
            pltpu.VMEM((2, 2, frames, hidden), BF16),
            pltpu.VMEM((2, 2, frames, width), BF16),
            pltpu.VMEM((2, 2, frames, width), BF16),
            pltpu.VMEM((2, 2, frames, hidden), BF16),
            pltpu.VMEM((2, hidden, width), BF16),
            pltpu.VMEM((2, hidden, width), BF16),
            pltpu.VMEM((2, width, hidden), BF16),
            pltpu.VMEM(vectors.shape, F32),
            pltpu.VMEM((2, shares, VECTORS, width), BF16),
            pltpu.SemaphoreType.DMA((2, 9)),
            pltpu.SemaphoreType.DMA((2, 2)),
            pltpu.SemaphoreType.DMA,
        ],
        compiler_params=pltpu.CompilerParams(vmem_limit_bytes=VMEM_LIMIT),
        cost_estimate=COST,
    )(flags, owners, weights[1], weights[3], hid, gb, saved, gp, vectors, *ties)


def run_place(kept, rows, at, tie):
    return pl.pallas_call(
        place_kernel,
        out_shape=jax.ShapeDtypeStruct(kept.shape, kept.dtype),
        in_specs=[SMEM, ANY, ANY, ANY],
        out_specs=ANY,
        input_output_aliases={1: 0},
        scratch_shapes=[pltpu.VMEM(rows.shape, rows.dtype), pltpu.SemaphoreType.DMA(rows.shape[:1])],
        cost_estimate=COST,
    )(at.reshape(1).astype(jnp.int32), kept, rows, tie)


def hold(value, tie):
    return pl.pallas_call(
        hold_kernel,
        out_shape=jax.ShapeDtypeStruct(value.shape, value.dtype),
        in_specs=[HBM, ANY],
        out_specs=HBM,
        input_output_aliases={0: 0},
        cost_estimate=COST,
    )(value, tie)


def run_final(down, up, kept, other, scales, shares, hidden):
    width = kept.shape[2]
    size, wide = width // shares, hidden // shares
    shapes = ((2, CONV_B, size), (2, size), (2, size), (2, size), (2, size, hidden), (2, wide), (2, wide, width), (2, size), (2, size))
    return pl.pallas_call(
        final_kernel,
        out_shape=tuple(jax.ShapeDtypeStruct(shape, F32) for shape in shapes),
        in_specs=[VMEM] * 7,
        out_specs=(VMEM,) * len(shapes),
        compiler_params=pltpu.CompilerParams(vmem_limit_bytes=VMEM_LIMIT // 2),
        cost_estimate=COST,
    )(*down, *up, kept, other, scales)


def ring_order(count):
    return list(range(0, count, 2)) + list(range(count - 1, 0, -2))


def ring_owners(ways, axis):
    count = lax.axis_size(axis)
    device = lax.axis_index(axis)
    mine = jnp.where(device % 2 == 0, device // 2, count - 1 - device // 2)
    places = jnp.stack([lax.rem(mine - way * (1 + jnp.arange(count, dtype=jnp.int32)) + 2 * count, count) for way in ways])
    return jnp.where(places < count - count // 2, 2 * places, 2 * (count - places) - 1)


def after(value, earlier):
    return lax.optimization_barrier((value, earlier))[0]


def ring_step(flows, ways, axis):
    count = lax.axis_size(axis)
    order = ring_order(count)
    return [
        lax.ppermute(value, axis, [(order[p], order[(p + way) % count]) for p in range(count)]) for value, way in zip(flows, ways)
    ]


def per_device(
    inputs,
    segment_ids,
    cotangent,
    conv_weight,
    conv_bias,
    norm_gain,
    norm_bias,
    up_weight,
    up_bias,
    down_weight,
    down_bias,
    layer_scale,
):
    micro, _, frames, width = inputs.shape
    hidden = up_weight.shape[2]
    shares = lax.axis_size("dp")
    section = lax.axis_index("section")
    chip, core = section // 2, section % 2
    exchange = [(0, 1), (1, 0), (2, 3), (3, 2)]

    small = jnp.concatenate(
        [
            conv_weight,
            conv_bias[:, None],
            norm_gain[:, None],
            norm_bias[:, None],
            down_bias[:, None],
            layer_scale[:, None],
            up_bias.reshape(2, -1, width),
            jnp.zeros((2, 1, width), BF16),
        ],
        axis=1,
    )
    small_peer = lax.ppermute(small, "section", exchange)
    up_peer = lax.ppermute(up_weight, "section", exchange)
    down_peer = lax.ppermute(down_weight, "section", exchange)
    vec = jnp.where(core == 0, jnp.concatenate([small, small_peer]), jnp.concatenate([small_peer, small])).astype(F32)
    weights = (up_weight, down_weight, up_peer, down_peer)
    masks = jnp.broadcast_to(segment_ids[:, 0, :, None].astype(F32), (micro, frames, LANES))
    inputs, cotangent = inputs[:, 0], cotangent[:, 0]

    def flags(active, row, choice=0):
        return jnp.stack([jnp.asarray(v, jnp.int32) for v in (active, core, 2 * core + row, row, choice)])

    first, last = chip == 0, chip == 1
    ways = ((1, -1), (-1, 1))
    owners = ring_owners([way for kind in ways for way in kind], "dp")

    def row_of(array, row):
        return lax.dynamic_index_in_dim(array, 2 * core + row, 0, keepdims=False)

    down_pairs, up_pairs = [(0, 2), (1, 3)], [(2, 0), (3, 1)]
    state = run_forward(flags(first, 0), row_of(inputs, 0), masks, vec, weights, ())
    arrived = lax.ppermute(state[6], "section", down_pairs)
    state = run_forward(flags(first, 1), row_of(inputs, 1), masks, vec, weights, state[:6])
    arrived_next = lax.ppermute(state[6], "section", down_pairs)
    state = run_forward(flags(last, 0), near(arrived), masks, vec, weights, state[:6])
    gradient = row_of(cotangent, 0)
    back = run_backward(flags(last, 0), (gradient, gradient), masks, vec, weights, state[1:4], ())
    returned = lax.ppermute(back[5], "section", up_pairs)
    state = run_forward(flags(last, 1), near(arrived_next), masks, vec, weights, state[:6])
    gradients = (row_of(cotangent, 1), near(returned))
    back = run_backward(flags(True, jnp.where(last, 1, 0), first), gradients, masks, vec, weights, state[1:4], back[:5], riders=state[4:6])
    returned = near(lax.ppermute(back[5], "section", up_pairs))
    gb, gp, vectors, grads_kept, grads_other, _, outputs_kept, outputs_other = back

    def assemble(mine, other, tie):
        return run_place(mine, lax.ppermute(other, "section", exchange), 2 * (1 - core), tie)[None, :, None]

    section_outputs = assemble(outputs_kept, outputs_other, vectors)
    sums = run_weights(flags(last, 0), owners, weights, state[0], gb, state[2], gp, vectors, (returned, section_outputs))
    shard = lax.axis_index("dp")
    scales = jnp.stack([down_bias, layer_scale]).astype(F32)
    scales = lax.dynamic_slice_in_dim(scales, shard * (width // shares), width // shares, 2)
    *sums, grads_kept, grads_other = run_backward(
        flags(first, 1),
        (returned, returned),
        masks,
        vec,
        weights,
        state[1:4],
        (*sums, grads_kept, grads_other),
        (owners, state[0], gb, gp, vectors),
        (scales,),
    )

    kept, kept_last, head, tail = sums
    head = lax.ppermute(head, "section", exchange)
    tail = lax.ppermute(hold(tail, head), "section", exchange)
    size = hidden // shares
    spans = (slice(0, size + VECTORS), slice(size + VECTORS, None))

    def addend(stop, kind, layer):
        other = head[stop, layer, spans[kind]] if stop < HEAD else tail[stop - HEAD, layer, spans[kind]]
        return kept[stop, layer, spans[kind]].astype(F32) + other.astype(F32)

    flows = [[addend(0, kind, layer).astype(BF16) for layer in range(2)] for kind in (DOWN, UP)]
    for stop in range(1, shares):
        for kind in (DOWN, UP):
            moved = ring_step(flows[kind], ways[kind], "dp")
            if kind == DOWN or stop > 1:
                moved = after(moved, flows[1 - kind])
            if stop < shares - 1:
                moved = [(value.astype(F32) + addend(stop, kind, layer)).astype(BF16) for layer, value in enumerate(moved)]
            flows[kind] = moved
        if stop == 3:
            input_grads = assemble(grads_kept, grads_other, flows[UP][0])
    grads = run_final(flows[DOWN], flows[UP], kept_last, tail[-1], scales, shares, hidden)
    return (section_outputs, input_grads, *grads)


def solution(mesh):
    in_specs = (
        P(None, "dp", None, None),
        P(None, "dp", None),
        P(None, "dp", None, None),
        P("section", None, None),
        P("section", None),
        P("section", None),
        P("section", None),
        P("section", None, None),
        P("section", None),
        P("section", None, None),
        P("section", None),
        P("section", None),
    )
    out_specs = (
        P("section", None, "dp", None, None),
        P("section", None, "dp", None, None),
        P("section", None, "dp"),
        P("section", "dp"),
        P("section", "dp"),
        P("section", "dp"),
        P("section", "dp", None),
        P("section", "dp"),
        P("section", "dp", None),
        P("section", "dp"),
        P("section", "dp"),
    )
    return jax.shard_map(per_device, mesh=mesh, in_specs=in_specs, out_specs=out_specs, check_vma=False)
```

```python
import functools

import jax
import jax.numpy as jnp
from jax import lax
from jax.experimental import pallas as pl
from jax.experimental.pallas import tpu as pltpu
from jax.sharding import PartitionSpec as P

EPSILON = 1e-06
INV_SQRT2 = 0.7071067811865476
INV_SQRT_PI = 0.5641895835477563
LOG2_E = 1.4426950408889634
F32 = jnp.float32
BF16 = jnp.bfloat16
TILE = 32
PAD = 8
COLS = 256
VMEM_LIMIT = 60 * 2**20
COST = pl.CostEstimate(flops=1, bytes_accessed=1, transcendentals=0)

CONV_B, GAIN, SHIFT, DOWN_B, SCALE, UP_B, VEC_ROWS = 7, 8, 9, 10, 11, 12, 16
XHAT, STREAM, NORMED, KINDS = 0, 1, 2, 3
LANES = 128
OFFSETS = (1, 2, 3, -1, -2, -3)
MASK_OF = {offset: k for k, offset in enumerate(OFFSETS)}


def slabs(width):
    return [slice(c, c + LANES) for c in range(0, width, LANES)]


def row_sum(parts):
    return jnp.sum(functools.reduce(jnp.add, parts), axis=1, keepdims=True)


def fold(value):
    return functools.reduce(jnp.add, [value[8 * i : 8 * i + 8] for i in range(value.shape[0] // 8)])


def clear_edges(padded, frames):
    for slab in range(padded.shape[0]):
        padded[slab, 0:PAD, :] = jnp.zeros((PAD, LANES), F32)
        padded[slab, PAD + frames : PAD + frames + PAD, :] = jnp.zeros((PAD, LANES), F32)


def build_masks(seg_v, masks):
    frames = masks.shape[1]
    seg_v[0:PAD, :] = jnp.full((PAD, LANES), -1.0, F32)
    seg_v[PAD + frames : PAD + frames + PAD, :] = jnp.full((PAD, LANES), -1.0, F32)

    def body(i, carry):
        base = pl.multiple_of(i * 64, 64)
        here = seg_v[pl.ds(base + PAD, 64), :]
        for k, offset in enumerate(OFFSETS):
            there = seg_v[pl.ds(base + PAD + offset, 64), :]
            masks[k, pl.ds(base, 64), :] = jnp.where(there == here, 1.0, 0.0)
        return carry

    lax.fori_loop(0, frames // 64, body, 0)


def start_weights(core, layer, own, peer, target, sem):
    @pl.when(core == lax.div(layer, 2))
    def _():
        pltpu.make_async_copy(own.at[lax.rem(layer, 2)], target, sem).start()

    @pl.when(core != lax.div(layer, 2))
    def _():
        pltpu.make_async_copy(peer.at[lax.rem(layer, 2)], target, sem).start()


def send_row(core, section, source, kept, other, sem):
    @pl.when(core == section)
    def _():
        pltpu.make_async_copy(source, kept, sem).start()

    @pl.when(core != section)
    def _():
        pltpu.make_async_copy(source, other, sem).start()


def forward_kernel(layers, aliased, flags, x_in, seg_hbm, vec, own_up, own_down, peer_up, peer_down, *rest):
    rest = rest[aliased:]
    hid, dge, saved, rst, kept, other, send = rest[:7]
    (up_v, down_v, hid_v, dge_v, saved_v, rst_v, stream, acc, out_v, x_v, seg_v, masks, w_sem, in_sem, o_sem, s_sem) = rest[7:]
    frames, width = acc.shape
    hidden = hid_v.shape[2]

    @pl.when(flags[0] == 1)
    def _():
        core, micro, row = flags[1], flags[2], flags[3]
        pltpu.make_async_copy(x_in, x_v, s_sem.at[2]).start()
        pltpu.make_async_copy(seg_hbm.at[micro], seg_v.at[pl.ds(PAD, frames)], in_sem).start()
        def fetch(j):
            start_weights(core, j, own_up, peer_up, up_v.at[j], w_sem.at[j, 0])
            start_weights(core, j, own_down, peer_down, down_v.at[j], w_sem.at[j, 1])

        fetch(0)
        clear_edges(stream, frames)
        pltpu.make_async_copy(seg_hbm.at[0], seg_v.at[pl.ds(PAD, frames)], in_sem).wait()
        build_masks(seg_v, masks)
        pltpu.make_async_copy(x_in, x_v, s_sem.at[2]).wait()
        for c, cols in enumerate(slabs(width)):
            stream[c, PAD : PAD + frames, :] = x_v[:, cols].astype(F32)

        def layer(j, carry):
            def conv_norm(i, c):
                base = pl.multiple_of(i * TILE, TILE)
                rows = pl.ds(base, TILE)
                parts = []
                for s, cols in enumerate(slabs(width)):
                    centre = stream[s, pl.ds(base + PAD, TILE), :]
                    saved_v[j, STREAM, rows, cols] = centre.astype(BF16)
                    total = vec[j, CONV_B : CONV_B + 1, cols] + vec[j, 3:4, cols] * centre
                    for offset in OFFSETS:
                        neighbour = stream[s, pl.ds(base + PAD + offset, TILE), :] * masks[MASK_OF[offset], rows, :]
                        total = total + vec[j, offset + 3 : offset + 4, cols] * neighbour
                    parts.append(total)
                mean = row_sum(parts) * (1.0 / width)
                parts = [part - mean for part in parts]
                rstd = lax.rsqrt(row_sum([part * part for part in parts]) * (1.0 / width) + EPSILON)
                for part, cols in zip(parts, slabs(width)):
                    xhat = part * rstd
                    saved_v[j, XHAT, rows, cols] = xhat.astype(BF16)
                    saved_v[j, NORMED, rows, cols] = (xhat * vec[j, GAIN : GAIN + 1, cols] + vec[j, SHIFT : SHIFT + 1, cols]).astype(BF16)
                rst_v[j, rows, :] = jnp.broadcast_to(rstd, (TILE, LANES))
                return c

            lax.fori_loop(0, frames // TILE, conv_norm, 0, unroll=8)
            pltpu.make_async_copy(saved_v.at[j], saved.at[row, j], o_sem.at[j, 3]).start()
            pltpu.make_async_copy(rst_v.at[j], rst.at[row, j], o_sem.at[j, 2]).start()
            pltpu.make_async_copy(own_up.at[0], up_v.at[j], w_sem.at[j, 0]).wait()

            @pl.when(j + 1 < layers)
            def _():
                fetch(j + 1)

            pltpu.make_async_copy(own_down.at[0], down_v.at[j], w_sem.at[j, 1]).wait()
            half = frames // 2
            for part in range(2):
                here = slice(part * half, (part + 1) * half)
                for n in range(hidden // COLS):
                    cols = slice(n * COLS, (n + 1) * COLS)
                    if part == 1 and n % 2 == 1 and n // 2 < width // COLS:
                        out = slice(n // 2 * COLS, (n // 2 + 1) * COLS)
                        acc[0:half, out] = jnp.dot(hid_v[j, 0:half, :], down_v[j, :, out], preferred_element_type=F32)
                    at, start = UP_B + n * COLS // width, (n * COLS) % width
                    value = jnp.dot(saved_v[j, NORMED, here], up_v[j, :, cols], preferred_element_type=F32) + vec[j, at : at + 1, start : start + COLS]
                    scaled = value * INV_SQRT2
                    phi_sum = 0.5 + 0.5 * lax.erf(scaled)
                    hid_v[j, here, cols] = (value * phi_sum).astype(BF16)
                    dge_v[j, here, cols] = (phi_sum + scaled * INV_SQRT_PI * jnp.exp2(scaled * scaled * -LOG2_E)).astype(BF16)
            pltpu.make_async_copy(hid_v.at[j], hid.at[row, j], o_sem.at[j, 0]).start()
            pltpu.make_async_copy(dge_v.at[j], dge.at[row, j], o_sem.at[j, 1]).start()
            acc[half:, :] = jnp.dot(hid_v[j, half:, :], down_v[j], preferred_element_type=F32)

            def finish(ends_section, i, c):
                base = pl.multiple_of(i * TILE, TILE)
                rows = pl.ds(base, TILE)
                for s, cols in enumerate(slabs(width)):
                    inner = pl.ds(pl.multiple_of(base + PAD, 8), TILE)
                    branch = acc[rows, cols] + vec[j, DOWN_B : DOWN_B + 1, cols]
                    fresh = stream[s, inner, :] + vec[j, SCALE : SCALE + 1, cols] * branch
                    if ends_section:
                        rounded = fresh.astype(BF16)
                        out_v[lax.div(j, 2), rows, cols] = fresh
                        x_v[rows, cols] = rounded
                        fresh = rounded.astype(F32)
                    stream[s, inner, :] = fresh
                return c

            @pl.when(lax.rem(j, 2) == 1)
            def _():
                lax.fori_loop(0, frames // TILE, functools.partial(finish, True), 0)

            @pl.when(lax.rem(j, 2) == 0)
            def _():
                lax.fori_loop(0, frames // TILE, functools.partial(finish, False), 0)

            @pl.when(j == 1)
            def _():
                send_row(core, 0, out_v.at[0], kept.at[micro], other.at[row], s_sem.at[0])

            return carry

        lax.fori_loop(0, layers, layer, 0)
        send_row(core, 1, out_v.at[1], kept.at[micro], other.at[row], s_sem.at[1])
        pltpu.make_async_copy(x_v, send, s_sem.at[2]).start()
        for j in range(layers):
            pltpu.make_async_copy(hid_v.at[j], hid.at[row, j], o_sem.at[j, 0]).wait()
            pltpu.make_async_copy(dge_v.at[j], dge.at[row, j], o_sem.at[j, 1]).wait()
            pltpu.make_async_copy(rst_v.at[j], rst.at[row, j], o_sem.at[j, 2]).wait()
            pltpu.make_async_copy(saved_v.at[j], saved.at[row, j], o_sem.at[j, 3]).wait()
        pltpu.make_async_copy(out_v.at[0], other.at[row], s_sem.at[0]).wait()
        pltpu.make_async_copy(out_v.at[1], other.at[row], s_sem.at[1]).wait()
        pltpu.make_async_copy(x_v, send, s_sem.at[2]).wait()


SUMS, HEAD = 4, 2
DOWN, UP = 0, 1
VECTORS = 16


def send_sums(core, section, owners, kind, layer, source, vectors, targets, sem):
    kept, kept_last, head, tail = targets
    _, _, block, width = kept.shape
    shares = kept.shape[0] + 1
    size = (block - VECTORS) // 2
    first = 0 if kind == DOWN else size + VECTORS
    columns = source.shape[1] // width
    rows = size // columns
    for stop in range(shares):
        owner = owners[2 * kind + layer, stop]
        pieces = [
            (source.at[pl.ds(pl.multiple_of(owner * rows, 16), rows), pl.ds(b * width, width)], pl.ds(first + b * rows, rows))
            for b in range(columns)
        ]
        if vectors is not None:
            pieces.append((vectors.at[owners[2 * DOWN + layer, stop]], pl.ds(size, VECTORS)))
        for piece, place in pieces:

            @pl.when(core == section)
            def _():
                target = kept.at[stop, layer] if stop < shares - 1 else kept_last.at[layer]
                pltpu.make_async_copy(piece, target.at[place], sem).start()

            @pl.when(core != section)
            def _():
                target = head.at[stop, layer] if stop < HEAD else tail.at[stop - HEAD, layer]
                pltpu.make_async_copy(piece, target.at[place], sem).start()


def pack_vectors(sums, packed):
    shares, _, width = packed.shape
    parts = [sums[r : r + 1, :] for r in range(UP_B, VEC_ROWS - 1)]
    wide = jnp.broadcast_to(jnp.concatenate(parts, axis=1), (8, width * len(parts)))
    size, wide_size = width // shares, width * len(parts) // shares
    is_bias = lax.broadcasted_iota(jnp.int32, (VECTORS, width), 0) == UP_B
    for d in range(shares):
        part = sums if d == 0 else pltpu.roll(sums, width - d * size, 1)
        bias = wide if d == 0 else pltpu.roll(wide, wide.shape[1] - d * wide_size, 1)
        packed[d] = jnp.where(is_bias, jnp.broadcast_to(bias[0:1, :width], (VECTORS, width)), part).astype(BF16)


def backward_kernel(final, aliased, ties, riders, flags, g_one, g_two, seg_hbm, vec, own_up, own_down, peer_up, peer_down, dge, saved, rst, *rest):
    if final:
        owners, hid, down_in, up_in, vec_in = rest[:5]
        rest = rest[5 + ties + aliased :]
        sums_out, (kept, other) = rest[:SUMS], rest[SUMS : SUMS + 2]
        rest = rest[SUMS + 2 :]
    else:
        rest = rest[aliased:]
        gb, gp, vec_out, kept, other, send = rest[:6]
        rest = rest[6 + riders :]
    (up_v, down_v, dge_v, saved_v, rst_v, gb_v, gp_v, vg_v, g_now, fresh_v, gn_v, padded, x_v, seg_v, masks, w_sem, in_sem, g_sem, o_sem, s_sem) = rest[:20]
    if final:
        (hid_v, nrm_v, dwd_v, dwu_v, down_e, up_e, early_v, packed, b_sem) = rest[20:]
    frames, width = g_now.shape
    held, _, hidden = dge_v.shape
    layers = vec.shape[0]
    nt = (((1,), (1,)), ((), ()))
    tn = (((0,), (0,)), ((), ()))
    tall = 2 * TILE
    cols_of = slabs(width)

    @pl.when(flags[0] == 1)
    def _():
        core, micro, row = flags[1], flags[2], flags[3]
        pltpu.make_async_copy(seg_hbm.at[micro], seg_v.at[pl.ds(PAD, frames)], in_sem).start()

        def fetch(j):
            h = lax.rem(j, held)
            start_weights(core, j, own_down, peer_down, down_v.at[h], w_sem.at[h, 1])
            pltpu.make_async_copy(dge.at[row, j], dge_v.at[h], w_sem.at[h, 3]).start()
            start_weights(core, j, own_up, peer_up, up_v.at[h], w_sem.at[h, 0])
            pltpu.make_async_copy(rst.at[row, j], rst_v.at[h], w_sem.at[h, 4]).start()
            pltpu.make_async_copy(saved.at[row, j, 0:2], saved_v.at[h], w_sem.at[h, 2]).start()

        if final:
            pltpu.make_async_copy(vec_in.at[1 - row], early_v, s_sem.at[2]).start()
        source = [pltpu.make_async_copy(g, x_v, g_sem) for g in (g_one, g_two)]
        for k in range(2):

            @pl.when(flags[4] == k)
            def _():
                source[k].start()

        fetch(layers - 1)
        clear_edges(padded, frames)
        source[0].wait()
        for cols in cols_of:

            def enter(t, c):
                rows = pl.ds(pl.multiple_of(t * tall, tall), tall)
                scaled = (vec[layers - 1, SCALE : SCALE + 1, cols] * x_v[rows, cols].astype(F32)).astype(BF16)
                gb_v[layers, 0, rows, cols] = scaled
                return c + fold(scaled.astype(F32))

            total = lax.fori_loop(0, frames // tall, enter, jnp.zeros((8, LANES), F32))
            vg_v[layers, DOWN_B : DOWN_B + 1, cols] = jnp.sum(total, axis=0, keepdims=True)
        pltpu.make_async_copy(seg_hbm.at[0], seg_v.at[pl.ds(PAD, frames)], in_sem).wait()
        build_masks(seg_v, masks)

        def layer(step, carry):
            j = layers - 1 - step
            h = lax.rem(j, held)
            if not final:
                pltpu.make_async_copy(gb_v.at[j + 1, 0], gb.at[row, j], o_sem.at[j, 0]).start()
            pltpu.make_async_copy(own_down.at[0], down_v.at[h], w_sem.at[h, 1]).wait()
            pltpu.make_async_copy(dge.at[0, 0], dge_v.at[h], w_sem.at[h, 3]).wait()
            if final:
                pltpu.make_async_copy(hid.at[row, j], hid_v.at[h], b_sem.at[h, 0]).start()
                pltpu.make_async_copy(down_in.at[j], down_e.at[h], b_sem.at[h, 1]).start()
                pltpu.make_async_copy(saved.at[row, j, NORMED], nrm_v.at[h], b_sem.at[h, 2]).start()
                pltpu.make_async_copy(up_in.at[j], up_e.at[h], b_sem.at[h, 3]).start()
            for n in range(hidden // COLS):
                cols = slice(n * COLS, (n + 1) * COLS)
                value = lax.dot_general(gb_v[j + 1, 0], down_v[h, cols, :], nt, preferred_element_type=F32)
                rounded = (value * dge_v[h, :, cols].astype(F32)).astype(BF16)
                gp_v[h, 0, :, cols] = rounded
                at, start = UP_B + n * COLS // width, (n * COLS) % width
                vg_v[j + 1, at : at + 1, start : start + COLS] = jnp.sum(rounded.astype(F32), axis=0, keepdims=True)
            if not final:
                pltpu.make_async_copy(gp_v.at[h, 0], gp.at[row, j], o_sem.at[j, 1]).start()
            pltpu.make_async_copy(own_up.at[0], up_v.at[h], w_sem.at[h, 0]).wait()
            gn_v[...] = lax.dot_general(gp_v[h, 0], up_v[h], nt, preferred_element_type=F32)
            pltpu.make_async_copy(rst.at[0, 0], rst_v.at[h], w_sem.at[h, 4]).wait()
            pltpu.make_async_copy(saved.at[0, 0, 0:2], saved_v.at[h], w_sem.at[h, 2]).wait()

            @pl.when(j > 0)
            def _():
                fetch(j - 1)

            if final:
                pltpu.make_async_copy(hid.at[0, 0], hid_v.at[h], b_sem.at[h, 0]).wait()
                pltpu.make_async_copy(down_in.at[0], down_e.at[h], b_sem.at[h, 1]).wait()

                @pl.when(j + held < layers)
                def _():
                    pltpu.make_async_copy(dwd_v.at[h], dwd_v.at[h], o_sem.at[h, 0]).wait()
                    pltpu.make_async_copy(dwu_v.at[h], dwu_v.at[h], o_sem.at[h, 1]).wait()
                    pltpu.make_async_copy(packed.at[h], packed.at[h], o_sem.at[h, 1]).wait()

            def down_chunk(n):
                rows = slice(n * COLS, (n + 1) * COLS)
                value = lax.dot_general(hid_v[h, :, rows], gb_v[j + 1, 0], tn, preferred_element_type=F32) + down_e[h, rows, :].astype(F32)
                dwd_v[h, rows, :] = value.astype(BF16)
                return fold(value * down_v[h, rows, :].astype(F32))

            def up_chunk(m, n):
                rows = slice(m * COLS, (m + 1) * COLS)
                cols = slice(n * width, (n + 1) * width)
                value = lax.dot_general(nrm_v[h, :, rows], gp_v[h, 0, :, cols], tn, preferred_element_type=F32) + up_e[h, rows, cols].astype(F32)
                dwu_v[h, rows, cols] = value.astype(BF16)

            odd = lax.rem(j, 2) == 1

            def norm_back(t, c):
                base = t * TILE if isinstance(t, int) else pl.multiple_of(t * TILE, TILE)
                rows = pl.ds(base, TILE)
                inner = pl.ds(base + PAD if isinstance(t, int) else pl.multiple_of(base + PAD, 8), TILE)
                grads = [gn_v[rows, cols] for cols in cols_of]
                xhats = [saved_v[h, XHAT, rows, cols].astype(F32) for cols in cols_of]
                qs = [grad * vec[j, GAIN : GAIN + 1, cols] for grad, cols in zip(grads, cols_of)]
                mean_q = row_sum(qs) * (1.0 / width)
                mean_qx = row_sum([q * xhat for q, xhat in zip(qs, xhats)]) * (1.0 / width)
                rstd = rst_v[h, rows, :]
                out = []
                for s, cols in enumerate(cols_of):
                    grad_conv = rstd * (qs[s] - mean_q - xhats[s] * mean_qx)
                    padded[s, inner, :] = grad_conv
                    g_now[rows, cols] = jnp.where(odd, x_v[rows, cols].astype(F32), fresh_v[rows, cols])
                    out += [c[3 * s] + fold(grads[s] * xhats[s]), c[3 * s + 1] + fold(grads[s]), c[3 * s + 2] + fold(grad_conv)]
                return tuple(out)

            sums = (jnp.zeros((8, LANES), F32),) * (3 * len(cols_of))
            tiles = frames // TILE
            if final:
                parts = hidden // COLS
                scale = jnp.zeros((8, width), F32)
                done = 0
                for n in range(parts):
                    scale = scale + down_chunk(n)
                    while done < tiles * (n + 1) // parts:
                        sums = norm_back(done, sums)
                        done += 1
                vg_v[j + 1, SCALE : SCALE + 1, :] = jnp.sum(scale, axis=0, keepdims=True)
                send_sums(core, lax.div(j, 2), owners, DOWN, lax.rem(j, 2), dwd_v.at[h], None, sums_out, o_sem.at[h, 0])
                pltpu.make_async_copy(saved.at[0, 0, 0], nrm_v.at[h], b_sem.at[h, 2]).wait()
                pltpu.make_async_copy(up_in.at[0], up_e.at[h], b_sem.at[h, 3]).wait()
            else:
                sums = lax.fori_loop(0, tiles, norm_back, sums, unroll=8)
            for s, cols in enumerate(cols_of):
                for k, at in enumerate((GAIN, SHIFT, CONV_B)):
                    vg_v[j + 1, at : at + 1, cols] = jnp.sum(sums[3 * s + k], axis=0, keepdims=True)

            @pl.when(odd & (step > 0))
            def _():
                pltpu.make_async_copy(fresh_v, other.at[row], s_sem.at[0]).wait()

            below = lax.max(j - 1, 0)
            for s, cols in enumerate(cols_of):

                def conv_back(t, c):
                    base = t * tall if isinstance(t, int) else pl.multiple_of(t * tall, tall)
                    rows = pl.ds(base, tall)
                    source = saved_v[h, STREAM, rows, cols].astype(F32)
                    centre = padded[s, pl.ds(base + PAD if isinstance(t, int) else pl.multiple_of(base + PAD, 8), tall), :]
                    total = g_now[rows, cols] + vec[j, 3:4, cols] * centre
                    taps = [None] * 7
                    taps[3] = c[3] + fold(centre * source)
                    for offset in OFFSETS:
                        term = padded[s, pl.ds(base + PAD - offset, tall), :] * masks[MASK_OF[-offset], rows, :]
                        total = total + vec[j, offset + 3 : offset + 4, cols] * term
                        taps[offset + 3] = c[offset + 3] + fold(term * source)
                    rounded = total.astype(BF16)
                    fresh_v[rows, cols] = total
                    x_v[rows, cols] = rounded
                    scaled = (vec[below, SCALE : SCALE + 1, cols] * jnp.where(odd, total, rounded.astype(F32))).astype(BF16)
                    gb_v[j, 0, rows, cols] = scaled
                    return tuple(taps) + (c[7] + fold(scaled.astype(F32)),)

                sums = (jnp.zeros((8, LANES), F32),) * 8
                if final:
                    chunks = [(m, n) for m in range(width // COLS) for n in range(hidden // width)]
                    each = -(-len(chunks) // len(cols_of))
                    mine = chunks[s * each : (s + 1) * each]
                    done = 0
                    for k, (m, n) in enumerate(mine):
                        up_chunk(m, n)
                        while done < frames // tall * (k + 1) // len(mine):
                            sums = conv_back(done, sums)
                            done += 1
                    while done < frames // tall:
                        sums = conv_back(done, sums)
                        done += 1
                else:
                    sums = lax.fori_loop(0, frames // tall, conv_back, sums, unroll=8)
                for k in range(7):
                    vg_v[j + 1, k : k + 1, cols] = jnp.sum(sums[k], axis=0, keepdims=True)
                vg_v[j, DOWN_B : DOWN_B + 1, cols] = jnp.sum(sums[7], axis=0, keepdims=True)
            if final:

                @pl.when(step == 0)
                def _():
                    pltpu.make_async_copy(vec_in.at[0], early_v, s_sem.at[2]).wait()

                pack_vectors(vg_v[j + 1] + early_v[j], packed.at[h])
                send_vectors = packed.at[h]
                send_sums(core, lax.div(j, 2), owners, UP, lax.rem(j, 2), dwu_v.at[h], send_vectors, sums_out, o_sem.at[h, 1])

            @pl.when(jnp.logical_not(odd))
            def _():
                send_row(core, lax.div(j, 2), fresh_v, kept.at[micro], other.at[row], s_sem.at[0])

            return carry

        for i in range(1, layers + 1):
            vg_v[i, SCALE : SCALE + 1, :] = jnp.zeros((1, width), F32)
            vg_v[i, VEC_ROWS - 1 : VEC_ROWS, :] = jnp.zeros((1, width), F32)
        lax.fori_loop(0, layers, layer, 0)
        if final:
            for h in range(held):
                pltpu.make_async_copy(dwd_v.at[h], dwd_v.at[h], o_sem.at[h, 0]).wait()
                pltpu.make_async_copy(dwu_v.at[h], dwu_v.at[h], o_sem.at[h, 1]).wait()
                pltpu.make_async_copy(packed.at[h], packed.at[h], o_sem.at[h, 1]).wait()
        else:
            pltpu.make_async_copy(vg_v.at[pl.ds(1, layers)], vec_out.at[row], s_sem.at[2]).start()
            pltpu.make_async_copy(x_v, send, s_sem.at[1]).start()
            for j in range(layers):
                pltpu.make_async_copy(gb_v.at[j + 1, 0], gb.at[row, j], o_sem.at[j, 0]).wait()
                pltpu.make_async_copy(gp_v.at[j, 0], gp.at[row, j], o_sem.at[j, 1]).wait()
            pltpu.make_async_copy(x_v, send, s_sem.at[1]).wait()
            pltpu.make_async_copy(vg_v.at[pl.ds(1, layers)], vec_out.at[row], s_sem.at[2]).wait()
        pltpu.make_async_copy(fresh_v, other.at[row], s_sem.at[0]).wait()


def early_kernel(flags, hid, gb, saved, gp, down_out, up_out, hid_v, gb_v, nrm_v, gp_v, dwd_v, dwu_v, sem, o_sem):
    frames, width = gb_v.shape[1:]
    hidden = hid_v.shape[2]
    layers = hid.shape[1]
    tn = (((0,), (0,)), ((), ()))

    @pl.when(flags[0] == 1)
    def _():
        row = flags[3]

        def copies(j, h):
            pairs = ((hid.at[row, j], hid_v), (gb.at[row, j], gb_v), (saved.at[row, j, NORMED], nrm_v), (gp.at[row, j], gp_v))
            return [pltpu.make_async_copy(a, b.at[h], sem.at[h, k]) for k, (a, b) in enumerate(pairs)]

        def leaving(j, h):
            return [
                pltpu.make_async_copy(dwd_v.at[h], down_out.at[j], o_sem.at[h, 0]),
                pltpu.make_async_copy(dwu_v.at[h], up_out.at[j], o_sem.at[h, 1]),
            ]

        for copy in copies(layers - 1, (layers - 1) % 2):
            copy.start()

        def layer(step, carry):
            j = layers - 1 - step
            h = lax.rem(j, 2)

            @pl.when(j > 0)
            def _():
                for copy in copies(j - 1, 1 - h):
                    copy.start()

            for copy in copies(j, h):
                copy.wait()

            @pl.when(j + 2 < layers)
            def _():
                for copy in leaving(j + 2, h):
                    copy.wait()

            def down_chunk(n, c):
                rows = pl.ds(pl.multiple_of(n * width, width), width)
                dwd_v[h, rows, :] = lax.dot_general(hid_v[h, :, rows], gb_v[h], tn, preferred_element_type=F32).astype(BF16)
                return c

            def up_chunk(n, c):
                cols = pl.ds(pl.multiple_of(n * width, width), width)
                dwu_v[h, :, cols] = lax.dot_general(nrm_v[h], gp_v[h, :, cols], tn, preferred_element_type=F32).astype(BF16)
                return c

            lax.fori_loop(0, hidden // width, down_chunk, 0)
            lax.fori_loop(0, hidden // width, up_chunk, 0)
            for copy in leaving(j, h):
                copy.start()
            return carry

        lax.fori_loop(0, layers, layer, 0)
        for h in range(2):
            for copy in leaving(h, h):
                copy.wait()


def weight_kernel(ties, flags, owners, own_down, peer_down, all_hid, all_gb, all_saved, all_gp, vec_in, *rest):
    rest = rest[ties:]
    sums_out, rest = rest[:SUMS], rest[SUMS:]
    hid_v, gb_v, nrm_v, gp_v, down_v, dwd_v, dwu_v, vec_v, packed, sem, o_sem, s_sem = rest
    frames, width = gb_v.shape[2:]
    hidden = hid_v.shape[3]
    layers = all_hid.shape[1]
    tn = (((0,), (0,)), ((), ()))

    @pl.when(flags[0] == 1)
    def _():
        core = flags[1]

        def copies(j, h):
            pairs = []
            for row in range(2):
                pairs += [
                    (all_hid.at[row, j], hid_v.at[h, row]),
                    (all_gb.at[row, j], gb_v.at[h, row]),
                    (all_saved.at[row, j, NORMED], nrm_v.at[h, row]),
                    (all_gp.at[row, j], gp_v.at[h, row]),
                ]
            return [pltpu.make_async_copy(a, b, sem.at[h, k]) for k, (a, b) in enumerate(pairs)]

        def fetch(j):
            h = lax.rem(j, 2)
            start_weights(core, j, own_down, peer_down, down_v.at[h], sem.at[h, 8])
            for copy in copies(j, h):
                copy.start()

        fetch(layers - 1)
        pltpu.make_async_copy(vec_in, vec_v, s_sem).start()
        pltpu.make_async_copy(vec_in, vec_v, s_sem).wait()

        def layer(step, carry):
            j = layers - 1 - step
            h = lax.rem(j, 2)

            @pl.when(j > 0)
            def _():
                fetch(j - 1)

            pltpu.make_async_copy(own_down.at[0], down_v.at[h], sem.at[h, 8]).wait()
            for copy in copies(j, h):
                copy.wait()

            @pl.when(j + 2 < layers)
            def _():
                pltpu.make_async_copy(dwd_v.at[h], dwd_v.at[h], o_sem.at[h, 0]).wait()
                pltpu.make_async_copy(dwu_v.at[h], dwu_v.at[h], o_sem.at[h, 1]).wait()
                pltpu.make_async_copy(packed.at[h], packed.at[h], o_sem.at[h, 1]).wait()

            def down_chunk(n, scale):
                rows = pl.ds(pl.multiple_of(n * COLS, COLS), COLS)
                left = hid_v[h, :, :, rows].reshape(2 * frames, COLS)
                value = lax.dot_general(left, gb_v[h].reshape(2 * frames, width), tn, preferred_element_type=F32)
                dwd_v[h, rows, :] = value.astype(BF16)
                return scale + fold(value * down_v[h, rows, :].astype(F32))

            scale = lax.fori_loop(0, hidden // COLS, down_chunk, jnp.zeros((8, width), F32))
            scale = jnp.sum(scale, axis=0, keepdims=True)
            vectors = vec_v[0, j] + vec_v[1, j]
            is_scale = lax.broadcasted_iota(jnp.int32, vectors.shape, 0) == SCALE
            pack_vectors(jnp.where(is_scale, jnp.broadcast_to(scale, vectors.shape), vectors), packed.at[h])
            send_sums(core, lax.div(j, 2), owners, DOWN, lax.rem(j, 2), dwd_v.at[h], None, sums_out, o_sem.at[h, 0])

            def up_chunk(n, c):
                cols = pl.ds(pl.multiple_of(n * width, width), width)
                right = gp_v[h, :, :, cols].reshape(2 * frames, width)
                value = lax.dot_general(nrm_v[h].reshape(2 * frames, width), right, tn, preferred_element_type=F32)
                dwu_v[h, :, cols] = value.astype(BF16)
                return c

            lax.fori_loop(0, hidden // width, up_chunk, 0)
            send_sums(core, lax.div(j, 2), owners, UP, lax.rem(j, 2), dwu_v.at[h], packed.at[h], sums_out, o_sem.at[h, 1])
            return carry

        lax.fori_loop(0, layers, layer, 0)
        for h in range(2):
            pltpu.make_async_copy(dwd_v.at[h], dwd_v.at[h], o_sem.at[h, 0]).wait()
            pltpu.make_async_copy(dwu_v.at[h], dwu_v.at[h], o_sem.at[h, 1]).wait()
            pltpu.make_async_copy(packed.at[h], packed.at[h], o_sem.at[h, 1]).wait()


def place_kernel(at, kept_in, rows, tie, kept, held, sem):
    count = rows.shape[0]
    for i in range(count):
        pltpu.make_async_copy(rows.at[i], held.at[i], sem.at[i]).start()
    for i in range(count):
        pltpu.make_async_copy(rows.at[i], held.at[i], sem.at[i]).wait()
        pltpu.make_async_copy(held.at[i], kept.at[at[0] + i], sem.at[i]).start()
    for i in range(count):
        pltpu.make_async_copy(held.at[i], kept.at[at[0] + i], sem.at[i]).wait()


def hold_kernel(value_in, tie, value):
    pass


def final_kernel(down_0, down_1, up_0, up_1, kept, other, scales, *rest):
    conv_out, conv_b_out, gain_out, shift_out, up_out, up_b_out, down_out, down_b_out, scale_out = rest
    size, wide = conv_b_out.shape[1], up_b_out.shape[1]
    rows, width = down_out.shape[1:]
    for layer, (down, up) in enumerate(((down_0, up_0), (down_1, up_1))):
        total = down[...].astype(F32) + kept[layer, : rows + VECTORS].astype(F32) + other[layer, : rows + VECTORS].astype(F32)
        down_out[layer] = total[:rows]
        vectors = total[rows:]
        at = slice(layer, layer + 1)
        conv_out[layer] = vectors[:CONV_B, :size]
        conv_b_out[at, :] = vectors[CONV_B : CONV_B + 1, :size]
        gain_out[at, :] = vectors[GAIN : GAIN + 1, :size]
        shift_out[at, :] = vectors[SHIFT : SHIFT + 1, :size]
        down_b = vectors[DOWN_B : DOWN_B + 1, :size]
        down_b_out[at, :] = down_b
        scale_out[at, :] = (vectors[SCALE : SCALE + 1, :size] + scales[0, at, :] * down_b) / scales[1, at, :]
        up_b_out[at, :] = vectors[UP_B : UP_B + 1, :wide]
        total = up[...].astype(F32) + kept[layer, rows + VECTORS :].astype(F32) + other[layer, rows + VECTORS :].astype(F32)
        for b in range(up_out.shape[2] // width):
            up_out[layer, :, b * width : (b + 1) * width] = total[b * size : (b + 1) * size]


ANY = pl.BlockSpec(memory_space=pl.ANY)
HBM = pl.BlockSpec(memory_space=pltpu.HBM)
SMEM = pl.BlockSpec(memory_space=pltpu.SMEM)
VMEM = pl.BlockSpec(memory_space=pltpu.VMEM)


def near(value):
    return pltpu.with_memory_space_constraint(value, pltpu.VMEM)


def run_forward(flags, x, seg, vec, weights, earlier):
    layers = vec.shape[0]
    micro = seg.shape[0]
    frames, width = x.shape
    hidden = weights[0].shape[2]
    shapes = (
        jax.ShapeDtypeStruct((2, layers, frames, hidden), BF16),
        jax.ShapeDtypeStruct((2, layers, frames, hidden), BF16),
        jax.ShapeDtypeStruct((2, layers, KINDS, frames, width), BF16),
        jax.ShapeDtypeStruct((2, layers, frames, LANES), F32),
        jax.ShapeDtypeStruct((micro, frames, width), F32),
        jax.ShapeDtypeStruct((2, frames, width), F32),
        jax.ShapeDtypeStruct((frames, width), BF16),
    )
    aliased = len(earlier)
    return pl.pallas_call(
        functools.partial(forward_kernel, layers, aliased),
        out_shape=shapes,
        in_specs=[SMEM, ANY, ANY, VMEM] + [ANY] * (4 + aliased),
        out_specs=(ANY,) * len(shapes),
        input_output_aliases={8 + i: i for i in range(aliased)},
        scratch_shapes=[
            pltpu.VMEM((layers, width, hidden), BF16),
            pltpu.VMEM((layers, hidden, width), BF16),
            pltpu.VMEM((layers, frames, hidden), BF16),
            pltpu.VMEM((layers, frames, hidden), BF16),
            pltpu.VMEM((layers, KINDS, frames, width), BF16),
            pltpu.VMEM((layers, frames, LANES), F32),
            pltpu.VMEM((width // LANES, frames + 2 * PAD, LANES), F32),
            pltpu.VMEM((frames, width), F32),
            pltpu.VMEM((2, frames, width), F32),
            pltpu.VMEM((frames, width), BF16),
            pltpu.VMEM((frames + 2 * PAD, LANES), F32),
            pltpu.VMEM((6, frames, LANES), F32),
            pltpu.SemaphoreType.DMA((layers, 2)),
            pltpu.SemaphoreType.DMA,
            pltpu.SemaphoreType.DMA((layers, 4)),
            pltpu.SemaphoreType.DMA((3,)),
        ],
        compiler_params=pltpu.CompilerParams(vmem_limit_bytes=VMEM_LIMIT),
        cost_estimate=COST,
    )(flags, x, seg, vec, *weights, *earlier)


def sum_shapes(shares, hidden, width):
    block = (2, 2 * (hidden // shares) + VECTORS, width)
    return tuple(jax.ShapeDtypeStruct(shape, BF16) for shape in ((shares - 1, *block), block, (HEAD, *block), (shares - HEAD, *block)))


def run_backward(flags, g, seg, vec, weights, state, earlier, final=(), ties=(), riders=()):
    frames, width = g[0].shape
    hidden = weights[0].shape[2]
    layers, micro = vec.shape[0], seg.shape[0]
    held = 2 if final else layers
    grads = (
        jax.ShapeDtypeStruct((micro, frames, width), F32),
        jax.ShapeDtypeStruct((2, frames, width), F32),
    )
    if final:
        shapes = (*sum_shapes(final[0].shape[1], hidden, width), *grads)
    else:
        shapes = (
            jax.ShapeDtypeStruct((2, layers, frames, width), BF16),
            jax.ShapeDtypeStruct((2, layers, frames, hidden), BF16),
            jax.ShapeDtypeStruct((2, layers, VEC_ROWS, width), F32),
            *grads,
            jax.ShapeDtypeStruct((frames, width), BF16),
        )
    earlier = (*earlier, *riders)
    shapes = (*shapes, *(jax.ShapeDtypeStruct(rider.shape, rider.dtype) for rider in riders))
    aliased = len(earlier)
    targets = [*range(len(earlier) - len(riders)), *range(len(shapes) - len(riders), len(shapes))]
    scratch = [
        pltpu.VMEM((held, width, hidden), BF16),
        pltpu.VMEM((held, hidden, width), BF16),
        pltpu.VMEM((held, frames, hidden), BF16),
        pltpu.VMEM((held, 2, frames, width), BF16),
        pltpu.VMEM((held, frames, LANES), F32),
        pltpu.VMEM((layers + 1, 1, frames, width), BF16),
        pltpu.VMEM((held, 1, frames, hidden), BF16),
        pltpu.VMEM((layers + 1, VEC_ROWS, width), F32),
        pltpu.VMEM((frames, width), F32),
        pltpu.VMEM((frames, width), F32),
        pltpu.VMEM((frames, width), F32),
        pltpu.VMEM((width // LANES, frames + 2 * PAD, LANES), F32),
        pltpu.VMEM((frames, width), BF16),
        pltpu.VMEM((frames + 2 * PAD, LANES), F32),
        pltpu.VMEM((6, frames, LANES), F32),
        pltpu.SemaphoreType.DMA((held, 5)),
        pltpu.SemaphoreType.DMA,
        pltpu.SemaphoreType.DMA,
        pltpu.SemaphoreType.DMA((held, 2)),
        pltpu.SemaphoreType.DMA((3,)),
    ]
    if final:
        scratch += [
            pltpu.VMEM((held, frames, hidden), BF16),
            pltpu.VMEM((held, frames, width), BF16),
            pltpu.VMEM((held, hidden, width), BF16),
            pltpu.VMEM((held, width, hidden), BF16),
            pltpu.VMEM((held, hidden, width), BF16),
            pltpu.VMEM((held, width, hidden), BF16),
            pltpu.VMEM((layers, VEC_ROWS, width), F32),
            pltpu.VMEM((held, final[0].shape[1], VECTORS, width), BF16),
            pltpu.SemaphoreType.DMA((held, 4)),
        ]
    first_alias = 12 + len(final) + len(ties)
    return pl.pallas_call(
        functools.partial(backward_kernel, bool(final), aliased, len(ties), len(riders)),
        out_shape=shapes,
        in_specs=[SMEM, ANY, ANY, ANY, VMEM] + [ANY] * 7 + ([SMEM] + [ANY] * 4 if final else []) + [ANY] * (len(ties) + aliased),
        out_specs=tuple(HBM if final and k < SUMS else ANY for k in range(len(shapes))),
        input_output_aliases={first_alias + i: target for i, target in enumerate(targets)},
        scratch_shapes=scratch,
        compiler_params=pltpu.CompilerParams(vmem_limit_bytes=VMEM_LIMIT),
        cost_estimate=COST,
    )(flags, *g, seg, vec, *weights, *state, *final, *ties, *earlier)


def run_early(flags, hid, gb, saved, gp):
    _, layers, frames, hidden = hid.shape
    width = gb.shape[3]
    return pl.pallas_call(
        early_kernel,
        out_shape=(jax.ShapeDtypeStruct((layers, hidden, width), BF16), jax.ShapeDtypeStruct((layers, width, hidden), BF16)),
        in_specs=[SMEM] + [ANY] * 4,
        out_specs=(ANY,) * 2,
        scratch_shapes=[
            pltpu.VMEM((2, frames, hidden), BF16),
            pltpu.VMEM((2, frames, width), BF16),
            pltpu.VMEM((2, frames, width), BF16),
            pltpu.VMEM((2, frames, hidden), BF16),
            pltpu.VMEM((2, hidden, width), BF16),
            pltpu.VMEM((2, width, hidden), BF16),
            pltpu.SemaphoreType.DMA((2, 4)),
            pltpu.SemaphoreType.DMA((2, 2)),
        ],
        compiler_params=pltpu.CompilerParams(vmem_limit_bytes=VMEM_LIMIT),
        cost_estimate=COST,
    )(flags, hid, gb, saved, gp)


def run_weights(flags, owners, weights, hid, gb, saved, gp, vectors, ties):
    _, layers, frames, hidden = hid.shape
    width = gb.shape[3]
    shares = owners.shape[1]
    return pl.pallas_call(
        functools.partial(weight_kernel, len(ties)),
        out_shape=sum_shapes(shares, hidden, width),
        in_specs=[SMEM, SMEM] + [ANY] * (7 + len(ties)),
        out_specs=(HBM,) * SUMS,
        scratch_shapes=[
            pltpu.VMEM((2, 2, frames, hidden), BF16),
            pltpu.VMEM((2, 2, frames, width), BF16),
            pltpu.VMEM((2, 2, frames, width), BF16),
            pltpu.VMEM((2, 2, frames, hidden), BF16),
            pltpu.VMEM((2, hidden, width), BF16),
            pltpu.VMEM((2, hidden, width), BF16),
            pltpu.VMEM((2, width, hidden), BF16),
            pltpu.VMEM(vectors.shape, F32),
            pltpu.VMEM((2, shares, VECTORS, width), BF16),
            pltpu.SemaphoreType.DMA((2, 9)),
            pltpu.SemaphoreType.DMA((2, 2)),
            pltpu.SemaphoreType.DMA,
        ],
        compiler_params=pltpu.CompilerParams(vmem_limit_bytes=VMEM_LIMIT),
        cost_estimate=COST,
    )(flags, owners, weights[1], weights[3], hid, gb, saved, gp, vectors, *ties)


def run_place(kept, rows, at, tie):
    return pl.pallas_call(
        place_kernel,
        out_shape=jax.ShapeDtypeStruct(kept.shape, kept.dtype),
        in_specs=[SMEM, ANY, ANY, ANY],
        out_specs=ANY,
        input_output_aliases={1: 0},
        scratch_shapes=[pltpu.VMEM(rows.shape, rows.dtype), pltpu.SemaphoreType.DMA(rows.shape[:1])],
        cost_estimate=COST,
    )(at.reshape(1).astype(jnp.int32), kept, rows, tie)


def hold(value, tie):
    return pl.pallas_call(
        hold_kernel,
        out_shape=jax.ShapeDtypeStruct(value.shape, value.dtype),
        in_specs=[HBM, ANY],
        out_specs=HBM,
        input_output_aliases={0: 0},
        cost_estimate=COST,
    )(value, tie)


def run_final(down, up, kept, other, scales, shares, hidden):
    width = kept.shape[2]
    size, wide = width // shares, hidden // shares
    shapes = ((2, CONV_B, size), (2, size), (2, size), (2, size), (2, size, hidden), (2, wide), (2, wide, width), (2, size), (2, size))
    return pl.pallas_call(
        final_kernel,
        out_shape=tuple(jax.ShapeDtypeStruct(shape, F32) for shape in shapes),
        in_specs=[VMEM] * 7,
        out_specs=(VMEM,) * len(shapes),
        compiler_params=pltpu.CompilerParams(vmem_limit_bytes=VMEM_LIMIT // 2),
        cost_estimate=COST,
    )(*down, *up, kept, other, scales)


def ring_order(count):
    return list(range(0, count, 2)) + list(range(count - 1, 0, -2))


def ring_owners(ways, axis):
    count = lax.axis_size(axis)
    device = lax.axis_index(axis)
    mine = jnp.where(device % 2 == 0, device // 2, count - 1 - device // 2)
    places = jnp.stack([lax.rem(mine - way * (1 + jnp.arange(count, dtype=jnp.int32)) + 2 * count, count) for way in ways])
    return jnp.where(places < count - count // 2, 2 * places, 2 * (count - places) - 1)


def after(value, earlier):
    return lax.optimization_barrier((value, earlier))[0]


def ring_step(flows, ways, axis):
    count = lax.axis_size(axis)
    order = ring_order(count)
    return [
        lax.ppermute(value, axis, [(order[p], order[(p + way) % count]) for p in range(count)]) for value, way in zip(flows, ways)
    ]


def per_device(
    inputs,
    segment_ids,
    cotangent,
    conv_weight,
    conv_bias,
    norm_gain,
    norm_bias,
    up_weight,
    up_bias,
    down_weight,
    down_bias,
    layer_scale,
):
    micro, _, frames, width = inputs.shape
    hidden = up_weight.shape[2]
    shares = lax.axis_size("dp")
    section = lax.axis_index("section")
    chip, core = section // 2, section % 2
    exchange = [(0, 1), (1, 0), (2, 3), (3, 2)]

    small = jnp.concatenate(
        [
            conv_weight,
            conv_bias[:, None],
            norm_gain[:, None],
            norm_bias[:, None],
            down_bias[:, None],
            layer_scale[:, None],
            up_bias.reshape(2, -1, width),
            jnp.zeros((2, 1, width), BF16),
        ],
        axis=1,
    )
    small_peer = lax.ppermute(small, "section", exchange)
    up_peer = lax.ppermute(up_weight, "section", exchange)
    down_peer = lax.ppermute(down_weight, "section", exchange)
    vec = jnp.where(core == 0, jnp.concatenate([small, small_peer]), jnp.concatenate([small_peer, small])).astype(F32)
    weights = (up_weight, down_weight, up_peer, down_peer)
    masks = jnp.broadcast_to(segment_ids[:, 0, :, None].astype(F32), (micro, frames, LANES))
    inputs, cotangent = inputs[:, 0], cotangent[:, 0]

    def flags(active, row, choice=0):
        return jnp.stack([jnp.asarray(v, jnp.int32) for v in (active, core, 2 * core + row, row, choice)])

    first, last = chip == 0, chip == 1
    ways = ((1, -1), (-1, 1))
    owners = ring_owners([way for kind in ways for way in kind], "dp")

    def row_of(array, row):
        return lax.dynamic_index_in_dim(array, 2 * core + row, 0, keepdims=False)

    down_pairs, up_pairs = [(0, 2), (1, 3)], [(2, 0), (3, 1)]
    state = run_forward(flags(first, 0), row_of(inputs, 0), masks, vec, weights, ())
    arrived = lax.ppermute(state[6], "section", down_pairs)
    state = run_forward(flags(first, 1), row_of(inputs, 1), masks, vec, weights, state[:6])
    arrived_next = lax.ppermute(state[6], "section", down_pairs)
    state = run_forward(flags(last, 0), near(arrived), masks, vec, weights, state[:6])
    gradient = row_of(cotangent, 0)
    back = run_backward(flags(last, 0), (gradient, gradient), masks, vec, weights, state[1:4], ())
    returned = lax.ppermute(back[5], "section", up_pairs)
    state = run_forward(flags(last, 1), near(arrived_next), masks, vec, weights, state[:6])
    gradients = (row_of(cotangent, 1), near(returned))
    back = run_backward(flags(True, jnp.where(last, 1, 0), first), gradients, masks, vec, weights, state[1:4], back[:5], riders=state[4:6])
    returned = near(lax.ppermute(back[5], "section", up_pairs))
    gb, gp, vectors, grads_kept, grads_other, _, outputs_kept, outputs_other = back

    def assemble(mine, other, tie):
        return run_place(mine, lax.ppermute(other, "section", exchange), 2 * (1 - core), tie)[None, :, None]

    section_outputs = assemble(outputs_kept, outputs_other, vectors)
    early = run_early(flags(first, 0), state[0], gb, state[2], gp)
    sums = run_weights(flags(last, 0), owners, weights, state[0], gb, state[2], gp, vectors, (returned, section_outputs))
    shard = lax.axis_index("dp")
    scales = jnp.stack([down_bias, layer_scale]).astype(F32)
    scales = lax.dynamic_slice_in_dim(scales, shard * (width // shares), width // shares, 2)
    *sums, grads_kept, grads_other = run_backward(
        flags(first, 1),
        (returned, returned),
        masks,
        vec,
        weights,
        state[1:4],
        (*sums, grads_kept, grads_other),
        (owners, state[0], *early, vectors),
        (scales,),
    )

    kept, kept_last, head, tail = sums
    head = lax.ppermute(head, "section", exchange)
    tail = lax.ppermute(hold(tail, head), "section", exchange)
    size = hidden // shares
    spans = (slice(0, size + VECTORS), slice(size + VECTORS, None))

    def addend(stop, kind, layer):
        other = head[stop, layer, spans[kind]] if stop < HEAD else tail[stop - HEAD, layer, spans[kind]]
        return kept[stop, layer, spans[kind]].astype(F32) + other.astype(F32)

    flows = [[addend(0, kind, layer).astype(BF16) for layer in range(2)] for kind in (DOWN, UP)]
    for stop in range(1, shares):
        for kind in (DOWN, UP):
            moved = ring_step(flows[kind], ways[kind], "dp")
            if kind == DOWN or stop > 1:
                moved = after(moved, flows[1 - kind])
            if stop < shares - 1:
                moved = [(value.astype(F32) + addend(stop, kind, layer)).astype(BF16) for layer, value in enumerate(moved)]
            flows[kind] = moved
        if stop == 3:
            input_grads = assemble(grads_kept, grads_other, flows[UP][0])
    grads = run_final(flows[DOWN], flows[UP], kept_last, tail[-1], scales, shares, hidden)
    return (section_outputs, input_grads, *grads)


def solution(mesh):
    in_specs = (
        P(None, "dp", None, None),
        P(None, "dp", None),
        P(None, "dp", None, None),
        P("section", None, None),
        P("section", None),
        P("section", None),
        P("section", None),
        P("section", None, None),
        P("section", None),
        P("section", None, None),
        P("section", None),
        P("section", None),
    )
    out_specs = (
        P("section", None, "dp", None, None),
        P("section", None, "dp", None, None),
        P("section", None, "dp"),
        P("section", "dp"),
        P("section", "dp"),
        P("section", "dp"),
        P("section", "dp", None),
        P("section", "dp"),
        P("section", "dp", None),
        P("section", "dp"),
        P("section", "dp"),
    )
    return jax.shard_map(per_device, mesh=mesh, in_specs=in_specs, out_specs=out_specs, check_vma=False)
```

```python
import functools

import jax
import jax.numpy as jnp
from jax import lax
from jax.experimental import pallas as pl
from jax.experimental.pallas import tpu as pltpu
from jax.sharding import PartitionSpec as P

EPSILON = 1e-06
INV_SQRT2 = 0.7071067811865476
INV_SQRT_PI = 0.5641895835477563
LOG2_E = 1.4426950408889634
F32 = jnp.float32
BF16 = jnp.bfloat16
TILE = 32
PAD = 8
COLS = 256
VMEM_LIMIT = 60 * 2**20
COST = pl.CostEstimate(flops=1, bytes_accessed=1, transcendentals=0)

CONV_B, GAIN, SHIFT, DOWN_B, SCALE, UP_B, VEC_ROWS = 7, 8, 9, 10, 11, 12, 16
XHAT, STREAM, NORMED, KINDS = 0, 1, 2, 3
LANES = 128
OFFSETS = (1, 2, 3, -1, -2, -3)
MASK_OF = {offset: k for k, offset in enumerate(OFFSETS)}


def slabs(width):
    return [slice(c, c + LANES) for c in range(0, width, LANES)]


def row_sum(parts):
    return jnp.sum(functools.reduce(jnp.add, parts), axis=1, keepdims=True)


def fold(value):
    return functools.reduce(jnp.add, [value[8 * i : 8 * i + 8] for i in range(value.shape[0] // 8)])


def clear_edges(padded, frames):
    for slab in range(padded.shape[0]):
        padded[slab, 0:PAD, :] = jnp.zeros((PAD, LANES), F32)
        padded[slab, PAD + frames : PAD + frames + PAD, :] = jnp.zeros((PAD, LANES), F32)


def build_masks(seg_v, masks):
    frames = masks.shape[1]
    seg_v[0:PAD, :] = jnp.full((PAD, LANES), -1.0, F32)
    seg_v[PAD + frames : PAD + frames + PAD, :] = jnp.full((PAD, LANES), -1.0, F32)

    def body(i, carry):
        base = pl.multiple_of(i * 64, 64)
        here = seg_v[pl.ds(base + PAD, 64), :]
        for k, offset in enumerate(OFFSETS):
            there = seg_v[pl.ds(base + PAD + offset, 64), :]
            masks[k, pl.ds(base, 64), :] = jnp.where(there == here, 1.0, 0.0)
        return carry

    lax.fori_loop(0, frames // 64, body, 0)


def start_weights(core, layer, own, peer, target, sem):
    @pl.when(core == lax.div(layer, 2))
    def _():
        pltpu.make_async_copy(own.at[lax.rem(layer, 2)], target, sem).start()

    @pl.when(core != lax.div(layer, 2))
    def _():
        pltpu.make_async_copy(peer.at[lax.rem(layer, 2)], target, sem).start()


def send_row(core, section, source, kept, other, sem):
    @pl.when(core == section)
    def _():
        pltpu.make_async_copy(source, kept, sem).start()

    @pl.when(core != section)
    def _():
        pltpu.make_async_copy(source, other, sem).start()


def forward_kernel(layers, aliased, unroll, flags, x_in, seg_hbm, vec, own_up, own_down, peer_up, peer_down, *rest):
    rest = rest[aliased:]
    hid, dge, saved, rst, kept, other, send = rest[:7]
    (up_v, down_v, hid_v, dge_v, saved_v, rst_v, stream, acc, out_v, x_v, seg_v, masks, w_sem, in_sem, o_sem, s_sem) = rest[7:]
    frames, width = acc.shape
    hidden = hid_v.shape[2]

    @pl.when(flags[0] == 1)
    def _():
        core, micro, row = flags[1], flags[2], flags[3]
        pltpu.make_async_copy(x_in, x_v, s_sem.at[2]).start()
        pltpu.make_async_copy(seg_hbm.at[micro], seg_v.at[pl.ds(PAD, frames)], in_sem).start()
        def fetch(j):
            start_weights(core, j, own_up, peer_up, up_v.at[j], w_sem.at[j, 0])
            start_weights(core, j, own_down, peer_down, down_v.at[j], w_sem.at[j, 1])

        fetch(0)
        clear_edges(stream, frames)
        pltpu.make_async_copy(seg_hbm.at[0], seg_v.at[pl.ds(PAD, frames)], in_sem).wait()
        build_masks(seg_v, masks)
        pltpu.make_async_copy(x_in, x_v, s_sem.at[2]).wait()
        for c, cols in enumerate(slabs(width)):
            stream[c, PAD : PAD + frames, :] = x_v[:, cols].astype(F32)

        def layer(j, carry):
            def conv_norm(i, c):
                base = pl.multiple_of(i * TILE, TILE)
                rows = pl.ds(base, TILE)
                parts = []
                for s, cols in enumerate(slabs(width)):
                    centre = stream[s, pl.ds(base + PAD, TILE), :]
                    saved_v[j, STREAM, rows, cols] = centre.astype(BF16)
                    total = vec[j, CONV_B : CONV_B + 1, cols] + vec[j, 3:4, cols] * centre
                    for offset in OFFSETS:
                        neighbour = stream[s, pl.ds(base + PAD + offset, TILE), :] * masks[MASK_OF[offset], rows, :]
                        total = total + vec[j, offset + 3 : offset + 4, cols] * neighbour
                    parts.append(total)
                mean = row_sum(parts) * (1.0 / width)
                parts = [part - mean for part in parts]
                rstd = lax.rsqrt(row_sum([part * part for part in parts]) * (1.0 / width) + EPSILON)
                for part, cols in zip(parts, slabs(width)):
                    xhat = part * rstd
                    saved_v[j, XHAT, rows, cols] = xhat.astype(BF16)
                    saved_v[j, NORMED, rows, cols] = (xhat * vec[j, GAIN : GAIN + 1, cols] + vec[j, SHIFT : SHIFT + 1, cols]).astype(BF16)
                rst_v[j, rows, :] = jnp.broadcast_to(rstd, (TILE, LANES))
                return c

            lax.fori_loop(0, frames // TILE, conv_norm, 0, unroll=unroll)
            pltpu.make_async_copy(saved_v.at[j], saved.at[row, j], o_sem.at[j, 3]).start()
            pltpu.make_async_copy(rst_v.at[j], rst.at[row, j], o_sem.at[j, 2]).start()
            pltpu.make_async_copy(own_up.at[0], up_v.at[j], w_sem.at[j, 0]).wait()

            @pl.when(j + 1 < layers)
            def _():
                fetch(j + 1)

            pltpu.make_async_copy(own_down.at[0], down_v.at[j], w_sem.at[j, 1]).wait()
            half = frames // 2
            for part in range(2):
                here = slice(part * half, (part + 1) * half)
                for n in range(hidden // COLS):
                    cols = slice(n * COLS, (n + 1) * COLS)
                    if part == 1 and n % 2 == 1 and n // 2 < width // COLS:
                        out = slice(n // 2 * COLS, (n // 2 + 1) * COLS)
                        acc[0:half, out] = jnp.dot(hid_v[j, 0:half, :], down_v[j, :, out], preferred_element_type=F32)
                    at, start = UP_B + n * COLS // width, (n * COLS) % width
                    value = jnp.dot(saved_v[j, NORMED, here], up_v[j, :, cols], preferred_element_type=F32) + vec[j, at : at + 1, start : start + COLS]
                    scaled = value * INV_SQRT2
                    phi_sum = 0.5 + 0.5 * lax.erf(scaled)
                    hid_v[j, here, cols] = (value * phi_sum).astype(BF16)
                    dge_v[j, here, cols] = (phi_sum + scaled * INV_SQRT_PI * jnp.exp2(scaled * scaled * -LOG2_E)).astype(BF16)
            pltpu.make_async_copy(hid_v.at[j], hid.at[row, j], o_sem.at[j, 0]).start()
            pltpu.make_async_copy(dge_v.at[j], dge.at[row, j], o_sem.at[j, 1]).start()
            acc[half:, :] = jnp.dot(hid_v[j, half:, :], down_v[j], preferred_element_type=F32)

            def finish(ends_section, i, c):
                base = pl.multiple_of(i * TILE, TILE)
                rows = pl.ds(base, TILE)
                for s, cols in enumerate(slabs(width)):
                    inner = pl.ds(pl.multiple_of(base + PAD, 8), TILE)
                    branch = acc[rows, cols] + vec[j, DOWN_B : DOWN_B + 1, cols]
                    fresh = stream[s, inner, :] + vec[j, SCALE : SCALE + 1, cols] * branch
                    if ends_section:
                        rounded = fresh.astype(BF16)
                        out_v[lax.div(j, 2), rows, cols] = fresh
                        x_v[rows, cols] = rounded
                        fresh = rounded.astype(F32)
                    stream[s, inner, :] = fresh
                return c

            @pl.when(lax.rem(j, 2) == 1)
            def _():
                lax.fori_loop(0, frames // TILE, functools.partial(finish, True), 0)

            @pl.when(lax.rem(j, 2) == 0)
            def _():
                lax.fori_loop(0, frames // TILE, functools.partial(finish, False), 0)

            @pl.when(j == 1)
            def _():
                send_row(core, 0, out_v.at[0], kept.at[micro], other.at[row], s_sem.at[0])

            return carry

        lax.fori_loop(0, layers, layer, 0)
        send_row(core, 1, out_v.at[1], kept.at[micro], other.at[row], s_sem.at[1])
        pltpu.make_async_copy(x_v, send, s_sem.at[2]).start()
        for j in range(layers):
            pltpu.make_async_copy(hid_v.at[j], hid.at[row, j], o_sem.at[j, 0]).wait()
            pltpu.make_async_copy(dge_v.at[j], dge.at[row, j], o_sem.at[j, 1]).wait()
            pltpu.make_async_copy(rst_v.at[j], rst.at[row, j], o_sem.at[j, 2]).wait()
            pltpu.make_async_copy(saved_v.at[j], saved.at[row, j], o_sem.at[j, 3]).wait()
        pltpu.make_async_copy(out_v.at[0], other.at[row], s_sem.at[0]).wait()
        pltpu.make_async_copy(out_v.at[1], other.at[row], s_sem.at[1]).wait()
        pltpu.make_async_copy(x_v, send, s_sem.at[2]).wait()


SUMS, HEAD = 4, 1
DOWN, UP = 0, 1
VECTORS = 16


def send_sums(core, section, owners, kind, layer, source, vectors, targets, sem):
    kept, kept_last, head, tail = targets
    _, _, block, width = kept.shape
    shares = kept.shape[0] + 1
    size = (block - VECTORS) // 2
    first = 0 if kind == DOWN else size + VECTORS
    columns = source.shape[1] // width
    rows = size // columns
    for stop in range(shares):
        owner = owners[2 * kind + layer, stop]
        pieces = [
            (source.at[pl.ds(pl.multiple_of(owner * rows, 16), rows), pl.ds(b * width, width)], pl.ds(first + b * rows, rows))
            for b in range(columns)
        ]
        if vectors is not None:
            pieces.append((vectors.at[owners[2 * DOWN + layer, stop]], pl.ds(size, VECTORS)))
        for piece, place in pieces:

            @pl.when(core == section)
            def _():
                target = kept.at[stop, layer] if stop < shares - 1 else kept_last.at[layer]
                pltpu.make_async_copy(piece, target.at[place], sem).start()

            @pl.when(core != section)
            def _():
                target = head.at[stop, layer] if stop < HEAD else tail.at[stop - HEAD, layer]
                pltpu.make_async_copy(piece, target.at[place], sem).start()


def pack_vectors(sums, packed):
    shares, _, width = packed.shape
    parts = [sums[r : r + 1, :] for r in range(UP_B, VEC_ROWS - 1)]
    wide = jnp.broadcast_to(jnp.concatenate(parts, axis=1), (8, width * len(parts)))
    size, wide_size = width // shares, width * len(parts) // shares
    is_bias = lax.broadcasted_iota(jnp.int32, (VECTORS, width), 0) == UP_B
    for d in range(shares):
        part = sums if d == 0 else pltpu.roll(sums, width - d * size, 1)
        bias = wide if d == 0 else pltpu.roll(wide, wide.shape[1] - d * wide_size, 1)
        packed[d] = jnp.where(is_bias, jnp.broadcast_to(bias[0:1, :width], (VECTORS, width)), part).astype(BF16)


def backward_kernel(final, aliased, ties, riders, flags, g_one, g_two, seg_hbm, vec, own_up, own_down, peer_up, peer_down, dge, saved, rst, *rest):
    if final:
        owners, hid, down_in, up_in, vec_in = rest[:5]
        rest = rest[5 + ties + aliased :]
        sums_out, (kept, other) = rest[:SUMS], rest[SUMS : SUMS + 2]
        rest = rest[SUMS + 2 :]
    else:
        rest = rest[aliased:]
        gb, gp, vec_out, kept, other, send = rest[:6]
        rest = rest[6 + riders :]
    (up_v, down_v, dge_v, saved_v, rst_v, gb_v, gp_v, vg_v, g_now, fresh_v, gn_v, padded, x_v, seg_v, masks, w_sem, in_sem, g_sem, o_sem, s_sem) = rest[:20]
    if final:
        (hid_v, nrm_v, dwd_v, dwu_v, down_e, up_e, early_v, packed, b_sem) = rest[20:]
    frames, width = g_now.shape
    held, _, hidden = dge_v.shape
    layers = vec.shape[0]
    nt = (((1,), (1,)), ((), ()))
    tn = (((0,), (0,)), ((), ()))
    tall = 2 * TILE
    cols_of = slabs(width)

    @pl.when(flags[0] == 1)
    def _():
        core, micro, row = flags[1], flags[2], flags[3]
        pltpu.make_async_copy(seg_hbm.at[micro], seg_v.at[pl.ds(PAD, frames)], in_sem).start()

        def fetch(j):
            h = lax.rem(j, held)
            start_weights(core, j, own_down, peer_down, down_v.at[h], w_sem.at[h, 1])
            pltpu.make_async_copy(dge.at[row, j], dge_v.at[h], w_sem.at[h, 3]).start()
            start_weights(core, j, own_up, peer_up, up_v.at[h], w_sem.at[h, 0])
            pltpu.make_async_copy(rst.at[row, j], rst_v.at[h], w_sem.at[h, 4]).start()
            pltpu.make_async_copy(saved.at[row, j, 0:2], saved_v.at[h], w_sem.at[h, 2]).start()

        if final:
            pltpu.make_async_copy(vec_in.at[1 - row], early_v, s_sem.at[2]).start()
        source = [pltpu.make_async_copy(g, x_v, g_sem) for g in (g_one, g_two)]
        for k in range(2):

            @pl.when(flags[4] == k)
            def _():
                source[k].start()

        fetch(layers - 1)
        clear_edges(padded, frames)
        source[0].wait()
        for cols in cols_of:

            def enter(t, c):
                rows = pl.ds(pl.multiple_of(t * tall, tall), tall)
                scaled = (vec[layers - 1, SCALE : SCALE + 1, cols] * x_v[rows, cols].astype(F32)).astype(BF16)
                gb_v[layers, 0, rows, cols] = scaled
                return c + fold(scaled.astype(F32))

            total = lax.fori_loop(0, frames // tall, enter, jnp.zeros((8, LANES), F32))
            vg_v[layers, DOWN_B : DOWN_B + 1, cols] = jnp.sum(total, axis=0, keepdims=True)
        pltpu.make_async_copy(seg_hbm.at[0], seg_v.at[pl.ds(PAD, frames)], in_sem).wait()
        build_masks(seg_v, masks)

        def layer(step, carry):
            j = layers - 1 - step
            h = lax.rem(j, held)
            if not final:
                pltpu.make_async_copy(gb_v.at[j + 1, 0], gb.at[row, j], o_sem.at[j, 0]).start()
            pltpu.make_async_copy(own_down.at[0], down_v.at[h], w_sem.at[h, 1]).wait()
            pltpu.make_async_copy(dge.at[0, 0], dge_v.at[h], w_sem.at[h, 3]).wait()
            if final:
                pltpu.make_async_copy(hid.at[row, j], hid_v.at[h], b_sem.at[h, 0]).start()
                pltpu.make_async_copy(down_in.at[j], down_e.at[h], b_sem.at[h, 1]).start()
                pltpu.make_async_copy(saved.at[row, j, NORMED], nrm_v.at[h], b_sem.at[h, 2]).start()
                pltpu.make_async_copy(up_in.at[j], up_e.at[h], b_sem.at[h, 3]).start()
            for n in range(hidden // COLS):
                cols = slice(n * COLS, (n + 1) * COLS)
                value = lax.dot_general(gb_v[j + 1, 0], down_v[h, cols, :], nt, preferred_element_type=F32)
                rounded = (value * dge_v[h, :, cols].astype(F32)).astype(BF16)
                gp_v[h, 0, :, cols] = rounded
                at, start = UP_B + n * COLS // width, (n * COLS) % width
                vg_v[j + 1, at : at + 1, start : start + COLS] = jnp.sum(rounded.astype(F32), axis=0, keepdims=True)
            if not final:
                pltpu.make_async_copy(gp_v.at[h, 0], gp.at[row, j], o_sem.at[j, 1]).start()
            pltpu.make_async_copy(own_up.at[0], up_v.at[h], w_sem.at[h, 0]).wait()
            gn_v[...] = lax.dot_general(gp_v[h, 0], up_v[h], nt, preferred_element_type=F32)
            pltpu.make_async_copy(rst.at[0, 0], rst_v.at[h], w_sem.at[h, 4]).wait()
            pltpu.make_async_copy(saved.at[0, 0, 0:2], saved_v.at[h], w_sem.at[h, 2]).wait()

            @pl.when(j > 0)
            def _():
                fetch(j - 1)

            if final:
                pltpu.make_async_copy(hid.at[0, 0], hid_v.at[h], b_sem.at[h, 0]).wait()
                pltpu.make_async_copy(down_in.at[0], down_e.at[h], b_sem.at[h, 1]).wait()

                @pl.when(j + held < layers)
                def _():
                    pltpu.make_async_copy(dwd_v.at[h], dwd_v.at[h], o_sem.at[h, 0]).wait()
                    pltpu.make_async_copy(dwu_v.at[h], dwu_v.at[h], o_sem.at[h, 1]).wait()
                    pltpu.make_async_copy(packed.at[h], packed.at[h], o_sem.at[h, 1]).wait()

            def down_chunk(n):
                rows = slice(n * COLS, (n + 1) * COLS)
                value = lax.dot_general(hid_v[h, :, rows], gb_v[j + 1, 0], tn, preferred_element_type=F32) + down_e[h, rows, :].astype(F32)
                dwd_v[h, rows, :] = value.astype(BF16)
                return fold(value * down_v[h, rows, :].astype(F32))

            def up_chunk(m, n):
                rows = slice(m * COLS, (m + 1) * COLS)
                cols = slice(n * width, (n + 1) * width)
                value = lax.dot_general(nrm_v[h, :, rows], gp_v[h, 0, :, cols], tn, preferred_element_type=F32) + up_e[h, rows, cols].astype(F32)
                dwu_v[h, rows, cols] = value.astype(BF16)

            odd = lax.rem(j, 2) == 1

            def norm_back(t, c):
                base = t * TILE if isinstance(t, int) else pl.multiple_of(t * TILE, TILE)
                rows = pl.ds(base, TILE)
                inner = pl.ds(base + PAD if isinstance(t, int) else pl.multiple_of(base + PAD, 8), TILE)
                grads = [gn_v[rows, cols] for cols in cols_of]
                xhats = [saved_v[h, XHAT, rows, cols].astype(F32) for cols in cols_of]
                qs = [grad * vec[j, GAIN : GAIN + 1, cols] for grad, cols in zip(grads, cols_of)]
                mean_q = row_sum(qs) * (1.0 / width)
                mean_qx = row_sum([q * xhat for q, xhat in zip(qs, xhats)]) * (1.0 / width)
                rstd = rst_v[h, rows, :]
                out = []
                for s, cols in enumerate(cols_of):
                    grad_conv = rstd * (qs[s] - mean_q - xhats[s] * mean_qx)
                    padded[s, inner, :] = grad_conv
                    g_now[rows, cols] = jnp.where(odd, x_v[rows, cols].astype(F32), fresh_v[rows, cols])
                    out += [c[3 * s] + fold(grads[s] * xhats[s]), c[3 * s + 1] + fold(grads[s]), c[3 * s + 2] + fold(grad_conv)]
                return tuple(out)

            sums = (jnp.zeros((8, LANES), F32),) * (3 * len(cols_of))
            tiles = frames // TILE
            if final:
                parts = hidden // COLS
                scale = jnp.zeros((8, width), F32)
                done = 0
                for n in range(parts):
                    scale = scale + down_chunk(n)
                    while done < tiles * (n + 1) // parts:
                        sums = norm_back(done, sums)
                        done += 1
                vg_v[j + 1, SCALE : SCALE + 1, :] = jnp.sum(scale, axis=0, keepdims=True)
                send_sums(core, lax.div(j, 2), owners, DOWN, lax.rem(j, 2), dwd_v.at[h], None, sums_out, o_sem.at[h, 0])
                pltpu.make_async_copy(saved.at[0, 0, 0], nrm_v.at[h], b_sem.at[h, 2]).wait()
                pltpu.make_async_copy(up_in.at[0], up_e.at[h], b_sem.at[h, 3]).wait()
            else:
                sums = lax.fori_loop(0, tiles, norm_back, sums, unroll=8)
            for s, cols in enumerate(cols_of):
                for k, at in enumerate((GAIN, SHIFT, CONV_B)):
                    vg_v[j + 1, at : at + 1, cols] = jnp.sum(sums[3 * s + k], axis=0, keepdims=True)

            @pl.when(odd & (step > 0))
            def _():
                pltpu.make_async_copy(fresh_v, other.at[row], s_sem.at[0]).wait()

            below = lax.max(j - 1, 0)
            for s, cols in enumerate(cols_of):

                def conv_back(t, c):
                    base = t * tall if isinstance(t, int) else pl.multiple_of(t * tall, tall)
                    rows = pl.ds(base, tall)
                    source = saved_v[h, STREAM, rows, cols].astype(F32)
                    centre = padded[s, pl.ds(base + PAD if isinstance(t, int) else pl.multiple_of(base + PAD, 8), tall), :]
                    total = g_now[rows, cols] + vec[j, 3:4, cols] * centre
                    taps = [None] * 7
                    taps[3] = c[3] + fold(centre * source)
                    for offset in OFFSETS:
                        term = padded[s, pl.ds(base + PAD - offset, tall), :] * masks[MASK_OF[-offset], rows, :]
                        total = total + vec[j, offset + 3 : offset + 4, cols] * term
                        taps[offset + 3] = c[offset + 3] + fold(term * source)
                    rounded = total.astype(BF16)
                    fresh_v[rows, cols] = total
                    x_v[rows, cols] = rounded
                    scaled = (vec[below, SCALE : SCALE + 1, cols] * jnp.where(odd, total, rounded.astype(F32))).astype(BF16)
                    gb_v[j, 0, rows, cols] = scaled
                    return tuple(taps) + (c[7] + fold(scaled.astype(F32)),)

                sums = (jnp.zeros((8, LANES), F32),) * 8
                if final:
                    chunks = [(m, n) for m in range(width // COLS) for n in range(hidden // width)]
                    each = -(-len(chunks) // len(cols_of))
                    mine = chunks[s * each : (s + 1) * each]
                    done = 0
                    for k, (m, n) in enumerate(mine):
                        up_chunk(m, n)
                        while done < frames // tall * (k + 1) // len(mine):
                            sums = conv_back(done, sums)
                            done += 1
                    while done < frames // tall:
                        sums = conv_back(done, sums)
                        done += 1
                else:
                    sums = lax.fori_loop(0, frames // tall, conv_back, sums, unroll=8)
                for k in range(7):
                    vg_v[j + 1, k : k + 1, cols] = jnp.sum(sums[k], axis=0, keepdims=True)
                vg_v[j, DOWN_B : DOWN_B + 1, cols] = jnp.sum(sums[7], axis=0, keepdims=True)
            if final:

                @pl.when(step == 0)
                def _():
                    pltpu.make_async_copy(vec_in.at[0], early_v, s_sem.at[2]).wait()

                pack_vectors(vg_v[j + 1] + early_v[j], packed.at[h])
                send_vectors = packed.at[h]
                send_sums(core, lax.div(j, 2), owners, UP, lax.rem(j, 2), dwu_v.at[h], send_vectors, sums_out, o_sem.at[h, 1])

            @pl.when(jnp.logical_not(odd))
            def _():
                send_row(core, lax.div(j, 2), fresh_v, kept.at[micro], other.at[row], s_sem.at[0])

            return carry

        for i in range(1, layers + 1):
            vg_v[i, SCALE : SCALE + 1, :] = jnp.zeros((1, width), F32)
            vg_v[i, VEC_ROWS - 1 : VEC_ROWS, :] = jnp.zeros((1, width), F32)
        lax.fori_loop(0, layers, layer, 0)
        if final:
            for h in range(held):
                pltpu.make_async_copy(dwd_v.at[h], dwd_v.at[h], o_sem.at[h, 0]).wait()
                pltpu.make_async_copy(dwu_v.at[h], dwu_v.at[h], o_sem.at[h, 1]).wait()
                pltpu.make_async_copy(packed.at[h], packed.at[h], o_sem.at[h, 1]).wait()
        else:
            pltpu.make_async_copy(vg_v.at[pl.ds(1, layers)], vec_out.at[row], s_sem.at[2]).start()
            pltpu.make_async_copy(x_v, send, s_sem.at[1]).start()
            for j in range(layers):
                pltpu.make_async_copy(gb_v.at[j + 1, 0], gb.at[row, j], o_sem.at[j, 0]).wait()
                pltpu.make_async_copy(gp_v.at[j, 0], gp.at[row, j], o_sem.at[j, 1]).wait()
            pltpu.make_async_copy(x_v, send, s_sem.at[1]).wait()
            pltpu.make_async_copy(vg_v.at[pl.ds(1, layers)], vec_out.at[row], s_sem.at[2]).wait()
        pltpu.make_async_copy(fresh_v, other.at[row], s_sem.at[0]).wait()


def early_kernel(flags, hid, gb, saved, gp, down_out, up_out, hid_v, gb_v, nrm_v, gp_v, dwd_v, dwu_v, sem, o_sem):
    frames, width = gb_v.shape[1:]
    hidden = hid_v.shape[2]
    layers = hid.shape[1]
    tn = (((0,), (0,)), ((), ()))

    @pl.when(flags[0] == 1)
    def _():
        row = flags[3]

        def copies(j, h):
            pairs = ((hid.at[row, j], hid_v), (gb.at[row, j], gb_v), (saved.at[row, j, NORMED], nrm_v), (gp.at[row, j], gp_v))
            return [pltpu.make_async_copy(a, b.at[h], sem.at[h, k]) for k, (a, b) in enumerate(pairs)]

        def leaving(j, h):
            return [
                pltpu.make_async_copy(dwd_v.at[h], down_out.at[j], o_sem.at[h, 0]),
                pltpu.make_async_copy(dwu_v.at[h], up_out.at[j], o_sem.at[h, 1]),
            ]

        for copy in copies(layers - 1, (layers - 1) % 2):
            copy.start()

        def layer(step, carry):
            j = layers - 1 - step
            h = lax.rem(j, 2)

            @pl.when(j > 0)
            def _():
                for copy in copies(j - 1, 1 - h):
                    copy.start()

            for copy in copies(j, h):
                copy.wait()

            @pl.when(j + 2 < layers)
            def _():
                for copy in leaving(j + 2, h):
                    copy.wait()

            def down_chunk(n, c):
                rows = pl.ds(pl.multiple_of(n * width, width), width)
                dwd_v[h, rows, :] = lax.dot_general(hid_v[h, :, rows], gb_v[h], tn, preferred_element_type=F32).astype(BF16)
                return c

            def up_chunk(n, c):
                cols = pl.ds(pl.multiple_of(n * width, width), width)
                dwu_v[h, :, cols] = lax.dot_general(nrm_v[h], gp_v[h, :, cols], tn, preferred_element_type=F32).astype(BF16)
                return c

            lax.fori_loop(0, hidden // width, down_chunk, 0)
            lax.fori_loop(0, hidden // width, up_chunk, 0)
            for copy in leaving(j, h):
                copy.start()
            return carry

        lax.fori_loop(0, layers, layer, 0)
        for h in range(2):
            for copy in leaving(h, h):
                copy.wait()


def weight_kernel(ties, flags, owners, own_down, peer_down, all_hid, all_gb, all_saved, all_gp, vec_in, *rest):
    rest = rest[ties:]
    sums_out, rest = rest[:SUMS], rest[SUMS:]
    hid_v, gb_v, nrm_v, gp_v, down_v, dwd_v, dwu_v, vec_v, packed, sem, o_sem, s_sem = rest
    frames, width = gb_v.shape[2:]
    hidden = hid_v.shape[3]
    layers = all_hid.shape[1]
    tn = (((0,), (0,)), ((), ()))

    @pl.when(flags[0] == 1)
    def _():
        core = flags[1]

        def copies(j, h):
            pairs = []
            for row in range(2):
                pairs += [
                    (all_hid.at[row, j], hid_v.at[h, row]),
                    (all_gb.at[row, j], gb_v.at[h, row]),
                    (all_saved.at[row, j, NORMED], nrm_v.at[h, row]),
                    (all_gp.at[row, j], gp_v.at[h, row]),
                ]
            return [pltpu.make_async_copy(a, b, sem.at[h, k]) for k, (a, b) in enumerate(pairs)]

        def fetch(j):
            h = lax.rem(j, 2)
            start_weights(core, j, own_down, peer_down, down_v.at[h], sem.at[h, 8])
            for copy in copies(j, h):
                copy.start()

        fetch(layers - 1)
        pltpu.make_async_copy(vec_in, vec_v, s_sem).start()
        pltpu.make_async_copy(vec_in, vec_v, s_sem).wait()

        def layer(step, carry):
            j = layers - 1 - step
            h = lax.rem(j, 2)

            @pl.when(j > 0)
            def _():
                fetch(j - 1)

            pltpu.make_async_copy(own_down.at[0], down_v.at[h], sem.at[h, 8]).wait()
            for copy in copies(j, h):
                copy.wait()

            @pl.when(j + 2 < layers)
            def _():
                pltpu.make_async_copy(dwd_v.at[h], dwd_v.at[h], o_sem.at[h, 0]).wait()
                pltpu.make_async_copy(dwu_v.at[h], dwu_v.at[h], o_sem.at[h, 1]).wait()
                pltpu.make_async_copy(packed.at[h], packed.at[h], o_sem.at[h, 1]).wait()

            def down_chunk(n, scale):
                rows = pl.ds(pl.multiple_of(n * COLS, COLS), COLS)
                left = hid_v[h, :, :, rows].reshape(2 * frames, COLS)
                value = lax.dot_general(left, gb_v[h].reshape(2 * frames, width), tn, preferred_element_type=F32)
                dwd_v[h, rows, :] = value.astype(BF16)
                return scale + fold(value * down_v[h, rows, :].astype(F32))

            scale = lax.fori_loop(0, hidden // COLS, down_chunk, jnp.zeros((8, width), F32))
            scale = jnp.sum(scale, axis=0, keepdims=True)
            vectors = vec_v[0, j] + vec_v[1, j]
            is_scale = lax.broadcasted_iota(jnp.int32, vectors.shape, 0) == SCALE
            pack_vectors(jnp.where(is_scale, jnp.broadcast_to(scale, vectors.shape), vectors), packed.at[h])
            send_sums(core, lax.div(j, 2), owners, DOWN, lax.rem(j, 2), dwd_v.at[h], None, sums_out, o_sem.at[h, 0])

            def up_chunk(n, c):
                cols = pl.ds(pl.multiple_of(n * width, width), width)
                right = gp_v[h, :, :, cols].reshape(2 * frames, width)
                value = lax.dot_general(nrm_v[h].reshape(2 * frames, width), right, tn, preferred_element_type=F32)
                dwu_v[h, :, cols] = value.astype(BF16)
                return c

            lax.fori_loop(0, hidden // width, up_chunk, 0)
            send_sums(core, lax.div(j, 2), owners, UP, lax.rem(j, 2), dwu_v.at[h], packed.at[h], sums_out, o_sem.at[h, 1])
            return carry

        lax.fori_loop(0, layers, layer, 0)
        for h in range(2):
            pltpu.make_async_copy(dwd_v.at[h], dwd_v.at[h], o_sem.at[h, 0]).wait()
            pltpu.make_async_copy(dwu_v.at[h], dwu_v.at[h], o_sem.at[h, 1]).wait()
            pltpu.make_async_copy(packed.at[h], packed.at[h], o_sem.at[h, 1]).wait()


def place_kernel(at, kept_in, rows, tie, kept, held, sem):
    count = rows.shape[0]
    for i in range(count):
        pltpu.make_async_copy(rows.at[i], held.at[i], sem.at[i]).start()
    for i in range(count):
        pltpu.make_async_copy(rows.at[i], held.at[i], sem.at[i]).wait()
        pltpu.make_async_copy(held.at[i], kept.at[at[0] + i], sem.at[i]).start()
    for i in range(count):
        pltpu.make_async_copy(held.at[i], kept.at[at[0] + i], sem.at[i]).wait()


def hold_kernel(value_in, tie, value):
    pass


def final_kernel(down_0, down_1, up_0, up_1, kept, other, scales, *rest):
    conv_out, conv_b_out, gain_out, shift_out, up_out, up_b_out, down_out, down_b_out, scale_out = rest
    size, wide = conv_b_out.shape[1], up_b_out.shape[1]
    rows, width = down_out.shape[1:]
    for layer, (down, up) in enumerate(((down_0, up_0), (down_1, up_1))):
        total = down[...].astype(F32) + kept[layer, : rows + VECTORS].astype(F32) + other[layer, : rows + VECTORS].astype(F32)
        down_out[layer] = total[:rows]
        vectors = total[rows:]
        at = slice(layer, layer + 1)
        conv_out[layer] = vectors[:CONV_B, :size]
        conv_b_out[at, :] = vectors[CONV_B : CONV_B + 1, :size]
        gain_out[at, :] = vectors[GAIN : GAIN + 1, :size]
        shift_out[at, :] = vectors[SHIFT : SHIFT + 1, :size]
        down_b = vectors[DOWN_B : DOWN_B + 1, :size]
        down_b_out[at, :] = down_b
        scale_out[at, :] = (vectors[SCALE : SCALE + 1, :size] + scales[0, at, :] * down_b) / scales[1, at, :]
        up_b_out[at, :] = vectors[UP_B : UP_B + 1, :wide]
        total = up[...].astype(F32) + kept[layer, rows + VECTORS :].astype(F32) + other[layer, rows + VECTORS :].astype(F32)
        for b in range(up_out.shape[2] // width):
            up_out[layer, :, b * width : (b + 1) * width] = total[b * size : (b + 1) * size]


ANY = pl.BlockSpec(memory_space=pl.ANY)
HBM = pl.BlockSpec(memory_space=pltpu.HBM)
SMEM = pl.BlockSpec(memory_space=pltpu.SMEM)
VMEM = pl.BlockSpec(memory_space=pltpu.VMEM)


def near(value):
    return pltpu.with_memory_space_constraint(value, pltpu.VMEM)


def run_forward(flags, x, seg, vec, weights, earlier, unroll=16):
    layers = vec.shape[0]
    micro = seg.shape[0]
    frames, width = x.shape
    hidden = weights[0].shape[2]
    shapes = (
        jax.ShapeDtypeStruct((2, layers, frames, hidden), BF16),
        jax.ShapeDtypeStruct((2, layers, frames, hidden), BF16),
        jax.ShapeDtypeStruct((2, layers, KINDS, frames, width), BF16),
        jax.ShapeDtypeStruct((2, layers, frames, LANES), F32),
        jax.ShapeDtypeStruct((micro, frames, width), F32),
        jax.ShapeDtypeStruct((2, frames, width), F32),
        jax.ShapeDtypeStruct((frames, width), BF16),
    )
    aliased = len(earlier)
    return pl.pallas_call(
        functools.partial(forward_kernel, layers, aliased, unroll),
        out_shape=shapes,
        in_specs=[SMEM, ANY, ANY, VMEM] + [ANY] * (4 + aliased),
        out_specs=(ANY,) * len(shapes),
        input_output_aliases={8 + i: i for i in range(aliased)},
        scratch_shapes=[
            pltpu.VMEM((layers, width, hidden), BF16),
            pltpu.VMEM((layers, hidden, width), BF16),
            pltpu.VMEM((layers, frames, hidden), BF16),
            pltpu.VMEM((layers, frames, hidden), BF16),
            pltpu.VMEM((layers, KINDS, frames, width), BF16),
            pltpu.VMEM((layers, frames, LANES), F32),
            pltpu.VMEM((width // LANES, frames + 2 * PAD, LANES), F32),
            pltpu.VMEM((frames, width), F32),
            pltpu.VMEM((2, frames, width), F32),
            pltpu.VMEM((frames, width), BF16),
            pltpu.VMEM((frames + 2 * PAD, LANES), F32),
            pltpu.VMEM((6, frames, LANES), F32),
            pltpu.SemaphoreType.DMA((layers, 2)),
            pltpu.SemaphoreType.DMA,
            pltpu.SemaphoreType.DMA((layers, 4)),
            pltpu.SemaphoreType.DMA((3,)),
        ],
        compiler_params=pltpu.CompilerParams(vmem_limit_bytes=VMEM_LIMIT),
        cost_estimate=COST,
    )(flags, x, seg, vec, *weights, *earlier)


def sum_shapes(shares, hidden, width):
    block = (2, 2 * (hidden // shares) + VECTORS, width)
    return tuple(jax.ShapeDtypeStruct(shape, BF16) for shape in ((shares - 1, *block), block, (HEAD, *block), (shares - HEAD, *block)))


def run_backward(flags, g, seg, vec, weights, state, earlier, final=(), ties=(), riders=()):
    frames, width = g[0].shape
    hidden = weights[0].shape[2]
    layers, micro = vec.shape[0], seg.shape[0]
    held = 2 if final else layers
    grads = (
        jax.ShapeDtypeStruct((micro, frames, width), F32),
        jax.ShapeDtypeStruct((2, frames, width), F32),
    )
    if final:
        shapes = (*sum_shapes(final[0].shape[1], hidden, width), *grads)
    else:
        shapes = (
            jax.ShapeDtypeStruct((2, layers, frames, width), BF16),
            jax.ShapeDtypeStruct((2, layers, frames, hidden), BF16),
            jax.ShapeDtypeStruct((2, layers, VEC_ROWS, width), F32),
            *grads,
            jax.ShapeDtypeStruct((frames, width), BF16),
        )
    earlier = (*earlier, *riders)
    shapes = (*shapes, *(jax.ShapeDtypeStruct(rider.shape, rider.dtype) for rider in riders))
    aliased = len(earlier)
    targets = [*range(len(earlier) - len(riders)), *range(len(shapes) - len(riders), len(shapes))]
    scratch = [
        pltpu.VMEM((held, width, hidden), BF16),
        pltpu.VMEM((held, hidden, width), BF16),
        pltpu.VMEM((held, frames, hidden), BF16),
        pltpu.VMEM((held, 2, frames, width), BF16),
        pltpu.VMEM((held, frames, LANES), F32),
        pltpu.VMEM((layers + 1, 1, frames, width), BF16),
        pltpu.VMEM((held, 1, frames, hidden), BF16),
        pltpu.VMEM((layers + 1, VEC_ROWS, width), F32),
        pltpu.VMEM((frames, width), F32),
        pltpu.VMEM((frames, width), F32),
        pltpu.VMEM((frames, width), F32),
        pltpu.VMEM((width // LANES, frames + 2 * PAD, LANES), F32),
        pltpu.VMEM((frames, width), BF16),
        pltpu.VMEM((frames + 2 * PAD, LANES), F32),
        pltpu.VMEM((6, frames, LANES), F32),
        pltpu.SemaphoreType.DMA((held, 5)),
        pltpu.SemaphoreType.DMA,
        pltpu.SemaphoreType.DMA,
        pltpu.SemaphoreType.DMA((held, 2)),
        pltpu.SemaphoreType.DMA((3,)),
    ]
    if final:
        scratch += [
            pltpu.VMEM((held, frames, hidden), BF16),
            pltpu.VMEM((held, frames, width), BF16),
            pltpu.VMEM((held, hidden, width), BF16),
            pltpu.VMEM((held, width, hidden), BF16),
            pltpu.VMEM((held, hidden, width), BF16),
            pltpu.VMEM((held, width, hidden), BF16),
            pltpu.VMEM((layers, VEC_ROWS, width), F32),
            pltpu.VMEM((held, final[0].shape[1], VECTORS, width), BF16),
            pltpu.SemaphoreType.DMA((held, 4)),
        ]
    first_alias = 12 + len(final) + len(ties)
    return pl.pallas_call(
        functools.partial(backward_kernel, bool(final), aliased, len(ties), len(riders)),
        out_shape=shapes,
        in_specs=[SMEM, ANY, ANY, ANY, VMEM] + [ANY] * 7 + ([SMEM] + [ANY] * 4 if final else []) + [ANY] * (len(ties) + aliased),
        out_specs=tuple(HBM if final and k < SUMS else ANY for k in range(len(shapes))),
        input_output_aliases={first_alias + i: target for i, target in enumerate(targets)},
        scratch_shapes=scratch,
        compiler_params=pltpu.CompilerParams(vmem_limit_bytes=VMEM_LIMIT),
        cost_estimate=COST,
    )(flags, *g, seg, vec, *weights, *state, *final, *ties, *earlier)


def run_early(flags, hid, gb, saved, gp):
    _, layers, frames, hidden = hid.shape
    width = gb.shape[3]
    return pl.pallas_call(
        early_kernel,
        out_shape=(jax.ShapeDtypeStruct((layers, hidden, width), BF16), jax.ShapeDtypeStruct((layers, width, hidden), BF16)),
        in_specs=[SMEM] + [ANY] * 4,
        out_specs=(ANY,) * 2,
        scratch_shapes=[
            pltpu.VMEM((2, frames, hidden), BF16),
            pltpu.VMEM((2, frames, width), BF16),
            pltpu.VMEM((2, frames, width), BF16),
            pltpu.VMEM((2, frames, hidden), BF16),
            pltpu.VMEM((2, hidden, width), BF16),
            pltpu.VMEM((2, width, hidden), BF16),
            pltpu.SemaphoreType.DMA((2, 4)),
            pltpu.SemaphoreType.DMA((2, 2)),
        ],
        compiler_params=pltpu.CompilerParams(vmem_limit_bytes=VMEM_LIMIT),
        cost_estimate=COST,
    )(flags, hid, gb, saved, gp)


def run_weights(flags, owners, weights, hid, gb, saved, gp, vectors, ties):
    _, layers, frames, hidden = hid.shape
    width = gb.shape[3]
    shares = owners.shape[1]
    return pl.pallas_call(
        functools.partial(weight_kernel, len(ties)),
        out_shape=sum_shapes(shares, hidden, width),
        in_specs=[SMEM, SMEM] + [ANY] * (7 + len(ties)),
        out_specs=(HBM,) * SUMS,
        scratch_shapes=[
            pltpu.VMEM((2, 2, frames, hidden), BF16),
            pltpu.VMEM((2, 2, frames, width), BF16),
            pltpu.VMEM((2, 2, frames, width), BF16),
            pltpu.VMEM((2, 2, frames, hidden), BF16),
            pltpu.VMEM((2, hidden, width), BF16),
            pltpu.VMEM((2, hidden, width), BF16),
            pltpu.VMEM((2, width, hidden), BF16),
            pltpu.VMEM(vectors.shape, F32),
            pltpu.VMEM((2, shares, VECTORS, width), BF16),
            pltpu.SemaphoreType.DMA((2, 9)),
            pltpu.SemaphoreType.DMA((2, 2)),
            pltpu.SemaphoreType.DMA,
        ],
        compiler_params=pltpu.CompilerParams(vmem_limit_bytes=VMEM_LIMIT),
        cost_estimate=COST,
    )(flags, owners, weights[1], weights[3], hid, gb, saved, gp, vectors, *ties)


def run_place(kept, rows, at, tie):
    return pl.pallas_call(
        place_kernel,
        out_shape=jax.ShapeDtypeStruct(kept.shape, kept.dtype),
        in_specs=[SMEM, ANY, ANY, ANY],
        out_specs=ANY,
        input_output_aliases={1: 0},
        scratch_shapes=[pltpu.VMEM(rows.shape, rows.dtype), pltpu.SemaphoreType.DMA(rows.shape[:1])],
        cost_estimate=COST,
    )(at.reshape(1).astype(jnp.int32), kept, rows, tie)


def hold(value, tie):
    return pl.pallas_call(
        hold_kernel,
        out_shape=jax.ShapeDtypeStruct(value.shape, value.dtype),
        in_specs=[HBM, ANY],
        out_specs=HBM,
        input_output_aliases={0: 0},
        cost_estimate=COST,
    )(value, tie)


def run_final(down, up, kept, other, scales, shares, hidden):
    width = kept.shape[2]
    size, wide = width // shares, hidden // shares
    shapes = ((2, CONV_B, size), (2, size), (2, size), (2, size), (2, size, hidden), (2, wide), (2, wide, width), (2, size), (2, size))
    return pl.pallas_call(
        final_kernel,
        out_shape=tuple(jax.ShapeDtypeStruct(shape, F32) for shape in shapes),
        in_specs=[VMEM] * 7,
        out_specs=(VMEM,) * len(shapes),
        compiler_params=pltpu.CompilerParams(vmem_limit_bytes=VMEM_LIMIT // 2),
        cost_estimate=COST,
    )(*down, *up, kept, other, scales)


def ring_order(count):
    return list(range(0, count, 2)) + list(range(count - 1, 0, -2))


def ring_owners(ways, axis):
    count = lax.axis_size(axis)
    device = lax.axis_index(axis)
    mine = jnp.where(device % 2 == 0, device // 2, count - 1 - device // 2)
    places = jnp.stack([lax.rem(mine - way * (1 + jnp.arange(count, dtype=jnp.int32)) + 2 * count, count) for way in ways])
    return jnp.where(places < count - count // 2, 2 * places, 2 * (count - places) - 1)


def after(value, earlier):
    return lax.optimization_barrier((value, earlier))[0]


def ring_step(flows, ways, axis):
    count = lax.axis_size(axis)
    order = ring_order(count)
    return [
        lax.ppermute(value, axis, [(order[p], order[(p + way) % count]) for p in range(count)]) for value, way in zip(flows, ways)
    ]


def per_device(
    inputs,
    segment_ids,
    cotangent,
    conv_weight,
    conv_bias,
    norm_gain,
    norm_bias,
    up_weight,
    up_bias,
    down_weight,
    down_bias,
    layer_scale,
):
    micro, _, frames, width = inputs.shape
    hidden = up_weight.shape[2]
    shares = lax.axis_size("dp")
    section = lax.axis_index("section")
    chip, core = section // 2, section % 2
    exchange = [(0, 1), (1, 0), (2, 3), (3, 2)]

    small = jnp.concatenate(
        [
            conv_weight,
            conv_bias[:, None],
            norm_gain[:, None],
            norm_bias[:, None],
            down_bias[:, None],
            layer_scale[:, None],
            up_bias.reshape(2, -1, width),
            jnp.zeros((2, 1, width), BF16),
        ],
        axis=1,
    )
    small_peer = lax.ppermute(small, "section", exchange)
    up_peer = lax.ppermute(up_weight, "section", exchange)
    down_peer = lax.ppermute(down_weight, "section", exchange)
    vec = jnp.where(core == 0, jnp.concatenate([small, small_peer]), jnp.concatenate([small_peer, small])).astype(F32)
    weights = (up_weight, down_weight, up_peer, down_peer)
    masks = jnp.broadcast_to(segment_ids[:, 0, :, None].astype(F32), (micro, frames, LANES))
    inputs, cotangent = inputs[:, 0], cotangent[:, 0]

    def flags(active, row, choice=0):
        return jnp.stack([jnp.asarray(v, jnp.int32) for v in (active, core, 2 * core + row, row, choice)])

    first, last = chip == 0, chip == 1
    ways = ((1, -1), (-1, 1))
    owners = ring_owners([way for kind in ways for way in kind], "dp")

    def row_of(array, row):
        return lax.dynamic_index_in_dim(array, 2 * core + row, 0, keepdims=False)

    down_pairs, up_pairs = [(0, 2), (1, 3)], [(2, 0), (3, 1)]
    state = run_forward(flags(first, 0), row_of(inputs, 0), masks, vec, weights, ())
    arrived = lax.ppermute(state[6], "section", down_pairs)
    state = run_forward(flags(first, 1), row_of(inputs, 1), masks, vec, weights, state[:6], unroll=1)
    arrived_next = lax.ppermute(state[6], "section", down_pairs)
    state = run_forward(flags(last, 0), near(arrived), masks, vec, weights, state[:6])
    gradient = row_of(cotangent, 0)
    back = run_backward(flags(last, 0), (gradient, gradient), masks, vec, weights, state[1:4], ())
    returned = lax.ppermute(back[5], "section", up_pairs)
    state = run_forward(flags(last, 1), near(arrived_next), masks, vec, weights, state[:6])
    gradients = (row_of(cotangent, 1), near(returned))
    back = run_backward(flags(True, jnp.where(last, 1, 0), first), gradients, masks, vec, weights, state[1:4], back[:5], riders=state[4:6])
    returned = near(lax.ppermute(back[5], "section", up_pairs))
    gb, gp, vectors, grads_kept, grads_other, _, outputs_kept, outputs_other = back

    def assemble(mine, other, tie):
        return run_place(mine, lax.ppermute(other, "section", exchange), 2 * (1 - core), tie)[None, :, None]

    section_outputs = assemble(outputs_kept, outputs_other, vectors)
    early = run_early(flags(first, 0), state[0], gb, state[2], gp)
    sums = run_weights(flags(last, 0), owners, weights, state[0], gb, state[2], gp, vectors, (returned, section_outputs))
    shard = lax.axis_index("dp")
    scales = jnp.stack([down_bias, layer_scale]).astype(F32)
    scales = lax.dynamic_slice_in_dim(scales, shard * (width // shares), width // shares, 2)
    *sums, grads_kept, grads_other = run_backward(
        flags(first, 1),
        (returned, returned),
        masks,
        vec,
        weights,
        state[1:4],
        (*sums, grads_kept, grads_other),
        (owners, state[0], *early, vectors),
        (scales,),
    )

    kept, kept_last, head, tail = sums
    head = lax.ppermute(head, "section", exchange)
    tail = lax.ppermute(hold(tail, head), "section", exchange)
    size = hidden // shares
    spans = (slice(0, size + VECTORS), slice(size + VECTORS, None))

    def addend(stop, kind, layer):
        other = head[stop, layer, spans[kind]] if stop < HEAD else tail[stop - HEAD, layer, spans[kind]]
        return kept[stop, layer, spans[kind]].astype(F32) + other.astype(F32)

    flows = [[addend(0, kind, layer).astype(BF16) for layer in range(2)] for kind in (DOWN, UP)]
    for stop in range(1, shares):
        for kind in (DOWN, UP):
            moved = ring_step(flows[kind], ways[kind], "dp")
            if kind == DOWN or stop > 1:
                moved = after(moved, flows[1 - kind])
            if stop < shares - 1:
                moved = [(value.astype(F32) + addend(stop, kind, layer)).astype(BF16) for layer, value in enumerate(moved)]
            flows[kind] = moved
        if stop == 3:
            input_grads = assemble(grads_kept, grads_other, flows[UP][0])
    grads = run_final(flows[DOWN], flows[UP], kept_last, tail[-1], scales, shares, hidden)
    return (section_outputs, input_grads, *grads)


def solution(mesh):
    in_specs = (
        P(None, "dp", None, None),
        P(None, "dp", None),
        P(None, "dp", None, None),
        P("section", None, None),
        P("section", None),
        P("section", None),
        P("section", None),
        P("section", None, None),
        P("section", None),
        P("section", None, None),
        P("section", None),
        P("section", None),
    )
    out_specs = (
        P("section", None, "dp", None, None),
        P("section", None, "dp", None, None),
        P("section", None, "dp"),
        P("section", "dp"),
        P("section", "dp"),
        P("section", "dp"),
        P("section", "dp", None),
        P("section", "dp"),
        P("section", "dp", None),
        P("section", "dp"),
        P("section", "dp"),
    )
    return jax.shard_map(per_device, mesh=mesh, in_specs=in_specs, out_specs=out_specs, check_vma=False)
```

```python
import functools

import jax
import jax.numpy as jnp
from jax import lax
from jax.experimental import pallas as pl
from jax.experimental.pallas import tpu as pltpu
from jax.sharding import PartitionSpec as P

EPSILON = 1e-06
INV_SQRT2 = 0.7071067811865476
INV_SQRT_PI = 0.5641895835477563
LOG2_E = 1.4426950408889634
F32 = jnp.float32
BF16 = jnp.bfloat16
TILE = 32
PAD = 8
COLS = 256
VMEM_LIMIT = 60 * 2**20
COST = pl.CostEstimate(flops=1, bytes_accessed=1, transcendentals=0)

CONV_B, GAIN, SHIFT, DOWN_B, SCALE, UP_B, VEC_ROWS = 7, 8, 9, 10, 11, 12, 16
XHAT, STREAM, NORMED, KINDS = 0, 1, 2, 3
LANES = 128
OFFSETS = (1, 2, 3, -1, -2, -3)
MASK_OF = {offset: k for k, offset in enumerate(OFFSETS)}


def slabs(width):
    return [slice(c, c + LANES) for c in range(0, width, LANES)]


def row_sum(parts):
    return jnp.sum(functools.reduce(jnp.add, parts), axis=1, keepdims=True)


def fold(value):
    return functools.reduce(jnp.add, [value[8 * i : 8 * i + 8] for i in range(value.shape[0] // 8)])


def clear_edges(padded, frames):
    for slab in range(padded.shape[0]):
        padded[slab, 0:PAD, :] = jnp.zeros((PAD, LANES), F32)
        padded[slab, PAD + frames : PAD + frames + PAD, :] = jnp.zeros((PAD, LANES), F32)


def build_masks(seg_v, masks):
    frames = masks.shape[1]
    seg_v[0:PAD, :] = jnp.full((PAD, LANES), -1.0, F32)
    seg_v[PAD + frames : PAD + frames + PAD, :] = jnp.full((PAD, LANES), -1.0, F32)

    def body(i, carry):
        base = pl.multiple_of(i * 64, 64)
        here = seg_v[pl.ds(base + PAD, 64), :]
        for k, offset in enumerate(OFFSETS):
            there = seg_v[pl.ds(base + PAD + offset, 64), :]
            masks[k, pl.ds(base, 64), :] = jnp.where(there == here, 1.0, 0.0)
        return carry

    lax.fori_loop(0, frames // 64, body, 0)


def start_weights(core, layer, own, peer, target, sem):
    @pl.when(core == lax.div(layer, 2))
    def _():
        pltpu.make_async_copy(own.at[lax.rem(layer, 2)], target, sem).start()

    @pl.when(core != lax.div(layer, 2))
    def _():
        pltpu.make_async_copy(peer.at[lax.rem(layer, 2)], target, sem).start()


def send_row(core, section, source, kept, other, sem):
    @pl.when(core == section)
    def _():
        pltpu.make_async_copy(source, kept, sem).start()

    @pl.when(core != section)
    def _():
        pltpu.make_async_copy(source, other, sem).start()


def forward_kernel(layers, aliased, unroll, flags, x_in, seg_hbm, vec, own_up, own_down, peer_up, peer_down, *rest):
    rest = rest[aliased:]
    hid, dge, saved, rst, kept, other, send = rest[:7]
    (up_v, down_v, hid_v, dge_v, saved_v, rst_v, stream, acc, out_v, x_v, seg_v, masks, w_sem, in_sem, o_sem, s_sem) = rest[7:]
    frames, width = acc.shape
    hidden = hid_v.shape[2]

    @pl.when(flags[0] == 1)
    def _():
        core, micro, row = flags[1], flags[2], flags[3]
        pltpu.make_async_copy(x_in, x_v, s_sem.at[2]).start()
        pltpu.make_async_copy(seg_hbm.at[micro], seg_v.at[pl.ds(PAD, frames)], in_sem).start()
        def fetch(j):
            start_weights(core, j, own_up, peer_up, up_v.at[j], w_sem.at[j, 0])
            start_weights(core, j, own_down, peer_down, down_v.at[j], w_sem.at[j, 1])

        fetch(0)
        clear_edges(stream, frames)
        pltpu.make_async_copy(seg_hbm.at[0], seg_v.at[pl.ds(PAD, frames)], in_sem).wait()
        build_masks(seg_v, masks)
        pltpu.make_async_copy(x_in, x_v, s_sem.at[2]).wait()
        for c, cols in enumerate(slabs(width)):
            stream[c, PAD : PAD + frames, :] = x_v[:, cols].astype(F32)

        def layer(j, carry):
            def conv_norm(i, c):
                base = pl.multiple_of(i * TILE, TILE)
                rows = pl.ds(base, TILE)
                parts = []
                for s, cols in enumerate(slabs(width)):
                    centre = stream[s, pl.ds(base + PAD, TILE), :]
                    saved_v[j, STREAM, rows, cols] = centre.astype(BF16)
                    total = vec[j, CONV_B : CONV_B + 1, cols] + vec[j, 3:4, cols] * centre
                    for offset in OFFSETS:
                        neighbour = stream[s, pl.ds(base + PAD + offset, TILE), :] * masks[MASK_OF[offset], rows, :]
                        total = total + vec[j, offset + 3 : offset + 4, cols] * neighbour
                    parts.append(total)
                mean = row_sum(parts) * (1.0 / width)
                parts = [part - mean for part in parts]
                rstd = lax.rsqrt(row_sum([part * part for part in parts]) * (1.0 / width) + EPSILON)
                for part, cols in zip(parts, slabs(width)):
                    xhat = part * rstd
                    saved_v[j, XHAT, rows, cols] = xhat.astype(BF16)
                    saved_v[j, NORMED, rows, cols] = (xhat * vec[j, GAIN : GAIN + 1, cols] + vec[j, SHIFT : SHIFT + 1, cols]).astype(BF16)
                rst_v[j, rows, :] = jnp.broadcast_to(rstd, (TILE, LANES))
                return c

            lax.fori_loop(0, frames // TILE, conv_norm, 0, unroll=unroll)
            pltpu.make_async_copy(saved_v.at[j], saved.at[row, j], o_sem.at[j, 3]).start()
            pltpu.make_async_copy(rst_v.at[j], rst.at[row, j], o_sem.at[j, 2]).start()
            pltpu.make_async_copy(own_up.at[0], up_v.at[j], w_sem.at[j, 0]).wait()

            @pl.when(j + 1 < layers)
            def _():
                fetch(j + 1)

            pltpu.make_async_copy(own_down.at[0], down_v.at[j], w_sem.at[j, 1]).wait()
            half = frames // 2
            for part in range(2):
                here = slice(part * half, (part + 1) * half)
                for n in range(hidden // COLS):
                    cols = slice(n * COLS, (n + 1) * COLS)
                    if part == 1 and n % 2 == 1 and n // 2 < width // COLS:
                        out = slice(n // 2 * COLS, (n // 2 + 1) * COLS)
                        acc[0:half, out] = jnp.dot(hid_v[j, 0:half, :], down_v[j, :, out], preferred_element_type=F32)
                    at, start = UP_B + n * COLS // width, (n * COLS) % width
                    value = jnp.dot(saved_v[j, NORMED, here], up_v[j, :, cols], preferred_element_type=F32) + vec[j, at : at + 1, start : start + COLS]
                    scaled = value * INV_SQRT2
                    phi_sum = 0.5 + 0.5 * lax.erf(scaled)
                    hid_v[j, here, cols] = (value * phi_sum).astype(BF16)
                    dge_v[j, here, cols] = (phi_sum + scaled * INV_SQRT_PI * jnp.exp2(scaled * scaled * -LOG2_E)).astype(BF16)
            pltpu.make_async_copy(hid_v.at[j], hid.at[row, j], o_sem.at[j, 0]).start()
            pltpu.make_async_copy(dge_v.at[j], dge.at[row, j], o_sem.at[j, 1]).start()
            acc[half:, :] = jnp.dot(hid_v[j, half:, :], down_v[j], preferred_element_type=F32)

            def finish(ends_section, i, c):
                base = pl.multiple_of(i * TILE, TILE)
                rows = pl.ds(base, TILE)
                for s, cols in enumerate(slabs(width)):
                    inner = pl.ds(pl.multiple_of(base + PAD, 8), TILE)
                    branch = acc[rows, cols] + vec[j, DOWN_B : DOWN_B + 1, cols]
                    fresh = stream[s, inner, :] + vec[j, SCALE : SCALE + 1, cols] * branch
                    if ends_section:
                        rounded = fresh.astype(BF16)
                        out_v[lax.div(j, 2), rows, cols] = fresh
                        x_v[rows, cols] = rounded
                        fresh = rounded.astype(F32)
                    stream[s, inner, :] = fresh
                return c

            @pl.when(lax.rem(j, 2) == 1)
            def _():
                lax.fori_loop(0, frames // TILE, functools.partial(finish, True), 0, unroll=min(unroll, 2))

            @pl.when(lax.rem(j, 2) == 0)
            def _():
                lax.fori_loop(0, frames // TILE, functools.partial(finish, False), 0, unroll=min(unroll, 2))

            @pl.when(j == 1)
            def _():
                send_row(core, 0, out_v.at[0], kept.at[micro], other.at[row], s_sem.at[0])

            return carry

        lax.fori_loop(0, layers, layer, 0)
        send_row(core, 1, out_v.at[1], kept.at[micro], other.at[row], s_sem.at[1])
        pltpu.make_async_copy(x_v, send, s_sem.at[2]).start()
        for j in range(layers):
            pltpu.make_async_copy(hid_v.at[j], hid.at[row, j], o_sem.at[j, 0]).wait()
            pltpu.make_async_copy(dge_v.at[j], dge.at[row, j], o_sem.at[j, 1]).wait()
            pltpu.make_async_copy(rst_v.at[j], rst.at[row, j], o_sem.at[j, 2]).wait()
            pltpu.make_async_copy(saved_v.at[j], saved.at[row, j], o_sem.at[j, 3]).wait()
        pltpu.make_async_copy(out_v.at[0], other.at[row], s_sem.at[0]).wait()
        pltpu.make_async_copy(out_v.at[1], other.at[row], s_sem.at[1]).wait()
        pltpu.make_async_copy(x_v, send, s_sem.at[2]).wait()


SUMS, HEAD = 4, 1
DOWN, UP = 0, 1
VECTORS = 16


def send_sums(core, section, owners, kind, layer, source, vectors, targets, sem):
    kept, kept_last, head, tail = targets
    _, _, block, width = kept.shape
    shares = kept.shape[0] + 1
    size = (block - VECTORS) // 2
    first = 0 if kind == DOWN else size + VECTORS
    columns = source.shape[1] // width
    rows = size // columns
    for stop in range(shares):
        owner = owners[2 * kind + layer, stop]
        pieces = [
            (source.at[pl.ds(pl.multiple_of(owner * rows, 16), rows), pl.ds(b * width, width)], pl.ds(first + b * rows, rows))
            for b in range(columns)
        ]
        if vectors is not None:
            pieces.append((vectors.at[owners[2 * DOWN + layer, stop]], pl.ds(size, VECTORS)))
        for piece, place in pieces:

            @pl.when(core == section)
            def _():
                target = kept.at[stop, layer] if stop < shares - 1 else kept_last.at[layer]
                pltpu.make_async_copy(piece, target.at[place], sem).start()

            @pl.when(core != section)
            def _():
                target = head.at[stop, layer] if stop < HEAD else tail.at[stop - HEAD, layer]
                pltpu.make_async_copy(piece, target.at[place], sem).start()


def pack_vectors(sums, packed):
    shares, _, width = packed.shape
    parts = [sums[r : r + 1, :] for r in range(UP_B, VEC_ROWS - 1)]
    wide = jnp.broadcast_to(jnp.concatenate(parts, axis=1), (8, width * len(parts)))
    size, wide_size = width // shares, width * len(parts) // shares
    is_bias = lax.broadcasted_iota(jnp.int32, (VECTORS, width), 0) == UP_B
    for d in range(shares):
        part = sums if d == 0 else pltpu.roll(sums, width - d * size, 1)
        bias = wide if d == 0 else pltpu.roll(wide, wide.shape[1] - d * wide_size, 1)
        packed[d] = jnp.where(is_bias, jnp.broadcast_to(bias[0:1, :width], (VECTORS, width)), part).astype(BF16)


def backward_kernel(final, aliased, ties, riders, flags, g_one, g_two, seg_hbm, vec, own_up, own_down, peer_up, peer_down, dge, saved, rst, *rest):
    if final:
        owners, hid, down_in, up_in, vec_in = rest[:5]
        rest = rest[5 + ties + aliased :]
        sums_out, (kept, other) = rest[:SUMS], rest[SUMS : SUMS + 2]
        rest = rest[SUMS + 2 :]
    else:
        rest = rest[aliased:]
        gb, gp, vec_out, kept, other, send = rest[:6]
        rest = rest[6 + riders :]
    (up_v, down_v, dge_v, saved_v, rst_v, gb_v, gp_v, vg_v, g_now, fresh_v, gn_v, padded, x_v, seg_v, masks, w_sem, in_sem, g_sem, o_sem, s_sem) = rest[:20]
    if final:
        (hid_v, nrm_v, dwd_v, dwu_v, down_e, up_e, early_v, packed, b_sem) = rest[20:]
    frames, width = g_now.shape
    held, _, hidden = dge_v.shape
    layers = vec.shape[0]
    nt = (((1,), (1,)), ((), ()))
    tn = (((0,), (0,)), ((), ()))
    tall = 2 * TILE
    cols_of = slabs(width)

    @pl.when(flags[0] == 1)
    def _():
        core, micro, row = flags[1], flags[2], flags[3]
        pltpu.make_async_copy(seg_hbm.at[micro], seg_v.at[pl.ds(PAD, frames)], in_sem).start()

        def fetch(j):
            h = lax.rem(j, held)
            start_weights(core, j, own_down, peer_down, down_v.at[h], w_sem.at[h, 1])
            pltpu.make_async_copy(dge.at[row, j], dge_v.at[h], w_sem.at[h, 3]).start()
            start_weights(core, j, own_up, peer_up, up_v.at[h], w_sem.at[h, 0])
            pltpu.make_async_copy(rst.at[row, j], rst_v.at[h], w_sem.at[h, 4]).start()
            pltpu.make_async_copy(saved.at[row, j, 0:2], saved_v.at[h], w_sem.at[h, 2]).start()

        if final:
            pltpu.make_async_copy(vec_in.at[1 - row], early_v, s_sem.at[2]).start()
        source = [pltpu.make_async_copy(g, x_v, g_sem) for g in (g_one, g_two)]
        for k in range(2):

            @pl.when(flags[4] == k)
            def _():
                source[k].start()

        fetch(layers - 1)
        clear_edges(padded, frames)
        source[0].wait()
        for cols in cols_of:

            def enter(t, c):
                rows = pl.ds(pl.multiple_of(t * tall, tall), tall)
                scaled = (vec[layers - 1, SCALE : SCALE + 1, cols] * x_v[rows, cols].astype(F32)).astype(BF16)
                gb_v[layers, 0, rows, cols] = scaled
                return c + fold(scaled.astype(F32))

            total = lax.fori_loop(0, frames // tall, enter, jnp.zeros((8, LANES), F32))
            vg_v[layers, DOWN_B : DOWN_B + 1, cols] = jnp.sum(total, axis=0, keepdims=True)
        pltpu.make_async_copy(seg_hbm.at[0], seg_v.at[pl.ds(PAD, frames)], in_sem).wait()
        build_masks(seg_v, masks)

        def layer(step, carry):
            j = layers - 1 - step
            h = lax.rem(j, held)
            if not final:
                pltpu.make_async_copy(gb_v.at[j + 1, 0], gb.at[row, j], o_sem.at[j, 0]).start()
            pltpu.make_async_copy(own_down.at[0], down_v.at[h], w_sem.at[h, 1]).wait()
            pltpu.make_async_copy(dge.at[0, 0], dge_v.at[h], w_sem.at[h, 3]).wait()
            if final:
                pltpu.make_async_copy(hid.at[row, j], hid_v.at[h], b_sem.at[h, 0]).start()
                pltpu.make_async_copy(down_in.at[j], down_e.at[h], b_sem.at[h, 1]).start()
                pltpu.make_async_copy(saved.at[row, j, NORMED], nrm_v.at[h], b_sem.at[h, 2]).start()
                pltpu.make_async_copy(up_in.at[j], up_e.at[h], b_sem.at[h, 3]).start()
            for n in range(hidden // COLS):
                cols = slice(n * COLS, (n + 1) * COLS)
                value = lax.dot_general(gb_v[j + 1, 0], down_v[h, cols, :], nt, preferred_element_type=F32)
                rounded = (value * dge_v[h, :, cols].astype(F32)).astype(BF16)
                gp_v[h, 0, :, cols] = rounded
                at, start = UP_B + n * COLS // width, (n * COLS) % width
                vg_v[j + 1, at : at + 1, start : start + COLS] = jnp.sum(rounded.astype(F32), axis=0, keepdims=True)
            if not final:
                pltpu.make_async_copy(gp_v.at[h, 0], gp.at[row, j], o_sem.at[j, 1]).start()
            pltpu.make_async_copy(own_up.at[0], up_v.at[h], w_sem.at[h, 0]).wait()
            gn_v[...] = lax.dot_general(gp_v[h, 0], up_v[h], nt, preferred_element_type=F32)
            pltpu.make_async_copy(rst.at[0, 0], rst_v.at[h], w_sem.at[h, 4]).wait()
            pltpu.make_async_copy(saved.at[0, 0, 0:2], saved_v.at[h], w_sem.at[h, 2]).wait()

            @pl.when(j > 0)
            def _():
                fetch(j - 1)

            if final:
                pltpu.make_async_copy(hid.at[0, 0], hid_v.at[h], b_sem.at[h, 0]).wait()
                pltpu.make_async_copy(down_in.at[0], down_e.at[h], b_sem.at[h, 1]).wait()

                @pl.when(j + held < layers)
                def _():
                    pltpu.make_async_copy(dwd_v.at[h], dwd_v.at[h], o_sem.at[h, 0]).wait()
                    pltpu.make_async_copy(dwu_v.at[h], dwu_v.at[h], o_sem.at[h, 1]).wait()
                    pltpu.make_async_copy(packed.at[h], packed.at[h], o_sem.at[h, 1]).wait()

            def down_chunk(n):
                rows = slice(n * COLS, (n + 1) * COLS)
                value = lax.dot_general(hid_v[h, :, rows], gb_v[j + 1, 0], tn, preferred_element_type=F32) + down_e[h, rows, :].astype(F32)
                dwd_v[h, rows, :] = value.astype(BF16)
                return fold(value * down_v[h, rows, :].astype(F32))

            def up_chunk(m, n):
                rows = slice(m * COLS, (m + 1) * COLS)
                cols = slice(n * width, (n + 1) * width)
                value = lax.dot_general(nrm_v[h, :, rows], gp_v[h, 0, :, cols], tn, preferred_element_type=F32) + up_e[h, rows, cols].astype(F32)
                dwu_v[h, rows, cols] = value.astype(BF16)

            odd = lax.rem(j, 2) == 1

            def norm_back(t, c):
                base = t * TILE if isinstance(t, int) else pl.multiple_of(t * TILE, TILE)
                rows = pl.ds(base, TILE)
                inner = pl.ds(base + PAD if isinstance(t, int) else pl.multiple_of(base + PAD, 8), TILE)
                grads = [gn_v[rows, cols] for cols in cols_of]
                xhats = [saved_v[h, XHAT, rows, cols].astype(F32) for cols in cols_of]
                qs = [grad * vec[j, GAIN : GAIN + 1, cols] for grad, cols in zip(grads, cols_of)]
                mean_q = row_sum(qs) * (1.0 / width)
                mean_qx = row_sum([q * xhat for q, xhat in zip(qs, xhats)]) * (1.0 / width)
                rstd = rst_v[h, rows, :]
                out = []
                for s, cols in enumerate(cols_of):
                    grad_conv = rstd * (qs[s] - mean_q - xhats[s] * mean_qx)
                    padded[s, inner, :] = grad_conv
                    g_now[rows, cols] = jnp.where(odd, x_v[rows, cols].astype(F32), fresh_v[rows, cols])
                    out += [c[3 * s] + fold(grads[s] * xhats[s]), c[3 * s + 1] + fold(grads[s]), c[3 * s + 2] + fold(grad_conv)]
                return tuple(out)

            sums = (jnp.zeros((8, LANES), F32),) * (3 * len(cols_of))
            tiles = frames // TILE
            if final:
                parts = hidden // COLS
                scale = jnp.zeros((8, width), F32)
                done = 0
                for n in range(parts):
                    scale = scale + down_chunk(n)
                    while done < tiles * (n + 1) // parts:
                        sums = norm_back(done, sums)
                        done += 1
                vg_v[j + 1, SCALE : SCALE + 1, :] = jnp.sum(scale, axis=0, keepdims=True)
                send_sums(core, lax.div(j, 2), owners, DOWN, lax.rem(j, 2), dwd_v.at[h], None, sums_out, o_sem.at[h, 0])
                pltpu.make_async_copy(saved.at[0, 0, 0], nrm_v.at[h], b_sem.at[h, 2]).wait()
                pltpu.make_async_copy(up_in.at[0], up_e.at[h], b_sem.at[h, 3]).wait()
            else:
                sums = lax.fori_loop(0, tiles, norm_back, sums, unroll=8)
            for s, cols in enumerate(cols_of):
                for k, at in enumerate((GAIN, SHIFT, CONV_B)):
                    vg_v[j + 1, at : at + 1, cols] = jnp.sum(sums[3 * s + k], axis=0, keepdims=True)

            @pl.when(odd & (step > 0))
            def _():
                pltpu.make_async_copy(fresh_v, other.at[row], s_sem.at[0]).wait()

            below = lax.max(j - 1, 0)
            for s, cols in enumerate(cols_of):

                def conv_back(t, c):
                    base = t * tall if isinstance(t, int) else pl.multiple_of(t * tall, tall)
                    rows = pl.ds(base, tall)
                    source = saved_v[h, STREAM, rows, cols].astype(F32)
                    centre = padded[s, pl.ds(base + PAD if isinstance(t, int) else pl.multiple_of(base + PAD, 8), tall), :]
                    total = g_now[rows, cols] + vec[j, 3:4, cols] * centre
                    taps = [None] * 7
                    taps[3] = c[3] + fold(centre * source)
                    for offset in OFFSETS:
                        term = padded[s, pl.ds(base + PAD - offset, tall), :] * masks[MASK_OF[-offset], rows, :]
                        total = total + vec[j, offset + 3 : offset + 4, cols] * term
                        taps[offset + 3] = c[offset + 3] + fold(term * source)
                    rounded = total.astype(BF16)
                    fresh_v[rows, cols] = total
                    x_v[rows, cols] = rounded
                    scaled = (vec[below, SCALE : SCALE + 1, cols] * jnp.where(odd, total, rounded.astype(F32))).astype(BF16)
                    gb_v[j, 0, rows, cols] = scaled
                    return tuple(taps) + (c[7] + fold(scaled.astype(F32)),)

                sums = (jnp.zeros((8, LANES), F32),) * 8
                if final:
                    chunks = [(m, n) for m in range(width // COLS) for n in range(hidden // width)]
                    each = -(-len(chunks) // len(cols_of))
                    mine = chunks[s * each : (s + 1) * each]
                    done = 0
                    for k, (m, n) in enumerate(mine):
                        up_chunk(m, n)
                        while done < frames // tall * (k + 1) // len(mine):
                            sums = conv_back(done, sums)
                            done += 1
                    while done < frames // tall:
                        sums = conv_back(done, sums)
                        done += 1
                else:
                    sums = lax.fori_loop(0, frames // tall, conv_back, sums, unroll=8)
                for k in range(7):
                    vg_v[j + 1, k : k + 1, cols] = jnp.sum(sums[k], axis=0, keepdims=True)
                vg_v[j, DOWN_B : DOWN_B + 1, cols] = jnp.sum(sums[7], axis=0, keepdims=True)
            if final:

                @pl.when(step == 0)
                def _():
                    pltpu.make_async_copy(vec_in.at[0], early_v, s_sem.at[2]).wait()

                pack_vectors(vg_v[j + 1] + early_v[j], packed.at[h])
                send_vectors = packed.at[h]
                send_sums(core, lax.div(j, 2), owners, UP, lax.rem(j, 2), dwu_v.at[h], send_vectors, sums_out, o_sem.at[h, 1])

            @pl.when(jnp.logical_not(odd))
            def _():
                send_row(core, lax.div(j, 2), fresh_v, kept.at[micro], other.at[row], s_sem.at[0])

            return carry

        for i in range(1, layers + 1):
            vg_v[i, SCALE : SCALE + 1, :] = jnp.zeros((1, width), F32)
            vg_v[i, VEC_ROWS - 1 : VEC_ROWS, :] = jnp.zeros((1, width), F32)
        lax.fori_loop(0, layers, layer, 0)
        if final:
            for h in range(held):
                pltpu.make_async_copy(dwd_v.at[h], dwd_v.at[h], o_sem.at[h, 0]).wait()
                pltpu.make_async_copy(dwu_v.at[h], dwu_v.at[h], o_sem.at[h, 1]).wait()
                pltpu.make_async_copy(packed.at[h], packed.at[h], o_sem.at[h, 1]).wait()
        else:
            pltpu.make_async_copy(vg_v.at[pl.ds(1, layers)], vec_out.at[row], s_sem.at[2]).start()
            pltpu.make_async_copy(x_v, send, s_sem.at[1]).start()
            for j in range(layers):
                pltpu.make_async_copy(gb_v.at[j + 1, 0], gb.at[row, j], o_sem.at[j, 0]).wait()
                pltpu.make_async_copy(gp_v.at[j, 0], gp.at[row, j], o_sem.at[j, 1]).wait()
            pltpu.make_async_copy(x_v, send, s_sem.at[1]).wait()
            pltpu.make_async_copy(vg_v.at[pl.ds(1, layers)], vec_out.at[row], s_sem.at[2]).wait()
        pltpu.make_async_copy(fresh_v, other.at[row], s_sem.at[0]).wait()


def early_kernel(flags, hid, gb, saved, gp, down_out, up_out, hid_v, gb_v, nrm_v, gp_v, dwd_v, dwu_v, sem, o_sem):
    frames, width = gb_v.shape[1:]
    hidden = hid_v.shape[2]
    layers = hid.shape[1]
    tn = (((0,), (0,)), ((), ()))

    @pl.when(flags[0] == 1)
    def _():
        row = flags[3]

        def copies(j, h):
            pairs = ((hid.at[row, j], hid_v), (gb.at[row, j], gb_v), (saved.at[row, j, NORMED], nrm_v), (gp.at[row, j], gp_v))
            return [pltpu.make_async_copy(a, b.at[h], sem.at[h, k]) for k, (a, b) in enumerate(pairs)]

        def leaving(j, h):
            return [
                pltpu.make_async_copy(dwd_v.at[h], down_out.at[j], o_sem.at[h, 0]),
                pltpu.make_async_copy(dwu_v.at[h], up_out.at[j], o_sem.at[h, 1]),
            ]

        for copy in copies(layers - 1, (layers - 1) % 2):
            copy.start()

        def layer(step, carry):
            j = layers - 1 - step
            h = lax.rem(j, 2)

            @pl.when(j > 0)
            def _():
                for copy in copies(j - 1, 1 - h):
                    copy.start()

            for copy in copies(j, h):
                copy.wait()

            @pl.when(j + 2 < layers)
            def _():
                for copy in leaving(j + 2, h):
                    copy.wait()

            def down_chunk(n, c):
                rows = pl.ds(pl.multiple_of(n * width, width), width)
                dwd_v[h, rows, :] = lax.dot_general(hid_v[h, :, rows], gb_v[h], tn, preferred_element_type=F32).astype(BF16)
                return c

            def up_chunk(n, c):
                cols = pl.ds(pl.multiple_of(n * width, width), width)
                dwu_v[h, :, cols] = lax.dot_general(nrm_v[h], gp_v[h, :, cols], tn, preferred_element_type=F32).astype(BF16)
                return c

            lax.fori_loop(0, hidden // width, down_chunk, 0)
            lax.fori_loop(0, hidden // width, up_chunk, 0)
            for copy in leaving(j, h):
                copy.start()
            return carry

        lax.fori_loop(0, layers, layer, 0)
        for h in range(2):
            for copy in leaving(h, h):
                copy.wait()


def weight_kernel(ties, flags, owners, own_down, peer_down, all_hid, all_gb, all_saved, all_gp, vec_in, *rest):
    rest = rest[ties:]
    sums_out, rest = rest[:SUMS], rest[SUMS:]
    hid_v, gb_v, nrm_v, gp_v, down_v, dwd_v, dwu_v, vec_v, packed, sem, o_sem, s_sem = rest
    frames, width = gb_v.shape[2:]
    hidden = hid_v.shape[3]
    layers = all_hid.shape[1]
    tn = (((0,), (0,)), ((), ()))

    @pl.when(flags[0] == 1)
    def _():
        core = flags[1]

        def copies(j, h):
            pairs = []
            for row in range(2):
                pairs += [
                    (all_hid.at[row, j], hid_v.at[h, row]),
                    (all_gb.at[row, j], gb_v.at[h, row]),
                    (all_saved.at[row, j, NORMED], nrm_v.at[h, row]),
                    (all_gp.at[row, j], gp_v.at[h, row]),
                ]
            return [pltpu.make_async_copy(a, b, sem.at[h, k]) for k, (a, b) in enumerate(pairs)]

        def fetch(j):
            h = lax.rem(j, 2)
            start_weights(core, j, own_down, peer_down, down_v.at[h], sem.at[h, 8])
            for copy in copies(j, h):
                copy.start()

        fetch(layers - 1)
        pltpu.make_async_copy(vec_in, vec_v, s_sem).start()
        pltpu.make_async_copy(vec_in, vec_v, s_sem).wait()

        def layer(step, carry):
            j = layers - 1 - step
            h = lax.rem(j, 2)

            @pl.when(j > 0)
            def _():
                fetch(j - 1)

            pltpu.make_async_copy(own_down.at[0], down_v.at[h], sem.at[h, 8]).wait()
            for copy in copies(j, h):
                copy.wait()

            @pl.when(j + 2 < layers)
            def _():
                pltpu.make_async_copy(dwd_v.at[h], dwd_v.at[h], o_sem.at[h, 0]).wait()
                pltpu.make_async_copy(dwu_v.at[h], dwu_v.at[h], o_sem.at[h, 1]).wait()
                pltpu.make_async_copy(packed.at[h], packed.at[h], o_sem.at[h, 1]).wait()

            def down_chunk(n, scale):
                rows = pl.ds(pl.multiple_of(n * COLS, COLS), COLS)
                left = hid_v[h, :, :, rows].reshape(2 * frames, COLS)
                value = lax.dot_general(left, gb_v[h].reshape(2 * frames, width), tn, preferred_element_type=F32)
                dwd_v[h, rows, :] = value.astype(BF16)
                return scale + fold(value * down_v[h, rows, :].astype(F32))

            scale = lax.fori_loop(0, hidden // COLS, down_chunk, jnp.zeros((8, width), F32))
            scale = jnp.sum(scale, axis=0, keepdims=True)
            vectors = vec_v[0, j] + vec_v[1, j]
            is_scale = lax.broadcasted_iota(jnp.int32, vectors.shape, 0) == SCALE
            pack_vectors(jnp.where(is_scale, jnp.broadcast_to(scale, vectors.shape), vectors), packed.at[h])
            send_sums(core, lax.div(j, 2), owners, DOWN, lax.rem(j, 2), dwd_v.at[h], None, sums_out, o_sem.at[h, 0])

            def up_chunk(n, c):
                cols = pl.ds(pl.multiple_of(n * width, width), width)
                right = gp_v[h, :, :, cols].reshape(2 * frames, width)
                value = lax.dot_general(nrm_v[h].reshape(2 * frames, width), right, tn, preferred_element_type=F32)
                dwu_v[h, :, cols] = value.astype(BF16)
                return c

            lax.fori_loop(0, hidden // width, up_chunk, 0)
            send_sums(core, lax.div(j, 2), owners, UP, lax.rem(j, 2), dwu_v.at[h], packed.at[h], sums_out, o_sem.at[h, 1])
            return carry

        lax.fori_loop(0, layers, layer, 0)
        for h in range(2):
            pltpu.make_async_copy(dwd_v.at[h], dwd_v.at[h], o_sem.at[h, 0]).wait()
            pltpu.make_async_copy(dwu_v.at[h], dwu_v.at[h], o_sem.at[h, 1]).wait()
            pltpu.make_async_copy(packed.at[h], packed.at[h], o_sem.at[h, 1]).wait()


def place_kernel(at, kept_in, rows, tie, kept, held, sem):
    count = rows.shape[0]
    for i in range(count):
        pltpu.make_async_copy(rows.at[i], held.at[i], sem.at[i]).start()
    for i in range(count):
        pltpu.make_async_copy(rows.at[i], held.at[i], sem.at[i]).wait()
        pltpu.make_async_copy(held.at[i], kept.at[at[0] + i], sem.at[i]).start()
    for i in range(count):
        pltpu.make_async_copy(held.at[i], kept.at[at[0] + i], sem.at[i]).wait()


def hold_kernel(value_in, tie, value):
    pass


def final_kernel(down_0, down_1, up_0, up_1, kept, other, scales, *rest):
    conv_out, conv_b_out, gain_out, shift_out, up_out, up_b_out, down_out, down_b_out, scale_out = rest
    size, wide = conv_b_out.shape[1], up_b_out.shape[1]
    rows, width = down_out.shape[1:]
    for layer, (down, up) in enumerate(((down_0, up_0), (down_1, up_1))):
        total = down[...].astype(F32) + kept[layer, : rows + VECTORS].astype(F32) + other[layer, : rows + VECTORS].astype(F32)
        down_out[layer] = total[:rows]
        vectors = total[rows:]
        at = slice(layer, layer + 1)
        conv_out[layer] = vectors[:CONV_B, :size]
        conv_b_out[at, :] = vectors[CONV_B : CONV_B + 1, :size]
        gain_out[at, :] = vectors[GAIN : GAIN + 1, :size]
        shift_out[at, :] = vectors[SHIFT : SHIFT + 1, :size]
        down_b = vectors[DOWN_B : DOWN_B + 1, :size]
        down_b_out[at, :] = down_b
        scale_out[at, :] = (vectors[SCALE : SCALE + 1, :size] + scales[0, at, :] * down_b) / scales[1, at, :]
        up_b_out[at, :] = vectors[UP_B : UP_B + 1, :wide]
        total = up[...].astype(F32) + kept[layer, rows + VECTORS :].astype(F32) + other[layer, rows + VECTORS :].astype(F32)
        for b in range(up_out.shape[2] // width):
            up_out[layer, :, b * width : (b + 1) * width] = total[b * size : (b + 1) * size]


ANY = pl.BlockSpec(memory_space=pl.ANY)
HBM = pl.BlockSpec(memory_space=pltpu.HBM)
SMEM = pl.BlockSpec(memory_space=pltpu.SMEM)
VMEM = pl.BlockSpec(memory_space=pltpu.VMEM)


def near(value):
    return pltpu.with_memory_space_constraint(value, pltpu.VMEM)


def run_forward(flags, x, seg, vec, weights, earlier, unroll=16):
    layers = vec.shape[0]
    micro = seg.shape[0]
    frames, width = x.shape
    hidden = weights[0].shape[2]
    shapes = (
        jax.ShapeDtypeStruct((2, layers, frames, hidden), BF16),
        jax.ShapeDtypeStruct((2, layers, frames, hidden), BF16),
        jax.ShapeDtypeStruct((2, layers, KINDS, frames, width), BF16),
        jax.ShapeDtypeStruct((2, layers, frames, LANES), F32),
        jax.ShapeDtypeStruct((micro, frames, width), F32),
        jax.ShapeDtypeStruct((2, frames, width), F32),
        jax.ShapeDtypeStruct((frames, width), BF16),
    )
    aliased = len(earlier)
    return pl.pallas_call(
        functools.partial(forward_kernel, layers, aliased, unroll),
        out_shape=shapes,
        in_specs=[SMEM, ANY, ANY, VMEM] + [ANY] * (4 + aliased),
        out_specs=(ANY,) * len(shapes),
        input_output_aliases={8 + i: i for i in range(aliased)},
        scratch_shapes=[
            pltpu.VMEM((layers, width, hidden), BF16),
            pltpu.VMEM((layers, hidden, width), BF16),
            pltpu.VMEM((layers, frames, hidden), BF16),
            pltpu.VMEM((layers, frames, hidden), BF16),
            pltpu.VMEM((layers, KINDS, frames, width), BF16),
            pltpu.VMEM((layers, frames, LANES), F32),
            pltpu.VMEM((width // LANES, frames + 2 * PAD, LANES), F32),
            pltpu.VMEM((frames, width), F32),
            pltpu.VMEM((2, frames, width), F32),
            pltpu.VMEM((frames, width), BF16),
            pltpu.VMEM((frames + 2 * PAD, LANES), F32),
            pltpu.VMEM((6, frames, LANES), F32),
            pltpu.SemaphoreType.DMA((layers, 2)),
            pltpu.SemaphoreType.DMA,
            pltpu.SemaphoreType.DMA((layers, 4)),
            pltpu.SemaphoreType.DMA((3,)),
        ],
        compiler_params=pltpu.CompilerParams(vmem_limit_bytes=VMEM_LIMIT),
        cost_estimate=COST,
    )(flags, x, seg, vec, *weights, *earlier)


def sum_shapes(shares, hidden, width):
    block = (2, 2 * (hidden // shares) + VECTORS, width)
    return tuple(jax.ShapeDtypeStruct(shape, BF16) for shape in ((shares - 1, *block), block, (HEAD, *block), (shares - HEAD, *block)))


def run_backward(flags, g, seg, vec, weights, state, earlier, final=(), ties=(), riders=()):
    frames, width = g[0].shape
    hidden = weights[0].shape[2]
    layers, micro = vec.shape[0], seg.shape[0]
    held = 2 if final else layers
    grads = (
        jax.ShapeDtypeStruct((micro, frames, width), F32),
        jax.ShapeDtypeStruct((2, frames, width), F32),
    )
    if final:
        shapes = (*sum_shapes(final[0].shape[1], hidden, width), *grads)
    else:
        shapes = (
            jax.ShapeDtypeStruct((2, layers, frames, width), BF16),
            jax.ShapeDtypeStruct((2, layers, frames, hidden), BF16),
            jax.ShapeDtypeStruct((2, layers, VEC_ROWS, width), F32),
            *grads,
            jax.ShapeDtypeStruct((frames, width), BF16),
        )
    earlier = (*earlier, *riders)
    shapes = (*shapes, *(jax.ShapeDtypeStruct(rider.shape, rider.dtype) for rider in riders))
    aliased = len(earlier)
    targets = [*range(len(earlier) - len(riders)), *range(len(shapes) - len(riders), len(shapes))]
    scratch = [
        pltpu.VMEM((held, width, hidden), BF16),
        pltpu.VMEM((held, hidden, width), BF16),
        pltpu.VMEM((held, frames, hidden), BF16),
        pltpu.VMEM((held, 2, frames, width), BF16),
        pltpu.VMEM((held, frames, LANES), F32),
        pltpu.VMEM((layers + 1, 1, frames, width), BF16),
        pltpu.VMEM((held, 1, frames, hidden), BF16),
        pltpu.VMEM((layers + 1, VEC_ROWS, width), F32),
        pltpu.VMEM((frames, width), F32),
        pltpu.VMEM((frames, width), F32),
        pltpu.VMEM((frames, width), F32),
        pltpu.VMEM((width // LANES, frames + 2 * PAD, LANES), F32),
        pltpu.VMEM((frames, width), BF16),
        pltpu.VMEM((frames + 2 * PAD, LANES), F32),
        pltpu.VMEM((6, frames, LANES), F32),
        pltpu.SemaphoreType.DMA((held, 5)),
        pltpu.SemaphoreType.DMA,
        pltpu.SemaphoreType.DMA,
        pltpu.SemaphoreType.DMA((held, 2)),
        pltpu.SemaphoreType.DMA((3,)),
    ]
    if final:
        scratch += [
            pltpu.VMEM((held, frames, hidden), BF16),
            pltpu.VMEM((held, frames, width), BF16),
            pltpu.VMEM((held, hidden, width), BF16),
            pltpu.VMEM((held, width, hidden), BF16),
            pltpu.VMEM((held, hidden, width), BF16),
            pltpu.VMEM((held, width, hidden), BF16),
            pltpu.VMEM((layers, VEC_ROWS, width), F32),
            pltpu.VMEM((held, final[0].shape[1], VECTORS, width), BF16),
            pltpu.SemaphoreType.DMA((held, 4)),
        ]
    first_alias = 12 + len(final) + len(ties)
    return pl.pallas_call(
        functools.partial(backward_kernel, bool(final), aliased, len(ties), len(riders)),
        out_shape=shapes,
        in_specs=[SMEM, ANY, ANY, ANY, VMEM] + [ANY] * 7 + ([SMEM] + [ANY] * 4 if final else []) + [ANY] * (len(ties) + aliased),
        out_specs=tuple(HBM if final and k < SUMS else ANY for k in range(len(shapes))),
        input_output_aliases={first_alias + i: target for i, target in enumerate(targets)},
        scratch_shapes=scratch,
        compiler_params=pltpu.CompilerParams(vmem_limit_bytes=VMEM_LIMIT),
        cost_estimate=COST,
    )(flags, *g, seg, vec, *weights, *state, *final, *ties, *earlier)


def run_early(flags, hid, gb, saved, gp):
    _, layers, frames, hidden = hid.shape
    width = gb.shape[3]
    return pl.pallas_call(
        early_kernel,
        out_shape=(jax.ShapeDtypeStruct((layers, hidden, width), BF16), jax.ShapeDtypeStruct((layers, width, hidden), BF16)),
        in_specs=[SMEM] + [ANY] * 4,
        out_specs=(ANY,) * 2,
        scratch_shapes=[
            pltpu.VMEM((2, frames, hidden), BF16),
            pltpu.VMEM((2, frames, width), BF16),
            pltpu.VMEM((2, frames, width), BF16),
            pltpu.VMEM((2, frames, hidden), BF16),
            pltpu.VMEM((2, hidden, width), BF16),
            pltpu.VMEM((2, width, hidden), BF16),
            pltpu.SemaphoreType.DMA((2, 4)),
            pltpu.SemaphoreType.DMA((2, 2)),
        ],
        compiler_params=pltpu.CompilerParams(vmem_limit_bytes=VMEM_LIMIT),
        cost_estimate=COST,
    )(flags, hid, gb, saved, gp)


def run_weights(flags, owners, weights, hid, gb, saved, gp, vectors, ties):
    _, layers, frames, hidden = hid.shape
    width = gb.shape[3]
    shares = owners.shape[1]
    return pl.pallas_call(
        functools.partial(weight_kernel, len(ties)),
        out_shape=sum_shapes(shares, hidden, width),
        in_specs=[SMEM, SMEM] + [ANY] * (7 + len(ties)),
        out_specs=(HBM,) * SUMS,
        scratch_shapes=[
            pltpu.VMEM((2, 2, frames, hidden), BF16),
            pltpu.VMEM((2, 2, frames, width), BF16),
            pltpu.VMEM((2, 2, frames, width), BF16),
            pltpu.VMEM((2, 2, frames, hidden), BF16),
            pltpu.VMEM((2, hidden, width), BF16),
            pltpu.VMEM((2, hidden, width), BF16),
            pltpu.VMEM((2, width, hidden), BF16),
            pltpu.VMEM(vectors.shape, F32),
            pltpu.VMEM((2, shares, VECTORS, width), BF16),
            pltpu.SemaphoreType.DMA((2, 9)),
            pltpu.SemaphoreType.DMA((2, 2)),
            pltpu.SemaphoreType.DMA,
        ],
        compiler_params=pltpu.CompilerParams(vmem_limit_bytes=VMEM_LIMIT),
        cost_estimate=COST,
    )(flags, owners, weights[1], weights[3], hid, gb, saved, gp, vectors, *ties)


def run_place(kept, rows, at, tie):
    return pl.pallas_call(
        place_kernel,
        out_shape=jax.ShapeDtypeStruct(kept.shape, kept.dtype),
        in_specs=[SMEM, ANY, ANY, ANY],
        out_specs=ANY,
        input_output_aliases={1: 0},
        scratch_shapes=[pltpu.VMEM(rows.shape, rows.dtype), pltpu.SemaphoreType.DMA(rows.shape[:1])],
        cost_estimate=COST,
    )(at.reshape(1).astype(jnp.int32), kept, rows, tie)


def hold(value, tie):
    return pl.pallas_call(
        hold_kernel,
        out_shape=jax.ShapeDtypeStruct(value.shape, value.dtype),
        in_specs=[HBM, ANY],
        out_specs=HBM,
        input_output_aliases={0: 0},
        cost_estimate=COST,
    )(value, tie)


def run_final(down, up, kept, other, scales, shares, hidden):
    width = kept.shape[2]
    size, wide = width // shares, hidden // shares
    shapes = ((2, CONV_B, size), (2, size), (2, size), (2, size), (2, size, hidden), (2, wide), (2, wide, width), (2, size), (2, size))
    return pl.pallas_call(
        final_kernel,
        out_shape=tuple(jax.ShapeDtypeStruct(shape, F32) for shape in shapes),
        in_specs=[VMEM] * 7,
        out_specs=(VMEM,) * len(shapes),
        compiler_params=pltpu.CompilerParams(vmem_limit_bytes=VMEM_LIMIT // 2),
        cost_estimate=COST,
    )(*down, *up, kept, other, scales)


def ring_order(count):
    return list(range(0, count, 2)) + list(range(count - 1, 0, -2))


def ring_owners(ways, axis):
    count = lax.axis_size(axis)
    device = lax.axis_index(axis)
    mine = jnp.where(device % 2 == 0, device // 2, count - 1 - device // 2)
    places = jnp.stack([lax.rem(mine - way * (1 + jnp.arange(count, dtype=jnp.int32)) + 2 * count, count) for way in ways])
    return jnp.where(places < count - count // 2, 2 * places, 2 * (count - places) - 1)


def after(value, earlier):
    return lax.optimization_barrier((value, earlier))[0]


def ring_step(flows, ways, axis):
    count = lax.axis_size(axis)
    order = ring_order(count)
    return [
        lax.ppermute(value, axis, [(order[p], order[(p + way) % count]) for p in range(count)]) for value, way in zip(flows, ways)
    ]


def per_device(
    inputs,
    segment_ids,
    cotangent,
    conv_weight,
    conv_bias,
    norm_gain,
    norm_bias,
    up_weight,
    up_bias,
    down_weight,
    down_bias,
    layer_scale,
):
    micro, _, frames, width = inputs.shape
    hidden = up_weight.shape[2]
    shares = lax.axis_size("dp")
    section = lax.axis_index("section")
    chip, core = section // 2, section % 2
    exchange = [(0, 1), (1, 0), (2, 3), (3, 2)]

    small = jnp.concatenate(
        [
            conv_weight,
            conv_bias[:, None],
            norm_gain[:, None],
            norm_bias[:, None],
            down_bias[:, None],
            layer_scale[:, None],
            up_bias.reshape(2, -1, width),
            jnp.zeros((2, 1, width), BF16),
        ],
        axis=1,
    )
    small_peer = lax.ppermute(small, "section", exchange)
    up_peer = lax.ppermute(up_weight, "section", exchange)
    down_peer = lax.ppermute(down_weight, "section", exchange)
    vec = jnp.where(core == 0, jnp.concatenate([small, small_peer]), jnp.concatenate([small_peer, small])).astype(F32)
    weights = (up_weight, down_weight, up_peer, down_peer)
    masks = jnp.broadcast_to(segment_ids[:, 0, :, None].astype(F32), (micro, frames, LANES))
    inputs, cotangent = inputs[:, 0], cotangent[:, 0]

    def flags(active, row, choice=0):
        return jnp.stack([jnp.asarray(v, jnp.int32) for v in (active, core, 2 * core + row, row, choice)])

    first, last = chip == 0, chip == 1
    ways = ((1, -1), (-1, 1))
    owners = ring_owners([way for kind in ways for way in kind], "dp")

    def row_of(array, row):
        return lax.dynamic_index_in_dim(array, 2 * core + row, 0, keepdims=False)

    down_pairs, up_pairs = [(0, 2), (1, 3)], [(2, 0), (3, 1)]
    state = run_forward(flags(first, 0), row_of(inputs, 0), masks, vec, weights, ())
    arrived = lax.ppermute(state[6], "section", down_pairs)
    state = run_forward(flags(first, 1), row_of(inputs, 1), masks, vec, weights, state[:6], unroll=1)
    arrived_next = lax.ppermute(state[6], "section", down_pairs)
    state = run_forward(flags(last, 0), near(arrived), masks, vec, weights, state[:6])
    gradient = row_of(cotangent, 0)
    back = run_backward(flags(last, 0), (gradient, gradient), masks, vec, weights, state[1:4], ())
    returned = lax.ppermute(back[5], "section", up_pairs)
    state = run_forward(flags(last, 1), near(arrived_next), masks, vec, weights, state[:6])
    gradients = (row_of(cotangent, 1), near(returned))
    back = run_backward(flags(True, jnp.where(last, 1, 0), first), gradients, masks, vec, weights, state[1:4], back[:5], riders=state[4:6])
    returned = near(lax.ppermute(back[5], "section", up_pairs))
    gb, gp, vectors, grads_kept, grads_other, _, outputs_kept, outputs_other = back

    def assemble(mine, other, tie):
        return run_place(mine, lax.ppermute(other, "section", exchange), 2 * (1 - core), tie)[None, :, None]

    section_outputs = assemble(outputs_kept, outputs_other, vectors)
    early = run_early(flags(first, 0), state[0], gb, state[2], gp)
    sums = run_weights(flags(last, 0), owners, weights, state[0], gb, state[2], gp, vectors, (returned, section_outputs))
    shard = lax.axis_index("dp")
    scales = jnp.stack([down_bias, layer_scale]).astype(F32)
    scales = lax.dynamic_slice_in_dim(scales, shard * (width // shares), width // shares, 2)
    *sums, grads_kept, grads_other = run_backward(
        flags(first, 1),
        (returned, returned),
        masks,
        vec,
        weights,
        state[1:4],
        (*sums, grads_kept, grads_other),
        (owners, state[0], *early, vectors),
        (scales,),
    )

    kept, kept_last, head, tail = sums
    head = lax.ppermute(head, "section", exchange)
    tail = lax.ppermute(hold(tail, head), "section", exchange)
    size = hidden // shares
    spans = (slice(0, size + VECTORS), slice(size + VECTORS, None))

    def addend(stop, kind, layer):
        other = head[stop, layer, spans[kind]] if stop < HEAD else tail[stop - HEAD, layer, spans[kind]]
        return kept[stop, layer, spans[kind]].astype(F32) + other.astype(F32)

    flows = [[addend(0, kind, layer).astype(BF16) for layer in range(2)] for kind in (DOWN, UP)]
    for stop in range(1, shares):
        for kind in (DOWN, UP):
            moved = ring_step(flows[kind], ways[kind], "dp")
            if kind == DOWN or stop > 1:
                moved = after(moved, flows[1 - kind])
            if stop < shares - 1:
                moved = [(value.astype(F32) + addend(stop, kind, layer)).astype(BF16) for layer, value in enumerate(moved)]
            flows[kind] = moved
        if stop == 3:
            input_grads = assemble(grads_kept, grads_other, flows[UP][0])
    grads = run_final(flows[DOWN], flows[UP], kept_last, tail[-1], scales, shares, hidden)
    return (section_outputs, input_grads, *grads)


def solution(mesh):
    in_specs = (
        P(None, "dp", None, None),
        P(None, "dp", None),
        P(None, "dp", None, None),
        P("section", None, None),
        P("section", None),
        P("section", None),
        P("section", None),
        P("section", None, None),
        P("section", None),
        P("section", None, None),
        P("section", None),
        P("section", None),
    )
    out_specs = (
        P("section", None, "dp", None, None),
        P("section", None, "dp", None, None),
        P("section", None, "dp"),
        P("section", "dp"),
        P("section", "dp"),
        P("section", "dp"),
        P("section", "dp", None),
        P("section", "dp"),
        P("section", "dp", None),
        P("section", "dp"),
        P("section", "dp"),
    )
    return jax.shard_map(per_device, mesh=mesh, in_specs=in_specs, out_specs=out_specs, check_vma=False)
```
